32 devices in a mesh: wide: 8 (over z, x), narrow: 4 (over y, core).
Axes of the slice: x: 2, y: 2, z: 4, core: 2. Of those that a mesh axis runs over, the one named last changes fastest.
Arguments:
- features: bfloat16 [32, 20, 24, 2048], P(('wide', 'narrow')), may hold values from -40 to 40
- low_level: bfloat16 [32, 80, 96, 256], P(('wide', 'narrow')), may hold values from -40 to 40
- widths: int32 [32, 4], P(('wide', 'narrow')), may hold values from 1 to 20, 24 in all within a row
- w_point: bfloat16 [2, 2048, 256], P(None, 'wide', 'narrow'), may hold values from -0.125 to 0.125
- w_atrous: bfloat16 [3, 9, 2048, 256], P(None, None, 'wide', 'narrow'), may hold values from -0.046875 to 0.046875
- w_proj: bfloat16 [1280, 256], P('wide', 'narrow'), may hold values from -0.15625 to 0.15625
- w_low: bfloat16 [256, 48], P('wide', 'narrow'), may hold values from -0.375 to 0.375
- w_dec1: bfloat16 [9, 304, 256], P(None, 'narrow', 'wide'), may hold values from -0.109375 to 0.109375
- w_dec2: bfloat16 [9, 256, 256], P(None, 'wide', 'narrow'), may hold values from -0.125 to 0.125
- w_cls: bfloat16 [256, 21], replicated, may hold values from -0.375 to 0.375
- b_cls: float32 [21], replicated, may hold values from -3 to 3
- gains: float32 [8, 256], replicated, may hold values from 0.5 to 1.5
- biases: float32 [8, 256], replicated, may hold values from -3 to 3
- low_gain: float32 [48], replicated, may hold values from 0.5 to 1.5
- low_bias: float32 [48], replicated, may hold values from -3 to 3
- logit_grad: bfloat16 [32, 80, 96, 21], P(('wide', 'narrow')), may hold values from -6 to 6
Outputs:
- logits: bfloat16 [32, 80, 96, 21], P(('wide', 'narrow'))
- grad_features: bfloat16 [32, 20, 24, 2048], P(('wide', 'narrow'))
- grad_low_level: bfloat16 [32, 80, 96, 256], P(('wide', 'narrow'))
- grad_w_point: float32 [2, 2048, 256], P(None, 'wide', 'narrow')
- grad_w_atrous: float32 [3, 9, 2048, 256], P(None, None, 'wide', 'narrow')
- grad_w_proj: float32 [1280, 256], P('wide', 'narrow')
- grad_w_low: float32 [256, 48], P('wide', 'narrow')
- grad_w_dec1: float32 [9, 304, 256], P(None, 'narrow', 'wide')
- grad_w_dec2: float32 [9, 256, 256], P(None, 'wide', 'narrow')
- grad_w_cls: float32 [256, 21], replicated
- grad_b_cls: float32 [21], replicated
- grad_gains: float32 [8, 256], replicated
- grad_biases: float32 [8, 256], replicated
- grad_low_gain: float32 [48], replicated
- grad_low_bias: float32 [48], replicated
The draws below stay inside these ranges and needn't reach their ends.
All inputs are finite; a program needn't handle non-finite values.
Results may differ from the reference program's by a relative error of at most 0.04.
Values may be sent and summed in bfloat16 or wider, within the bound.
No kernel may reach another device: no remote copies, remote signals or barrier semaphores. Data moves between devices by JAX's collectives and lax.ppermute only.
A program may use at most 512 MiB of HBM per device.

```python
import math
from functools import partial
import jax
import jax.numpy as jnp
import numpy as np
from jax import lax

C_IN = 2048
WIDTH = 256
C_LOW_IN = 256
C_LOW = 48
CLASSES = 21
H16 = 20
W16 = 24
IMGS = 3
MOST_W = 20
CANVASES = 32
H4 = 80
W4 = 96


def rising_field(key, shape, rise):
    noise_key = jax.random.fold_in(key, 0)
    pixel_key = jax.random.fold_in(key, 2)
    channel_key = jax.random.fold_in(key, 3)
    normal_part = jnp.clip(jax.random.normal(noise_key, shape, jnp.float32), -4.0, 4.0)
    noise = normal_part
    canvas_place = jnp.arange(shape[0], dtype=jnp.float32) / max(shape[0] - 1, 1)
    canvas_scale = jnp.exp(jnp.log(rise) * canvas_place).reshape(shape[0], 1, 1, 1)
    pixel_scale = jnp.exp(jax.random.uniform(pixel_key, (shape[0], shape[1], shape[2], 1), jnp.float32, -0.693, 0.693))
    channel_mean = jax.random.uniform(channel_key, (shape[3],), jnp.float32, -1.0, 1.0)
    return jnp.clip(canvas_scale * pixel_scale * (channel_mean + noise), -40.0, 40.0)


def draw_features(key, part):
    key = jax.random.fold_in(key, 11)
    return rising_field(key, (CANVASES, H16, W16, C_IN), 3.0).astype(jnp.bfloat16)


def draw_low_level(key, part):
    key = jax.random.fold_in(key, 12)
    return rising_field(key, (CANVASES, H4, W4, C_LOW_IN), 3.0).astype(jnp.bfloat16)


def block_scale(own_key, extent, cuts, least, largest):
    level = 1.0
    for dim, parts in cuts:
        draws = jax.random.uniform(jax.random.fold_in(jax.random.fold_in(own_key, 6), dim), (parts,), jnp.float32, least / len(cuts), largest / len(cuts))
        level = level * jnp.repeat(jnp.exp(draws), extent[dim] // parts).reshape((-1,) + (1,) * (len(extent) - 1 - dim))
    return level


def profile(amount, total, reach, lean):
    loads = [(1 << 20) // math.isqrt(rank ** lean) + 1 for rank in range(2, amount + 1)]
    spare, holding = total - reach - (amount - 1), [1] * (amount - 1)
    while spare > 0:
        movable = [i for i in range(amount - 1) if holding[i] < reach]
        whole, remaining = sum([loads[i] for i in movable]), spare
        for i in movable:
            more = min(reach - holding[i], max(1, remaining * loads[i] // whole), spare)
            holding[i] = holding[i] + more
            spare = spare - more
    return np.array([reach] + holding)


def uneven(rng, amount, total, bound, lean):
    if amount == 2:
        one = jax.random.randint(rng, (), max(1, total - bound), min(bound, total - 1) + 1)
        return jnp.stack([one, total - one])
    tallies = jnp.asarray(profile(amount, total, bound, lean), jnp.int32)
    pairs = (amount - 1) // 2
    giver, sink = tallies[1:1 + 2 * pairs:2], tallies[2:2 + 2 * pairs:2]
    slack = jnp.minimum(giver - 1, bound - sink)
    moved = jax.random.randint(jax.random.fold_in(rng, 1), (pairs,), 0, 1 << 20) % (slack + 1)
    tallies = tallies.at[1:1 + 2 * pairs:2].set(giver - moved).at[2:2 + 2 * pairs:2].set(sink + moved)
    return tallies[jax.random.permutation(jax.random.fold_in(rng, 2), amount)]


def gaussian(rng, extent, deviation, bound, cuts=(), held_as=jnp.bfloat16):
    factor_of = block_scale(rng, extent, cuts, -0.22, 0.18) if cuts else 1.0
    entries = jax.random.normal(rng, extent, jnp.float32) * deviation * factor_of
    return jnp.minimum(jnp.maximum(entries, -bound), bound).astype(held_as)


def setup_inputs(seed: int = 0) -> dict:
    key_list = jax.random.split(jax.random.key(seed), 17)
    features = draw_features(jax.random.fold_in(key_list[16], 71), 0)
    low_level = draw_low_level(jax.random.fold_in(key_list[16], 71), 0)
    widths = jax.vmap(lambda own: uneven(own, IMGS + 1, W16, MOST_W, 1))(jax.random.split(key_list[2], CANVASES)).reshape((CANVASES, IMGS + 1)).astype(jnp.int32)
    w_point = gaussian(key_list[3], (2, C_IN, WIDTH), C_IN ** -0.5, 0.125, ((1, 8), (2, 4)))
    w_atrous = gaussian(key_list[4], (3, 9, C_IN, WIDTH), (9 * C_IN) ** -0.5, 0.046875, ((2, 8), (3, 4)))
    w_proj = gaussian(key_list[5], (5 * WIDTH, WIDTH), (5 * WIDTH) ** -0.5, 0.15625, ((0, 8), (1, 4)))
    w_low = gaussian(key_list[6], (C_LOW_IN, C_LOW), C_LOW_IN ** -0.5, 0.375, ((0, 8), (1, 4)))
    w_dec1 = gaussian(key_list[7], (9, WIDTH + C_LOW, WIDTH), (9 * (WIDTH + C_LOW)) ** -0.5, 0.109375, ((1, 4), (2, 8)))
    w_dec2 = gaussian(key_list[8], (9, WIDTH, WIDTH), (9 * WIDTH) ** -0.5, 0.125, ((1, 8), (2, 4)))
    w_cls = gaussian(key_list[9], (WIDTH, CLASSES), WIDTH ** -0.5, 0.375)
    b_cls = gaussian(key_list[10], (CLASSES,), 0.5, 3.0, (), jnp.float32)
    gains = jnp.clip(1.0 + 0.1 * jax.random.normal(key_list[11], (8, WIDTH), jnp.float32), 0.5, 1.5)
    biases = gaussian(key_list[12], (8, WIDTH), 0.5, 3.0, (), jnp.float32)
    low_gain = jnp.clip(1.0 + 0.1 * jax.random.normal(key_list[13], (C_LOW,), jnp.float32), 0.5, 1.5)
    low_bias = gaussian(key_list[14], (C_LOW,), 0.5, 3.0, (), jnp.float32)
    logit_grad = gaussian(key_list[15], (CANVASES, H4, W4, CLASSES), 1.0, 6.0, ((0, 32),))
    return {"features": features, "low_level": low_level, "widths": widths, "w_point": w_point, "w_atrous": w_atrous, "w_proj": w_proj, "w_low": w_low, "w_dec1": w_dec1, "w_dec2": w_dec2, "w_cls": w_cls, "b_cls": b_cls, "gains": gains, "biases": biases, "low_gain": low_gain, "low_bias": low_bias, "logit_grad": logit_grad}


@jax.custom_vjp
def low(v):
    return lax.optimization_barrier(v.astype(jnp.bfloat16)).astype(jnp.float32)

@jax.custom_vjp
def low_back(v):
    return v

def low_keep(v):
    return (low(v), None)

def low_pass(kept, grad):
    return (grad,)

def back_keep(v):
    return (v, None)

def back_low(kept, grad):
    return (low(grad),)
low.defvjp(low_keep, low_pass)
low_back.defvjp(back_keep, back_low)
epsilon = 1e-05
highest = lax.Precision.HIGHEST
dilations = (6, 12, 18)

def band_ids(widths, columns):
    ends_all = jnp.cumsum(widths, axis=1)
    position = jnp.arange(columns, dtype=jnp.int32)
    band_index = lax.optimization_barrier(jnp.sum((position[None, :, None] >= ends_all[:, None, :]).astype(jnp.int32), axis=2))
    return jnp.where(band_index < widths.shape[1] - 1, band_index, -1).astype(jnp.int32)

def shifted(values, row_shift, col_shift):
    height = values.shape[1]
    columns = values.shape[2]
    padded = jnp.pad(values, ((0, 0), (abs(row_shift), abs(row_shift)), (abs(col_shift), abs(col_shift)), (0, 0)))
    row_start = abs(row_shift) + row_shift
    col_start = abs(col_shift) + col_shift
    return padded[:, row_start:row_start + height, col_start:col_start + columns, :]

def tap_mask(image_ids, height, row_shift, col_shift):
    columns = image_ids.shape[1]
    padded = jnp.pad(image_ids, ((0, 0), (abs(col_shift), abs(col_shift))), constant_values=-2)
    col_start = abs(col_shift) + col_shift
    other_ids = padded[:, col_start:col_start + columns]
    same_image = (other_ids == image_ids).astype(jnp.float32)
    row_place = jnp.arange(height) + row_shift
    inside = ((row_place >= 0) & (row_place < height)).astype(jnp.float32)
    return (inside[None, :, None] * same_image[:, None, :])[..., None]

def masked_conv(values, kernel, image_ids, dilation):
    running = None
    for tap_index in range(9):
        row_shift = (tap_index // 3 - 1) * dilation
        col_shift = (tap_index % 3 - 1) * dilation
        product = jnp.einsum('nhwc,cd->nhwd', values, kernel[tap_index], precision=highest)
        term = tap_mask(image_ids, values.shape[1], row_shift, col_shift) * shifted(product, row_shift, col_shift)
        running = term if running is None else running + term
    return running

def linear_weights(out_count, in_count):
    position = jnp.arange(out_count, dtype=jnp.int32)
    scaled = 2 * position - 3
    left_index = jnp.floor_divide(scaled, 8).astype(jnp.int32)
    fraction = (scaled - 8 * left_index).astype(jnp.float32) / 8.0
    lower_index = jnp.clip(left_index, 0, in_count - 1).astype(jnp.int32)
    upper_index = jnp.clip(left_index + 1, 0, in_count - 1).astype(jnp.int32)
    return (position, lower_index, upper_index, fraction)

def row_table(out_count, in_count):
    position, lower_index, upper_index, fraction = linear_weights(out_count, in_count)
    source = jnp.arange(in_count, dtype=jnp.int32)[None, :]
    lower_part = (1.0 - fraction)[:, None] * (source == lower_index[:, None]).astype(jnp.float32)
    upper_part = fraction[:, None] * (source == upper_index[:, None]).astype(jnp.float32)
    return (lower_part + upper_part).astype(jnp.float32)

def column_table(image_ids):
    columns = image_ids.shape[1]
    position, lower_index, upper_index, fraction = linear_weights(4 * columns, columns)
    source = jnp.arange(columns, dtype=jnp.int32)[None, :]

    def picker(index_row):
        return (source == index_row[:, None]).astype(jnp.int32)

    def lookup(index_row):
        return lax.optimization_barrier(jnp.sum(image_ids[:, None, :] * picker(index_row)[None], axis=2))
    own_index = (position // 4).astype(jnp.int32)
    own_id = lookup(own_index)
    weight_lower = (1.0 - fraction)[None, :] * (lookup(lower_index) == own_id).astype(jnp.float32)
    weight_upper = fraction[None, :] * (lookup(upper_index) == own_id).astype(jnp.float32)
    weight_own = 1.0 - weight_lower - weight_upper
    table = weight_lower[:, :, None] * picker(lower_index)[None].astype(jnp.float32)
    table = table + weight_upper[:, :, None] * picker(upper_index)[None].astype(jnp.float32)
    table = table + weight_own[:, :, None] * picker(own_index)[None].astype(jnp.float32)
    return table.astype(jnp.float32)

def norm_silu(values, valid_map, count_all, gain_row, bias_row):
    axes = tuple(range(values.ndim - 1))
    mean_row = lax.optimization_barrier(jnp.sum(values * valid_map, axis=axes)) / count_all
    centered = values - mean_row
    variance = lax.optimization_barrier(jnp.sum(centered * centered * valid_map, axis=axes)) / count_all
    return valid_map * jax.nn.silu(centered * lax.rsqrt(variance + epsilon) * gain_row + bias_row)

def forward(widths, features, low_level, w_point, w_atrous, w_proj, w_low, w_dec1, w_dec2, w_cls, b_cls, gains, biases, low_gain, low_bias):
    canvases = features.shape[0]
    height = features.shape[1]
    columns = features.shape[2]
    images = widths.shape[1] - 1
    channels = gains.shape[1]
    ids_coarse = band_ids(widths, columns)
    ids_fine = band_ids(4 * widths, low_level.shape[2])
    valid_coarse = (ids_coarse >= 0).astype(jnp.float32)[:, None, :, None]
    valid_fine = (ids_fine >= 0).astype(jnp.float32)[:, None, :, None]
    pixel_count = (height * jnp.sum(widths[:, :images])).astype(jnp.float32)
    fine_count = 16.0 * pixel_count
    member = (ids_coarse[:, :, None] == jnp.arange(images, dtype=jnp.int32)[None, None, :]).astype(jnp.float32)
    image_sizes = (height * widths[:, :images]).astype(jnp.float32)
    activations = []
    point_z = low_back(jnp.einsum('nhwc,cd->nhwd', features, w_point[0], precision=highest))
    activations.append(low(norm_silu(point_z, valid_coarse, pixel_count, gains[0], biases[0])))
    for branch in range(3):
        atrous_z = low_back(masked_conv(features, w_atrous[branch], ids_coarse, dilations[branch]))
        activations.append(low(norm_silu(atrous_z, valid_coarse, pixel_count, gains[branch + 1], biases[branch + 1])))
    pooled = low(jnp.einsum('nhwc,nwk->nkc', features, member, precision=highest) / image_sizes[:, :, None])
    pool_z = low_back(jnp.einsum('nkc,cd->nkd', pooled, w_point[1], precision=highest))
    pool_act = low(norm_silu(pool_z, jnp.ones((1, 1, 1), jnp.float32), float(canvases * images), gains[4], biases[4]))
    spread = jnp.einsum('nwk,nkd->nwd', member, pool_act, precision=highest)
    activations.append(jnp.broadcast_to(spread[:, None], (canvases, height, columns, channels)))
    joined_coarse = jnp.concatenate(activations, axis=-1)
    proj_z = low_back(jnp.einsum('nhwc,cd->nhwd', joined_coarse, w_proj, precision=highest))
    proj_act = low(norm_silu(proj_z, valid_coarse, pixel_count, gains[5], biases[5]))
    rows_up = jnp.einsum('Yy,nyxc->nYxc', row_table(4 * height, height), proj_act, precision=highest)
    upsampled = low_back(low(jnp.einsum('nXx,nYxc->nYXc', column_table(ids_coarse), rows_up, precision=highest)))
    reduce_z = low_back(jnp.einsum('nhwc,cd->nhwd', low_level, w_low, precision=highest))
    reduce_act = low(norm_silu(reduce_z, valid_fine, fine_count, low_gain, low_bias))
    joined_fine = jnp.concatenate([upsampled, reduce_act], axis=-1)
    decode_z = low_back(masked_conv(joined_fine, w_dec1, ids_fine, 1))
    decode_act = low(norm_silu(decode_z, valid_fine, fine_count, gains[6], biases[6]))
    refine_z = low_back(masked_conv(decode_act, w_dec2, ids_fine, 1))
    refine_act = low(norm_silu(refine_z, valid_fine, fine_count, gains[7], biases[7]))
    return valid_fine * (jnp.einsum('nhwc,ck->nhwk', refine_act, w_cls, precision=highest) + b_cls)

def reference(features, low_level, widths, w_point, w_atrous, w_proj, w_low, w_dec1, w_dec2, w_cls, b_cls, gains, biases, low_gain, low_bias, logit_grad):
    arguments = (features, low_level, w_point, w_atrous, w_proj, w_low, w_dec1, w_dec2, w_cls, b_cls, gains, biases, low_gain, low_bias)
    floats = tuple((argument.astype(jnp.float32) for argument in arguments))
    logits, pullback = jax.vjp(partial(forward, widths), *floats)
    gradients = pullback(logit_grad.astype(jnp.float32))
    return (logits.astype(jnp.bfloat16), gradients[0].astype(jnp.bfloat16), gradients[1].astype(jnp.bfloat16), gradients[2], gradients[3], gradients[4], gradients[5], gradients[6], gradients[7], gradients[8], gradients[9], gradients[10], gradients[11], gradients[12], gradients[13])
```

```python
import functools

import jax
import jax.numpy as jnp
from jax import lax
from jax.experimental import pallas as pl
from jax.experimental.pallas import tpu as pltpu
from jax.sharding import PartitionSpec as P

epsilon = 1e-05
highest = lax.Precision.HIGHEST
dilations = (6, 12, 18)
ROUNDS = 4
CHUNKS = (8, 6, 6, 9)
VMEM_BYTES = 48 * 1024 * 1024


def exchange(values, axis, bit):
    size = lax.axis_size(axis)
    return lax.ppermute(values, axis, [(place, place ^ bit) for place in range(size)])


def rotate(values, axis, step, stride):
    size = lax.axis_size(axis)
    rounds = size // stride
    pairs = []
    for place in range(size):
        outer, inner = place // stride, place % stride
        pairs.append((place, ((outer + step) % rounds) * stride + inner))
    return lax.ppermute(values, axis, pairs)


def bits_of(axis):
    size = lax.axis_size(axis)
    bits = []
    bit = 1
    while bit < size:
        bits.append((axis, bit))
        bit = bit * 2
    return bits


def sum_all(values):
    for axis, bit in bits_of("narrow") + bits_of("wide"):
        values = values + exchange(values, axis, bit)
    return values


def merge_all(counts, means, squares):
    for axis, bit in bits_of("narrow") + bits_of("wide"):
        other = exchange(jnp.stack([counts, means, squares]), axis, bit)
        total = counts + other[0]
        gap = means - other[1]
        squares = squares + other[2] + gap * gap * (counts * other[0] / total)
        means = (counts * means + other[0] * other[1]) / total
        counts = total
    return (counts, means, squares)


def local_moments(values, valid_map, count):
    axes = tuple(range(values.ndim - 1))
    mean = jnp.sum(values * valid_map, axis=axes) / count
    centered = values - mean
    return (jnp.full_like(mean, 1.0) * count, mean, jnp.sum(centered * centered * valid_map, axis=axes))


def place():
    wide = lax.axis_index("wide")
    narrow = lax.axis_index("narrow")
    return (wide // 2, wide % 2, narrow // 2, narrow % 2)


def share_core(shard):
    core = place()[3]
    half = shard.shape[1] // 2
    parts = shard.reshape(shard.shape[0], 2, half, shard.shape[2])
    kept = lax.dynamic_index_in_dim(parts, core, 1, keepdims=False)
    given = lax.dynamic_index_in_dim(parts, 1 - core, 1, keepdims=False)
    got = exchange(given, "narrow", 1)
    lower = jnp.where(core == 0, kept, got)
    upper = jnp.where(core == 0, got, kept)
    return jnp.concatenate([lower, upper], axis=2)


def depth_groups():
    size = lax.axis_size("wide")
    return [list(range(inner, size, 2)) for inner in range(2)]


def gather_depth(block):
    rounds = lax.axis_size("wide") // 2
    if rounds > 4:
        stack = lax.all_gather(block, "wide", axis_index_groups=depth_groups())
        return jnp.take(stack, (place()[0] - jnp.arange(rounds)) % rounds, axis=0)
    parts = [block] + [rotate(block, "wide", step, 2) for step in range(1, rounds)]
    return jnp.stack(parts)


def tuned():
    return lax.axis_size("wide") == 2 * ROUNDS and lax.axis_size("narrow") == 4


def kernel_place():
    values = jnp.stack(place()).astype(jnp.int32)
    return values if tuned() else jnp.zeros_like(values)


def gather_chunk(block, x_first):
    order = [("wide", 1), ("narrow", 2)]
    if not x_first:
        order = order[::-1]
    stack = gather_depth(block)
    stack = jnp.stack([stack, exchange(stack, *order[0])])
    stack = jnp.stack([stack, exchange(stack, *order[1])])
    return (stack, exchange(stack, "narrow", 1))


def gather_taps(weights, sizes):
    chunks = []
    start = 0
    if tuned():
        shared = share_core(weights)
    else:
        full = lax.all_gather(weights, "narrow", axis=2, tiled=True)
        full = lax.all_gather(full, "wide", axis=1, tiled=True)
        rows = full.shape[1] // (4 * ROUNDS)
        full = full.reshape(full.shape[0], ROUNDS, 2, 2, rows, 2, full.shape[2] // 2)
    for index, size in enumerate(sizes):
        x_first = index % 2 == 0
        if tuned():
            chunks.append(gather_chunk(shared[start : start + size], x_first))
        else:
            part = full[start : start + size]
            part = part[:, [0] + list(range(ROUNDS - 1, 0, -1))]
            part = part.transpose((3, 5, 2, 1, 0, 4, 6) if x_first else (3, 2, 5, 1, 0, 4, 6))
            chunks.append((part[0], part[1]))
        start += size
    return chunks


def add_wide(first, second):
    return first.astype(jnp.float32) + second.astype(jnp.float32)


def scatter_chunk(keep, give, x_first):
    order = [("wide", 1), ("narrow", 2)]
    if not x_first:
        order = order[::-1]
    got = exchange(give, "narrow", 1)
    sent = add_wide(keep[1], got[1]).astype(jnp.bfloat16)
    total = add_wide(keep[0], got[0]) + exchange(sent, *order[0]).astype(jnp.float32)
    sent = total[1].astype(jnp.bfloat16)
    total = total[0] + exchange(sent, *order[1]).astype(jnp.float32)
    sent = total[1:].astype(jnp.bfloat16)
    total = total[0]
    for step in range(1, sent.shape[0] + 1):
        total = total + rotate(sent[step - 1], "wide", step, 2).astype(jnp.float32)
    return total


def scatter_taps(chunks, shape):
    if tuned():
        owned = [scatter_chunk(*pair, index % 2 == 0) for index, pair in enumerate(chunks)]
        return settle_core(jnp.concatenate(owned))
    parts = []
    for index, pair in enumerate(chunks):
        x_first = index % 2 == 0
        part = jnp.stack(pair)
        part = part.transpose((4, 3, 1, 0, 5, 2, 6) if x_first else (4, 3, 2, 0, 5, 1, 6))
        taps = part.shape[0]
        parts.append(part.reshape(taps, -1, 2 * part.shape[6]))
    full = jnp.concatenate(parts)
    full = lax.psum_scatter(full, "wide", scatter_dimension=1, tiled=True)
    return lax.psum_scatter(full, "narrow", scatter_dimension=2, tiled=True).astype(jnp.float32)


def row_span(dilation, row, height):
    step = (row - 1) * dilation
    return (max(step, 0), max(-step, 0), height - abs(step))


def tap_matrix(pair, tap, place_ref, x_first):
    row, core = place_ref[2], place_ref[3]

    def half(ref):
        if x_first:
            return jnp.concatenate([ref[row, 0, 0, tap], ref[1 - row, 0, 0, tap]], axis=1)
        return jnp.concatenate([ref[0, row, 0, tap], ref[0, 1 - row, 0, tap]], axis=1)

    mine = half(pair[0])
    other = half(pair[1])
    lower = jnp.where(core == 0, mine, other)
    upper = jnp.where(core == 0, other, mine)
    return jnp.concatenate([lower, upper], axis=0)


def weight_specs(chunk, x_first):
    taps, rows, cols = chunk[0].shape[3:]
    shape = (2, 1, 1, taps, rows, cols) if x_first else (1, 2, 1, taps, rows, cols)

    def index_map(step, place_ref):
        flip = lax.rem(step + place_ref[1], 2)
        slot = lax.rem(place_ref[0] - step // 2 + ROUNDS, ROUNDS)
        return (0, flip, slot, 0, 0, 0) if x_first else (flip, 0, slot, 0, 0, 0)

    return [pl.BlockSpec(shape, index_map)] * 2


def full_spec(array):
    return pl.BlockSpec(array.shape, lambda step, place_ref: (0,) * array.ndim)


def lane_spec(array):
    return pl.BlockSpec(
        (array.shape[0], array.shape[1] // (2 * ROUNDS)), lambda step, place_ref: (0, step)
    )


def store_moments(z_ref, mask_ref, stats_ref):
    mask = mask_ref[...]
    count = jnp.sum(mask)
    values = z_ref[...]
    mean = jnp.sum(values * mask, axis=0, keepdims=True) / count
    centered = (values - mean) * mask
    stats_ref[0:1, :] = mean
    stats_ref[1:2, :] = jnp.sum(centered * centered, axis=0, keepdims=True)


def coarse_forward_kernel(plan, place_ref, *refs):
    refs = list(refs)
    mask_ref = refs.pop(0)
    sides = [refs.pop(0) for _ in range(3)]
    if plan["pool"]:
        member_ref = refs.pop(0)
        sizes_ref = refs.pop(0)
    pairs = {}
    for index in plan["chunks"]:
        pairs[index] = (refs.pop(0), refs.pop(0))
    z_ref = refs.pop(0)
    stats_ref = refs.pop(0)
    step = pl.program_id(0)

    @pl.when(step == 0)
    def _():
        z_ref[...] = jnp.zeros_like(z_ref)

    columns = plan["columns"]
    for row, chunk, tap in plan["rows"]:
        x_first = chunk % 2 == 0
        source, target, extent = row_span(plan["dilation"], row, plan["height"])
        matrix = jnp.concatenate(
            [tap_matrix(pairs[chunk], tap + k, place_ref, x_first) for k in range(3)], axis=0
        )
        rows_in = pl.ds(source * columns, extent * columns)
        rows_out = pl.ds(target * columns, extent * columns)
        values = jnp.concatenate([side[rows_in, :] for side in sides], axis=1)
        z_ref[rows_out, :] += jnp.dot(values, matrix, preferred_element_type=jnp.float32)
    if plan["pool"]:
        point_ref, point_stats_ref, pool_ref, pooled_ref = refs

        @pl.when(step == 0)
        def _():
            point_ref[...] = jnp.zeros_like(point_ref)
            pool_ref[...] = jnp.zeros_like(pool_ref)

        center = sides[1][...]
        point_ref[...] += jnp.dot(
            center, tap_matrix(pairs[0], 0, place_ref, True), preferred_element_type=jnp.float32
        )
        pooled = jnp.dot(member_ref[...], center, preferred_element_type=jnp.float32)
        pooled = (pooled * sizes_ref[...]).astype(jnp.bfloat16)
        pooled_ref[...] = pooled
        pool_ref[...] += jnp.dot(
            pooled, tap_matrix(pairs[0], 1, place_ref, True), preferred_element_type=jnp.float32
        )

    @pl.when(step == 2 * ROUNDS - 1)
    def _():
        store_moments(z_ref, mask_ref, stats_ref)
        if plan["pool"]:
            store_moments(point_ref, mask_ref, point_stats_ref)


def coarse_forward(branch, mask, sides, chunks, shape, pool=None):
    height, columns, channels = shape
    positions = height * columns
    layout = atrous_layout()[branch]
    used = sorted({chunk for _, chunk, _ in layout} | ({0} if pool else set()))
    plan = {
        "pool": pool is not None,
        "chunks": used,
        "columns": columns,
        "height": height,
        "dilation": dilations[branch],
        "rows": layout,
    }
    args = [mask] + list(sides)
    specs = [full_spec(mask)] + [lane_spec(side) for side in sides]
    if pool:
        args += list(pool)
        specs += [full_spec(item) for item in pool]
    for index in used:
        args += list(chunks[index])
        specs += weight_specs(chunks[index], index % 2 == 0)
    outs = [
        jax.ShapeDtypeStruct((positions, channels), jnp.float32),
        jax.ShapeDtypeStruct((8, channels), jnp.float32),
    ]
    if pool:
        outs += outs
        outs += [
            jax.ShapeDtypeStruct((8, channels), jnp.float32),
            jax.ShapeDtypeStruct((8, sides[1].shape[1]), jnp.bfloat16),
        ]
    out_specs = [full_spec(item) for item in outs]
    if pool:
        out_specs[-1] = lane_spec(outs[-1])
    return pl.pallas_call(
        functools.partial(coarse_forward_kernel, plan),
        out_shape=outs,
        grid_spec=pltpu.PrefetchScalarGridSpec(
            num_scalar_prefetch=1, grid=(2 * ROUNDS,), in_specs=specs, out_specs=out_specs
        ),
        compiler_params=pltpu.CompilerParams(vmem_limit_bytes=VMEM_BYTES),
        name="coarse_forward",
    )(kernel_place(), *args)


def coarse_weight_kernel(plan, place_ref, *refs):
    refs = list(refs)
    sides = {branch: [refs.pop(0) for _ in range(3)] for branch in plan["branches"]}
    grads = {branch: refs.pop(0) for branch in plan["branches"]}
    if plan["pool"]:
        point_ref, pooled_ref, pool_ref = refs.pop(0), refs.pop(0), refs.pop(0)
    keep_ref, give_ref = refs
    row, core = place_ref[2], place_ref[3]
    rows = keep_ref.shape[-2]
    cols = keep_ref.shape[-1]
    columns = plan["columns"]

    def store(tap, value):
        value = value.astype(jnp.bfloat16)
        lower, upper = value[:rows], value[rows:]
        mine = jnp.where(core == 0, lower, upper)
        other = jnp.where(core == 0, upper, lower)
        for ref, part in ((keep_ref, mine), (give_ref, other)):
            for side, lane_part in ((row, part[:, :cols]), (1 - row, part[:, cols:])):
                if plan["x_first"]:
                    ref[0, side, 0, tap] = lane_part
                else:
                    ref[side, 0, 0, tap] = lane_part

    across = (((0,), (0,)), ((), ()))
    for branch, line, tap in plan["rows"]:
        source, target, extent = row_span(dilations[branch], line, plan["height"])
        values = jnp.concatenate(
            [side[pl.ds(source * columns, extent * columns), :] for side in sides[branch]], axis=1
        )
        result = lax.dot_general(
            values,
            grads[branch][pl.ds(target * columns, extent * columns), :],
            across,
            preferred_element_type=jnp.float32,
        )
        for k in range(3):
            store(tap + k, result[2 * rows * k : 2 * rows * (k + 1)])
    if plan["pool"]:
        center = sides[plan["branches"][0]][1][...]
        store(
            0,
            lax.dot_general(center, point_ref[...], across, preferred_element_type=jnp.float32),
        )
        store(
            1,
            lax.dot_general(
                pooled_ref[...], pool_ref[...], across, preferred_element_type=jnp.float32
            ),
        )


def coarse_weight(chunk, taps, sides, grads, shape, pool=None):
    height, columns, channels = shape
    entries = [
        (branch, line, tap)
        for branch, rows in enumerate(atrous_layout())
        for line, own, tap in rows
        if own == chunk
    ]
    branches = sorted({branch for branch, _, _ in entries})
    x_first = chunk % 2 == 0
    plan = {
        "pool": pool is not None,
        "branches": branches,
        "rows": entries,
        "columns": columns,
        "height": height,
        "x_first": x_first,
    }
    args = []
    specs = []
    for branch in branches:
        args += list(sides[branch])
        specs += [lane_spec(side) for side in sides[branch]]
    for branch in branches:
        args.append(grads[branch])
        specs.append(full_spec(grads[branch]))
    if pool:
        args += list(pool)
        specs += [full_spec(pool[0]), lane_spec(pool[1]), full_spec(pool[2])]
    rows = sides[0][1].shape[1] // (4 * ROUNDS)
    out = jax.ShapeDtypeStruct((2, 2, ROUNDS, taps, rows, channels // 2), jnp.bfloat16)
    shape = (1, 2, 1, taps, rows, channels // 2) if x_first else (2, 1, 1, taps, rows, channels // 2)

    def index_map(step, place_ref):
        flip = lax.rem(step + place_ref[1], 2)
        slot = lax.rem(step // 2 - place_ref[0] + ROUNDS, ROUNDS)
        return (flip, 0, slot, 0, 0, 0) if x_first else (0, flip, slot, 0, 0, 0)

    return pl.pallas_call(
        functools.partial(coarse_weight_kernel, plan),
        out_shape=[out, out],
        grid_spec=pltpu.PrefetchScalarGridSpec(
            num_scalar_prefetch=1,
            grid=(2 * ROUNDS,),
            in_specs=specs,
            out_specs=[pl.BlockSpec(shape, index_map)] * 2,
        ),
        compiler_params=pltpu.CompilerParams(vmem_limit_bytes=VMEM_BYTES),
        name="coarse_weight",
    )(kernel_place(), *args)


def coarse_input_kernel(plan, place_ref, *refs):
    refs = list(refs)
    point_ref, pool_ref, spread_ref = refs.pop(0), refs.pop(0), refs.pop(0)
    grads = [refs.pop(0) for _ in range(3)]
    pairs = [(refs.pop(0), refs.pop(0)) for _ in range(plan["chunks"])]
    out_ref, total_ref = refs
    columns = plan["columns"]
    turned = (((1,), (1,)), ((), ()))
    total_ref[...] = lax.dot_general(
        point_ref[...],
        tap_matrix(pairs[0], 0, place_ref, True),
        turned,
        preferred_element_type=jnp.float32,
    )
    pooled = lax.dot_general(
        pool_ref[...],
        tap_matrix(pairs[0], 1, place_ref, True),
        turned,
        preferred_element_type=jnp.float32,
    )
    total_ref[...] += jnp.dot(
        spread_ref[...], pooled, preferred_element_type=jnp.float32, precision=highest
    )
    for branch, rows in enumerate(plan["rows"]):
        for line, chunk, tap in rows:
            source, target, extent = row_span(dilations[branch], line, plan["height"])
            matrix = jnp.concatenate(
                [tap_matrix(pairs[chunk], tap + k, place_ref, chunk % 2 == 0) for k in range(3)],
                axis=1,
            )
            total_ref[pl.ds(source * columns, extent * columns), :] += lax.dot_general(
                grads[branch][pl.ds(target * columns, extent * columns), :],
                matrix,
                turned,
                preferred_element_type=jnp.float32,
            )
    out_ref[...] = total_ref[...].astype(jnp.bfloat16)


def coarse_input(point_dz, pool_dz, spread, grads, chunks, shape, width):
    height, columns, channels = shape
    plan = {
        "chunks": len(chunks),
        "columns": columns,
        "height": height,
        "rows": atrous_layout(),
    }
    args = [point_dz, pool_dz, spread] + list(grads)
    specs = [full_spec(item) for item in args]
    for index, pair in enumerate(chunks):
        args += list(pair)
        specs += weight_specs(pair, index % 2 == 0)
    out = jax.ShapeDtypeStruct((height * columns, width), jnp.bfloat16)
    return pl.pallas_call(
        functools.partial(coarse_input_kernel, plan),
        out_shape=out,
        grid_spec=pltpu.PrefetchScalarGridSpec(
            num_scalar_prefetch=1,
            grid=(2 * ROUNDS,),
            in_specs=specs,
            out_specs=lane_spec(out),
            scratch_shapes=[pltpu.VMEM((height * columns, width // (2 * ROUNDS)), jnp.float32)],
        ),
        compiler_params=pltpu.CompilerParams(vmem_limit_bytes=VMEM_BYTES),
        name="coarse_input",
    )(kernel_place(), *args)


def atrous_layout():
    places = [(chunk, tap) for chunk, size in enumerate(CHUNKS) for tap in range(size)]
    places = places[2:]
    return [
        [(line,) + places[9 * branch + 3 * line] for line in range(3)] for branch in range(3)
    ]


def side_values(values, image_ids, dilation):
    result = []
    for step in (-dilation, dilation):
        mask = tap_mask(image_ids, values.shape[1], 0, step).astype(values.dtype)
        result.append(mask * shifted(values, 0, step))
    return [result[0], values, result[1]]


def side_grads(values, image_ids, dilation):
    result = []
    for step in (-dilation, 0, dilation):
        masked = tap_mask(image_ids, values.shape[1], 0, step).astype(values.dtype) * values
        result.append(shifted(masked, 0, -step))
    return jnp.concatenate(result, axis=-1)


def cast_add(first, second):
    return (first.astype(jnp.float32) + second.astype(jnp.float32)).astype(jnp.bfloat16)


def reduce_half(values, dim, index, axis, bit):
    kept = lax.dynamic_index_in_dim(values, index, dim, keepdims=False)
    given = lax.dynamic_index_in_dim(values, 1 - index, dim, keepdims=False)
    return cast_add(kept, exchange(given, axis, bit))


def reduce_depth(values, dim, depth):
    rounds = lax.axis_size("wide") // 2
    if rounds > 4:
        return lax.psum_scatter(
            values.astype(jnp.float32),
            "wide",
            scatter_dimension=dim,
            axis_index_groups=depth_groups(),
        )
    total = lax.dynamic_index_in_dim(values, depth, dim, keepdims=False).astype(jnp.float32)
    for step in range(1, rounds):
        given = lax.dynamic_index_in_dim(
            values, lax.rem(depth + step, rounds), dim, keepdims=False
        )
        total = total + rotate(given, "wide", step, 2).astype(jnp.float32)
    return total


def settle_core(values):
    core = place()[3]
    taps, rows, cols = values.shape
    parts = values.reshape(taps, rows, 2, cols // 2)
    kept = lax.dynamic_index_in_dim(parts, core, 2, keepdims=False)
    given = lax.dynamic_index_in_dim(parts, 1 - core, 2, keepdims=False).astype(jnp.bfloat16)
    got = exchange(given, "narrow", 1).astype(jnp.float32)
    lower = jnp.where(core == 0, kept, got)
    upper = jnp.where(core == 0, got, kept)
    return jnp.concatenate([lower, upper], axis=1)


def gather_small(flat):
    rounds = lax.axis_size("wide") // 2
    depth, side, row, core = place()
    stack = jnp.take(gather_depth(flat), (depth - jnp.arange(rounds)) % rounds, axis=0)

    def both(values, index, axis, bit, dim):
        other = exchange(values, axis, bit)
        return jnp.stack(
            [jnp.where(index == 0, values, other), jnp.where(index == 0, other, values)], axis=dim
        )

    stack = both(stack, row, "narrow", 2, 1)
    stack = both(stack, side, "wide", 1, 1)
    stack = both(stack, core, "narrow", 1, 3)
    return stack.reshape((lax.axis_size("wide"), lax.axis_size("narrow")) + flat.shape)


def scatter_small(values):
    depth, side, row, core = place()
    rounds = lax.axis_size("wide") // 2
    shape = values.shape[2:]
    values = values.reshape((rounds, 2, 2, 2) + shape)
    values = reduce_half(values, 3, core, "narrow", 1)
    values = reduce_half(values, 1, side, "wide", 1)
    values = reduce_half(values, 1, row, "narrow", 2)
    return reduce_depth(values, 0, depth)


def band_ids(widths, columns):
    ends_all = jnp.cumsum(widths, axis=1)
    position = jnp.arange(columns, dtype=jnp.int32)
    band_index = jnp.sum(
        (position[None, :, None] >= ends_all[:, None, :]).astype(jnp.int32), axis=2
    )
    return jnp.where(band_index < widths.shape[1] - 1, band_index, -1)


def shifted(values, row_shift, col_shift):
    height = values.shape[1]
    columns = values.shape[2]
    padded = jnp.pad(
        values, ((0, 0), (abs(row_shift), abs(row_shift)), (abs(col_shift), abs(col_shift)), (0, 0))
    )
    row_start = abs(row_shift) + row_shift
    col_start = abs(col_shift) + col_shift
    return padded[:, row_start : row_start + height, col_start : col_start + columns, :]


def tap_mask(image_ids, height, row_shift, col_shift):
    columns = image_ids.shape[1]
    padded = jnp.pad(image_ids, ((0, 0), (abs(col_shift), abs(col_shift))), constant_values=-2)
    col_start = abs(col_shift) + col_shift
    other_ids = padded[:, col_start : col_start + columns]
    same_image = (other_ids == image_ids).astype(jnp.float32)
    row_place = jnp.arange(height) + row_shift
    inside = ((row_place >= 0) & (row_place < height)).astype(jnp.float32)
    return (inside[None, :, None] * same_image[:, None, :])[..., None]


def tap_offsets(dilation):
    return [
        ((tap_index // 3 - 1) * dilation, (tap_index % 3 - 1) * dilation) for tap_index in range(9)
    ]


def conv_forward(values, kernel, image_ids, dilation):
    products = jnp.einsum("nhwc,tcd->tnhwd", values, kernel, preferred_element_type=jnp.float32)
    running = jnp.zeros(products.shape[1:], jnp.float32)
    for tap_index, offset_pair in enumerate(tap_offsets(dilation)):
        row_shift, col_shift = offset_pair
        running = running + tap_mask(image_ids, values.shape[1], row_shift, col_shift) * shifted(
            products[tap_index], row_shift, col_shift
        )
    return running


def conv_backward(values, kernel, grad_low, image_ids, dilation):
    sources = []
    for row_shift, col_shift in tap_offsets(dilation):
        masked = (
            tap_mask(image_ids, grad_low.shape[1], row_shift, col_shift).astype(jnp.bfloat16)
            * grad_low
        )
        sources.append(shifted(masked, -row_shift, -col_shift))
    stacked = jnp.stack(sources)
    input_grad = jnp.einsum("tnhwd,tcd->nhwc", stacked, kernel, preferred_element_type=jnp.float32)
    kernel_grad = jnp.einsum("nhwc,tnhwd->tcd", values, stacked, preferred_element_type=jnp.float32)
    return (input_grad, kernel_grad)


def linear_weights(out_count, in_count):
    position = jnp.arange(out_count, dtype=jnp.int32)
    scaled = 2 * position - 3
    left_index = jnp.floor_divide(scaled, 8)
    fraction = (scaled - 8 * left_index).astype(jnp.float32) / 8.0
    lower_index = jnp.clip(left_index, 0, in_count - 1)
    upper_index = jnp.clip(left_index + 1, 0, in_count - 1)
    return (position, lower_index, upper_index, fraction)


def row_table(out_count, in_count):
    position, lower_index, upper_index, fraction = linear_weights(out_count, in_count)
    source = jnp.arange(in_count, dtype=jnp.int32)[None, :]
    lower_part = (1.0 - fraction)[:, None] * (source == lower_index[:, None]).astype(jnp.float32)
    upper_part = fraction[:, None] * (source == upper_index[:, None]).astype(jnp.float32)
    return lower_part + upper_part


def column_table(image_ids):
    columns = image_ids.shape[1]
    position, lower_index, upper_index, fraction = linear_weights(4 * columns, columns)
    source = jnp.arange(columns, dtype=jnp.int32)[None, :]

    def picker(index_row):
        return (source == index_row[:, None]).astype(jnp.int32)

    def lookup(index_row):
        return jnp.sum(image_ids[:, None, :] * picker(index_row)[None], axis=2)

    own_index = position // 4
    own_id = lookup(own_index)
    weight_lower = (1.0 - fraction)[None, :] * (lookup(lower_index) == own_id).astype(jnp.float32)
    weight_upper = fraction[None, :] * (lookup(upper_index) == own_id).astype(jnp.float32)
    weight_own = 1.0 - weight_lower - weight_upper
    table = weight_lower[:, :, None] * picker(lower_index)[None].astype(jnp.float32)
    table = table + weight_upper[:, :, None] * picker(upper_index)[None].astype(jnp.float32)
    table = table + weight_own[:, :, None] * picker(own_index)[None].astype(jnp.float32)
    return table


def normalize(values, valid_map, mean_row, variance, gain_row, bias_row):
    norm_scale = lax.rsqrt(variance + epsilon)
    centered = (values - mean_row) * norm_scale
    shaped = centered * gain_row + bias_row
    return (valid_map * jax.nn.silu(shaped), centered, shaped, norm_scale)


def norm_grad_terms(upstream, valid_map, centered, shaped):
    sigmoid_value = jax.nn.sigmoid(shaped)
    local_term = valid_map * upstream * sigmoid_value * (1.0 + shaped * (1.0 - sigmoid_value))
    axes = tuple(range(local_term.ndim - 1))
    return (local_term, jnp.sum(local_term * centered, axis=axes), jnp.sum(local_term, axis=axes))


def norm_grad_finish(
    local_term, valid_map, centered, norm_scale, gain_row, gain_sum, bias_sum, count_all
):
    inner = local_term - bias_sum / count_all - centered * gain_sum / count_all
    return (valid_map * gain_row * norm_scale * inner).astype(jnp.bfloat16)


def moments(values, valid_map, local_count, count_all):
    counts, means, squares = merge_all(*local_moments(values, valid_map, local_count))
    return (means, squares / count_all)


def pack_pairs(pairs):
    return jnp.concatenate(
        [pair_item[0] for pair_item in pairs] + [pair_item[1] for pair_item in pairs]
    )


def unpack_pairs(flat, pairs):
    lengths = [pair_item[0].shape[0] for pair_item in pairs]
    half_point = sum(lengths)
    result_pairs = []
    offset = 0
    for length_now in lengths:
        result_pairs.append(
            (
                flat[offset : offset + length_now],
                flat[half_point + offset : half_point + offset + length_now],
            )
        )
        offset = offset + length_now
    return result_pairs


def gradient_sums(pairs):
    return unpack_pairs(sum_all(pack_pairs(pairs)), pairs)


def gather_weights(small):
    sizes = [item.size for item in small]
    total = sum(sizes)
    padded = -(-total // 2048) * 2048
    flat = jnp.concatenate(
        [item.reshape(-1) for item in small] + [jnp.zeros((padded - total,), jnp.bfloat16)]
    ).reshape(-1, 128)
    everything = gather_small(flat)
    wide, narrow = everything.shape[:2]
    everything = everything.reshape(wide, narrow, -1)
    pieces = []
    start = 0
    for item in small:
        pieces.append(
            everything[:, :, start : start + item.size].reshape((wide, narrow) + item.shape)
        )
        start += item.size
    proj, reduce, decode, refine = pieces
    proj = proj.transpose(0, 2, 1, 3).reshape(wide * proj.shape[2], -1)
    reduce = reduce.transpose(0, 2, 1, 3).reshape(wide * reduce.shape[2], -1)
    decode = decode.transpose(2, 1, 3, 0, 4).reshape(decode.shape[2], narrow * decode.shape[3], -1)
    refine = refine.transpose(2, 0, 3, 1, 4).reshape(refine.shape[2], wide * refine.shape[3], -1)
    return (proj, reduce, decode, refine)


def scatter_weights(grads, shapes):
    wide = lax.axis_size("wide")
    narrow = lax.axis_size("narrow")
    proj, reduce, decode, refine = grads
    shape_p, shape_r, shape_d, shape_f = shapes
    proj = proj.reshape(wide, shape_p[0], narrow, shape_p[1]).transpose(0, 2, 1, 3)
    reduce = reduce.reshape(wide, shape_r[0], narrow, shape_r[1]).transpose(0, 2, 1, 3)
    decode = decode.reshape(shape_d[0], narrow, shape_d[1], wide, shape_d[2]).transpose(3, 1, 0, 2, 4)
    refine = refine.reshape(shape_f[0], wide, shape_f[1], narrow, shape_f[2]).transpose(1, 3, 0, 2, 4)
    flats = [
        item.astype(jnp.bfloat16).reshape(wide, narrow, -1)
        for item in (proj, reduce, decode, refine)
    ]
    total = sum(item.shape[2] for item in flats)
    padded = -(-total // 2048) * 2048
    flats.append(jnp.zeros((wide, narrow, padded - total), jnp.bfloat16))
    packed = jnp.concatenate(flats, axis=2).reshape(wide, narrow, -1, 128)
    owned = scatter_small(packed).reshape(-1)
    pieces = []
    start = 0
    for shape in shapes:
        size = 1
        for extent in shape:
            size *= extent
        pieces.append(owned[start : start + size].reshape(shape))
        start += size
    return pieces


def per_device(
    features,
    low_level,
    widths,
    w_point,
    w_atrous,
    w_proj,
    w_low,
    w_dec1,
    w_dec2,
    w_cls,
    b_cls,
    gains,
    biases,
    low_gain,
    low_bias,
    logit_grad,
):
    canvases = features.shape[0]
    height = features.shape[1]
    columns = features.shape[2]
    fine_columns = low_level.shape[2]
    images = widths.shape[1] - 1
    channels = gains.shape[1]
    images_total = float(canvases * lax.axis_size("wide") * lax.axis_size("narrow") * images)
    small = [w_proj, w_low, w_dec1, w_dec2]
    proj_full, reduce_full, decode_full, refine_full = gather_weights(small)
    all_taps = jnp.concatenate([w_point, w_atrous.reshape((-1,) + w_atrous.shape[2:])])
    chunks = gather_taps(all_taps, CHUNKS)
    ids_coarse = band_ids(widths, columns)
    ids_fine = band_ids(4 * widths, fine_columns)
    valid_coarse = (ids_coarse >= 0).astype(jnp.float32)[:, None, :, None]
    valid_fine = (ids_fine >= 0).astype(jnp.float32)[:, None, :, None]
    all_ones = jnp.ones((1, 1, 1), jnp.float32)
    local_count = (height * jnp.sum(widths[:, :images])).astype(jnp.float32)
    member = (ids_coarse[:, :, None] == jnp.arange(images, dtype=jnp.int32)[None, None, :]).astype(
        jnp.float32
    )
    member_low = member.astype(jnp.bfloat16)
    image_sizes = (height * widths[:, :images]).astype(jnp.float32)
    flat_features = features.reshape(height * columns, -1)
    coarse_shape = (height, columns, channels)
    sides = [
        [
            item.reshape(height * columns, -1)
            for item in side_values(features, ids_coarse, dilation)
        ]
        for dilation in dilations
    ]
    mask_column = jnp.broadcast_to(valid_coarse, (1, height, columns, 1)).reshape(-1, 1)
    member_wide = jnp.pad(member[0], ((0, 0), (0, 8 - images)))
    member_rows = jnp.tile(member_wide, (height, 1))
    sizes_inverse = jnp.pad(1.0 / image_sizes[0], (0, 8 - images)).reshape(8, 1)
    first = coarse_forward(
        0,
        mask_column,
        sides[0],
        chunks,
        coarse_shape,
        (member_rows.T.astype(jnp.bfloat16), sizes_inverse),
    )
    second = coarse_forward(1, mask_column, sides[1], chunks, coarse_shape)
    third = coarse_forward(2, mask_column, sides[2], chunks, coarse_shape)
    pool_z = first[4][None, :images]
    pooled = first[5]
    coarse_stats = [first[3], first[1], second[1], third[1]]
    coarse_z = [
        item.reshape(1, height, columns, channels)
        for item in (first[2], first[0], second[0], third[0])
    ]
    reduce_z = jnp.einsum(
        "nhwc,cd->nhwd", low_level, reduce_full, preferred_element_type=jnp.float32
    )
    blocks = [(item_z, valid_coarse) for item_z in coarse_z] + [
        (pool_z, all_ones),
        (reduce_z, valid_fine),
    ]
    local_images = float(canvases * images)
    local_counts = [local_count] * 4 + [local_images, 16.0 * local_count]
    states = [
        (jnp.full((channels,), 1.0) * local_count, item[0], item[1]) for item in coarse_stats
    ] + [
        local_moments(block[0], block[1], count)
        for block, count in zip(blocks[4:], local_counts[4:])
    ]
    counts_flat, means_flat, squares_flat = merge_all(
        *[jnp.concatenate([state[item] for state in states]) for item in range(3)]
    )
    vars_flat = squares_flat / counts_flat
    section_means = []
    section_vars = []
    offset = 0
    for block in blocks:
        section_means.append(means_flat[offset : offset + block[0].shape[-1]])
        section_vars.append(vars_flat[offset : offset + block[0].shape[-1]])
        offset += block[0].shape[-1]
    pixel_count = counts_flat[0]
    fine_count = 16.0 * pixel_count
    fine_local = 16.0 * local_count
    gain_rows = [gains[0], gains[1], gains[2], gains[3], gains[4], low_gain]
    bias_rows = [biases[0], biases[1], biases[2], biases[3], biases[4], low_bias]
    kept = []
    activations = []
    for index in range(6):
        block_values, block_valid = blocks[index]
        result = normalize(
            block_values,
            block_valid,
            section_means[index],
            section_vars[index],
            gain_rows[index],
            bias_rows[index],
        )
        kept.append(result[1:])
        activations.append(result[0].astype(jnp.bfloat16))
    spread = jnp.einsum(
        "nwk,nkd->nwd", member_low, activations[4], preferred_element_type=jnp.float32
    ).astype(jnp.bfloat16)
    spread = jnp.broadcast_to(spread[:, None], (canvases, height, columns, channels))
    joined_coarse = jnp.concatenate(activations[:4] + [spread], axis=-1)
    proj_z = jnp.einsum(
        "nhwc,cd->nhwd", joined_coarse, proj_full, preferred_element_type=jnp.float32
    )
    proj_mean, proj_var = moments(proj_z, valid_coarse, local_count, pixel_count)
    proj_act, proj_centered, proj_shaped, proj_scale = normalize(
        proj_z, valid_coarse, proj_mean, proj_var, gains[5], biases[5]
    )
    proj_act = proj_act.astype(jnp.bfloat16)
    rows_table = row_table(4 * height, height)
    cols_table = column_table(ids_coarse)
    rows_up = jnp.einsum(
        "Yy,nyxc->nYxc",
        rows_table.astype(jnp.bfloat16),
        proj_act,
        preferred_element_type=jnp.float32,
    )
    upsampled = jnp.einsum("nXx,nYxc->nYXc", cols_table, rows_up, precision=highest).astype(
        jnp.bfloat16
    )
    joined_fine = jnp.concatenate([upsampled, activations[5]], axis=-1)
    decode_z = conv_forward(joined_fine, decode_full, ids_fine, 1)
    decode_mean, decode_var = moments(decode_z, valid_fine, fine_local, fine_count)
    decode_act, decode_centered, decode_shaped, decode_scale = normalize(
        decode_z, valid_fine, decode_mean, decode_var, gains[6], biases[6]
    )
    decode_act = decode_act.astype(jnp.bfloat16)
    refine_z = conv_forward(decode_act, refine_full, ids_fine, 1)
    refine_mean, refine_var = moments(refine_z, valid_fine, fine_local, fine_count)
    refine_act, refine_centered, refine_shaped, refine_scale = normalize(
        refine_z, valid_fine, refine_mean, refine_var, gains[7], biases[7]
    )
    refine_act = refine_act.astype(jnp.bfloat16)
    logits = (
        valid_fine
        * (
            jnp.einsum("nhwc,ck->nhwk", refine_act, w_cls, preferred_element_type=jnp.float32)
            + b_cls
        )
    ).astype(jnp.bfloat16)
    masked_grad = valid_fine.astype(jnp.bfloat16) * logit_grad
    cls_weight_grad = jnp.einsum(
        "nhwc,nhwk->ck", refine_act, masked_grad, preferred_element_type=jnp.float32
    )
    cls_bias_grad = jnp.sum(masked_grad.astype(jnp.float32), axis=(0, 1, 2))
    refine_up = jnp.einsum("nhwk,ck->nhwc", masked_grad, w_cls, preferred_element_type=jnp.float32)
    refine_local, refine_gain, refine_bias = norm_grad_terms(
        refine_up, valid_fine, refine_centered, refine_shaped
    )
    refine_gain, refine_bias = gradient_sums([(refine_gain, refine_bias)])[0]
    refine_dz = norm_grad_finish(
        refine_local,
        valid_fine,
        refine_centered,
        refine_scale,
        gains[7],
        refine_gain,
        refine_bias,
        fine_count,
    )
    decode_up, refine_kernel_grad = conv_backward(decode_act, refine_full, refine_dz, ids_fine, 1)
    decode_local, decode_gain, decode_bias = norm_grad_terms(
        decode_up, valid_fine, decode_centered, decode_shaped
    )
    decode_gain, decode_bias = gradient_sums([(decode_gain, decode_bias)])[0]
    decode_dz = norm_grad_finish(
        decode_local,
        valid_fine,
        decode_centered,
        decode_scale,
        gains[6],
        decode_gain,
        decode_bias,
        fine_count,
    )
    joined_grad, decode_kernel_grad = conv_backward(
        joined_fine, decode_full, decode_dz, ids_fine, 1
    )
    up_grad = joined_grad[..., :channels].astype(jnp.bfloat16)
    reduce_up = joined_grad[..., channels:]
    rows_grad = jnp.einsum(
        "nXx,nYXc->nYxc",
        cols_table.astype(jnp.bfloat16),
        up_grad,
        preferred_element_type=jnp.float32,
    )
    proj_up = jnp.einsum("Yy,nYxc->nyxc", rows_table, rows_grad, precision=highest)
    proj_local, proj_gain, proj_bias = norm_grad_terms(
        proj_up, valid_coarse, proj_centered, proj_shaped
    )
    reduce_local, reduce_gain, reduce_bias = norm_grad_terms(
        reduce_up, valid_fine, kept[5][0], kept[5][1]
    )
    summed_pairs = gradient_sums([(proj_gain, proj_bias), (reduce_gain, reduce_bias)])
    proj_gain, proj_bias = summed_pairs[0]
    reduce_gain, reduce_bias = summed_pairs[1]
    proj_dz = norm_grad_finish(
        proj_local,
        valid_coarse,
        proj_centered,
        proj_scale,
        gains[5],
        proj_gain,
        proj_bias,
        pixel_count,
    )
    reduce_dz = norm_grad_finish(
        reduce_local,
        valid_fine,
        kept[5][0],
        kept[5][2],
        low_gain,
        reduce_gain,
        reduce_bias,
        fine_count,
    )
    reduce_kernel_grad = jnp.einsum(
        "nhwc,nhwd->cd", low_level, reduce_dz, preferred_element_type=jnp.float32
    )
    low_level_grad = jnp.einsum(
        "nhwd,cd->nhwc", reduce_dz, reduce_full, preferred_element_type=jnp.float32
    ).astype(jnp.bfloat16)
    proj_kernel_grad = jnp.einsum(
        "nhwc,nhwd->cd", joined_coarse, proj_dz, preferred_element_type=jnp.float32
    )
    concat_grad = jnp.einsum(
        "nhwd,cd->nhwc", proj_dz, proj_full, preferred_element_type=jnp.float32
    )
    branch_terms = []
    for index in range(4):
        upstream = concat_grad[..., index * channels : (index + 1) * channels]
        branch_terms.append(norm_grad_terms(upstream, valid_coarse, kept[index][0], kept[index][1]))
    pool_up = jnp.einsum(
        "nhwd,nwk->nkd", concat_grad[..., 4 * channels :], member, precision=highest
    )
    branch_terms.append(norm_grad_terms(pool_up, all_ones, kept[4][0], kept[4][1]))
    local_pairs = [(term_item[1], term_item[2]) for term_item in branch_terms]
    flat_pairs = pack_pairs(local_pairs)
    flat_sums = sum_all(
        jnp.concatenate([flat_pairs, cls_bias_grad, cls_weight_grad.reshape(-1)])
    )
    classes = cls_bias_grad.shape[0]
    cls_weight_grad = flat_sums[flat_pairs.shape[0] + classes :].reshape(cls_weight_grad.shape)
    cls_bias_grad = flat_sums[flat_pairs.shape[0] : flat_pairs.shape[0] + classes]
    flat_sums = flat_sums[: flat_pairs.shape[0]]
    last_pairs = unpack_pairs(flat_sums, local_pairs)
    valid_list = [valid_coarse, valid_coarse, valid_coarse, valid_coarse, all_ones]
    count_list = [pixel_count, pixel_count, pixel_count, pixel_count, images_total]
    branch_dz = [
        norm_grad_finish(
            branch_terms[index][0],
            valid_list[index],
            kept[index][0],
            kept[index][2],
            gains[index],
            last_pairs[index][0],
            last_pairs[index][1],
            count_list[index],
        )
        for index in range(5)
    ]
    flat_dz = [item.reshape(height * columns, channels) for item in branch_dz[:4]]
    pool_dz = jnp.pad(branch_dz[4][0], ((0, 8 - images), (0, 0)))
    grad_chunks = []
    for index, size in enumerate(CHUNKS):
        grad_chunks.append(
            coarse_weight(
                index,
                size,
                sides,
                flat_dz[1:],
                coarse_shape,
                (flat_dz[0], pooled, pool_dz) if index == 0 else None,
            )
        )
    big_owned = scatter_taps(grad_chunks, all_taps.shape)
    point_owned = big_owned[: w_point.shape[0]]
    atrous_owned = big_owned[w_point.shape[0] :].reshape(w_atrous.shape)
    spread_rows = member_rows * sizes_inverse.reshape(1, 8)
    features_grad = coarse_input(
        flat_dz[0],
        pool_dz,
        spread_rows,
        [
            side_grads(branch_dz[branch + 1], ids_coarse, dilations[branch]).reshape(
                height * columns, -1
            )
            for branch in range(3)
        ],
        chunks,
        coarse_shape,
        flat_features.shape[1],
    ).reshape(features.shape)
    small_owned = scatter_weights(
        (proj_kernel_grad, reduce_kernel_grad, decode_kernel_grad, refine_kernel_grad),
        [item.shape for item in small],
    )
    proj_owned, reduce_owned, decode_owned, refine_owned = small_owned
    gains_grad = jnp.stack(
        [
            last_pairs[0][0],
            last_pairs[1][0],
            last_pairs[2][0],
            last_pairs[3][0],
            last_pairs[4][0],
            proj_gain,
            decode_gain,
            refine_gain,
        ]
    )
    biases_grad = jnp.stack(
        [
            last_pairs[0][1],
            last_pairs[1][1],
            last_pairs[2][1],
            last_pairs[3][1],
            last_pairs[4][1],
            proj_bias,
            decode_bias,
            refine_bias,
        ]
    )
    return (
        logits,
        features_grad,
        low_level_grad,
        point_owned,
        atrous_owned,
        proj_owned,
        reduce_owned,
        decode_owned,
        refine_owned,
        cls_weight_grad,
        cls_bias_grad,
        gains_grad,
        biases_grad,
        reduce_gain,
        reduce_bias,
    )


def solution(mesh):
    in_specs = (
        P(("wide", "narrow"), None, None, None),
        P(("wide", "narrow"), None, None, None),
        P(("wide", "narrow"), None),
        P(None, "wide", "narrow"),
        P(None, None, "wide", "narrow"),
        P("wide", "narrow"),
        P("wide", "narrow"),
        P(None, "narrow", "wide"),
        P(None, "wide", "narrow"),
        P(),
        P(),
        P(),
        P(),
        P(),
        P(),
        P(("wide", "narrow"), None, None, None),
    )
    out_specs = (
        P(("wide", "narrow"), None, None, None),
        P(("wide", "narrow"), None, None, None),
        P(("wide", "narrow"), None, None, None),
        P(None, "wide", "narrow"),
        P(None, None, "wide", "narrow"),
        P("wide", "narrow"),
        P("wide", "narrow"),
        P(None, "narrow", "wide"),
        P(None, "wide", "narrow"),
        P(),
        P(),
        P(),
        P(),
        P(),
        P(),
    )
    return jax.shard_map(
        per_device, mesh=mesh, in_specs=in_specs, out_specs=out_specs, check_vma=False
    )
```

```python
import functools

import jax
import jax.numpy as jnp
from jax import lax
from jax.experimental import pallas as pl
from jax.experimental.pallas import tpu as pltpu
from jax.sharding import PartitionSpec as P

epsilon = 1e-05
highest = lax.Precision.HIGHEST
dilations = (6, 12, 18)
ROUNDS = 4
CHUNKS = (3, 3, 5, 6, 6, 6)
PARTS = ((0, 1), (2, 3), (4, 5))
POINT_CHUNK = 2
VMEM_BYTES = 48 * 1024 * 1024


def exchange(values, axis, bit):
    size = lax.axis_size(axis)
    return lax.ppermute(values, axis, [(place, place ^ bit) for place in range(size)])


def rotate(values, axis, step, stride):
    size = lax.axis_size(axis)
    rounds = size // stride
    pairs = []
    for place in range(size):
        outer, inner = place // stride, place % stride
        pairs.append((place, ((outer + step) % rounds) * stride + inner))
    return lax.ppermute(values, axis, pairs)


def bits_of(axis):
    size = lax.axis_size(axis)
    bits = []
    bit = 1
    while bit < size:
        bits.append((axis, bit))
        bit = bit * 2
    return bits


def sum_all(values):
    for axis, bit in bits_of("narrow") + bits_of("wide"):
        values = values + exchange(values, axis, bit)
    return values


def merge_all(counts, means, squares):
    for axis, bit in bits_of("narrow") + bits_of("wide"):
        other = exchange(jnp.stack([counts, means, squares]), axis, bit)
        total = counts + other[0]
        gap = means - other[1]
        squares = squares + other[2] + gap * gap * (counts * other[0] / total)
        means = (counts * means + other[0] * other[1]) / total
        counts = total
    return (counts, means, squares)


def local_moments(values, valid_map, count):
    axes = tuple(range(values.ndim - 1))
    mean = jnp.sum(values * valid_map, axis=axes) / count
    centered = values - mean
    return (jnp.full_like(mean, 1.0) * count, mean, jnp.sum(centered * centered * valid_map, axis=axes))


def place():
    wide = lax.axis_index("wide")
    narrow = lax.axis_index("narrow")
    return (wide // 2, wide % 2, narrow // 2, narrow % 2)


def share_core(shard):
    core = place()[3]
    half = shard.shape[1] // 2
    parts = shard.reshape(shard.shape[0], 2, half, shard.shape[2])
    kept = lax.dynamic_index_in_dim(parts, core, 1, keepdims=False)
    given = lax.dynamic_index_in_dim(parts, 1 - core, 1, keepdims=False)
    got = exchange(given, "narrow", 1)
    lower = jnp.where(core == 0, kept, got)
    upper = jnp.where(core == 0, got, kept)
    return jnp.concatenate([lower, upper], axis=2)


def tuned():
    return lax.axis_size("wide") == 2 * ROUNDS and lax.axis_size("narrow") == 4


def kernel_place():
    values = jnp.stack(place()).astype(jnp.int32)
    return values if tuned() else jnp.zeros_like(values)


class Order:
    def __init__(self):
        self.last = None

    def take(self, values):
        if self.last is None:
            return values
        values, self.last = lax.optimization_barrier((values, self.last))
        return values

    def give(self, values):
        self.last = values
        return values

    def run(self, function, *values):
        return self.give(function(*self.take(values)))


def chunk_order(index):
    return [("wide", 1), ("narrow", 2)] if index % 2 == 0 else [("narrow", 2), ("wide", 1)]


def gather_taps(weights, small, fillers, kernels):
    rounds = ROUNDS
    sizes = [[CHUNKS[index] for index in part] for part in PARTS]
    shapes = [item.shape for item in small]
    if not tuned():
        chunks = []
        for part, values in zip(PARTS, weights):
            full = lax.all_gather(values, "narrow", axis=2, tiled=True)
            full = lax.all_gather(full, "wide", axis=1, tiled=True)
            rows = full.shape[1] // (4 * rounds)
            full = full.reshape(full.shape[0], rounds, 2, 2, rows, 2, full.shape[2] // 2)
            start = 0
            for index in part:
                piece = full[start : start + CHUNKS[index]]
                start += CHUNKS[index]
                piece = piece[:, [0] + list(range(rounds - 1, 0, -1))]
                order = (3, 5, 2, 1, 0, 4, 6) if index % 2 == 0 else (3, 2, 5, 1, 0, 4, 6)
                piece = piece.transpose(order)
                chunks.append((piece[0], piece[1]))
        flat = pack_small(small)
        everything = lax.all_gather(flat, ("wide", "narrow"))
        everything = everything.reshape(lax.axis_size("wide"), lax.axis_size("narrow"), -1)
        unpacked = unpack_small(everything, small)
        ready = fillers[0]()
        results = fillers[1](*unpacked)
        result = None
        for part, kernel in zip(PARTS, kernels):
            own = [chunks[index][0] for index in part]
            other = [chunks[index][1] for index in part]
            result = kernel(ready, own, other, result)
        return (chunks, unpacked, ready, results, result)

    def depth(values):
        return [rotate(values, "wide", step, 2) for step in range(1, rounds)]

    def split(part, own, others):
        values = jnp.stack([own] + list(others))
        result = []
        start = 0
        for size in sizes[part]:
            result.append(values[:, start : start + size])
            start += size
        return result

    def along(part, stacks, turn):
        return [
            exchange(stack, *chunk_order(index)[turn]) for stack, index in zip(stacks, PARTS[part])
        ]

    def pair(values, others):
        return [jnp.stack(item) for item in zip(values, others)]

    def across(stacks):
        return [exchange(stack, "narrow", 1) for stack in stacks]

    order = Order()
    shared = [None, None, None]
    shared[0] = order.run(share_core, weights[0])
    z0 = depth(shared[0])
    small = order.run(small_block, list(small))
    xs = exchange(small, "wide", 1)
    shared[1] = order.run(share_core, weights[1])
    z1 = depth(shared[1])
    small = order.run(lambda *items: jnp.stack(items), small, xs)
    ys = exchange(small, "narrow", 2)
    s0 = order.run(functools.partial(split, 0), shared[0], z0)
    f0 = along(0, s0, 0)
    shared[2] = order.run(share_core, weights[2])
    z2 = depth(shared[2])
    small = order.run(lambda *items: jnp.stack(items), small, ys)
    zs = depth(small)
    s0 = order.run(pair, s0, f0)
    g0 = along(0, s0, 1)
    ready = order.run(fillers[0])
    s1 = order.run(functools.partial(split, 1), shared[1], z1)
    f1 = along(1, s1, 0)
    s0 = order.run(pair, s0, g0)
    c0 = across(s0)
    s1 = order.run(pair, s1, f1)
    g1 = along(1, s1, 1)
    result = order.run(kernels[0], ready, s0, c0, None)
    s2 = order.run(functools.partial(split, 2), shared[2], z2)
    f2 = along(2, s2, 0)
    s1 = order.run(pair, s1, g1)
    c1 = across(s1)
    s2 = order.run(pair, s2, f2)
    g2 = along(2, s2, 1)
    small = order.run(lambda own, others: jnp.stack([own] + others), small, zs)
    cs = exchange(small, "narrow", 1)
    result = order.run(kernels[1], ready, s1, c1, result)
    unpacked = order.run(functools.partial(unpack_block, shapes=shapes), small, cs)
    results = order.run(fillers[1], *unpacked)
    s2 = order.run(pair, s2, g2)
    c2 = across(s2)
    result = order.run(kernels[2], ready, s2, c2, result)
    chunks = list(zip(s0 + s1 + s2, c0 + c1 + c2))
    return (chunks, unpacked, ready, results, result)


def add_wide(first, second):
    return first.astype(jnp.float32) + second.astype(jnp.float32)


def narrow(values):
    return values.astype(jnp.bfloat16)


def scatter_taps(grads, shapes, kernels, pack, fillers):
    rounds = ROUNDS
    if not tuned():
        owned = []
        for part, kernel in zip(PARTS, kernels):
            pieces = []
            for index, pair in zip(part, kernel(grads)):
                piece = jnp.stack(pair)
                order = (4, 3, 1, 0, 5, 2, 6) if index % 2 == 0 else (4, 3, 2, 0, 5, 1, 6)
                piece = piece.transpose(order)
                pieces.append(piece.reshape(piece.shape[0], -1, 2 * piece.shape[6]))
            full = jnp.concatenate(pieces)
            full = lax.psum_scatter(full, "wide", scatter_dimension=1, tiled=True)
            full = lax.psum_scatter(full, "narrow", scatter_dimension=2, tiled=True)
            owned.append(full.astype(jnp.float32))
        low, low_weight = fillers[0](grads[0])
        small = pack_grads(low_weight, *pack, shapes)
        small = lax.psum_scatter(small, "wide", scatter_dimension=0, tiled=True)
        small = lax.psum_scatter(small, "narrow", scatter_dimension=1, tiled=True)
        small = unpack_grads(small[0, 0].astype(jnp.float32), shapes)
        return (owned, small, low, fillers[1](None))

    def across(pairs):
        return [exchange(pair[1], "narrow", 1) for pair in pairs]

    def first(pairs, others):
        return [narrow(add_wide(pair[0][1], other[1])) for pair, other in zip(pairs, others)]

    def second(pairs, others, values):
        sent = []
        kept = []
        for pair, other, value in zip(pairs, others, values):
            total = add_wide(pair[0][0], other[0]) + value.astype(jnp.float32)
            kept.append(total[0])
            sent.append(narrow(total[1]))
        return (kept, sent)

    def along(indices, values, turn):
        return [
            exchange(value, *chunk_order(index)[turn]) for value, index in zip(values, indices)
        ]

    def deep(kept, values):
        total = jnp.concatenate(
            [own + value.astype(jnp.float32) for own, value in zip(kept, values)], axis=1
        )
        return (total[0], [narrow(total[step]) for step in range(1, rounds)])

    def turned(values):
        return [rotate(value, "wide", step + 1, 2) for step, value in enumerate(values)]

    def finish(total, values):
        for value in values:
            total = total + value.astype(jnp.float32)
        return total

    def settle(total, values):
        return settle_core(finish(total, values))

    order = Order()
    a, b, c = 2, 1, 0
    pairs_a = kernels[a](grads)
    core_a = across(pairs_a)
    pairs_b = kernels[b](grads, tie=pairs_a[0][0])
    core_b = across(pairs_b)
    sent_a = first(pairs_a, core_a)
    first_a = along(PARTS[a], sent_a, 0)
    pairs_c = kernels[c](grads, tie=sent_a[1])
    core_c = across(pairs_c)
    sent_b = first(pairs_b, core_b)
    first_b = along(PARTS[b], sent_b, 0)
    low, low_weight = fillers[0](sent_b[0])
    pairs_s = [pack_block(pack[0], low_weight, *pack[1:], shapes=shapes, tie=sent_b[1])]
    core_s = across(pairs_s)
    filled = fillers[1](sent_b[1])
    kept_a, sent = order.run(second, pairs_a, core_a, first_a)
    second_a = along(PARTS[a], sent, 1)
    first_c = along(PARTS[c], order.run(first, pairs_c, core_c), 0)
    first_s = along((0,), order.run(first, pairs_s, core_s), 0)
    kept_b, sent = order.run(second, pairs_b, core_b, first_b)
    second_b = along(PARTS[b], sent, 1)
    total_a, sent = order.run(deep, kept_a, second_a)
    deep_a = turned(sent)
    kept_c, sent = order.run(second, pairs_c, core_c, first_c)
    second_c = along(PARTS[c], sent, 1)
    kept_s, sent = order.run(second, pairs_s, core_s, first_s)
    second_s = along((0,), sent, 1)
    total_b, sent = order.run(deep, kept_b, second_b)
    deep_b = turned(sent)
    total_c, sent = order.run(deep, kept_c, second_c)
    deep_c = turned(sent)
    total_s, sent = order.run(deep, kept_s, second_s)
    deep_s = turned(sent)
    owned = [None, None, None]
    owned[a] = settle_core(order.run(finish, total_a, deep_a))
    owned[b] = settle_core(order.run(finish, total_b, deep_b))
    owned[c] = settle_core(order.run(finish, total_c, deep_c))
    small = settle_small(order.run(finish, total_s, deep_s), shapes)
    return (owned, small, low, filled)


def row_span(dilation, row, height):
    step = (row - 1) * dilation
    return (max(step, 0), max(-step, 0), height - abs(step))


def tap_matrix(pair, tap, place_ref, x_first):
    row, core = place_ref[2], place_ref[3]

    def half(ref):
        if x_first:
            return jnp.concatenate([ref[row, 0, 0, tap], ref[1 - row, 0, 0, tap]], axis=1)
        return jnp.concatenate([ref[0, row, 0, tap], ref[0, 1 - row, 0, tap]], axis=1)

    mine = half(pair[0])
    other = half(pair[1])
    lower = jnp.where(core == 0, mine, other)
    upper = jnp.where(core == 0, other, mine)
    return jnp.concatenate([lower, upper], axis=0)


def weight_specs(chunk, x_first):
    taps, rows, cols = chunk[0].shape[3:]
    shape = (2, 1, 1, taps, rows, cols) if x_first else (1, 2, 1, taps, rows, cols)

    def index_map(step, place_ref):
        flip = lax.rem(step + place_ref[1], 2)
        slot = lax.rem(place_ref[0] - step // 2 + ROUNDS, ROUNDS)
        return (0, flip, slot, 0, 0, 0) if x_first else (flip, 0, slot, 0, 0, 0)

    return [pl.BlockSpec(shape, index_map)] * 2


def cost(flops, arrays):
    return pl.CostEstimate(flops=1, bytes_accessed=1, transcendentals=0)


def coarse_flops(rows, shape, width):
    height, columns, channels = shape
    extents = sum(row_span(dilations[branch], line, height)[2] for branch, line in rows)
    return 2 * 3 * extents * columns * channels * width


def full_spec(array):
    return pl.BlockSpec(array.shape, lambda step, place_ref: (0,) * array.ndim)


def lane_spec(array):
    return pl.BlockSpec(
        (array.shape[0], array.shape[1] // (2 * ROUNDS)), lambda step, place_ref: (0, step)
    )


def store_moments(z_ref, mask_ref, stats_ref):
    mask = mask_ref[...]
    count = jnp.sum(mask)
    values = z_ref[...]
    mean = jnp.sum(values * mask, axis=0, keepdims=True) / count
    centered = (values - mean) * mask
    stats_ref[0:1, :] = mean
    stats_ref[1:2, :] = jnp.sum(centered * centered, axis=0, keepdims=True)


def behind_tie(kernel):
    def run(place_ref, tie_ref, *refs):
        kernel(place_ref, *refs)

    return run


def coarse_forward_kernel(plan, place_ref, *refs):
    refs = list(refs)
    mask_ref = refs.pop(0)
    center = refs.pop(0)
    outer = {branch: (refs.pop(0), refs.pop(0)) for branch in plan["branches"]}
    before = {branch: refs.pop(0) for branch in plan["begun"]}
    if plan["pool"]:
        member_ref = refs.pop(0)
        sizes_ref = refs.pop(0)
    pairs = {index: (refs.pop(0), refs.pop(0)) for index in plan["chunks"]}
    results = {branch: refs.pop(0) for branch in plan["branches"]}
    stats = {branch: refs.pop(0) for branch in plan["done"]}
    step = pl.program_id(0)

    @pl.when(step == 0)
    def _():
        for branch in plan["branches"]:
            if branch in before:
                results[branch][...] = before[branch][...]
            else:
                results[branch][...] = jnp.zeros_like(results[branch])

    columns = plan["columns"]
    for branch, row, chunk, tap in plan["rows"]:
        source, target, extent = row_span(dilations[branch], row, plan["height"])
        matrix = jnp.concatenate(
            [tap_matrix(pairs[chunk], tap + k, place_ref, chunk % 2 == 0) for k in range(3)],
            axis=0,
        )
        rows_in = pl.ds(source * columns, extent * columns)
        rows_out = pl.ds(target * columns, extent * columns)
        sides = (outer[branch][0], center, outer[branch][1])
        values = jnp.concatenate([side[rows_in, :] for side in sides], axis=1)
        results[branch][rows_out, :] += jnp.dot(
            values, matrix, preferred_element_type=jnp.float32
        )
    if plan["pool"]:
        point_ref, point_stats_ref, pool_ref, pooled_ref = refs

        @pl.when(step == 0)
        def _():
            point_ref[...] = jnp.zeros_like(point_ref)
            pool_ref[...] = jnp.zeros_like(pool_ref)

        values = center[...]
        x_first = POINT_CHUNK % 2 == 0
        pair = pairs[POINT_CHUNK]
        point_ref[...] += jnp.dot(
            values, tap_matrix(pair, 0, place_ref, x_first), preferred_element_type=jnp.float32
        )
        pooled = jnp.dot(member_ref[...], values, preferred_element_type=jnp.float32)
        pooled = (pooled * sizes_ref[...]).astype(jnp.bfloat16)
        pooled_ref[...] = pooled
        pool_ref[...] += jnp.dot(
            pooled, tap_matrix(pair, 1, place_ref, x_first), preferred_element_type=jnp.float32
        )

    @pl.when(step == 2 * ROUNDS - 1)
    def _():
        for branch in plan["done"]:
            store_moments(results[branch], mask_ref, stats[branch])
        if plan["pool"]:
            store_moments(point_ref, mask_ref, point_stats_ref)


def coarse_forward(part, mask, sides, chunks, shape, begun, pool=None):
    height, columns, channels = shape
    positions = height * columns
    rows = part_rows(part)
    branches = sorted({row[0] for row in rows})
    done = [branch for branch in branches if atrous_layout()[branch][-1][1] in PARTS[part]]
    plan = {
        "pool": pool is not None,
        "chunks": PARTS[part],
        "branches": branches,
        "begun": [branch for branch in branches if branch in begun],
        "done": done,
        "columns": columns,
        "height": height,
        "rows": rows,
    }
    center = sides[0][1]
    args = [mask, center]
    specs = [full_spec(mask), lane_spec(center)]
    for branch in branches:
        args += [sides[branch][0], sides[branch][2]]
        specs += [lane_spec(center)] * 2
    for branch in plan["begun"]:
        args.append(begun[branch])
        specs.append(full_spec(begun[branch]))
    if pool:
        args += list(pool)
        specs += [full_spec(item) for item in pool]
    for index in PARTS[part]:
        args += list(chunks[index])
        specs += weight_specs(chunks[index], index % 2 == 0)
    flat = jax.ShapeDtypeStruct((positions, channels), jnp.float32)
    small = jax.ShapeDtypeStruct((8, channels), jnp.float32)
    outs = [flat] * len(branches) + [small] * len(done)
    if pool:
        outs += [flat, small, small, jax.ShapeDtypeStruct((8, center.shape[1]), jnp.bfloat16)]
    out_specs = [full_spec(item) for item in outs]
    if pool:
        out_specs[-1] = lane_spec(outs[-1])
    results = pl.pallas_call(
        functools.partial(coarse_forward_kernel, plan),
        out_shape=outs,
        grid_spec=pltpu.PrefetchScalarGridSpec(
            num_scalar_prefetch=1, grid=(2 * ROUNDS,), in_specs=specs, out_specs=out_specs
        ),
        compiler_params=pltpu.CompilerParams(vmem_limit_bytes=VMEM_BYTES),
        cost_estimate=cost(
            coarse_flops([row[:2] for row in rows], shape, center.shape[1])
            + (2 * positions * channels * center.shape[1] if pool else 0),
            args + outs,
        ),
        name="coarse_forward",
    )(kernel_place(), *args)
    sums = dict(zip(branches, results))
    stats = dict(zip(done, results[len(branches) :]))
    return (sums, stats, results[len(branches) + len(done) :])


def coarse_weight_kernel(plan, place_ref, *refs):
    refs = list(refs)
    center = refs.pop(0)
    outer = {branch: (refs.pop(0), refs.pop(0)) for branch in plan["branches"]}
    grads = {branch: refs.pop(0) for branch in plan["branches"]}
    if plan["pool"]:
        point_ref, pooled_ref, pool_ref = refs.pop(0), refs.pop(0), refs.pop(0)
    outs = {index: (refs.pop(0), refs.pop(0)) for index in plan["chunks"]}
    row, core = place_ref[2], place_ref[3]
    rows, cols = outs[plan["chunks"][0]][0].shape[-2:]
    columns = plan["columns"]

    def store(chunk, tap, value):
        value = value.astype(jnp.bfloat16)
        lower, upper = value[:rows], value[rows:]
        mine = jnp.where(core == 0, lower, upper)
        other = jnp.where(core == 0, upper, lower)
        for ref, part in zip(outs[chunk], (mine, other)):
            for side, lane_part in ((row, part[:, :cols]), (1 - row, part[:, cols:])):
                if chunk % 2 == 0:
                    ref[0, side, 0, tap] = lane_part
                else:
                    ref[side, 0, 0, tap] = lane_part

    across = (((0,), (0,)), ((), ()))
    for branch, line, chunk, tap in plan["rows"]:
        source, target, extent = row_span(dilations[branch], line, plan["height"])
        sides = (outer[branch][0], center, outer[branch][1])
        values = jnp.concatenate(
            [side[pl.ds(source * columns, extent * columns), :] for side in sides], axis=1
        )
        result = lax.dot_general(
            values,
            grads[branch][pl.ds(target * columns, extent * columns), :],
            across,
            preferred_element_type=jnp.float32,
        )
        for k in range(3):
            store(chunk, tap + k, result[2 * rows * k : 2 * rows * (k + 1)])
    if plan["pool"]:
        for tap, left, right in ((0, center, point_ref), (1, pooled_ref, pool_ref)):
            store(
                POINT_CHUNK,
                tap,
                lax.dot_general(
                    left[...], right[...], across, preferred_element_type=jnp.float32
                ),
            )


def coarse_weight(part, sides, grads, shape, pool=None, tie=None):
    height, columns, channels = shape
    rows = part_rows(part)
    branches = sorted({row[0] for row in rows})
    plan = {
        "pool": pool is not None,
        "branches": branches,
        "chunks": PARTS[part],
        "rows": rows,
        "columns": columns,
        "height": height,
    }
    center = sides[0][1]
    args = [center]
    specs = [lane_spec(center)]
    for branch in branches:
        args += [sides[branch][0], sides[branch][2]]
        specs += [lane_spec(center)] * 2
    for branch in branches:
        args.append(grads[branch])
        specs.append(full_spec(grads[branch]))
    if pool:
        args += list(pool)
        specs += [full_spec(pool[0]), lane_spec(pool[1]), full_spec(pool[2])]
    kernel = functools.partial(coarse_weight_kernel, plan)
    if tie is not None:
        kernel = behind_tie(kernel)
        args.insert(0, tie)
        specs.insert(0, pl.BlockSpec(memory_space=pl.ANY))
    height_now = center.shape[1] // (4 * ROUNDS)
    outs = []
    out_specs = []
    for index in PARTS[part]:
        tail = (CHUNKS[index], height_now, channels // 2)
        block = (1, 2, 1) if index % 2 == 0 else (2, 1, 1)

        def index_map(step, place_ref, x_first=index % 2 == 0):
            flip = lax.rem(step + place_ref[1], 2)
            slot = lax.rem(step // 2 - place_ref[0] + ROUNDS, ROUNDS)
            return (flip, 0, slot, 0, 0, 0) if x_first else (0, flip, slot, 0, 0, 0)

        outs += [jax.ShapeDtypeStruct((2, 2, ROUNDS) + tail, jnp.bfloat16)] * 2
        out_specs += [pl.BlockSpec(block + tail, index_map)] * 2
    results = pl.pallas_call(
        kernel,
        out_shape=outs,
        grid_spec=pltpu.PrefetchScalarGridSpec(
            num_scalar_prefetch=1, grid=(2 * ROUNDS,), in_specs=specs, out_specs=out_specs
        ),
        compiler_params=pltpu.CompilerParams(vmem_limit_bytes=VMEM_BYTES),
        cost_estimate=cost(
            coarse_flops([row[:2] for row in rows], shape, center.shape[1])
            + (2 * height * columns * channels * center.shape[1] if pool else 0),
            args + outs,
        ),
        name="coarse_weight",
    )(kernel_place(), *args)
    return [(results[0], results[1]), (results[2], results[3])]


def coarse_input_kernel(plan, place_ref, *refs):
    refs = list(refs)
    point_ref, pool_ref, spread_ref = refs.pop(0), refs.pop(0), refs.pop(0)
    grads = [refs.pop(0) for _ in range(3)]
    pairs = [(refs.pop(0), refs.pop(0)) for _ in range(plan["chunks"])]
    out_ref, total_ref = refs
    columns = plan["columns"]
    turned = (((1,), (1,)), ((), ()))
    total_ref[...] = lax.dot_general(
        point_ref[...],
        tap_matrix(pairs[POINT_CHUNK], 0, place_ref, POINT_CHUNK % 2 == 0),
        turned,
        preferred_element_type=jnp.float32,
    )
    pooled = lax.dot_general(
        pool_ref[...],
        tap_matrix(pairs[POINT_CHUNK], 1, place_ref, POINT_CHUNK % 2 == 0),
        turned,
        preferred_element_type=jnp.float32,
    )
    total_ref[...] += jnp.dot(
        spread_ref[...], pooled, preferred_element_type=jnp.float32, precision=highest
    )
    for branch, rows in enumerate(plan["rows"]):
        for line, chunk, tap in rows:
            source, target, extent = row_span(dilations[branch], line, plan["height"])
            matrix = jnp.concatenate(
                [tap_matrix(pairs[chunk], tap + k, place_ref, chunk % 2 == 0) for k in range(3)],
                axis=1,
            )
            total_ref[pl.ds(source * columns, extent * columns), :] += lax.dot_general(
                grads[branch][pl.ds(target * columns, extent * columns), :],
                matrix,
                turned,
                preferred_element_type=jnp.float32,
            )
    out_ref[...] = total_ref[...].astype(jnp.bfloat16)


def coarse_input(point_dz, pool_dz, spread, grads, chunks, shape, width, tie=None):
    height, columns, channels = shape
    plan = {
        "chunks": len(chunks),
        "columns": columns,
        "height": height,
        "rows": atrous_layout(),
    }
    args = [point_dz, pool_dz, spread] + list(grads)
    specs = [full_spec(item) for item in args]
    for index, pair in enumerate(chunks):
        args += list(pair)
        specs += weight_specs(pair, index % 2 == 0)
    kernel = functools.partial(coarse_input_kernel, plan)
    if tie is not None:
        kernel = behind_tie(kernel)
        args.insert(0, tie)
        specs.insert(0, pl.BlockSpec(memory_space=pl.ANY))
    out = jax.ShapeDtypeStruct((height * columns, width), jnp.bfloat16)
    return pl.pallas_call(
        kernel,
        out_shape=out,
        grid_spec=pltpu.PrefetchScalarGridSpec(
            num_scalar_prefetch=1,
            grid=(2 * ROUNDS,),
            in_specs=specs,
            out_specs=lane_spec(out),
            scratch_shapes=[pltpu.VMEM((height * columns, width // (2 * ROUNDS)), jnp.float32)],
        ),
        compiler_params=pltpu.CompilerParams(vmem_limit_bytes=VMEM_BYTES),
        cost_estimate=cost(
            coarse_flops([(b, k) for b in range(3) for k in range(3)], shape, width)
            + 2 * height * columns * channels * width,
            args + [out],
        ),
        name="coarse_input",
    )(kernel_place(), *args)


STRIP = 8


def norm_vectors(mean, variance, gain, bias, *more):
    rows = [mean, lax.rsqrt(variance + epsilon), gain, bias] + list(more)
    rows += [jnp.zeros_like(mean)] * (8 - len(rows))
    return jnp.stack(rows)


def sigmoid(values):
    return 0.5 * jnp.tanh(0.5 * values) + 0.5


def vector(ref, index):
    return ref[index : index + 1, :]


def shaped_of(values, vector_ref):
    centered = (values - vector(vector_ref, 0)) * vector(vector_ref, 1)
    return (centered, centered * vector(vector_ref, 2) + vector(vector_ref, 3))


def slope_of(shaped, gate):
    return gate * (1.0 + shaped * (1.0 - gate))


def lag_specs(steps):
    def ahead(array, block):
        return pl.BlockSpec(block, lambda step: (jnp.minimum(step, steps - 1), 0))

    def behind(array, block):
        return pl.BlockSpec(block, lambda step: (jnp.maximum(step - 1, 0), 0))

    return (ahead, behind)


def whole(array):
    return pl.BlockSpec(array.shape, lambda step: (0,) * len(array.shape))


def window(ref, start, step, columns):
    return ref[pl.ds(pl.multiple_of((start + step) * columns, columns), STRIP * columns), :]


def run_moments(values, mask, stats_ref, step):
    count = jnp.sum(mask)
    mean = jnp.sum(values * mask, axis=0, keepdims=True) / count
    centered = (values - mean) * mask
    squares = jnp.sum(centered * centered, axis=0, keepdims=True)
    done = (step - 1).astype(jnp.float32)
    old_mean = jnp.where(step > 1, stats_ref[0:1, :], mean)
    old_squares = jnp.where(step > 1, stats_ref[1:2, :], 0.0)
    gap = mean - old_mean
    stats_ref[0:1, :] = old_mean + gap / (done + 1.0)
    stats_ref[1:2, :] = old_squares + squares + gap * gap * (count * done / (done + 1.0))


def spread_columns(products, masks_ref):
    size = products.shape[0]
    width = products.shape[1] // 3
    result = products[:, width : 2 * width]
    result = result + masks_ref[:, 1:2] * pltpu.roll(products[:, :width], 1, 0)
    return result + masks_ref[:, 2:3] * pltpu.roll(products[:, 2 * width :], size - 1, 0)


def clear_edges(ref, columns):
    ref[:columns, :] = jnp.zeros((columns, ref.shape[1]), ref.dtype)
    ref[ref.shape[0] - columns :, :] = jnp.zeros((columns, ref.shape[1]), ref.dtype)


def row_taps(w_ref, row, start, stop):
    return jnp.concatenate([w_ref[3 * row + k, start:stop, :] for k in range(3)], axis=1)


def low_lanes(width):
    return lax.broadcasted_iota(jnp.int32, (1, width), 1)


def decode_forward_kernel(
    steps, act_ref, table_ref, low_ref, wide_ref, vector_ref, masks_ref, w_ref, z_ref, stats_ref,
    up_ref, joined_ref, reduced_ref
):
    step = pl.program_id(0)
    columns = table_ref.shape[0]
    channels = act_ref.shape[2]
    rows = act_ref.shape[0]

    @pl.when(step == 0)
    def _():
        clear_edges(joined_ref, columns)
        clear_edges(reduced_ref, columns)

    @pl.when(step < steps)
    def _():
        for offset in range(STRIP):
            base = step * (STRIP // 4) + offset // 4 + (offset % 4 - 2) // 2
            fraction = ((2 * (offset % 4) - 3) % 8) / 8.0
            lower = act_ref[jnp.maximum(base, 0)]
            upper = act_ref[jnp.minimum(base + 1, rows - 1)]
            mixed = (1.0 - fraction) * lower + fraction * upper
            coarse = mixed.astype(jnp.bfloat16)
            fine = (mixed - coarse.astype(jnp.float32)).astype(jnp.bfloat16)
            value = jnp.dot(
                table_ref[...],
                jnp.concatenate([coarse, fine], axis=0),
                preferred_element_type=jnp.float32,
            ).astype(jnp.bfloat16)
            up_ref[offset * columns : (offset + 1) * columns, :] = value
            start = pl.multiple_of((step * STRIP + offset + 1) * columns, columns)
            joined_ref[pl.ds(start, columns), :] = value
        reduced = jnp.dot(low_ref[...], wide_ref[...], preferred_element_type=jnp.float32)
        _, shaped = shaped_of(reduced, vector_ref)
        value = masks_ref[:, 0:1] * (shaped * sigmoid(shaped))
        start = pl.multiple_of((step * STRIP + 1) * columns, columns)
        reduced_ref[pl.ds(start, STRIP * columns), :] = value.astype(jnp.bfloat16)

    @pl.when(step > 0)
    def _():
        start = (step - 1) * STRIP
        lane = low_lanes(reduced_ref.shape[1])
        lows = [window(reduced_ref, start, k, columns) for k in range(3)]
        low = jnp.where(lane < 64, lows[0], jnp.where(lane < 128, lows[1], lows[2]))
        values = jnp.concatenate(
            [window(joined_ref, start, k, columns) for k in range(3)] + [low], axis=1
        )
        extra = w_ref.shape[1] - channels
        parts = [row_taps(w_ref, k, 0, channels) for k in range(3)]
        for k in range(3):
            parts.append(row_taps(w_ref, k, channels, channels + extra))
            parts.append(jnp.zeros((64 - extra, 3 * channels), jnp.bfloat16))
        parts.append(jnp.zeros((64, 3 * channels), jnp.bfloat16))
        products = jnp.dot(
            values, jnp.concatenate(parts, axis=0), preferred_element_type=jnp.float32
        )
        result = spread_columns(products, masks_ref)
        z_ref[...] = result
        run_moments(result, masks_ref[:, 0:1], stats_ref, step)


def decode_forward(act, table, low, wide, vectors, masks, weights):
    positions = low.shape[0]
    columns = table.shape[0]
    block = STRIP * columns
    steps = positions // block
    channels = act.shape[2]
    ahead, behind = lag_specs(steps)
    flat = jax.ShapeDtypeStruct((positions, channels), jnp.float32)
    stats = jax.ShapeDtypeStruct((8, channels), jnp.float32)
    up = jax.ShapeDtypeStruct((positions, channels), jnp.bfloat16)
    return pl.pallas_call(
        functools.partial(decode_forward_kernel, steps),
        out_shape=[flat, stats, up],
        grid=(steps + 1,),
        in_specs=[
            whole(act),
            whole(table),
            ahead(low, (block, low.shape[1])),
            whole(wide),
            whole(vectors),
            whole(masks),
            whole(weights),
        ],
        out_specs=[
            behind(flat, (block, channels)),
            whole(stats),
            ahead(up, (block, channels)),
        ],
        scratch_shapes=[
            pltpu.VMEM((positions + 2 * columns, channels), jnp.bfloat16),
            pltpu.VMEM((positions + 2 * columns, wide.shape[1]), jnp.bfloat16),
        ],
        compiler_params=pltpu.CompilerParams(vmem_limit_bytes=VMEM_BYTES),
        cost_estimate=cost(2 * positions * 3 * channels * 4 * channels, [low, flat, up]),
        name="decode_forward",
    )(act, table, low, wide, vectors, masks, weights)


def refine_forward_kernel(
    steps, columns, z_in_ref, vector_ref, masks_ref, w_ref, z_ref, stats_ref, act_ref
):
    step = pl.program_id(0)
    channels = w_ref.shape[1]

    @pl.when(step == 0)
    def _():
        clear_edges(act_ref, columns)

    @pl.when(step < steps)
    def _():
        _, shaped = shaped_of(z_in_ref[...], vector_ref)
        value = masks_ref[:, 0:1] * (shaped * sigmoid(shaped))
        start = pl.multiple_of((step * STRIP + 1) * columns, columns)
        act_ref[pl.ds(start, STRIP * columns), :] = value.astype(jnp.bfloat16)

    @pl.when(step > 0)
    def _():
        start = (step - 1) * STRIP
        values = jnp.concatenate([window(act_ref, start, k, columns) for k in range(3)], axis=1)
        matrix = jnp.concatenate([row_taps(w_ref, k, 0, channels) for k in range(3)], axis=0)
        products = jnp.dot(values, matrix, preferred_element_type=jnp.float32)
        result = spread_columns(products, masks_ref)
        z_ref[...] = result
        run_moments(result, masks_ref[:, 0:1], stats_ref, step)


def refine_forward(z_in, vectors, masks, weights):
    positions, channels = z_in.shape
    block = masks.shape[0]
    columns = block // STRIP
    steps = positions // block
    ahead, behind = lag_specs(steps)
    flat = jax.ShapeDtypeStruct((positions, channels), jnp.float32)
    stats = jax.ShapeDtypeStruct((8, channels), jnp.float32)
    return pl.pallas_call(
        functools.partial(refine_forward_kernel, steps, columns),
        out_shape=[flat, stats],
        grid=(steps + 1,),
        in_specs=[ahead(z_in, (block, channels)), whole(vectors), whole(masks), whole(weights)],
        out_specs=[behind(flat, (block, channels)), whole(stats)],
        scratch_shapes=[pltpu.VMEM((positions + 2 * columns, channels), jnp.bfloat16)],
        compiler_params=pltpu.CompilerParams(vmem_limit_bytes=VMEM_BYTES),
        cost_estimate=cost(2 * positions * 9 * channels * channels, [z_in, flat]),
        name="refine_forward",
    )(z_in, vectors, masks, weights)


def class_kernel(
    z_ref, grad_ref, vector_ref, masks_ref, w_ref, b_ref, logits_ref, sums_ref, weight_ref, bias_ref
):
    step = pl.program_id(0)

    @pl.when(step == 0)
    def _():
        sums_ref[...] = jnp.zeros_like(sums_ref)
        weight_ref[...] = jnp.zeros_like(weight_ref)
        bias_ref[...] = jnp.zeros_like(bias_ref)

    mask = masks_ref[:, 0:1]
    centered, shaped = shaped_of(z_ref[...], vector_ref)
    gate = sigmoid(shaped)
    act = (mask * (shaped * gate)).astype(jnp.bfloat16)
    logits = jnp.dot(act, w_ref[...], preferred_element_type=jnp.float32) + b_ref[...]
    logits_ref[...] = (mask * logits).astype(jnp.bfloat16)
    grad = (mask * grad_ref[...].astype(jnp.float32)).astype(jnp.bfloat16)
    upstream = lax.dot_general(
        grad, w_ref[...], (((1,), (1,)), ((), ())), preferred_element_type=jnp.float32
    )
    local = mask * upstream * slope_of(shaped, gate)
    sums_ref[0:1, :] += jnp.sum(local * centered, axis=0, keepdims=True)
    sums_ref[1:2, :] += jnp.sum(local, axis=0, keepdims=True)
    weight_ref[...] += lax.dot_general(
        grad, act, (((0,), (0,)), ((), ())), preferred_element_type=jnp.float32
    )
    bias_ref[...] += jnp.sum(grad.astype(jnp.float32), axis=0, keepdims=True)


def classify(z, grad, vectors, masks, weights, bias):
    positions, channels = z.shape
    block = masks.shape[0]
    classes = grad.shape[1]
    outs = [
        jax.ShapeDtypeStruct((positions, classes), jnp.bfloat16),
        jax.ShapeDtypeStruct((8, channels), jnp.float32),
        jax.ShapeDtypeStruct((classes, channels), jnp.float32),
        jax.ShapeDtypeStruct((1, classes), jnp.float32),
    ]

    def strip(width):
        return pl.BlockSpec((block, width), lambda step: (step, 0))

    return pl.pallas_call(
        class_kernel,
        out_shape=outs,
        grid=(positions // block,),
        in_specs=[
            strip(channels),
            strip(classes),
            whole(vectors),
            whole(masks),
            whole(weights),
            whole(bias),
        ],
        out_specs=[strip(classes)] + [whole(item) for item in outs[1:]],
        compiler_params=pltpu.CompilerParams(vmem_limit_bytes=VMEM_BYTES),
        cost_estimate=cost(6 * positions * channels * 128, [z, grad, grad]),
        name="classify",
    )(z, grad, vectors, masks, weights, bias)


def finish_grad(local, centered, mask, vector_ref):
    inner = local - vector(vector_ref, 5) - centered * vector(vector_ref, 4)
    return mask * vector(vector_ref, 2) * vector(vector_ref, 1) * inner


def store_sides(grad, masks_ref, side_ref, start):
    size, width = grad.shape
    grad = grad.astype(jnp.bfloat16).astype(jnp.float32)
    rows = pl.ds(start, size)
    side_ref[rows, :width] = pltpu.roll(masks_ref[:, 1:2] * grad, size - 1, 0).astype(jnp.bfloat16)
    side_ref[rows, width : 2 * width] = grad.astype(jnp.bfloat16)
    side_ref[rows, 2 * width :] = pltpu.roll(masks_ref[:, 2:3] * grad, 1, 0).astype(jnp.bfloat16)


def refine_backward_kernel(
    steps, columns, z_ref, grad_ref, vector_ref, cls_ref, z_in_ref, vector_in_ref, masks_ref, w_ref,
    local_ref, sums_ref, weight_ref, side_ref
):
    step = pl.program_id(0)
    channels = w_ref.shape[1]
    mask = masks_ref[:, 0:1]

    @pl.when(step == 0)
    def _():
        clear_edges(side_ref, columns)
        sums_ref[...] = jnp.zeros_like(sums_ref)
        weight_ref[...] = jnp.zeros_like(weight_ref)

    @pl.when(step < steps)
    def _():
        centered, shaped = shaped_of(z_ref[...], vector_ref)
        grad = (mask * grad_ref[...].astype(jnp.float32)).astype(jnp.bfloat16)
        upstream = lax.dot_general(
            grad, cls_ref[...], (((1,), (1,)), ((), ())), preferred_element_type=jnp.float32
        )
        local = mask * upstream * slope_of(shaped, sigmoid(shaped))
        start = pl.multiple_of((step * STRIP + 1) * columns, columns)
        store_sides(finish_grad(local, centered, mask, vector_ref), masks_ref, side_ref, start)

    @pl.when(step > 0)
    def _():
        start = (step - 1) * STRIP
        centered, shaped = shaped_of(z_in_ref[...], vector_in_ref)
        gate = sigmoid(shaped)
        act = (mask * (shaped * gate)).astype(jnp.bfloat16)
        sides = [window(side_ref, start, 2 - k, columns) for k in range(3)]
        upstream = lax.dot_general(
            jnp.concatenate(sides, axis=1),
            jnp.concatenate([w_ref[tap] for tap in range(9)], axis=1),
            (((1,), (1,)), ((), ())),
            preferred_element_type=jnp.float32,
        )
        local = mask * upstream * slope_of(shaped, gate)
        local_ref[...] = local
        sums_ref[0:1, :] += jnp.sum(local * centered, axis=0, keepdims=True)
        sums_ref[1:2, :] += jnp.sum(local, axis=0, keepdims=True)
        turned = act.T
        for k in range(3):
            weight_ref[k] += jnp.dot(turned, sides[k], preferred_element_type=jnp.float32)


def refine_backward(z, grad, vectors, classes, z_in, vectors_in, masks, weights):
    positions, channels = z.shape
    block = masks.shape[0]
    columns = block // STRIP
    steps = positions // block
    ahead, behind = lag_specs(steps)
    outs = [
        jax.ShapeDtypeStruct((positions, channels), jnp.float32),
        jax.ShapeDtypeStruct((8, channels), jnp.float32),
        jax.ShapeDtypeStruct((3, channels, 3 * channels), jnp.float32),
    ]
    return pl.pallas_call(
        functools.partial(refine_backward_kernel, steps, columns),
        out_shape=outs,
        grid=(steps + 1,),
        in_specs=[
            ahead(z, (block, channels)),
            ahead(grad, (block, grad.shape[1])),
            whole(vectors),
            whole(classes),
            behind(z_in, (block, channels)),
            whole(vectors_in),
            whole(masks),
            whole(weights),
        ],
        out_specs=[behind(z, (block, channels)), whole(outs[1]), whole(outs[2])],
        scratch_shapes=[pltpu.VMEM((positions + 2 * columns, 3 * channels), jnp.bfloat16)],
        compiler_params=pltpu.CompilerParams(vmem_limit_bytes=VMEM_BYTES),
        cost_estimate=cost(4 * positions * 9 * channels * channels, [z, z_in, grad, outs[0], weights]),
        name="refine_backward",
    )(z, grad, vectors, classes, z_in, vectors_in, masks, weights)


def decode_backward_kernel(
    steps, columns, local_ref, z_ref, vector_ref, up_ref, low_ref, wide_ref, low_vector_ref,
    table_ref, masks_ref, w_ref, coarse_ref, low_local_ref, sums_ref, weight_ref, low_weight_ref,
    side_ref, total_ref
):
    step = pl.program_id(0)
    channels = w_ref.shape[2]
    extra = w_ref.shape[1] - channels
    mask = masks_ref[:, 0:1]

    @pl.when(step == 0)
    def _():
        clear_edges(side_ref, columns)
        sums_ref[...] = jnp.zeros_like(sums_ref)
        weight_ref[...] = jnp.zeros_like(weight_ref)
        low_weight_ref[...] = jnp.zeros_like(low_weight_ref)
        total_ref[...] = jnp.zeros_like(total_ref)

    @pl.when(step < steps)
    def _():
        centered, _ = shaped_of(z_ref[...], vector_ref)
        start = pl.multiple_of((step * STRIP + 1) * columns, columns)
        grad = finish_grad(local_ref[...], centered, mask, vector_ref)
        store_sides(grad, masks_ref, side_ref, start)

    @pl.when(step > 0)
    def _():
        start = (step - 1) * STRIP
        sides = [window(side_ref, start, 2 - k, columns) for k in range(3)]
        pieces = []
        for tap in range(9):
            pieces.append(
                jnp.concatenate(
                    [w_ref[tap], jnp.zeros((64 - extra, channels), jnp.bfloat16)], axis=0
                )
            )
        upstream = lax.dot_general(
            jnp.concatenate(sides, axis=1),
            jnp.concatenate(pieces, axis=1),
            (((1,), (1,)), ((), ())),
            preferred_element_type=jnp.float32,
        )
        for offset in range(STRIP):
            base = (step - 1) * (STRIP // 4) + offset // 4 + (offset % 4 - 2) // 2
            fraction = ((2 * (offset % 4) - 3) % 8) / 8.0
            value = upstream[offset * columns : (offset + 1) * columns, :channels]
            value = value.astype(jnp.bfloat16).astype(jnp.float32)
            total_ref[base + 1] += (1.0 - fraction) * value
            total_ref[base + 2] += fraction * value
        reduced = jnp.dot(low_ref[...], wide_ref[...], preferred_element_type=jnp.float32)
        centered, shaped = shaped_of(reduced, low_vector_ref)
        gate = sigmoid(shaped)
        low_act = (mask * (shaped * gate)).astype(jnp.bfloat16)
        low_up = upstream[:, channels:]
        local = mask * low_up * slope_of(shaped, gate)[:, :64]
        low_local_ref[...] = local
        sums_ref[0:1, :64] += jnp.sum(local * centered[:, :64], axis=0, keepdims=True)
        sums_ref[1:2, :64] += jnp.sum(local, axis=0, keepdims=True)
        turned = up_ref[...].T
        low_turned = low_act[:, :128].T[:64]
        for k in range(3):
            weight_ref[k] += jnp.dot(turned, sides[k], preferred_element_type=jnp.float32)
            low_weight_ref[k] += jnp.dot(low_turned, sides[k], preferred_element_type=jnp.float32)

    @pl.when(step == steps)
    def _():
        rows = coarse_ref.shape[0]
        total_ref[1] += total_ref[0]
        total_ref[rows] += total_ref[rows + 1]
        for row in range(rows):
            value = total_ref[row + 1]
            upper = value.astype(jnp.bfloat16)
            lower = (value - upper.astype(jnp.float32)).astype(jnp.bfloat16)
            coarse_ref[row] = jnp.dot(
                table_ref[...],
                jnp.concatenate([upper, lower], axis=0),
                preferred_element_type=jnp.float32,
            )


def decode_backward(local, z, vectors, up, low, wide, low_vectors, table, masks, weights, shape):
    positions, channels = z.shape
    block = masks.shape[0]
    columns = block // STRIP
    steps = positions // block
    height, coarse_columns, _ = shape
    ahead, behind = lag_specs(steps)
    outs = [
        jax.ShapeDtypeStruct((height, coarse_columns, channels), jnp.float32),
        jax.ShapeDtypeStruct((positions, 64), jnp.float32),
        jax.ShapeDtypeStruct((8, channels), jnp.float32),
        jax.ShapeDtypeStruct((3, channels, 3 * channels), jnp.float32),
        jax.ShapeDtypeStruct((3, 64, 3 * channels), jnp.float32),
    ]
    return pl.pallas_call(
        functools.partial(decode_backward_kernel, steps, columns),
        out_shape=outs,
        grid=(steps + 1,),
        in_specs=[
            ahead(local, (block, channels)),
            ahead(z, (block, channels)),
            whole(vectors),
            behind(up, (block, channels)),
            behind(low, (block, low.shape[1])),
            whole(wide),
            whole(low_vectors),
            whole(table),
            whole(masks),
            whole(weights),
        ],
        out_specs=[whole(outs[0]), behind(outs[1], (block, 64))]
        + [whole(item) for item in outs[2:]],
        scratch_shapes=[
            pltpu.VMEM((positions + 2 * columns, 3 * channels), jnp.bfloat16),
            pltpu.VMEM((height + 2, columns, channels), jnp.float32),
        ],
        compiler_params=pltpu.CompilerParams(vmem_limit_bytes=VMEM_BYTES),
        cost_estimate=cost(4 * positions * 9 * channels * (channels + 64), [local, z, up, low, outs[1], weights]),
        name="decode_backward",
    )(local, z, vectors, up, low, wide, low_vectors, table, masks, weights)


def low_backward_kernel(
    vector_ref, local_ref, low_ref, wide_ref, masks_ref, out_ref, weight_ref
):
    @pl.when(pl.program_id(0) == 0)
    def _():
        weight_ref[...] = jnp.zeros_like(weight_ref)

    low = low_ref[...]
    weights = wide_ref[:, :128]
    reduced = jnp.dot(low, weights, preferred_element_type=jnp.float32)
    mean, scale, gain = (vector_ref[k : k + 1, :64] for k in range(3))
    centered = (reduced[:, :64] - mean) * scale
    inner = local_ref[...] - vector_ref[5:6, :64] - centered * vector_ref[4:5, :64]
    grad = (masks_ref[:, 0:1] * gain * scale * inner).astype(jnp.bfloat16)
    out_ref[...] = lax.dot_general(
        grad, weights[:, :64], (((1,), (1,)), ((), ())), preferred_element_type=jnp.float32
    ).astype(jnp.bfloat16)
    weight_ref[...] += lax.dot_general(
        grad, low, (((0,), (0,)), ((), ())), preferred_element_type=jnp.float32
    )


def low_backward(local, low, wide, vectors, masks, tie):
    positions, width = low.shape
    block = masks.shape[0]
    outs = [
        jax.ShapeDtypeStruct((positions, width), jnp.bfloat16),
        jax.ShapeDtypeStruct((64, width), jnp.float32),
    ]
    return pl.pallas_call(
        behind_tie(low_backward_kernel),
        out_shape=outs,
        grid=(positions // block,),
        in_specs=[
            whole(vectors),
            pl.BlockSpec(memory_space=pl.ANY),
            pl.BlockSpec((block, 64), lambda step: (step, 0)),
            pl.BlockSpec((block, width), lambda step: (step, 0)),
            whole(wide),
            whole(masks),
        ],
        out_specs=[pl.BlockSpec((block, width), lambda step: (step, 0)), whole(outs[1])],
        compiler_params=pltpu.CompilerParams(vmem_limit_bytes=VMEM_BYTES),
        cost_estimate=cost(6 * positions * width * 128, [local, low, low]),
        name="low_backward",
    )(vectors, tie, local, low, wide, masks)


def atrous_layout():
    places = []
    for chunk, size in enumerate(CHUNKS):
        places += [(chunk, tap) for tap in range(2 if chunk == POINT_CHUNK else 0, size)]
    return [
        [(line,) + places[9 * branch + 3 * line] for line in range(3)] for branch in range(3)
    ]


def part_rows(part):
    return [
        (branch, line, chunk, tap)
        for branch, rows in enumerate(atrous_layout())
        for line, chunk, tap in rows
        if chunk in PARTS[part]
    ]


def order_taps(point, atrous):
    flat = atrous.reshape((-1,) + atrous.shape[2:])
    before = sum(CHUNKS[:POINT_CHUNK])
    flat = jnp.concatenate([flat[:before], point, flat[before:]])
    parts = []
    start = 0
    for part in PARTS:
        size = sum(CHUNKS[index] for index in part)
        parts.append(flat[start : start + size])
        start += size
    return parts


def restore_taps(parts, shape):
    flat = jnp.concatenate(parts)
    before = sum(CHUNKS[:POINT_CHUNK])
    atrous = jnp.concatenate([flat[:before], flat[before + 2 :]])
    return (flat[before : before + 2], atrous.reshape(shape))


def side_values(values, image_ids, dilation):
    result = []
    for step in (-dilation, dilation):
        mask = tap_mask(image_ids, values.shape[1], 0, step).astype(values.dtype)
        result.append(mask * shifted(values, 0, step))
    return [result[0], values, result[1]]


def side_grads(values, image_ids, dilation):
    result = []
    for step in (-dilation, 0, dilation):
        masked = tap_mask(image_ids, values.shape[1], 0, step).astype(values.dtype) * values
        result.append(shifted(masked, 0, -step))
    return jnp.concatenate(result, axis=-1)


def settle_core(values):
    core = place()[3]
    taps, rows, cols = values.shape
    parts = values.reshape(taps, rows, 2, cols // 2)
    kept = lax.dynamic_index_in_dim(parts, core, 2, keepdims=False)
    given = lax.dynamic_index_in_dim(parts, 1 - core, 2, keepdims=False).astype(jnp.bfloat16)
    got = exchange(given, "narrow", 1).astype(jnp.float32)
    lower = jnp.where(core == 0, kept, got)
    upper = jnp.where(core == 0, got, kept)
    return jnp.concatenate([lower, upper], axis=1)


def band_ids(widths, columns):
    ends_all = jnp.cumsum(widths, axis=1)
    position = jnp.arange(columns, dtype=jnp.int32)
    band_index = jnp.sum(
        (position[None, :, None] >= ends_all[:, None, :]).astype(jnp.int32), axis=2
    )
    return jnp.where(band_index < widths.shape[1] - 1, band_index, -1)


def shifted(values, row_shift, col_shift):
    height = values.shape[1]
    columns = values.shape[2]
    padded = jnp.pad(
        values, ((0, 0), (abs(row_shift), abs(row_shift)), (abs(col_shift), abs(col_shift)), (0, 0))
    )
    row_start = abs(row_shift) + row_shift
    col_start = abs(col_shift) + col_shift
    return padded[:, row_start : row_start + height, col_start : col_start + columns, :]


def tap_mask(image_ids, height, row_shift, col_shift):
    columns = image_ids.shape[1]
    padded = jnp.pad(image_ids, ((0, 0), (abs(col_shift), abs(col_shift))), constant_values=-2)
    col_start = abs(col_shift) + col_shift
    other_ids = padded[:, col_start : col_start + columns]
    same_image = (other_ids == image_ids).astype(jnp.float32)
    row_place = jnp.arange(height) + row_shift
    inside = ((row_place >= 0) & (row_place < height)).astype(jnp.float32)
    return (inside[None, :, None] * same_image[:, None, :])[..., None]


def tap_offsets(dilation):
    return [
        ((tap_index // 3 - 1) * dilation, (tap_index % 3 - 1) * dilation) for tap_index in range(9)
    ]


def linear_weights(out_count, in_count):
    position = jnp.arange(out_count, dtype=jnp.int32)
    scaled = 2 * position - 3
    left_index = jnp.floor_divide(scaled, 8)
    fraction = (scaled - 8 * left_index).astype(jnp.float32) / 8.0
    lower_index = jnp.clip(left_index, 0, in_count - 1)
    upper_index = jnp.clip(left_index + 1, 0, in_count - 1)
    return (position, lower_index, upper_index, fraction)


def column_table(image_ids):
    columns = image_ids.shape[1]
    position, lower_index, upper_index, fraction = linear_weights(4 * columns, columns)
    source = jnp.arange(columns, dtype=jnp.int32)[None, :]

    def picker(index_row):
        return (source == index_row[:, None]).astype(jnp.int32)

    def lookup(index_row):
        return jnp.sum(image_ids[:, None, :] * picker(index_row)[None], axis=2)

    own_index = position // 4
    own_id = lookup(own_index)
    weight_lower = (1.0 - fraction)[None, :] * (lookup(lower_index) == own_id).astype(jnp.float32)
    weight_upper = fraction[None, :] * (lookup(upper_index) == own_id).astype(jnp.float32)
    weight_own = 1.0 - weight_lower - weight_upper
    table = weight_lower[:, :, None] * picker(lower_index)[None].astype(jnp.float32)
    table = table + weight_upper[:, :, None] * picker(upper_index)[None].astype(jnp.float32)
    table = table + weight_own[:, :, None] * picker(own_index)[None].astype(jnp.float32)
    return table


def normalize(values, valid_map, mean_row, variance, gain_row, bias_row):
    norm_scale = lax.rsqrt(variance + epsilon)
    centered = (values - mean_row) * norm_scale
    shaped = centered * gain_row + bias_row
    return (valid_map * jax.nn.silu(shaped), centered, shaped, norm_scale)


def norm_grad_terms(upstream, valid_map, centered, shaped):
    sigmoid_value = jax.nn.sigmoid(shaped)
    local_term = valid_map * upstream * sigmoid_value * (1.0 + shaped * (1.0 - sigmoid_value))
    axes = tuple(range(local_term.ndim - 1))
    return (local_term, jnp.sum(local_term * centered, axis=axes), jnp.sum(local_term, axis=axes))


def norm_grad_finish(
    local_term, valid_map, centered, norm_scale, gain_row, gain_sum, bias_sum, count_all
):
    inner = local_term - bias_sum / count_all - centered * gain_sum / count_all
    return (valid_map * gain_row * norm_scale * inner).astype(jnp.bfloat16)


def moments(values, valid_map, local_count, count_all):
    counts, means, squares = merge_all(*local_moments(values, valid_map, local_count))
    return (means, squares / count_all)


def merged(stats, local_count, count_all):
    counts = jnp.full((stats.shape[1],), 1.0) * local_count
    counts, means, squares = merge_all(counts, stats[0], stats[1])
    return (means, squares / count_all)


def pack_pairs(pairs):
    return jnp.concatenate(
        [pair_item[0] for pair_item in pairs] + [pair_item[1] for pair_item in pairs]
    )


def unpack_pairs(flat, pairs):
    lengths = [pair_item[0].shape[0] for pair_item in pairs]
    half_point = sum(lengths)
    result_pairs = []
    offset = 0
    for length_now in lengths:
        result_pairs.append(
            (
                flat[offset : offset + length_now],
                flat[half_point + offset : half_point + offset + length_now],
            )
        )
        offset = offset + length_now
    return result_pairs


def gradient_sums(pairs):
    return unpack_pairs(sum_all(pack_pairs(pairs)), pairs)


def small_block(items):
    proj, reduce, decode, refine = items
    taps, rows, cols = refine.shape
    count = proj.shape[0] // rows
    proj = proj.reshape(2, count, rows // 2, cols).swapaxes(0, 1).reshape(count, rows, cols)
    reduce = jnp.pad(reduce, ((0, 0), (0, cols - reduce.shape[1])))[None]
    shared = share_core(jnp.concatenate([refine, proj, reduce]))
    lanes = shared.shape[2]
    decode = decode.swapaxes(1, 2)
    decode = jnp.pad(decode, ((0, 0), (0, 0), (0, lanes - decode.shape[2])))
    return jnp.concatenate([shared, decode.reshape(-1, shared.shape[1], lanes)])


def settle_small(owned, shapes):
    shape_p, shape_r, shape_d, shape_f = shapes
    taps, rows, cols = shape_f
    count = shape_p[0] // rows
    first = taps + count + 1
    settled = settle_core(owned[:first])
    proj = settled[taps : taps + count].reshape(count, 2, rows // 2, cols)
    proj = proj.swapaxes(0, 1).reshape(shape_p)
    reduce = settled[taps + count, :, : shape_r[1]]
    decode = owned[first:].reshape(taps, shape_d[2], -1)[:, :, : shape_d[1]].swapaxes(1, 2)
    return (proj, reduce, decode, settled[:taps])


def reduce_lanes(width, row, core, half):
    start = (2 * row + core) * width
    return start, core * half


def unpack_kernel(shapes, place_ref, own_ref, other_ref, proj_ref, wide_ref, decode_ref, refine_ref):
    deep, side, row, core = (place_ref[index] for index in range(4))
    shape_p, shape_r, shape_d, shape_f = shapes
    taps = shape_f[0]
    rows = shape_f[1] // 2
    count = shape_p[0] // (2 * rows)
    lanes = own_ref.shape[-1]

    def load(ref, z, x, y, start, size):
        slot = lax.rem(deep - z + ROUNDS, ROUNDS)
        return ref[slot, lax.rem(y + row, 2), lax.rem(x + side, 2), start : start + size]

    def both(z, x, y, start, size):
        mine = load(own_ref, z, x, y, start, size)
        others = load(other_ref, z, x, y, start, size)
        return (jnp.where(core == 0, mine, others), jnp.where(core == 0, others, mine))

    lane = lax.broadcasted_iota(jnp.int32, (1, lanes), 1)
    for z in range(ROUNDS):
        for x in range(2):
            wide = 2 * z + x
            halves = [both(z, x, y, 0, taps + count + 1) for y in range(2)]
            for h in range(2):
                joined = jnp.concatenate([halves[0][h], halves[1][h]], axis=-1)
                base = (2 * wide + h) * rows
                refine_ref[:, base : base + rows, :] = joined[:taps]
                base = (2 * wide + h) * rows * count
                proj_ref[base : base + rows * count, :] = joined[taps : taps + count].reshape(
                    rows * count, 2 * lanes
                )
                total = jnp.zeros((rows, lanes), jnp.float32)
                for y in range(2):
                    value = halves[y][h][taps + count].astype(jnp.float32)
                    for c in range(2):
                        start, held = reduce_lanes(shape_r[1], y, c, lanes // 2)
                        moved = pltpu.roll(value, (start - held) % lanes, 1)
                        inside = (lane >= start) & (lane < start + shape_r[1])
                        total = total + jnp.where(inside, moved, 0.0)
                base = (2 * wide + h) * rows
                left = total + pltpu.roll(total, 64, 1)
                wide_ref[base : base + rows, :] = jnp.concatenate([left, total], axis=1).astype(
                    jnp.bfloat16
                )
    height, width = shape_d[1], shape_d[2]
    blocks = width // rows
    for tap in range(taps):
        start = taps + count + 1 + tap * blocks
        pieces = []
        for y in range(2):
            columns = ([], [])
            for z in range(ROUNDS):
                for x in range(2):
                    for c, value in enumerate(both(z, x, y, start, blocks)):
                        columns[c].append(value.reshape(width, lanes))
            for c in range(2):
                joined = jnp.concatenate(columns[c], axis=0).astype(jnp.float32)
                pieces.append(joined.T[:height])
        decode_ref[tap] = jnp.concatenate(pieces, axis=0).astype(jnp.bfloat16)


def unpack_block(own, other, shapes):
    wide = 2 * ROUNDS
    shape_p, shape_r, shape_d, shape_f = shapes
    outs = [
        jax.ShapeDtypeStruct((wide * shape_p[0], 4 * shape_p[1]), jnp.bfloat16),
        jax.ShapeDtypeStruct((wide * shape_r[0], 256), jnp.bfloat16),
        jax.ShapeDtypeStruct((shape_d[0], 4 * shape_d[1], wide * shape_d[2]), jnp.bfloat16),
        jax.ShapeDtypeStruct((shape_f[0], wide * shape_f[1], 4 * shape_f[2]), jnp.bfloat16),
    ]
    return pl.pallas_call(
        functools.partial(unpack_kernel, shapes),
        out_shape=outs,
        in_specs=[pl.BlockSpec(memory_space=pltpu.SMEM)]
        + [pl.BlockSpec(memory_space=pltpu.VMEM)] * 2,
        out_specs=[pl.BlockSpec(memory_space=pltpu.VMEM)] * 4,
        compiler_params=pltpu.CompilerParams(vmem_limit_bytes=VMEM_BYTES),
        cost_estimate=cost(0, [own, other] + outs + outs),
        name="unpack_weights",
    )(kernel_place(), own, other)


def pack_kernel(
    shapes, place_ref, proj_ref, reduce_ref, decode_ref, low_ref, refine_ref, keep_ref, give_ref
):
    deep, side, row, core = (place_ref[index] for index in range(4))
    shape_p, shape_r, shape_d, shape_f = shapes
    taps = shape_f[0]
    rows = shape_f[1] // 2
    count = shape_p[0] // (2 * rows)
    lanes = keep_ref.shape[-1]
    channels = 2 * lanes

    def store(z, x, y, start, size, values):
        values = [value.astype(jnp.bfloat16) for value in values]
        index = (
            lax.rem(x + side, 2),
            lax.rem(y + row, 2),
            lax.rem(z - deep + ROUNDS, ROUNDS),
            pl.ds(start, size),
        )
        keep_ref[index] = jnp.where(core == 0, values[0], values[1])
        give_ref[index] = jnp.where(core == 0, values[1], values[0])

    lane = lax.broadcasted_iota(jnp.int32, (1, lanes), 1)
    reduce = jnp.concatenate(
        [reduce_ref[...], jnp.zeros((lanes - reduce_ref.shape[0], reduce_ref.shape[1]), jnp.float32)]
    ).T
    moved = []
    for y in range(2):
        total = jnp.zeros_like(reduce)
        for c in range(2):
            start, held = reduce_lanes(shape_r[1], y, c, lanes // 2)
            inside = (lane >= held) & (lane < held + shape_r[1])
            total = total + jnp.where(inside, pltpu.roll(reduce, (held - start) % lanes, 1), 0.0)
        moved.append(total)
    for z in range(ROUNDS):
        for x in range(2):
            wide = 2 * z + x
            for y in range(2):
                columns = slice(y * lanes, (y + 1) * lanes)
                for tap in range(taps):
                    line, k = tap // 3, tap % 3
                    left = k * channels + y * lanes
                    values = []
                    for h in range(2):
                        base = (2 * wide + h) * rows
                        values.append(
                            refine_ref[line, base : base + rows, left : left + lanes][None]
                        )
                    store(z, x, y, tap, 1, values)
                values = []
                for h in range(2):
                    base = (2 * wide + h) * rows * count
                    values.append(
                        proj_ref[base : base + rows * count, columns].reshape(count, rows, lanes)
                    )
                store(z, x, y, taps, count, values)
                values = [
                    moved[y][(2 * wide + h) * rows : (2 * wide + h + 1) * rows][None]
                    for h in range(2)
                ]
                store(z, x, y, taps + count, 1, values)
    height, width = shape_d[1], shape_d[2]
    blocks = width // rows
    for tap in range(taps):
        line, k = tap // 3, tap % 3
        columns = slice(k * channels, (k + 1) * channels)
        whole_tap = jnp.concatenate(
            [
                decode_ref[line, :, columns],
                low_ref[line, :, columns],
                jnp.zeros((lanes, channels), jnp.float32),
            ],
            axis=0,
        )
        turned = [whole_tap[n * height : n * height + lanes].T for n in range(4)]
        for z in range(ROUNDS):
            for x in range(2):
                base = (2 * z + x) * width
                for y in range(2):
                    values = [
                        turned[2 * y + c][base : base + width].reshape(blocks, rows, lanes)
                        for c in range(2)
                    ]
                    store(z, x, y, taps + count + 1 + tap * blocks, blocks, values)


def pack_block(proj, reduce, decode, low, refine, shapes, tie):
    shape_p, shape_r, shape_d, shape_f = shapes
    rows = shape_f[1] // 2
    total = shape_f[0] + shape_p[0] // (2 * rows) + 1 + shape_d[0] * shape_d[2] // rows
    out = jax.ShapeDtypeStruct((2, 2, ROUNDS, total, rows, 2 * shape_f[2]), jnp.bfloat16)
    return pl.pallas_call(
        behind_tie(functools.partial(pack_kernel, shapes)),
        out_shape=[out, out],
        in_specs=[pl.BlockSpec(memory_space=pltpu.SMEM), pl.BlockSpec(memory_space=pl.ANY)]
        + [pl.BlockSpec(memory_space=pltpu.VMEM)] * 5,
        out_specs=[pl.BlockSpec(memory_space=pltpu.VMEM)] * 2,
        compiler_params=pltpu.CompilerParams(vmem_limit_bytes=VMEM_BYTES),
        cost_estimate=cost(0, [proj, decode, low, refine, out, out, out]),
        name="pack_gradients",
    )(kernel_place(), tie, proj, reduce, decode, low, refine)


def low_moments_kernel(low_ref, wide_ref, masks_ref, stats_ref):
    reduced = jnp.dot(low_ref[...], wide_ref[...], preferred_element_type=jnp.float32)
    run_moments(reduced, masks_ref[:, 0:1], stats_ref, pl.program_id(0) + 1)


def low_moments(low, wide, masks):
    block = masks.shape[0]
    out = jax.ShapeDtypeStruct((8, wide.shape[1]), jnp.float32)
    return pl.pallas_call(
        low_moments_kernel,
        out_shape=out,
        grid=(low.shape[0] // block,),
        in_specs=[
            pl.BlockSpec((block, low.shape[1]), lambda step: (step, 0)),
            whole(wide),
            whole(masks),
        ],
        out_specs=whole(out),
        compiler_params=pltpu.CompilerParams(vmem_limit_bytes=VMEM_BYTES),
        cost_estimate=cost(2 * low.shape[0] * low.shape[1] * 256, [low]),
        name="low_moments",
    )(low, wide, masks)


def by_tap(values):
    width = values.shape[2] // 3
    split = values.reshape(3, values.shape[1], 3, width)
    return split.transpose(0, 2, 1, 3).reshape(9, values.shape[1], width)


def widen(values):
    padded = jnp.pad(values, ((0, 0), (0, 64 - values.shape[1])))
    return jnp.concatenate([padded, padded, padded, jnp.zeros_like(padded)], axis=1)


def pack_small(items):
    total = sum(item.size for item in items)
    padded = -(-total // 2048) * 2048
    flats = [item.reshape(-1) for item in items]
    return jnp.concatenate(flats + [jnp.zeros((padded - total,), jnp.bfloat16)]).reshape(-1, 128)


def unpack_small(everything, items):
    wide, narrow = everything.shape[:2]
    everything = everything.reshape(wide, narrow, -1)
    pieces = []
    start = 0
    for item in items:
        pieces.append(
            everything[:, :, start : start + item.size].reshape((wide, narrow) + item.shape)
        )
        start += item.size
    proj, reduce, decode, refine = pieces
    proj = proj.transpose(0, 2, 1, 3).reshape(wide * proj.shape[2], -1)
    reduce = reduce.transpose(0, 2, 1, 3).reshape(wide * reduce.shape[2], -1)
    decode = decode.transpose(2, 1, 3, 0, 4).reshape(decode.shape[2], narrow * decode.shape[3], -1)
    refine = refine.transpose(2, 0, 3, 1, 4).reshape(refine.shape[2], wide * refine.shape[3], -1)
    return (proj, widen(reduce), decode, refine)


def pack_grads(reduce, proj, decode, low, refine, shapes):
    wide = lax.axis_size("wide")
    narrow = lax.axis_size("narrow")
    extra = narrow * shapes[1][1]
    reduce = reduce[:extra].T
    decode = jnp.concatenate([by_tap(decode), by_tap(low)[:, :extra]], axis=1)
    refine = by_tap(refine)
    shape_p, shape_r, shape_d, shape_f = shapes
    proj = proj.reshape(wide, shape_p[0], narrow, shape_p[1]).transpose(0, 2, 1, 3)
    reduce = reduce.reshape(wide, shape_r[0], narrow, shape_r[1]).transpose(0, 2, 1, 3)
    decode = decode.reshape(shape_d[0], narrow, shape_d[1], wide, shape_d[2]).transpose(3, 1, 0, 2, 4)
    refine = refine.reshape(shape_f[0], wide, shape_f[1], narrow, shape_f[2]).transpose(1, 3, 0, 2, 4)
    flats = [
        item.astype(jnp.bfloat16).reshape(wide, narrow, -1)
        for item in (proj, reduce, decode, refine)
    ]
    total = sum(item.shape[2] for item in flats)
    padded = -(-total // 2048) * 2048
    flats.append(jnp.zeros((wide, narrow, padded - total), jnp.bfloat16))
    return jnp.concatenate(flats, axis=2).reshape(wide, narrow, -1, 128)


def unpack_grads(owned, shapes):
    owned = owned.reshape(-1)
    pieces = []
    start = 0
    for shape in shapes:
        size = 1
        for extent in shape:
            size *= extent
        pieces.append(owned[start : start + size].reshape(shape))
        start += size
    return pieces


def per_device(
    features,
    low_level,
    widths,
    w_point,
    w_atrous,
    w_proj,
    w_low,
    w_dec1,
    w_dec2,
    w_cls,
    b_cls,
    gains,
    biases,
    low_gain,
    low_bias,
    logit_grad,
):
    canvases = features.shape[0]
    height = features.shape[1]
    columns = features.shape[2]
    fine_columns = low_level.shape[2]
    images = widths.shape[1] - 1
    channels = gains.shape[1]
    images_total = float(canvases * lax.axis_size("wide") * lax.axis_size("narrow") * images)
    small = [w_proj, w_low, w_dec1, w_dec2]
    ids_coarse = band_ids(widths, columns)
    ids_fine = band_ids(4 * widths, fine_columns)
    valid_coarse = (ids_coarse >= 0).astype(jnp.float32)[:, None, :, None]
    valid_fine = (ids_fine >= 0).astype(jnp.float32)[:, None, :, None]
    all_ones = jnp.ones((1, 1, 1), jnp.float32)
    local_count = (height * jnp.sum(widths[:, :images])).astype(jnp.float32)
    member = (ids_coarse[:, :, None] == jnp.arange(images, dtype=jnp.int32)[None, None, :]).astype(
        jnp.float32
    )
    member_low = member.astype(jnp.bfloat16)
    image_sizes = (height * widths[:, :images]).astype(jnp.float32)
    positions = low_level.shape[1] * fine_columns
    low_flat = low_level.reshape(positions, -1)
    extra = low_gain.shape[0]
    side_masks = [tap_mask(ids_fine, STRIP, 0, step) for step in (-1, 1)]
    masks = jnp.concatenate([valid_fine * jnp.ones((1, STRIP, 1, 1))] + side_masks, axis=-1)
    masks = masks.reshape(STRIP * fine_columns, 3)
    coarse_shape = (height, columns, channels)
    mask_column = jnp.broadcast_to(valid_coarse, (1, height, columns, 1)).reshape(-1, 1)
    member_wide = jnp.pad(member[0], ((0, 0), (0, 8 - images)))
    member_rows = jnp.tile(member_wide, (height, 1))
    sizes_inverse = jnp.pad(1.0 / image_sizes[0], (0, 8 - images)).reshape(8, 1)
    pool_inputs = (member_rows.T.astype(jnp.bfloat16), sizes_inverse)

    def all_sides():
        sides = [
            [
                item.reshape(height * columns, -1)
                for item in side_values(features, ids_coarse, dilation)
            ]
            for dilation in dilations
        ]
        return (sides, logit_grad.reshape(-1, logit_grad.shape[-1]))

    def low_part(proj, wide, decode, refine):
        return low_moments(low_flat, wide, masks)

    def forward(part, ready, own, other, before):
        sums, stats, pooling = ({}, {}, ()) if before is None else before
        pair = dict(zip(PARTS[part], zip(own, other)))
        more, more_stats, more_pooling = coarse_forward(
            part,
            mask_column,
            ready[0],
            pair,
            coarse_shape,
            sums,
            pool_inputs if POINT_CHUNK in PARTS[part] else None,
        )
        return ({**sums, **more}, {**stats, **more_stats}, tuple(pooling) + tuple(more_pooling))

    chunks, unpacked, ready, low_stats, coarse = gather_taps(
        order_taps(w_point, w_atrous),
        small,
        [all_sides, low_part],
        [functools.partial(forward, part) for part in range(3)],
    )
    proj_full, low_wide, decode_full, refine_full = unpacked
    sides, grad_flat = ready
    sums, stats, pool_results = coarse
    point_z, point_stats, pool_z, pooled = pool_results
    pool_z = pool_z[None, :images]
    coarse_stats = [point_stats, stats[0], stats[1], stats[2]]
    coarse_z = [
        item.reshape(1, height, columns, channels) for item in (point_z, sums[0], sums[1], sums[2])
    ]
    blocks = [(item_z, valid_coarse) for item_z in coarse_z] + [(pool_z, all_ones)]
    local_images = float(canvases * images)
    states = [
        (jnp.full((channels,), 1.0) * local_count, item[0], item[1]) for item in coarse_stats
    ] + [
        local_moments(pool_z, all_ones, local_images),
        (
            jnp.full((extra,), 16.0) * local_count,
            low_stats[0, :extra],
            low_stats[1, :extra],
        ),
    ]
    counts_flat, means_flat, squares_flat = merge_all(
        *[jnp.concatenate([state[item] for state in states]) for item in range(3)]
    )
    vars_flat = squares_flat / counts_flat
    section_means = []
    section_vars = []
    offset = 0
    for width in [channels] * 5 + [extra]:
        section_means.append(means_flat[offset : offset + width])
        section_vars.append(vars_flat[offset : offset + width])
        offset += width
    pixel_count = counts_flat[0]
    fine_count = 16.0 * pixel_count
    fine_local = 16.0 * local_count
    gain_rows = [gains[0], gains[1], gains[2], gains[3], gains[4], low_gain]
    bias_rows = [biases[0], biases[1], biases[2], biases[3], biases[4], low_bias]
    kept = []
    activations = []
    for index in range(5):
        block_values, block_valid = blocks[index]
        result = normalize(
            block_values,
            block_valid,
            section_means[index],
            section_vars[index],
            gain_rows[index],
            bias_rows[index],
        )
        kept.append(result[1:])
        activations.append(result[0].astype(jnp.bfloat16))
    spread = jnp.einsum(
        "nwk,nkd->nwd", member_low, activations[4], preferred_element_type=jnp.float32
    ).astype(jnp.bfloat16)
    spread = jnp.broadcast_to(spread[:, None], (canvases, height, columns, channels))
    joined_coarse = jnp.concatenate(activations[:4] + [spread], axis=-1)
    proj_z = jnp.einsum(
        "nhwc,cd->nhwd", joined_coarse, proj_full, preferred_element_type=jnp.float32
    )
    proj_mean, proj_var = moments(proj_z, valid_coarse, local_count, pixel_count)
    proj_act, proj_centered, proj_shaped, proj_scale = normalize(
        proj_z, valid_coarse, proj_mean, proj_var, gains[5], biases[5]
    )
    proj_act = proj_act.astype(jnp.bfloat16).astype(jnp.float32)
    cols_table = column_table(ids_coarse)[0].astype(jnp.bfloat16)
    low_mean, low_var = section_means[5], section_vars[5]
    low_vectors = widen(norm_vectors(low_mean, low_var, low_gain, low_bias))
    decode_z, decode_stats, upsampled = decode_forward(
        proj_act[0],
        jnp.concatenate([cols_table, cols_table], axis=1),
        low_flat,
        low_wide,
        low_vectors,
        masks,
        decode_full,
    )
    decode_mean, decode_var = merged(decode_stats, fine_local, fine_count)
    decode_vectors = norm_vectors(decode_mean, decode_var, gains[6], biases[6])
    refine_z, refine_stats = refine_forward(decode_z, decode_vectors, masks, refine_full)
    refine_mean, refine_var = merged(refine_stats, fine_local, fine_count)
    refine_vectors = norm_vectors(refine_mean, refine_var, gains[7], biases[7])
    logits, refine_sums, cls_weight_grad, cls_bias_grad = classify(
        refine_z, grad_flat, refine_vectors, masks, w_cls, b_cls.reshape(1, -1)
    )
    logits = logits.reshape(logit_grad.shape)
    cls_weight_grad = cls_weight_grad.T
    cls_bias_grad = cls_bias_grad[0]
    refine_gain, refine_bias = gradient_sums([(refine_sums[0], refine_sums[1])])[0]
    refine_vectors = norm_vectors(
        refine_mean,
        refine_var,
        gains[7],
        biases[7],
        refine_gain / fine_count,
        refine_bias / fine_count,
    )
    decode_local, decode_sums, refine_kernel_grad = refine_backward(
        refine_z, grad_flat, refine_vectors, w_cls, decode_z, decode_vectors, masks, refine_full
    )
    decode_gain, decode_bias = gradient_sums([(decode_sums[0], decode_sums[1])])[0]
    decode_vectors = norm_vectors(
        decode_mean,
        decode_var,
        gains[6],
        biases[6],
        decode_gain / fine_count,
        decode_bias / fine_count,
    )
    proj_up, reduce_local, reduce_sums, decode_kernel_grad, low_kernel_grad = decode_backward(
        decode_local,
        decode_z,
        decode_vectors,
        upsampled,
        low_flat,
        low_wide,
        low_vectors,
        jnp.concatenate([cols_table.T, cols_table.T], axis=1),
        masks,
        decode_full,
        coarse_shape,
    )
    proj_up = proj_up[None]
    reduce_gain, reduce_bias = reduce_sums[0, :extra], reduce_sums[1, :extra]

    proj_local, proj_gain, proj_bias = norm_grad_terms(
        proj_up, valid_coarse, proj_centered, proj_shaped
    )
    summed_pairs = gradient_sums([(proj_gain, proj_bias), (reduce_gain, reduce_bias)])
    proj_gain, proj_bias = summed_pairs[0]
    reduce_gain, reduce_bias = summed_pairs[1]
    proj_dz = norm_grad_finish(
        proj_local,
        valid_coarse,
        proj_centered,
        proj_scale,
        gains[5],
        proj_gain,
        proj_bias,
        pixel_count,
    )
    proj_kernel_grad = jnp.einsum(
        "nhwc,nhwd->cd", joined_coarse, proj_dz, preferred_element_type=jnp.float32
    )
    concat_grad = jnp.einsum(
        "nhwd,cd->nhwc", proj_dz, proj_full, preferred_element_type=jnp.float32
    )
    branch_terms = []
    for index in range(4):
        upstream = concat_grad[..., index * channels : (index + 1) * channels]
        branch_terms.append(norm_grad_terms(upstream, valid_coarse, kept[index][0], kept[index][1]))
    pool_up = jnp.einsum(
        "nhwd,nwk->nkd", concat_grad[..., 4 * channels :], member, precision=highest
    )
    branch_terms.append(norm_grad_terms(pool_up, all_ones, kept[4][0], kept[4][1]))
    local_pairs = [(term_item[1], term_item[2]) for term_item in branch_terms]
    flat_pairs = pack_pairs(local_pairs)
    flat_sums = sum_all(
        jnp.concatenate([flat_pairs, cls_bias_grad, cls_weight_grad.reshape(-1)])
    )
    classes = cls_bias_grad.shape[0]
    cls_weight_grad = flat_sums[flat_pairs.shape[0] + classes :].reshape(cls_weight_grad.shape)
    cls_bias_grad = flat_sums[flat_pairs.shape[0] : flat_pairs.shape[0] + classes]
    flat_sums = flat_sums[: flat_pairs.shape[0]]
    last_pairs = unpack_pairs(flat_sums, local_pairs)
    valid_list = [valid_coarse, valid_coarse, valid_coarse, valid_coarse, all_ones]
    count_list = [pixel_count, pixel_count, pixel_count, pixel_count, images_total]
    branch_dz = [
        norm_grad_finish(
            branch_terms[index][0],
            valid_list[index],
            kept[index][0],
            kept[index][2],
            gains[index],
            last_pairs[index][0],
            last_pairs[index][1],
            count_list[index],
        )
        for index in range(5)
    ]
    flat_dz = [item.reshape(height * columns, channels) for item in branch_dz[:4]]
    pool_dz = jnp.pad(branch_dz[4][0], ((0, 8 - images), (0, 0)))
    low_vectors = widen(
        norm_vectors(
            low_mean,
            low_var,
            low_gain,
            low_bias,
            reduce_gain / fine_count,
            reduce_bias / fine_count,
        )
    )

    def low_late(tie):
        return low_backward(reduce_local, low_flat, low_wide, low_vectors, masks, tie)

    def input_late(tie):
        side_dz = [
            side_grads(branch_dz[branch + 1], ids_coarse, dilations[branch]).reshape(
                height * columns, -1
            )
            for branch in range(3)
        ]
        return coarse_input(
            flat_dz[0],
            pool_dz,
            member_rows * sizes_inverse.reshape(1, 8),
            side_dz,
            chunks,
            coarse_shape,
            features.shape[3],
            tie,
        )

    def weight_part(part, grads, tie=None):
        return coarse_weight(
            part,
            sides,
            grads[1:4],
            coarse_shape,
            (grads[0], pooled, grads[4]) if POINT_CHUNK in PARTS[part] else None,
            tie,
        )

    owned, small_owned, low_level_grad, features_grad = scatter_taps(
        flat_dz + [pool_dz],
        [item.shape for item in small],
        [functools.partial(weight_part, part) for part in range(3)],
        (proj_kernel_grad, decode_kernel_grad, low_kernel_grad, refine_kernel_grad),
        [low_late, input_late],
    )
    low_level_grad = low_level_grad.reshape(low_level.shape)
    features_grad = features_grad.reshape(features.shape)
    proj_owned, reduce_owned, decode_owned, refine_owned = small_owned
    point_owned, atrous_owned = restore_taps(owned, w_atrous.shape)
    gains_grad = jnp.stack(
        [
            last_pairs[0][0],
            last_pairs[1][0],
            last_pairs[2][0],
            last_pairs[3][0],
            last_pairs[4][0],
            proj_gain,
            decode_gain,
            refine_gain,
        ]
    )
    biases_grad = jnp.stack(
        [
            last_pairs[0][1],
            last_pairs[1][1],
            last_pairs[2][1],
            last_pairs[3][1],
            last_pairs[4][1],
            proj_bias,
            decode_bias,
            refine_bias,
        ]
    )
    return (
        logits,
        features_grad,
        low_level_grad,
        point_owned,
        atrous_owned,
        proj_owned,
        reduce_owned,
        decode_owned,
        refine_owned,
        cls_weight_grad,
        cls_bias_grad,
        gains_grad,
        biases_grad,
        reduce_gain,
        reduce_bias,
    )


def solution(mesh):
    in_specs = (
        P(("wide", "narrow"), None, None, None),
        P(("wide", "narrow"), None, None, None),
        P(("wide", "narrow"), None),
        P(None, "wide", "narrow"),
        P(None, None, "wide", "narrow"),
        P("wide", "narrow"),
        P("wide", "narrow"),
        P(None, "narrow", "wide"),
        P(None, "wide", "narrow"),
        P(),
        P(),
        P(),
        P(),
        P(),
        P(),
        P(("wide", "narrow"), None, None, None),
    )
    out_specs = (
        P(("wide", "narrow"), None, None, None),
        P(("wide", "narrow"), None, None, None),
        P(("wide", "narrow"), None, None, None),
        P(None, "wide", "narrow"),
        P(None, None, "wide", "narrow"),
        P("wide", "narrow"),
        P("wide", "narrow"),
        P(None, "narrow", "wide"),
        P(None, "wide", "narrow"),
        P(),
        P(),
        P(),
        P(),
        P(),
        P(),
    )
    return jax.shard_map(
        per_device, mesh=mesh, in_specs=in_specs, out_specs=out_specs, check_vma=False
    )
```

```python
import functools

import jax
import jax.numpy as jnp
from jax import lax
from jax.experimental import pallas as pl
from jax.experimental.pallas import tpu as pltpu
from jax.sharding import PartitionSpec as P

epsilon = 1e-05
highest = lax.Precision.HIGHEST
dilations = (6, 12, 18)
ROUNDS = 4
CHUNKS = (3, 3, 5, 6, 6, 6)
PARTS = ((0, 1), (2, 3), (4, 5))
POINT_CHUNK = 2
VMEM_BYTES = 48 * 1024 * 1024


def exchange(values, axis, bit):
    size = lax.axis_size(axis)
    return lax.ppermute(values, axis, [(place, place ^ bit) for place in range(size)])


def rotate(values, axis, step, stride):
    size = lax.axis_size(axis)
    rounds = size // stride
    pairs = []
    for place in range(size):
        outer, inner = place // stride, place % stride
        pairs.append((place, ((outer + step) % rounds) * stride + inner))
    return lax.ppermute(values, axis, pairs)


def device_count():
    return lax.axis_size("wide") * lax.axis_size("narrow")


def hand_out(rows):
    return lax.all_to_all(rows, ("wide", "narrow"), 0, 0, tiled=True)


def from_all(values):
    return hand_out(jnp.broadcast_to(values[None], (device_count(),) + values.shape))


def merge_rows(counts, means, squares):
    total = jnp.sum(counts, axis=0)
    mean = jnp.sum(counts * means, axis=0) / total
    gap = means - mean[None]
    return (total, mean, jnp.sum(squares + counts * gap * gap, axis=0))


def local_moments(values, valid_map, count):
    axes = tuple(range(values.ndim - 1))
    mean = jnp.sum(values * valid_map, axis=axes) / count
    centered = values - mean
    return (mean, jnp.sum(centered * centered * valid_map, axis=axes))


def place():
    wide = lax.axis_index("wide")
    narrow = lax.axis_index("narrow")
    return (wide // 2, wide % 2, narrow // 2, narrow % 2)


def share_core(shard):
    core = place()[3]
    half = shard.shape[1] // 2
    parts = shard.reshape(shard.shape[0], 2, half, shard.shape[2])
    kept = lax.dynamic_index_in_dim(parts, core, 1, keepdims=False)
    given = lax.dynamic_index_in_dim(parts, 1 - core, 1, keepdims=False)
    got = exchange(given, "narrow", 1)
    lower = jnp.where(core == 0, kept, got)
    upper = jnp.where(core == 0, got, kept)
    return jnp.concatenate([lower, upper], axis=2)


def tuned():
    return lax.axis_size("wide") == 2 * ROUNDS and lax.axis_size("narrow") == 4


def kernel_place():
    values = jnp.stack(place()).astype(jnp.int32)
    return values if tuned() else jnp.zeros_like(values)


class Order:
    def __init__(self):
        self.last = None

    def take(self, values):
        if self.last is None:
            return values
        values, self.last = lax.optimization_barrier((values, self.last))
        return values

    def give(self, values):
        self.last = values
        return values

    def run(self, function, *values):
        return self.give(function(*self.take(values)))


def one_step(body, outs, args, specs=None, tie=None):
    def whole_spec(array):
        return pl.BlockSpec(array.shape, lambda step: (0,) * len(array.shape))

    specs = list(specs or [None] * len(args))
    run = body
    if tie is not None:
        args = [tie] + list(args)
        specs = [pl.BlockSpec(memory_space=pl.ANY)] + specs

        def run(tie_ref, *refs):
            body(*refs)

    return pl.pallas_call(
        run,
        out_shape=outs,
        grid=(1,),
        in_specs=[spec or whole_spec(arg) for spec, arg in zip(specs, args)],
        out_specs=[whole_spec(out) for out in outs],
        compiler_params=pltpu.CompilerParams(vmem_limit_bytes=VMEM_BYTES),
        cost_estimate=cost(0, args),
        name="move",
    )(*args)


def entry_spec(array, index):
    block = (1,) + array.shape[1:]
    return pl.BlockSpec(block, lambda step: (index,) + (0,) * (len(block) - 1))


def cut(sizes):
    return [slice(sum(sizes[:index]), sum(sizes[: index + 1])) for index in range(len(sizes))]


def first_sums(sizes, keep, got, tie=None):
    tail = keep.shape[4:]
    outs = [jax.ShapeDtypeStruct((2, ROUNDS, size) + tail, jnp.bfloat16) for size in sizes]

    def body(keep_ref, got_ref, *targets):
        for target, taps in zip(targets, cut(sizes)):
            total = keep_ref[0, :, :, taps].astype(jnp.float32)
            total = total + got_ref[0, :, :, taps].astype(jnp.float32)
            target[...] = total.astype(jnp.bfloat16)

    return one_step(body, outs, [keep, got], [entry_spec(keep, 1), entry_spec(got, 1)], tie)


def second_sums(sizes, keep, got, values, tie=None):
    tail = keep.shape[4:]
    outs = [jax.ShapeDtypeStruct((ROUNDS, sum(sizes)) + tail, jnp.float32)]
    outs += [jax.ShapeDtypeStruct((ROUNDS, size) + tail, jnp.bfloat16) for size in sizes]
    count = len(sizes)

    def body(keep_ref, got_ref, *refs):
        kept = refs[count]
        for index, taps in enumerate(cut(sizes)):
            for half in range(2):
                total = keep_ref[0, half, :, taps].astype(jnp.float32)
                total = total + got_ref[0, half, :, taps].astype(jnp.float32)
                total = total + refs[index][half].astype(jnp.float32)
                if half:
                    refs[count + 1 + index][...] = total.astype(jnp.bfloat16)
                else:
                    kept[:, taps] = total

    specs = [entry_spec(keep, 0), entry_spec(got, 0)] + [None] * count
    results = one_step(body, outs, [keep, got] + list(values), specs, tie)
    return (results[0], results[1:])


def deep_sums(sizes, kept, values, tie=None):
    shape = (2,) + kept.shape[1:]
    outs = [jax.ShapeDtypeStruct(shape, dtype) for dtype in (jnp.float32, jnp.bfloat16)]
    count = len(sizes)

    def body(kept_ref, *refs):
        for slot in range(ROUNDS):
            target = refs[count + slot // 2]
            for value, taps in zip(refs, cut(sizes)):
                total = kept_ref[slot, taps] + value[slot].astype(jnp.float32)
                target[slot % 2, taps] = total.astype(target.dtype)

    return one_step(body, outs, [kept] + list(values), None, tie)


def near_sums(kept, far, tie=None):
    shape = kept.shape[1:]
    outs = [jax.ShapeDtypeStruct(shape, dtype) for dtype in (jnp.float32, jnp.bfloat16)]

    def body(kept_ref, far_ref, *targets):
        for slot, target in enumerate(targets):
            total = kept_ref[slot] + far_ref[slot].astype(jnp.float32)
            target[...] = total.astype(target.dtype)

    return one_step(body, outs, [kept, far], None, tie)


def last_sums(kept, near, tie=None):
    def body(kept_ref, near_ref, target):
        target[...] = kept_ref[...] + near_ref[...].astype(jnp.float32)

    outs = [jax.ShapeDtypeStruct(kept.shape, jnp.float32)]
    return one_step(body, outs, [kept, near], None, tie)[0]


def chunk_order(index):
    return [("wide", 1), ("narrow", 2)] if index % 2 == 0 else [("narrow", 2), ("wide", 1)]


def gather_taps(weights, small, fillers, kernels):
    rounds = ROUNDS
    sizes = [[CHUNKS[index] for index in part] for part in PARTS]
    shapes = [item.shape for item in small]
    if not tuned():
        chunks = []
        for part, values in zip(PARTS, weights):
            full = lax.all_gather(values, "narrow", axis=2, tiled=True)
            full = lax.all_gather(full, "wide", axis=1, tiled=True)
            rows = full.shape[1] // (4 * rounds)
            full = full.reshape(full.shape[0], rounds, 2, 2, rows, 2, full.shape[2] // 2)
            start = 0
            for index in part:
                piece = full[start : start + CHUNKS[index]]
                start += CHUNKS[index]
                piece = piece[:, [0] + list(range(rounds - 1, 0, -1))]
                order = (3, 5, 2, 1, 0, 4, 6) if index % 2 == 0 else (3, 2, 5, 1, 0, 4, 6)
                piece = piece.transpose(order)
                chunks.append((piece[0], piece[1]))
        flat = pack_small(small)
        everything = lax.all_gather(flat, ("wide", "narrow"))
        everything = everything.reshape(lax.axis_size("wide"), lax.axis_size("narrow"), -1)
        unpacked = unpack_small(everything, small)
        ready = fillers[0]()
        results = fillers[1](*unpacked)
        result = None
        for part, kernel in zip(PARTS, kernels):
            own = [chunks[index][0] for index in part]
            other = [chunks[index][1] for index in part]
            result = kernel(ready, own, other, result)
        return (chunks, unpacked, ready, results, result)

    def depth(values):
        return [rotate(values, "wide", step, 2) for step in range(1, rounds)]

    def split(part, own, others):
        values = jnp.stack([own] + list(others))
        result = []
        start = 0
        for size in sizes[part]:
            result.append(values[:, start : start + size])
            start += size
        return result

    def along(part, stacks, turn):
        return [
            exchange(stack, *chunk_order(index)[turn]) for stack, index in zip(stacks, PARTS[part])
        ]

    def pair(values, others):
        return [jnp.stack(item) for item in zip(values, others)]

    def across(stacks):
        return [exchange(stack, "narrow", 1) for stack in stacks]

    order = Order()
    shared = [None, None, None]
    shared[0] = order.run(share_core, weights[0])
    z0 = depth(shared[0])
    small = order.run(small_block, list(small))
    xs = exchange(small, "wide", 1)
    shared[1] = order.run(share_core, weights[1])
    z1 = depth(shared[1])
    small = order.run(lambda *items: jnp.stack(items), small, xs)
    ys = exchange(small, "narrow", 2)
    s0 = order.run(functools.partial(split, 0), shared[0], z0)
    f0 = along(0, s0, 0)
    shared[2] = order.run(share_core, weights[2])
    z2 = depth(shared[2])
    small = order.run(lambda *items: jnp.stack(items), small, ys)
    zs = depth(small)
    s0 = order.run(pair, s0, f0)
    g0 = along(0, s0, 1)
    ready = order.run(fillers[0])
    s1 = order.run(functools.partial(split, 1), shared[1], z1)
    f1 = along(1, s1, 0)
    s0 = order.run(pair, s0, g0)
    c0 = across(s0)
    s1 = order.run(pair, s1, f1)
    g1 = along(1, s1, 1)
    result = order.run(kernels[0], ready, s0, c0, None)
    s2 = order.run(functools.partial(split, 2), shared[2], z2)
    f2 = along(2, s2, 0)
    s1 = order.run(pair, s1, g1)
    c1 = across(s1)
    s2 = order.run(pair, s2, f2)
    g2 = along(2, s2, 1)
    small = order.run(lambda own, others: jnp.stack([own] + others), small, zs)
    cs = exchange(small, "narrow", 1)
    result = order.run(kernels[1], ready, s1, c1, result)
    unpacked = order.run(functools.partial(unpack_block, shapes=shapes), small, cs)
    results = order.run(fillers[1], *unpacked)
    s2 = order.run(pair, s2, g2)
    c2 = across(s2)
    result = order.run(kernels[2], ready, s2, c2, result)
    chunks = list(zip(s0 + s1 + s2, c0 + c1 + c2))
    return (chunks, unpacked, ready, results, result)


def add_wide(first, second):
    return first.astype(jnp.float32) + second.astype(jnp.float32)


def narrow(values):
    return values.astype(jnp.bfloat16)


def scatter_taps(grads, shapes, kernels, pack, fillers):
    rounds = ROUNDS
    if not tuned():
        owned = []
        for part, kernel in zip(PARTS, kernels):
            joined = jnp.stack(kernel(grads))
            pieces = []
            for index, taps in zip(part, cut([CHUNKS[index] for index in part])):
                piece = joined[:, :, :, :, taps]
                order = (4, 3, 1, 0, 5, 2, 6) if index % 2 == 0 else (4, 3, 2, 0, 5, 1, 6)
                piece = piece.transpose(order)
                pieces.append(piece.reshape(piece.shape[0], -1, 2 * piece.shape[6]))
            full = jnp.concatenate(pieces)
            full = lax.psum_scatter(full, "wide", scatter_dimension=1, tiled=True)
            full = lax.psum_scatter(full, "narrow", scatter_dimension=2, tiled=True)
            owned.append(full.astype(jnp.float32))
        low, low_weight = fillers[0](grads[0])
        small = pack_grads(low_weight, *pack, shapes)
        small = lax.psum_scatter(small, "wide", scatter_dimension=0, tiled=True)
        small = lax.psum_scatter(small, "narrow", scatter_dimension=1, tiled=True)
        small = unpack_grads(small[0, 0].astype(jnp.float32), shapes)
        return (owned, small, low, fillers[1](None))

    sizes = [[CHUNKS[index] for index in part] for part in PARTS]

    def across(pair):
        return (pair[0], exchange(pair[1], "narrow", 1))

    def along(indices, values, turn):
        return [
            exchange(value, *chunk_order(index)[turn]) for value, index in zip(values, indices)
        ]

    def far(sent):
        return exchange(sent, "wide", 4)

    def near(sent):
        return exchange(sent, "wide", 2)

    a, b, c = 2, 1, 0
    pair_a = across(kernels[a](grads))
    pair_b = across(kernels[b](grads, tie=pair_a[0]))
    sent = first_sums(sizes[a], *pair_a, pair_b[0])
    first_a = along(PARTS[a], sent, 0)
    low, low_weight = fillers[0](sent[0])
    pair_s = across(pack_block(pack[0], low_weight, *pack[1:], shapes=shapes, tie=low_weight))
    sizes_s = [pair_s[0].shape[3]]
    pair_c = across(kernels[c](grads, tie=pair_s[0]))
    kept_a, sent = second_sums(sizes[a], *pair_a, first_a, pair_c[0])
    second_a = along(PARTS[a], sent, 1)
    sent = first_sums(sizes[b], *pair_b, sent[0])
    first_b = along(PARTS[b], sent, 0)
    kept_a, sent = deep_sums(sizes[a], kept_a, second_a, sent[0])
    far_a = far(sent)
    sent = first_sums(sizes_s, *pair_s, sent)
    first_s = along((0,), sent, 0)
    filled = fillers[1](sent[0])
    kept_b, sent = second_sums(sizes[b], *pair_b, first_b, filled)
    second_b = along(PARTS[b], sent, 1)
    sent = first_sums(sizes[c], *pair_c, sent[0])
    first_c = along(PARTS[c], sent, 0)
    kept_s, sent = second_sums(sizes_s, *pair_s, first_s, sent[0])
    second_s = along((0,), sent, 1)
    total_a, sent = near_sums(kept_a, far_a, sent[0])
    near_a = near(sent)
    kept_b, sent = deep_sums(sizes[b], kept_b, second_b, sent)
    far_b = far(sent)
    kept_c, sent = second_sums(sizes[c], *pair_c, first_c, sent)
    second_c = along(PARTS[c], sent, 1)
    kept_s, sent = deep_sums(sizes_s, kept_s, second_s, sent[0])
    far_s = far(sent)
    total_a = last_sums(total_a, near_a, sent)
    kept_c, sent = deep_sums(sizes[c], kept_c, second_c, total_a)
    far_c = far(sent)
    total_b, sent = near_sums(kept_b, far_b, sent)
    near_b = near(sent)
    total_s, sent = near_sums(kept_s, far_s, sent)
    near_s = near(sent)
    total_c, sent = near_sums(kept_c, far_c, sent)
    near_c = near(sent)
    total_b = last_sums(total_b, near_b, sent)
    total_s = last_sums(total_s, near_s, total_b)
    total_c = last_sums(total_c, near_c, total_s)
    owned = [settle_core(total) for total in (total_c, total_b, total_a)]
    small = settle_small(total_s, shapes)
    return (owned, small, low, filled)


def row_span(dilation, row, height):
    step = (row - 1) * dilation
    return (max(step, 0), max(-step, 0), height - abs(step))


def tap_matrix(pair, tap, place_ref, x_first):
    row, core = place_ref[2], place_ref[3]

    def half(ref):
        if x_first:
            return jnp.concatenate([ref[row, 0, 0, tap], ref[1 - row, 0, 0, tap]], axis=1)
        return jnp.concatenate([ref[0, row, 0, tap], ref[0, 1 - row, 0, tap]], axis=1)

    mine = half(pair[0])
    other = half(pair[1])
    lower = jnp.where(core == 0, mine, other)
    upper = jnp.where(core == 0, other, mine)
    return jnp.concatenate([lower, upper], axis=0)


def weight_specs(chunk, x_first):
    taps, rows, cols = chunk[0].shape[3:]
    shape = (2, 1, 1, taps, rows, cols) if x_first else (1, 2, 1, taps, rows, cols)

    def index_map(step, place_ref):
        flip = lax.rem(step + place_ref[1], 2)
        slot = lax.rem(place_ref[0] - step // 2 + ROUNDS, ROUNDS)
        return (0, flip, slot, 0, 0, 0) if x_first else (flip, 0, slot, 0, 0, 0)

    return [pl.BlockSpec(shape, index_map)] * 2


def whole_cost(flops, arrays):
    total = 0
    for array in arrays:
        size = array.dtype.itemsize
        for extent in array.shape:
            size *= extent
        total += size
    return pl.CostEstimate(flops=int(flops), bytes_accessed=total, transcendentals=0)


def cost(flops, arrays):
    return pl.CostEstimate(flops=1, bytes_accessed=1, transcendentals=0)


def coarse_flops(rows, shape, width):
    height, columns, channels = shape
    extents = sum(row_span(dilations[branch], line, height)[2] for branch, line in rows)
    return 2 * 3 * extents * columns * channels * width


def chunk_part(chunk):
    return [index for index, part in enumerate(PARTS) if chunk in part][0]


def chunk_start(chunk):
    part = PARTS[chunk_part(chunk)]
    return sum(CHUNKS[index] for index in part[: part.index(chunk)])


def part_spec(array):
    def index_map(step, place_ref):
        return (0, 0, lax.bitwise_xor(step // 2, place_ref[0]), 0, 0, 0)

    return pl.BlockSpec((2, 2, 1) + array.shape[3:], index_map)


def full_spec(array):
    return pl.BlockSpec(array.shape, lambda step, place_ref: (0,) * array.ndim)


def lane_spec(array):
    return pl.BlockSpec(
        (array.shape[0], array.shape[1] // (2 * ROUNDS)), lambda step, place_ref: (0, step)
    )


def store_moments(z_ref, mask_ref, stats_ref):
    mask = mask_ref[...]
    count = jnp.sum(mask)
    values = z_ref[...]
    mean = jnp.sum(values * mask, axis=0, keepdims=True) / count
    centered = (values - mean) * mask
    stats_ref[0:1, :] = mean
    stats_ref[1:2, :] = jnp.sum(centered * centered, axis=0, keepdims=True)


def behind_tie(kernel):
    def run(place_ref, tie_ref, *refs):
        kernel(place_ref, *refs)

    return run


def coarse_forward_kernel(plan, place_ref, *refs):
    refs = list(refs)
    mask_ref = refs.pop(0)
    center = refs.pop(0)
    outer = {branch: (refs.pop(0), refs.pop(0)) for branch in plan["branches"]}
    before = {branch: refs.pop(0) for branch in plan["begun"]}
    if plan["pool"]:
        member_ref = refs.pop(0)
        sizes_ref = refs.pop(0)
    pairs = {index: (refs.pop(0), refs.pop(0)) for index in plan["chunks"]}
    results = {branch: refs.pop(0) for branch in plan["branches"]}
    stats = {branch: refs.pop(0) for branch in plan["done"]}
    step = pl.program_id(0)

    @pl.when(step == 0)
    def _():
        for branch in plan["branches"]:
            if branch in before:
                results[branch][...] = before[branch][...]
            else:
                results[branch][...] = jnp.zeros_like(results[branch])

    columns = plan["columns"]
    for branch, row, chunk, tap in plan["rows"]:
        source, target, extent = row_span(dilations[branch], row, plan["height"])
        matrix = jnp.concatenate(
            [tap_matrix(pairs[chunk], tap + k, place_ref, chunk % 2 == 0) for k in range(3)],
            axis=0,
        )
        rows_in = pl.ds(source * columns, extent * columns)
        rows_out = pl.ds(target * columns, extent * columns)
        sides = (outer[branch][0], center, outer[branch][1])
        values = jnp.concatenate([side[rows_in, :] for side in sides], axis=1)
        results[branch][rows_out, :] += jnp.dot(
            values, matrix, preferred_element_type=jnp.float32
        )
    if plan["pool"]:
        point_ref, point_stats_ref, pool_ref, pooled_ref = refs

        @pl.when(step == 0)
        def _():
            point_ref[...] = jnp.zeros_like(point_ref)
            pool_ref[...] = jnp.zeros_like(pool_ref)

        values = center[...]
        x_first = POINT_CHUNK % 2 == 0
        pair = pairs[POINT_CHUNK]
        point_ref[...] += jnp.dot(
            values, tap_matrix(pair, 0, place_ref, x_first), preferred_element_type=jnp.float32
        )
        pooled = jnp.dot(member_ref[...], values, preferred_element_type=jnp.float32)
        pooled = (pooled * sizes_ref[...]).astype(jnp.bfloat16)
        pooled_ref[...] = pooled
        pool_ref[...] += jnp.dot(
            pooled, tap_matrix(pair, 1, place_ref, x_first), preferred_element_type=jnp.float32
        )

    @pl.when(step == 2 * ROUNDS - 1)
    def _():
        for branch in plan["done"]:
            store_moments(results[branch], mask_ref, stats[branch])
        if plan["pool"]:
            store_moments(point_ref, mask_ref, point_stats_ref)


def coarse_forward(part, mask, sides, chunks, shape, begun, pool=None):
    height, columns, channels = shape
    positions = height * columns
    rows = part_rows(part)
    branches = sorted({row[0] for row in rows})
    done = [branch for branch in branches if atrous_layout()[branch][-1][1] in PARTS[part]]
    plan = {
        "pool": pool is not None,
        "chunks": PARTS[part],
        "branches": branches,
        "begun": [branch for branch in branches if branch in begun],
        "done": done,
        "columns": columns,
        "height": height,
        "rows": rows,
    }
    center = sides[0][1]
    args = [mask, center]
    specs = [full_spec(mask), lane_spec(center)]
    for branch in branches:
        args += [sides[branch][0], sides[branch][2]]
        specs += [lane_spec(center)] * 2
    for branch in plan["begun"]:
        args.append(begun[branch])
        specs.append(full_spec(begun[branch]))
    if pool:
        args += list(pool)
        specs += [full_spec(item) for item in pool]
    for index in PARTS[part]:
        args += list(chunks[index])
        specs += weight_specs(chunks[index], index % 2 == 0)
    flat = jax.ShapeDtypeStruct((positions, channels), jnp.float32)
    small = jax.ShapeDtypeStruct((8, channels), jnp.float32)
    outs = [flat] * len(branches) + [small] * len(done)
    if pool:
        outs += [flat, small, small, jax.ShapeDtypeStruct((8, center.shape[1]), jnp.bfloat16)]
    out_specs = [full_spec(item) for item in outs]
    if pool:
        out_specs[-1] = lane_spec(outs[-1])
    results = pl.pallas_call(
        functools.partial(coarse_forward_kernel, plan),
        out_shape=outs,
        grid_spec=pltpu.PrefetchScalarGridSpec(
            num_scalar_prefetch=1, grid=(2 * ROUNDS,), in_specs=specs, out_specs=out_specs
        ),
        compiler_params=pltpu.CompilerParams(vmem_limit_bytes=VMEM_BYTES),
        cost_estimate=cost(
            coarse_flops([row[:2] for row in rows], shape, center.shape[1])
            + (2 * positions * channels * center.shape[1] if pool else 0),
            args + outs,
        ),
        name="coarse_forward",
    )(kernel_place(), *args)
    sums = dict(zip(branches, results))
    stats = dict(zip(done, results[len(branches) :]))
    return (sums, stats, results[len(branches) + len(done) :])


def coarse_weight_kernel(plan, place_ref, *refs):
    refs = list(refs)
    center = refs.pop(0)
    outer = {branch: (refs.pop(0), refs.pop(0)) for branch in plan["branches"]}
    grads = {branch: refs.pop(0) for branch in plan["branches"]}
    if plan["pool"]:
        point_ref, pooled_ref, pool_ref = refs.pop(0), refs.pop(0), refs.pop(0)
    outs = (refs.pop(0), refs.pop(0))
    row, core = place_ref[2], place_ref[3]
    flip = lax.rem(pl.program_id(0) + place_ref[1], 2)
    rows, cols = outs[0].shape[-2:]
    columns = plan["columns"]

    def store(chunk, tap, value):
        value = value.astype(jnp.bfloat16)
        lower, upper = value[:rows], value[rows:]
        mine = jnp.where(core == 0, lower, upper)
        other = jnp.where(core == 0, upper, lower)
        place = chunk_start(chunk) + tap
        for ref, part in zip(outs, (mine, other)):
            for side, lane_part in ((row, part[:, :cols]), (1 - row, part[:, cols:])):
                if chunk % 2 == 0:
                    ref[flip, side, 0, place] = lane_part
                else:
                    ref[side, flip, 0, place] = lane_part

    across = (((0,), (0,)), ((), ()))
    for branch, line, chunk, tap in plan["rows"]:
        source, target, extent = row_span(dilations[branch], line, plan["height"])
        sides = (outer[branch][0], center, outer[branch][1])
        values = jnp.concatenate(
            [side[pl.ds(source * columns, extent * columns), :] for side in sides], axis=1
        )
        result = lax.dot_general(
            values,
            grads[branch][pl.ds(target * columns, extent * columns), :],
            across,
            preferred_element_type=jnp.float32,
        )
        for k in range(3):
            store(chunk, tap + k, result[2 * rows * k : 2 * rows * (k + 1)])
    if plan["pool"]:
        for tap, left, right in ((0, center, point_ref), (1, pooled_ref, pool_ref)):
            store(
                POINT_CHUNK,
                tap,
                lax.dot_general(
                    left[...], right[...], across, preferred_element_type=jnp.float32
                ),
            )


def coarse_weight(part, sides, grads, shape, pool=None, tie=None):
    height, columns, channels = shape
    rows = part_rows(part)
    branches = sorted({row[0] for row in rows})
    plan = {
        "pool": pool is not None,
        "branches": branches,
        "chunks": PARTS[part],
        "rows": rows,
        "columns": columns,
        "height": height,
    }
    center = sides[0][1]
    args = [center]
    specs = [lane_spec(center)]
    for branch in branches:
        args += [sides[branch][0], sides[branch][2]]
        specs += [lane_spec(center)] * 2
    for branch in branches:
        args.append(grads[branch])
        specs.append(full_spec(grads[branch]))
    if pool:
        args += list(pool)
        specs += [full_spec(pool[0]), lane_spec(pool[1]), full_spec(pool[2])]
    kernel = functools.partial(coarse_weight_kernel, plan)
    if tie is not None:
        kernel = behind_tie(kernel)
        args.insert(0, tie)
        specs.insert(0, pl.BlockSpec(memory_space=pl.ANY))
    total = sum(CHUNKS[index] for index in PARTS[part])
    tail = (total, center.shape[1] // (4 * ROUNDS), channels // 2)
    outs = [jax.ShapeDtypeStruct((2, 2, ROUNDS) + tail, jnp.bfloat16)] * 2
    out_specs = [part_spec(item) for item in outs]
    results = pl.pallas_call(
        kernel,
        out_shape=outs,
        grid_spec=pltpu.PrefetchScalarGridSpec(
            num_scalar_prefetch=1, grid=(2 * ROUNDS,), in_specs=specs, out_specs=out_specs
        ),
        compiler_params=pltpu.CompilerParams(vmem_limit_bytes=VMEM_BYTES),
        cost_estimate=cost(
            coarse_flops([row[:2] for row in rows], shape, center.shape[1])
            + (2 * height * columns * channels * center.shape[1] if pool else 0),
            args + outs,
        ),
        name="coarse_weight",
    )(kernel_place(), *args)
    return (results[0], results[1])


def coarse_input_kernel(plan, place_ref, *refs):
    refs = list(refs)
    point_ref, pool_ref, spread_ref = refs.pop(0), refs.pop(0), refs.pop(0)
    grads = [refs.pop(0) for _ in range(3)]
    pairs = [(refs.pop(0), refs.pop(0)) for _ in range(plan["chunks"])]
    out_ref, total_ref = refs
    columns = plan["columns"]
    turned = (((1,), (1,)), ((), ()))
    total_ref[...] = lax.dot_general(
        point_ref[...],
        tap_matrix(pairs[POINT_CHUNK], 0, place_ref, POINT_CHUNK % 2 == 0),
        turned,
        preferred_element_type=jnp.float32,
    )
    pooled = lax.dot_general(
        pool_ref[...],
        tap_matrix(pairs[POINT_CHUNK], 1, place_ref, POINT_CHUNK % 2 == 0),
        turned,
        preferred_element_type=jnp.float32,
    )
    total_ref[...] += jnp.dot(
        spread_ref[...], pooled, preferred_element_type=jnp.float32, precision=highest
    )
    for branch, rows in enumerate(plan["rows"]):
        for line, chunk, tap in rows:
            source, target, extent = row_span(dilations[branch], line, plan["height"])
            matrix = jnp.concatenate(
                [tap_matrix(pairs[chunk], tap + k, place_ref, chunk % 2 == 0) for k in range(3)],
                axis=1,
            )
            total_ref[pl.ds(source * columns, extent * columns), :] += lax.dot_general(
                grads[branch][pl.ds(target * columns, extent * columns), :],
                matrix,
                turned,
                preferred_element_type=jnp.float32,
            )
    out_ref[...] = total_ref[...].astype(jnp.bfloat16)


def coarse_input(point_dz, pool_dz, spread, grads, chunks, shape, width, tie=None):
    height, columns, channels = shape
    plan = {
        "chunks": len(chunks),
        "columns": columns,
        "height": height,
        "rows": atrous_layout(),
    }
    args = [point_dz, pool_dz, spread] + list(grads)
    specs = [full_spec(item) for item in args]
    for index, pair in enumerate(chunks):
        args += list(pair)
        specs += weight_specs(pair, index % 2 == 0)
    kernel = functools.partial(coarse_input_kernel, plan)
    if tie is not None:
        kernel = behind_tie(kernel)
        args.insert(0, tie)
        specs.insert(0, pl.BlockSpec(memory_space=pl.ANY))
    out = jax.ShapeDtypeStruct((height * columns, width), jnp.bfloat16)
    return pl.pallas_call(
        kernel,
        out_shape=out,
        grid_spec=pltpu.PrefetchScalarGridSpec(
            num_scalar_prefetch=1,
            grid=(2 * ROUNDS,),
            in_specs=specs,
            out_specs=lane_spec(out),
            scratch_shapes=[pltpu.VMEM((height * columns, width // (2 * ROUNDS)), jnp.float32)],
        ),
        compiler_params=pltpu.CompilerParams(vmem_limit_bytes=VMEM_BYTES),
        cost_estimate=cost(
            coarse_flops([(b, k) for b in range(3) for k in range(3)], shape, width)
            + 2 * height * columns * channels * width,
            args + [out],
        ),
        name="coarse_input",
    )(kernel_place(), *args)


STRIP = 8


def norm_vectors(mean, variance, gain, bias, *more):
    rows = [mean, lax.rsqrt(variance + epsilon), gain, bias] + list(more)
    rows += [jnp.zeros_like(mean)] * (8 - len(rows))
    return jnp.stack(rows)


def sigmoid(values):
    return 0.5 * jnp.tanh(0.5 * values) + 0.5


def vector(ref, index):
    return ref[index : index + 1, :]


def shaped_of(values, vector_ref):
    centered = (values - vector(vector_ref, 0)) * vector(vector_ref, 1)
    return (centered, centered * vector(vector_ref, 2) + vector(vector_ref, 3))


def slope_of(shaped, gate):
    return gate * (1.0 + shaped * (1.0 - gate))


def lag_specs(steps):
    def ahead(array, block):
        return pl.BlockSpec(block, lambda step: (jnp.minimum(step, steps - 1), 0))

    def behind(array, block):
        return pl.BlockSpec(block, lambda step: (jnp.maximum(step - 1, 0), 0))

    return (ahead, behind)


def whole(array):
    return pl.BlockSpec(array.shape, lambda step: (0,) * len(array.shape))


def window(ref, start, step, columns):
    return ref[pl.ds(pl.multiple_of((start + step) * columns, columns), STRIP * columns), :]


def run_moments(values, mask, stats_ref, step):
    count = jnp.sum(mask)
    mean = jnp.sum(values * mask, axis=0, keepdims=True) / count
    centered = (values - mean) * mask
    squares = jnp.sum(centered * centered, axis=0, keepdims=True)
    done = (step - 1).astype(jnp.float32)
    old_mean = jnp.where(step > 1, stats_ref[0:1, :], mean)
    old_squares = jnp.where(step > 1, stats_ref[1:2, :], 0.0)
    gap = mean - old_mean
    stats_ref[0:1, :] = old_mean + gap / (done + 1.0)
    stats_ref[1:2, :] = old_squares + squares + gap * gap * (count * done / (done + 1.0))


def spread_columns(products, masks_ref):
    size = products.shape[0]
    width = products.shape[1] // 3
    result = products[:, width : 2 * width]
    result = result + masks_ref[:, 1:2] * pltpu.roll(products[:, :width], 1, 0)
    return result + masks_ref[:, 2:3] * pltpu.roll(products[:, 2 * width :], size - 1, 0)


def clear_edges(ref, columns):
    ref[:columns, :] = jnp.zeros((columns, ref.shape[1]), ref.dtype)
    ref[ref.shape[0] - columns :, :] = jnp.zeros((columns, ref.shape[1]), ref.dtype)


def row_taps(w_ref, row, start, stop):
    return jnp.concatenate([w_ref[3 * row + k, start:stop, :] for k in range(3)], axis=1)


def low_lanes(width):
    return lax.broadcasted_iota(jnp.int32, (1, width), 1)


def decode_forward_kernel(
    steps, act_ref, table_ref, low_ref, wide_ref, vector_ref, masks_ref, w_ref, z_ref, stats_ref,
    up_ref, joined_ref, reduced_ref
):
    step = pl.program_id(0)
    columns = table_ref.shape[0]
    channels = act_ref.shape[2]
    rows = act_ref.shape[0]

    @pl.when(step == 0)
    def _():
        clear_edges(joined_ref, columns)
        clear_edges(reduced_ref, columns)

    @pl.when(step < steps)
    def _():
        for offset in range(STRIP):
            base = step * (STRIP // 4) + offset // 4 + (offset % 4 - 2) // 2
            fraction = ((2 * (offset % 4) - 3) % 8) / 8.0
            lower = act_ref[jnp.maximum(base, 0)]
            upper = act_ref[jnp.minimum(base + 1, rows - 1)]
            mixed = (1.0 - fraction) * lower + fraction * upper
            coarse = mixed.astype(jnp.bfloat16)
            fine = (mixed - coarse.astype(jnp.float32)).astype(jnp.bfloat16)
            value = jnp.dot(
                table_ref[...],
                jnp.concatenate([coarse, fine], axis=0),
                preferred_element_type=jnp.float32,
            ).astype(jnp.bfloat16)
            up_ref[offset * columns : (offset + 1) * columns, :] = value
            start = pl.multiple_of((step * STRIP + offset + 1) * columns, columns)
            joined_ref[pl.ds(start, columns), :] = value
        reduced = jnp.dot(low_ref[...], wide_ref[...], preferred_element_type=jnp.float32)
        _, shaped = shaped_of(reduced, vector_ref)
        value = masks_ref[:, 0:1] * (shaped * sigmoid(shaped))
        start = pl.multiple_of((step * STRIP + 1) * columns, columns)
        reduced_ref[pl.ds(start, STRIP * columns), :] = value.astype(jnp.bfloat16)

    @pl.when(step > 0)
    def _():
        start = (step - 1) * STRIP
        lane = low_lanes(reduced_ref.shape[1])
        lows = [window(reduced_ref, start, k, columns) for k in range(3)]
        low = jnp.where(lane < 64, lows[0], jnp.where(lane < 128, lows[1], lows[2]))
        values = jnp.concatenate(
            [window(joined_ref, start, k, columns) for k in range(3)] + [low], axis=1
        )
        extra = w_ref.shape[1] - channels
        parts = [row_taps(w_ref, k, 0, channels) for k in range(3)]
        for k in range(3):
            parts.append(row_taps(w_ref, k, channels, channels + extra))
            parts.append(jnp.zeros((64 - extra, 3 * channels), jnp.bfloat16))
        parts.append(jnp.zeros((64, 3 * channels), jnp.bfloat16))
        products = jnp.dot(
            values, jnp.concatenate(parts, axis=0), preferred_element_type=jnp.float32
        )
        result = spread_columns(products, masks_ref)
        z_ref[...] = result
        run_moments(result, masks_ref[:, 0:1], stats_ref, step)


def decode_forward(act, table, low, wide, vectors, masks, weights):
    positions = low.shape[0]
    columns = table.shape[0]
    block = STRIP * columns
    steps = positions // block
    channels = act.shape[2]
    ahead, behind = lag_specs(steps)
    flat = jax.ShapeDtypeStruct((positions, channels), jnp.float32)
    stats = jax.ShapeDtypeStruct((8, channels), jnp.float32)
    up = jax.ShapeDtypeStruct((positions, channels), jnp.bfloat16)
    return pl.pallas_call(
        functools.partial(decode_forward_kernel, steps),
        out_shape=[flat, stats, up],
        grid=(steps + 1,),
        in_specs=[
            whole(act),
            whole(table),
            ahead(low, (block, low.shape[1])),
            whole(wide),
            whole(vectors),
            whole(masks),
            whole(weights),
        ],
        out_specs=[
            behind(flat, (block, channels)),
            whole(stats),
            ahead(up, (block, channels)),
        ],
        scratch_shapes=[
            pltpu.VMEM((positions + 2 * columns, channels), jnp.bfloat16),
            pltpu.VMEM((positions + 2 * columns, wide.shape[1]), jnp.bfloat16),
        ],
        compiler_params=pltpu.CompilerParams(vmem_limit_bytes=VMEM_BYTES),
        cost_estimate=cost(2 * positions * 3 * channels * 4 * channels, [low, flat, up]),
        name="decode_forward",
    )(act, table, low, wide, vectors, masks, weights)


def refine_forward_kernel(
    steps, columns, z_in_ref, vector_ref, masks_ref, w_ref, z_ref, stats_ref, act_ref
):
    step = pl.program_id(0)
    channels = w_ref.shape[1]

    @pl.when(step == 0)
    def _():
        clear_edges(act_ref, columns)

    @pl.when(step < steps)
    def _():
        _, shaped = shaped_of(z_in_ref[...], vector_ref)
        value = masks_ref[:, 0:1] * (shaped * sigmoid(shaped))
        start = pl.multiple_of((step * STRIP + 1) * columns, columns)
        act_ref[pl.ds(start, STRIP * columns), :] = value.astype(jnp.bfloat16)

    @pl.when(step > 0)
    def _():
        start = (step - 1) * STRIP
        values = jnp.concatenate([window(act_ref, start, k, columns) for k in range(3)], axis=1)
        matrix = jnp.concatenate([row_taps(w_ref, k, 0, channels) for k in range(3)], axis=0)
        products = jnp.dot(values, matrix, preferred_element_type=jnp.float32)
        result = spread_columns(products, masks_ref)
        z_ref[...] = result
        run_moments(result, masks_ref[:, 0:1], stats_ref, step)


def refine_forward(z_in, vectors, masks, weights):
    positions, channels = z_in.shape
    block = masks.shape[0]
    columns = block // STRIP
    steps = positions // block
    ahead, behind = lag_specs(steps)
    flat = jax.ShapeDtypeStruct((positions, channels), jnp.float32)
    stats = jax.ShapeDtypeStruct((8, channels), jnp.float32)
    return pl.pallas_call(
        functools.partial(refine_forward_kernel, steps, columns),
        out_shape=[flat, stats],
        grid=(steps + 1,),
        in_specs=[ahead(z_in, (block, channels)), whole(vectors), whole(masks), whole(weights)],
        out_specs=[behind(flat, (block, channels)), whole(stats)],
        scratch_shapes=[pltpu.VMEM((positions + 2 * columns, channels), jnp.bfloat16)],
        compiler_params=pltpu.CompilerParams(vmem_limit_bytes=VMEM_BYTES),
        cost_estimate=cost(2 * positions * 9 * channels * channels, [z_in, flat]),
        name="refine_forward",
    )(z_in, vectors, masks, weights)


def class_kernel(
    z_ref, grad_ref, vector_ref, masks_ref, w_ref, b_ref, logits_ref, sums_ref, weight_ref, bias_ref
):
    step = pl.program_id(0)

    @pl.when(step == 0)
    def _():
        sums_ref[...] = jnp.zeros_like(sums_ref)
        weight_ref[...] = jnp.zeros_like(weight_ref)
        bias_ref[...] = jnp.zeros_like(bias_ref)

    mask = masks_ref[:, 0:1]
    centered, shaped = shaped_of(z_ref[...], vector_ref)
    gate = sigmoid(shaped)
    act = (mask * (shaped * gate)).astype(jnp.bfloat16)
    logits = jnp.dot(act, w_ref[...], preferred_element_type=jnp.float32) + b_ref[...]
    logits_ref[...] = (mask * logits).astype(jnp.bfloat16)
    grad = (mask * grad_ref[...].astype(jnp.float32)).astype(jnp.bfloat16)
    upstream = lax.dot_general(
        grad, w_ref[...], (((1,), (1,)), ((), ())), preferred_element_type=jnp.float32
    )
    local = mask * upstream * slope_of(shaped, gate)
    sums_ref[0:1, :] += jnp.sum(local * centered, axis=0, keepdims=True)
    sums_ref[1:2, :] += jnp.sum(local, axis=0, keepdims=True)
    weight_ref[...] += lax.dot_general(
        grad, act, (((0,), (0,)), ((), ())), preferred_element_type=jnp.float32
    )
    bias_ref[...] += jnp.sum(grad.astype(jnp.float32), axis=0, keepdims=True)


def classify(z, grad, vectors, masks, weights, bias):
    positions, channels = z.shape
    block = masks.shape[0]
    classes = grad.shape[1]
    outs = [
        jax.ShapeDtypeStruct((positions, classes), jnp.bfloat16),
        jax.ShapeDtypeStruct((8, channels), jnp.float32),
        jax.ShapeDtypeStruct((classes, channels), jnp.float32),
        jax.ShapeDtypeStruct((1, classes), jnp.float32),
    ]

    def strip(width):
        return pl.BlockSpec((block, width), lambda step: (step, 0))

    return pl.pallas_call(
        class_kernel,
        out_shape=outs,
        grid=(positions // block,),
        in_specs=[
            strip(channels),
            strip(classes),
            whole(vectors),
            whole(masks),
            whole(weights),
            whole(bias),
        ],
        out_specs=[strip(classes)] + [whole(item) for item in outs[1:]],
        compiler_params=pltpu.CompilerParams(vmem_limit_bytes=VMEM_BYTES),
        cost_estimate=cost(6 * positions * channels * 128, [z, grad, grad]),
        name="classify",
    )(z, grad, vectors, masks, weights, bias)


def finish_grad(local, centered, mask, vector_ref):
    inner = local - vector(vector_ref, 5) - centered * vector(vector_ref, 4)
    return mask * vector(vector_ref, 2) * vector(vector_ref, 1) * inner


def store_sides(grad, masks_ref, side_ref, start):
    size, width = grad.shape
    grad = grad.astype(jnp.bfloat16).astype(jnp.float32)
    rows = pl.ds(start, size)
    side_ref[rows, :width] = pltpu.roll(masks_ref[:, 1:2] * grad, size - 1, 0).astype(jnp.bfloat16)
    side_ref[rows, width : 2 * width] = grad.astype(jnp.bfloat16)
    side_ref[rows, 2 * width :] = pltpu.roll(masks_ref[:, 2:3] * grad, 1, 0).astype(jnp.bfloat16)


def refine_backward_kernel(
    steps, columns, z_ref, grad_ref, vector_ref, cls_ref, z_in_ref, vector_in_ref, masks_ref, w_ref,
    local_ref, sums_ref, weight_ref, side_ref
):
    step = pl.program_id(0)
    channels = w_ref.shape[1]
    mask = masks_ref[:, 0:1]

    @pl.when(step == 0)
    def _():
        clear_edges(side_ref, columns)
        sums_ref[...] = jnp.zeros_like(sums_ref)
        weight_ref[...] = jnp.zeros_like(weight_ref)

    @pl.when(step < steps)
    def _():
        centered, shaped = shaped_of(z_ref[...], vector_ref)
        grad = (mask * grad_ref[...].astype(jnp.float32)).astype(jnp.bfloat16)
        upstream = lax.dot_general(
            grad, cls_ref[...], (((1,), (1,)), ((), ())), preferred_element_type=jnp.float32
        )
        local = mask * upstream * slope_of(shaped, sigmoid(shaped))
        start = pl.multiple_of((step * STRIP + 1) * columns, columns)
        store_sides(finish_grad(local, centered, mask, vector_ref), masks_ref, side_ref, start)

    @pl.when(step > 0)
    def _():
        start = (step - 1) * STRIP
        centered, shaped = shaped_of(z_in_ref[...], vector_in_ref)
        gate = sigmoid(shaped)
        act = (mask * (shaped * gate)).astype(jnp.bfloat16)
        sides = [window(side_ref, start, 2 - k, columns) for k in range(3)]
        upstream = lax.dot_general(
            jnp.concatenate(sides, axis=1),
            jnp.concatenate([w_ref[tap] for tap in range(9)], axis=1),
            (((1,), (1,)), ((), ())),
            preferred_element_type=jnp.float32,
        )
        local = mask * upstream * slope_of(shaped, gate)
        local_ref[...] = local
        sums_ref[0:1, :] += jnp.sum(local * centered, axis=0, keepdims=True)
        sums_ref[1:2, :] += jnp.sum(local, axis=0, keepdims=True)
        turned = act.T
        for k in range(3):
            weight_ref[k] += jnp.dot(turned, sides[k], preferred_element_type=jnp.float32)


def refine_backward(z, grad, vectors, classes, z_in, vectors_in, masks, weights):
    positions, channels = z.shape
    block = masks.shape[0]
    columns = block // STRIP
    steps = positions // block
    ahead, behind = lag_specs(steps)
    outs = [
        jax.ShapeDtypeStruct((positions, channels), jnp.float32),
        jax.ShapeDtypeStruct((8, channels), jnp.float32),
        jax.ShapeDtypeStruct((3, channels, 3 * channels), jnp.float32),
    ]
    return pl.pallas_call(
        functools.partial(refine_backward_kernel, steps, columns),
        out_shape=outs,
        grid=(steps + 1,),
        in_specs=[
            ahead(z, (block, channels)),
            ahead(grad, (block, grad.shape[1])),
            whole(vectors),
            whole(classes),
            behind(z_in, (block, channels)),
            whole(vectors_in),
            whole(masks),
            whole(weights),
        ],
        out_specs=[behind(z, (block, channels)), whole(outs[1]), whole(outs[2])],
        scratch_shapes=[pltpu.VMEM((positions + 2 * columns, 3 * channels), jnp.bfloat16)],
        compiler_params=pltpu.CompilerParams(vmem_limit_bytes=VMEM_BYTES),
        cost_estimate=cost(4 * positions * 9 * channels * channels, [z, z_in, grad, outs[0], weights]),
        name="refine_backward",
    )(z, grad, vectors, classes, z_in, vectors_in, masks, weights)


def decode_backward_kernel(
    steps, columns, local_ref, z_ref, vector_ref, up_ref, low_ref, wide_ref, low_vector_ref,
    table_ref, masks_ref, w_ref, coarse_ref, low_local_ref, sums_ref, weight_ref, low_weight_ref,
    side_ref, total_ref
):
    step = pl.program_id(0)
    channels = w_ref.shape[2]
    extra = w_ref.shape[1] - channels
    mask = masks_ref[:, 0:1]

    @pl.when(step == 0)
    def _():
        clear_edges(side_ref, columns)
        sums_ref[...] = jnp.zeros_like(sums_ref)
        weight_ref[...] = jnp.zeros_like(weight_ref)
        low_weight_ref[...] = jnp.zeros_like(low_weight_ref)
        total_ref[...] = jnp.zeros_like(total_ref)

    @pl.when(step < steps)
    def _():
        centered, _ = shaped_of(z_ref[...], vector_ref)
        start = pl.multiple_of((step * STRIP + 1) * columns, columns)
        grad = finish_grad(local_ref[...], centered, mask, vector_ref)
        store_sides(grad, masks_ref, side_ref, start)

    @pl.when(step > 0)
    def _():
        start = (step - 1) * STRIP
        sides = [window(side_ref, start, 2 - k, columns) for k in range(3)]
        pieces = []
        for tap in range(9):
            pieces.append(
                jnp.concatenate(
                    [w_ref[tap], jnp.zeros((64 - extra, channels), jnp.bfloat16)], axis=0
                )
            )
        upstream = lax.dot_general(
            jnp.concatenate(sides, axis=1),
            jnp.concatenate(pieces, axis=1),
            (((1,), (1,)), ((), ())),
            preferred_element_type=jnp.float32,
        )
        for offset in range(STRIP):
            base = (step - 1) * (STRIP // 4) + offset // 4 + (offset % 4 - 2) // 2
            fraction = ((2 * (offset % 4) - 3) % 8) / 8.0
            value = upstream[offset * columns : (offset + 1) * columns, :channels]
            value = value.astype(jnp.bfloat16).astype(jnp.float32)
            total_ref[base + 1] += (1.0 - fraction) * value
            total_ref[base + 2] += fraction * value
        reduced = jnp.dot(low_ref[...], wide_ref[...], preferred_element_type=jnp.float32)
        centered, shaped = shaped_of(reduced, low_vector_ref)
        gate = sigmoid(shaped)
        low_act = (mask * (shaped * gate)).astype(jnp.bfloat16)
        low_up = upstream[:, channels:]
        local = mask * low_up * slope_of(shaped, gate)[:, :64]
        low_local_ref[...] = local
        sums_ref[0:1, :64] += jnp.sum(local * centered[:, :64], axis=0, keepdims=True)
        sums_ref[1:2, :64] += jnp.sum(local, axis=0, keepdims=True)
        turned = up_ref[...].T
        low_turned = low_act[:, :128].T[:64]
        for k in range(3):
            weight_ref[k] += jnp.dot(turned, sides[k], preferred_element_type=jnp.float32)
            low_weight_ref[k] += jnp.dot(low_turned, sides[k], preferred_element_type=jnp.float32)

    @pl.when(step == steps)
    def _():
        rows = coarse_ref.shape[0]
        total_ref[1] += total_ref[0]
        total_ref[rows] += total_ref[rows + 1]
        for row in range(rows):
            value = total_ref[row + 1]
            upper = value.astype(jnp.bfloat16)
            lower = (value - upper.astype(jnp.float32)).astype(jnp.bfloat16)
            coarse_ref[row] = jnp.dot(
                table_ref[...],
                jnp.concatenate([upper, lower], axis=0),
                preferred_element_type=jnp.float32,
            )


def decode_backward(local, z, vectors, up, low, wide, low_vectors, table, masks, weights, shape):
    positions, channels = z.shape
    block = masks.shape[0]
    columns = block // STRIP
    steps = positions // block
    height, coarse_columns, _ = shape
    ahead, behind = lag_specs(steps)
    outs = [
        jax.ShapeDtypeStruct((height, coarse_columns, channels), jnp.float32),
        jax.ShapeDtypeStruct((positions, 64), jnp.float32),
        jax.ShapeDtypeStruct((8, channels), jnp.float32),
        jax.ShapeDtypeStruct((3, channels, 3 * channels), jnp.float32),
        jax.ShapeDtypeStruct((3, 64, 3 * channels), jnp.float32),
    ]
    return pl.pallas_call(
        functools.partial(decode_backward_kernel, steps, columns),
        out_shape=outs,
        grid=(steps + 1,),
        in_specs=[
            ahead(local, (block, channels)),
            ahead(z, (block, channels)),
            whole(vectors),
            behind(up, (block, channels)),
            behind(low, (block, low.shape[1])),
            whole(wide),
            whole(low_vectors),
            whole(table),
            whole(masks),
            whole(weights),
        ],
        out_specs=[whole(outs[0]), behind(outs[1], (block, 64))]
        + [whole(item) for item in outs[2:]],
        scratch_shapes=[
            pltpu.VMEM((positions + 2 * columns, 3 * channels), jnp.bfloat16),
            pltpu.VMEM((height + 2, columns, channels), jnp.float32),
        ],
        compiler_params=pltpu.CompilerParams(vmem_limit_bytes=VMEM_BYTES),
        cost_estimate=cost(4 * positions * 9 * channels * (channels + 64), [local, z, up, low, outs[1], weights]),
        name="decode_backward",
    )(local, z, vectors, up, low, wide, low_vectors, table, masks, weights)


def low_backward_kernel(
    vector_ref, local_ref, low_ref, wide_ref, masks_ref, out_ref, weight_ref
):
    @pl.when(pl.program_id(0) == 0)
    def _():
        weight_ref[...] = jnp.zeros_like(weight_ref)

    low = low_ref[...]
    weights = wide_ref[:, :128]
    reduced = jnp.dot(low, weights, preferred_element_type=jnp.float32)
    mean, scale, gain = (vector_ref[k : k + 1, :64] for k in range(3))
    centered = (reduced[:, :64] - mean) * scale
    inner = local_ref[...] - vector_ref[5:6, :64] - centered * vector_ref[4:5, :64]
    grad = (masks_ref[:, 0:1] * gain * scale * inner).astype(jnp.bfloat16)
    out_ref[...] = lax.dot_general(
        grad, weights[:, :64], (((1,), (1,)), ((), ())), preferred_element_type=jnp.float32
    ).astype(jnp.bfloat16)
    weight_ref[...] += lax.dot_general(
        grad, low, (((0,), (0,)), ((), ())), preferred_element_type=jnp.float32
    )


def low_backward(local, low, wide, vectors, masks, tie):
    positions, width = low.shape
    block = masks.shape[0]
    outs = [
        jax.ShapeDtypeStruct((positions, width), jnp.bfloat16),
        jax.ShapeDtypeStruct((64, width), jnp.float32),
    ]
    return pl.pallas_call(
        behind_tie(low_backward_kernel),
        out_shape=outs,
        grid=(positions // block,),
        in_specs=[
            whole(vectors),
            pl.BlockSpec(memory_space=pl.ANY),
            pl.BlockSpec((block, 64), lambda step: (step, 0)),
            pl.BlockSpec((block, width), lambda step: (step, 0)),
            whole(wide),
            whole(masks),
        ],
        out_specs=[pl.BlockSpec((block, width), lambda step: (step, 0)), whole(outs[1])],
        compiler_params=pltpu.CompilerParams(vmem_limit_bytes=VMEM_BYTES),
        cost_estimate=cost(6 * positions * width * 128, [local, low, low]),
        name="low_backward",
    )(vectors, tie, local, low, wide, masks)


def atrous_layout():
    places = []
    for chunk, size in enumerate(CHUNKS):
        places += [(chunk, tap) for tap in range(2 if chunk == POINT_CHUNK else 0, size)]
    return [
        [(line,) + places[9 * branch + 3 * line] for line in range(3)] for branch in range(3)
    ]


def part_rows(part):
    return [
        (branch, line, chunk, tap)
        for branch, rows in enumerate(atrous_layout())
        for line, chunk, tap in rows
        if chunk in PARTS[part]
    ]


def order_taps(point, atrous):
    flat = atrous.reshape((-1,) + atrous.shape[2:])
    before = sum(CHUNKS[:POINT_CHUNK])
    flat = jnp.concatenate([flat[:before], point, flat[before:]])
    parts = []
    start = 0
    for part in PARTS:
        size = sum(CHUNKS[index] for index in part)
        parts.append(flat[start : start + size])
        start += size
    return parts


def restore_taps(parts, shape):
    flat = jnp.concatenate(parts)
    before = sum(CHUNKS[:POINT_CHUNK])
    atrous = jnp.concatenate([flat[:before], flat[before + 2 :]])
    return (flat[before : before + 2], atrous.reshape(shape))


def side_values(values, image_ids, dilation):
    result = []
    for step in (-dilation, dilation):
        mask = tap_mask(image_ids, values.shape[1], 0, step).astype(values.dtype)
        result.append(mask * shifted(values, 0, step))
    return [result[0], values, result[1]]


def side_grads(values, image_ids, dilation):
    result = []
    for step in (-dilation, 0, dilation):
        masked = tap_mask(image_ids, values.shape[1], 0, step).astype(values.dtype) * values
        result.append(shifted(masked, 0, -step))
    return jnp.concatenate(result, axis=-1)


def settle_core(values):
    core = place()[3]
    taps, rows, cols = values.shape
    parts = values.reshape(taps, rows, 2, cols // 2)
    kept = lax.dynamic_index_in_dim(parts, core, 2, keepdims=False)
    given = lax.dynamic_index_in_dim(parts, 1 - core, 2, keepdims=False).astype(jnp.bfloat16)
    got = exchange(given, "narrow", 1).astype(jnp.float32)
    lower = jnp.where(core == 0, kept, got)
    upper = jnp.where(core == 0, got, kept)
    return jnp.concatenate([lower, upper], axis=1)


def band_ids(widths, columns):
    ends_all = jnp.cumsum(widths, axis=1)
    position = jnp.arange(columns, dtype=jnp.int32)
    band_index = jnp.sum(
        (position[None, :, None] >= ends_all[:, None, :]).astype(jnp.int32), axis=2
    )
    return jnp.where(band_index < widths.shape[1] - 1, band_index, -1)


def shifted(values, row_shift, col_shift):
    height = values.shape[1]
    columns = values.shape[2]
    padded = jnp.pad(
        values, ((0, 0), (abs(row_shift), abs(row_shift)), (abs(col_shift), abs(col_shift)), (0, 0))
    )
    row_start = abs(row_shift) + row_shift
    col_start = abs(col_shift) + col_shift
    return padded[:, row_start : row_start + height, col_start : col_start + columns, :]


def tap_mask(image_ids, height, row_shift, col_shift):
    columns = image_ids.shape[1]
    padded = jnp.pad(image_ids, ((0, 0), (abs(col_shift), abs(col_shift))), constant_values=-2)
    col_start = abs(col_shift) + col_shift
    other_ids = padded[:, col_start : col_start + columns]
    same_image = (other_ids == image_ids).astype(jnp.float32)
    row_place = jnp.arange(height) + row_shift
    inside = ((row_place >= 0) & (row_place < height)).astype(jnp.float32)
    return (inside[None, :, None] * same_image[:, None, :])[..., None]


def tap_offsets(dilation):
    return [
        ((tap_index // 3 - 1) * dilation, (tap_index % 3 - 1) * dilation) for tap_index in range(9)
    ]


def linear_weights(out_count, in_count):
    position = jnp.arange(out_count, dtype=jnp.int32)
    scaled = 2 * position - 3
    left_index = jnp.floor_divide(scaled, 8)
    fraction = (scaled - 8 * left_index).astype(jnp.float32) / 8.0
    lower_index = jnp.clip(left_index, 0, in_count - 1)
    upper_index = jnp.clip(left_index + 1, 0, in_count - 1)
    return (position, lower_index, upper_index, fraction)


def column_table(image_ids):
    columns = image_ids.shape[1]
    position, lower_index, upper_index, fraction = linear_weights(4 * columns, columns)
    source = jnp.arange(columns, dtype=jnp.int32)[None, :]

    def picker(index_row):
        return (source == index_row[:, None]).astype(jnp.int32)

    def lookup(index_row):
        return jnp.sum(image_ids[:, None, :] * picker(index_row)[None], axis=2)

    own_index = position // 4
    own_id = lookup(own_index)
    weight_lower = (1.0 - fraction)[None, :] * (lookup(lower_index) == own_id).astype(jnp.float32)
    weight_upper = fraction[None, :] * (lookup(upper_index) == own_id).astype(jnp.float32)
    weight_own = 1.0 - weight_lower - weight_upper
    table = weight_lower[:, :, None] * picker(lower_index)[None].astype(jnp.float32)
    table = table + weight_upper[:, :, None] * picker(upper_index)[None].astype(jnp.float32)
    table = table + weight_own[:, :, None] * picker(own_index)[None].astype(jnp.float32)
    return table


def normalize(values, valid_map, mean_row, variance, gain_row, bias_row):
    norm_scale = lax.rsqrt(variance + epsilon)
    centered = (values - mean_row) * norm_scale
    shaped = centered * gain_row + bias_row
    return (valid_map * jax.nn.silu(shaped), centered, shaped, norm_scale)


def norm_grad_terms(upstream, valid_map, centered, shaped):
    sigmoid_value = jax.nn.sigmoid(shaped)
    local_term = valid_map * upstream * sigmoid_value * (1.0 + shaped * (1.0 - sigmoid_value))
    axes = tuple(range(local_term.ndim - 1))
    return (local_term, jnp.sum(local_term * centered, axis=axes), jnp.sum(local_term, axis=axes))


def norm_grad_finish(
    local_term, valid_map, centered, norm_scale, gain_row, gain_sum, bias_sum, count_all
):
    inner = local_term - bias_sum / count_all - centered * gain_sum / count_all
    return (valid_map * gain_row * norm_scale * inner).astype(jnp.bfloat16)


def moments(values, valid_map, local_count, count_all):
    mean, squares = local_moments(values, valid_map, local_count)
    return merged(jnp.stack([mean, squares]), local_count, count_all)


def merged(stats, local_count, count_all):
    width = stats.shape[1]
    own = jnp.concatenate([stats[0], stats[1], jnp.full((1,), 1.0) * local_count])
    rows = from_all(own)
    counts, means, squares = merge_rows(
        rows[:, 2 * width :], rows[:, :width], rows[:, width : 2 * width]
    )
    return (means, squares / count_all)


def pack_pairs(pairs):
    return jnp.concatenate(
        [pair_item[0] for pair_item in pairs] + [pair_item[1] for pair_item in pairs]
    )


def unpack_pairs(flat, pairs):
    lengths = [pair_item[0].shape[0] for pair_item in pairs]
    half_point = sum(lengths)
    result_pairs = []
    offset = 0
    for length_now in lengths:
        result_pairs.append(
            (
                flat[offset : offset + length_now],
                flat[half_point + offset : half_point + offset + length_now],
            )
        )
        offset = offset + length_now
    return result_pairs


def gradient_sums(pairs):
    return unpack_pairs(jnp.sum(from_all(pack_pairs(pairs)), axis=0), pairs)


def small_block(items):
    proj, reduce, decode, refine = items
    taps, rows, cols = refine.shape
    count = proj.shape[0] // rows
    proj = proj.reshape(2, count, rows // 2, cols).swapaxes(0, 1).reshape(count, rows, cols)
    reduce = jnp.pad(reduce, ((0, 0), (0, cols - reduce.shape[1])))[None]
    shared = share_core(jnp.concatenate([refine, proj, reduce]))
    lanes = shared.shape[2]
    decode = decode.swapaxes(1, 2)
    decode = jnp.pad(decode, ((0, 0), (0, 0), (0, lanes - decode.shape[2])))
    return jnp.concatenate([shared, decode.reshape(-1, shared.shape[1], lanes)])


def settle_small(owned, shapes):
    shape_p, shape_r, shape_d, shape_f = shapes
    taps, rows, cols = shape_f
    count = shape_p[0] // rows
    first = taps + count + 1
    settled = settle_core(owned[:first])
    proj = settled[taps : taps + count].reshape(count, 2, rows // 2, cols)
    proj = proj.swapaxes(0, 1).reshape(shape_p)
    reduce = settled[taps + count, :, : shape_r[1]]
    decode = owned[first:].reshape(taps, shape_d[2], -1)[:, :, : shape_d[1]].swapaxes(1, 2)
    return (proj, reduce, decode, settled[:taps])


def reduce_lanes(width, row, core, half):
    start = (2 * row + core) * width
    return start, core * half


def unpack_kernel(shapes, place_ref, own_ref, other_ref, proj_ref, wide_ref, decode_ref, refine_ref):
    deep, side, row, core = (place_ref[index] for index in range(4))
    shape_p, shape_r, shape_d, shape_f = shapes
    taps = shape_f[0]
    rows = shape_f[1] // 2
    count = shape_p[0] // (2 * rows)
    lanes = own_ref.shape[-1]

    def load(ref, z, x, y, start, size):
        slot = lax.rem(deep - z + ROUNDS, ROUNDS)
        return ref[slot, lax.rem(y + row, 2), lax.rem(x + side, 2), start : start + size]

    def both(z, x, y, start, size):
        mine = load(own_ref, z, x, y, start, size)
        others = load(other_ref, z, x, y, start, size)
        return (jnp.where(core == 0, mine, others), jnp.where(core == 0, others, mine))

    lane = lax.broadcasted_iota(jnp.int32, (1, lanes), 1)
    for z in range(ROUNDS):
        for x in range(2):
            wide = 2 * z + x
            halves = [both(z, x, y, 0, taps + count + 1) for y in range(2)]
            for h in range(2):
                joined = jnp.concatenate([halves[0][h], halves[1][h]], axis=-1)
                base = (2 * wide + h) * rows
                refine_ref[:, base : base + rows, :] = joined[:taps]
                base = (2 * wide + h) * rows * count
                proj_ref[base : base + rows * count, :] = joined[taps : taps + count].reshape(
                    rows * count, 2 * lanes
                )
                total = jnp.zeros((rows, lanes), jnp.float32)
                for y in range(2):
                    value = halves[y][h][taps + count].astype(jnp.float32)
                    for c in range(2):
                        start, held = reduce_lanes(shape_r[1], y, c, lanes // 2)
                        moved = pltpu.roll(value, (start - held) % lanes, 1)
                        inside = (lane >= start) & (lane < start + shape_r[1])
                        total = total + jnp.where(inside, moved, 0.0)
                base = (2 * wide + h) * rows
                left = total + pltpu.roll(total, 64, 1)
                wide_ref[base : base + rows, :] = jnp.concatenate([left, total], axis=1).astype(
                    jnp.bfloat16
                )
    height, width = shape_d[1], shape_d[2]
    blocks = width // rows
    for tap in range(taps):
        start = taps + count + 1 + tap * blocks
        pieces = []
        for y in range(2):
            columns = ([], [])
            for z in range(ROUNDS):
                for x in range(2):
                    for c, value in enumerate(both(z, x, y, start, blocks)):
                        columns[c].append(value.reshape(width, lanes))
            for c in range(2):
                joined = jnp.concatenate(columns[c], axis=0).astype(jnp.float32)
                pieces.append(joined.T[:height])
        decode_ref[tap] = jnp.concatenate(pieces, axis=0).astype(jnp.bfloat16)


def unpack_block(own, other, shapes):
    wide = 2 * ROUNDS
    shape_p, shape_r, shape_d, shape_f = shapes
    outs = [
        jax.ShapeDtypeStruct((wide * shape_p[0], 4 * shape_p[1]), jnp.bfloat16),
        jax.ShapeDtypeStruct((wide * shape_r[0], 256), jnp.bfloat16),
        jax.ShapeDtypeStruct((shape_d[0], 4 * shape_d[1], wide * shape_d[2]), jnp.bfloat16),
        jax.ShapeDtypeStruct((shape_f[0], wide * shape_f[1], 4 * shape_f[2]), jnp.bfloat16),
    ]
    return pl.pallas_call(
        functools.partial(unpack_kernel, shapes),
        out_shape=outs,
        in_specs=[pl.BlockSpec(memory_space=pltpu.SMEM)]
        + [pl.BlockSpec(memory_space=pltpu.VMEM)] * 2,
        out_specs=[pl.BlockSpec(memory_space=pltpu.VMEM)] * 4,
        compiler_params=pltpu.CompilerParams(vmem_limit_bytes=VMEM_BYTES),
        cost_estimate=cost(0, [own, other] + outs + outs),
        name="unpack_weights",
    )(kernel_place(), own, other)


def pack_kernel(
    shapes, place_ref, proj_ref, reduce_ref, decode_ref, low_ref, refine_ref, keep_ref, give_ref
):
    deep, side, row, core = (place_ref[index] for index in range(4))
    shape_p, shape_r, shape_d, shape_f = shapes
    taps = shape_f[0]
    rows = shape_f[1] // 2
    count = shape_p[0] // (2 * rows)
    lanes = keep_ref.shape[-1]
    channels = 2 * lanes

    def store(z, x, y, start, size, values):
        values = [value.astype(jnp.bfloat16) for value in values]
        index = (
            lax.rem(x + side, 2),
            lax.rem(y + row, 2),
            lax.bitwise_xor(deep, z),
            pl.ds(start, size),
        )
        keep_ref[index] = jnp.where(core == 0, values[0], values[1])
        give_ref[index] = jnp.where(core == 0, values[1], values[0])

    lane = lax.broadcasted_iota(jnp.int32, (1, lanes), 1)
    reduce = jnp.concatenate(
        [reduce_ref[...], jnp.zeros((lanes - reduce_ref.shape[0], reduce_ref.shape[1]), jnp.float32)]
    ).T
    moved = []
    for y in range(2):
        total = jnp.zeros_like(reduce)
        for c in range(2):
            start, held = reduce_lanes(shape_r[1], y, c, lanes // 2)
            inside = (lane >= held) & (lane < held + shape_r[1])
            total = total + jnp.where(inside, pltpu.roll(reduce, (held - start) % lanes, 1), 0.0)
        moved.append(total)
    for z in range(ROUNDS):
        for x in range(2):
            wide = 2 * z + x
            for y in range(2):
                columns = slice(y * lanes, (y + 1) * lanes)
                for tap in range(taps):
                    line, k = tap // 3, tap % 3
                    left = k * channels + y * lanes
                    values = []
                    for h in range(2):
                        base = (2 * wide + h) * rows
                        values.append(
                            refine_ref[line, base : base + rows, left : left + lanes][None]
                        )
                    store(z, x, y, tap, 1, values)
                values = []
                for h in range(2):
                    base = (2 * wide + h) * rows * count
                    values.append(
                        proj_ref[base : base + rows * count, columns].reshape(count, rows, lanes)
                    )
                store(z, x, y, taps, count, values)
                values = [
                    moved[y][(2 * wide + h) * rows : (2 * wide + h + 1) * rows][None]
                    for h in range(2)
                ]
                store(z, x, y, taps + count, 1, values)
    height, width = shape_d[1], shape_d[2]
    blocks = width // rows
    for tap in range(taps):
        line, k = tap // 3, tap % 3
        columns = slice(k * channels, (k + 1) * channels)
        whole_tap = jnp.concatenate(
            [
                decode_ref[line, :, columns],
                low_ref[line, :, columns],
                jnp.zeros((lanes, channels), jnp.float32),
            ],
            axis=0,
        )
        turned = [whole_tap[n * height : n * height + lanes].T for n in range(4)]
        for z in range(ROUNDS):
            for x in range(2):
                base = (2 * z + x) * width
                for y in range(2):
                    values = [
                        turned[2 * y + c][base : base + width].reshape(blocks, rows, lanes)
                        for c in range(2)
                    ]
                    store(z, x, y, taps + count + 1 + tap * blocks, blocks, values)


def pack_block(proj, reduce, decode, low, refine, shapes, tie):
    shape_p, shape_r, shape_d, shape_f = shapes
    rows = shape_f[1] // 2
    total = shape_f[0] + shape_p[0] // (2 * rows) + 1 + shape_d[0] * shape_d[2] // rows
    out = jax.ShapeDtypeStruct((2, 2, ROUNDS, total, rows, 2 * shape_f[2]), jnp.bfloat16)
    return pl.pallas_call(
        behind_tie(functools.partial(pack_kernel, shapes)),
        out_shape=[out, out],
        in_specs=[pl.BlockSpec(memory_space=pltpu.SMEM), pl.BlockSpec(memory_space=pl.ANY)]
        + [pl.BlockSpec(memory_space=pltpu.VMEM)] * 5,
        out_specs=[pl.BlockSpec(memory_space=pltpu.VMEM)] * 2,
        compiler_params=pltpu.CompilerParams(vmem_limit_bytes=VMEM_BYTES),
        cost_estimate=whole_cost(0, [proj, decode, low, refine, out, out, out]),
        name="pack_gradients",
    )(kernel_place(), tie, proj, reduce, decode, low, refine)


def low_moments_kernel(low_ref, wide_ref, masks_ref, stats_ref):
    reduced = jnp.dot(low_ref[...], wide_ref[...], preferred_element_type=jnp.float32)
    run_moments(reduced, masks_ref[:, 0:1], stats_ref, pl.program_id(0) + 1)


def low_moments(low, wide, masks):
    block = masks.shape[0]
    out = jax.ShapeDtypeStruct((8, wide.shape[1]), jnp.float32)
    return pl.pallas_call(
        low_moments_kernel,
        out_shape=out,
        grid=(low.shape[0] // block,),
        in_specs=[
            pl.BlockSpec((block, low.shape[1]), lambda step: (step, 0)),
            whole(wide),
            whole(masks),
        ],
        out_specs=whole(out),
        compiler_params=pltpu.CompilerParams(vmem_limit_bytes=VMEM_BYTES),
        cost_estimate=cost(2 * low.shape[0] * low.shape[1] * 256, [low]),
        name="low_moments",
    )(low, wide, masks)


def by_tap(values):
    width = values.shape[2] // 3
    split = values.reshape(3, values.shape[1], 3, width)
    return split.transpose(0, 2, 1, 3).reshape(9, values.shape[1], width)


def widen(values):
    padded = jnp.pad(values, ((0, 0), (0, 64 - values.shape[1])))
    return jnp.concatenate([padded, padded, padded, jnp.zeros_like(padded)], axis=1)


def pack_small(items):
    total = sum(item.size for item in items)
    padded = -(-total // 2048) * 2048
    flats = [item.reshape(-1) for item in items]
    return jnp.concatenate(flats + [jnp.zeros((padded - total,), jnp.bfloat16)]).reshape(-1, 128)


def unpack_small(everything, items):
    wide, narrow = everything.shape[:2]
    everything = everything.reshape(wide, narrow, -1)
    pieces = []
    start = 0
    for item in items:
        pieces.append(
            everything[:, :, start : start + item.size].reshape((wide, narrow) + item.shape)
        )
        start += item.size
    proj, reduce, decode, refine = pieces
    proj = proj.transpose(0, 2, 1, 3).reshape(wide * proj.shape[2], -1)
    reduce = reduce.transpose(0, 2, 1, 3).reshape(wide * reduce.shape[2], -1)
    decode = decode.transpose(2, 1, 3, 0, 4).reshape(decode.shape[2], narrow * decode.shape[3], -1)
    refine = refine.transpose(2, 0, 3, 1, 4).reshape(refine.shape[2], wide * refine.shape[3], -1)
    return (proj, widen(reduce), decode, refine)


def pack_grads(reduce, proj, decode, low, refine, shapes):
    wide = lax.axis_size("wide")
    narrow = lax.axis_size("narrow")
    extra = narrow * shapes[1][1]
    reduce = reduce[:extra].T
    decode = jnp.concatenate([by_tap(decode), by_tap(low)[:, :extra]], axis=1)
    refine = by_tap(refine)
    shape_p, shape_r, shape_d, shape_f = shapes
    proj = proj.reshape(wide, shape_p[0], narrow, shape_p[1]).transpose(0, 2, 1, 3)
    reduce = reduce.reshape(wide, shape_r[0], narrow, shape_r[1]).transpose(0, 2, 1, 3)
    decode = decode.reshape(shape_d[0], narrow, shape_d[1], wide, shape_d[2]).transpose(3, 1, 0, 2, 4)
    refine = refine.reshape(shape_f[0], wide, shape_f[1], narrow, shape_f[2]).transpose(1, 3, 0, 2, 4)
    flats = [
        item.astype(jnp.bfloat16).reshape(wide, narrow, -1)
        for item in (proj, reduce, decode, refine)
    ]
    total = sum(item.shape[2] for item in flats)
    padded = -(-total // 2048) * 2048
    flats.append(jnp.zeros((wide, narrow, padded - total), jnp.bfloat16))
    return jnp.concatenate(flats, axis=2).reshape(wide, narrow, -1, 128)


def unpack_grads(owned, shapes):
    owned = owned.reshape(-1)
    pieces = []
    start = 0
    for shape in shapes:
        size = 1
        for extent in shape:
            size *= extent
        pieces.append(owned[start : start + size].reshape(shape))
        start += size
    return pieces


def per_device(
    features,
    low_level,
    widths,
    w_point,
    w_atrous,
    w_proj,
    w_low,
    w_dec1,
    w_dec2,
    w_cls,
    b_cls,
    gains,
    biases,
    low_gain,
    low_bias,
    logit_grad,
):
    canvases = features.shape[0]
    height = features.shape[1]
    columns = features.shape[2]
    fine_columns = low_level.shape[2]
    images = widths.shape[1] - 1
    channels = gains.shape[1]
    images_total = float(canvases * lax.axis_size("wide") * lax.axis_size("narrow") * images)
    small = [w_proj, w_low, w_dec1, w_dec2]
    ids_coarse = band_ids(widths, columns)
    ids_fine = band_ids(4 * widths, fine_columns)
    valid_coarse = (ids_coarse >= 0).astype(jnp.float32)[:, None, :, None]
    valid_fine = (ids_fine >= 0).astype(jnp.float32)[:, None, :, None]
    all_ones = jnp.ones((1, 1, 1), jnp.float32)
    local_count = (height * jnp.sum(widths[:, :images])).astype(jnp.float32)
    member = (ids_coarse[:, :, None] == jnp.arange(images, dtype=jnp.int32)[None, None, :]).astype(
        jnp.float32
    )
    member_low = member.astype(jnp.bfloat16)
    image_sizes = (height * widths[:, :images]).astype(jnp.float32)
    positions = low_level.shape[1] * fine_columns
    low_flat = low_level.reshape(positions, -1)
    extra = low_gain.shape[0]
    side_masks = [tap_mask(ids_fine, STRIP, 0, step) for step in (-1, 1)]
    masks = jnp.concatenate([valid_fine * jnp.ones((1, STRIP, 1, 1))] + side_masks, axis=-1)
    masks = masks.reshape(STRIP * fine_columns, 3)
    coarse_shape = (height, columns, channels)
    mask_column = jnp.broadcast_to(valid_coarse, (1, height, columns, 1)).reshape(-1, 1)
    member_wide = jnp.pad(member[0], ((0, 0), (0, 8 - images)))
    member_rows = jnp.tile(member_wide, (height, 1))
    sizes_inverse = jnp.pad(1.0 / image_sizes[0], (0, 8 - images)).reshape(8, 1)
    pool_inputs = (member_rows.T.astype(jnp.bfloat16), sizes_inverse)

    def all_sides():
        sides = [
            [
                item.reshape(height * columns, -1)
                for item in side_values(features, ids_coarse, dilation)
            ]
            for dilation in dilations
        ]
        return (sides, logit_grad.reshape(-1, logit_grad.shape[-1]))

    def low_part(proj, wide, decode, refine):
        return low_moments(low_flat, wide, masks)

    def forward(part, ready, own, other, before):
        sums, stats, pooling = ({}, {}, ()) if before is None else before
        pair = dict(zip(PARTS[part], zip(own, other)))
        more, more_stats, more_pooling = coarse_forward(
            part,
            mask_column,
            ready[0],
            pair,
            coarse_shape,
            sums,
            pool_inputs if POINT_CHUNK in PARTS[part] else None,
        )
        return ({**sums, **more}, {**stats, **more_stats}, tuple(pooling) + tuple(more_pooling))

    chunks, unpacked, ready, low_stats, coarse = gather_taps(
        order_taps(w_point, w_atrous),
        small,
        [all_sides, low_part],
        [functools.partial(forward, part) for part in range(3)],
    )
    proj_full, low_wide, decode_full, refine_full = unpacked
    sides, grad_flat = ready
    sums, stats, pool_results = coarse
    point_z, point_stats, pool_z, pooled = pool_results
    pool_z = pool_z[None, :images]
    coarse_stats = [point_stats, stats[0], stats[1], stats[2]]
    coarse_z = [
        item.reshape(1, height, columns, channels) for item in (point_z, sums[0], sums[1], sums[2])
    ]
    blocks = [(item_z, valid_coarse) for item_z in coarse_z] + [(pool_z, all_ones)]
    local_images = float(canvases * images)
    states = [(item[0], item[1]) for item in coarse_stats] + [
        local_moments(pool_z, all_ones, local_images),
    ]
    own = [state[item] for item in range(2) for state in states]
    rows = from_all(jnp.concatenate(own + [jnp.full((1,), 1.0) * local_count]))
    width = 5 * channels
    pixels = rows[:, 2 * width :]
    count_rows = jnp.concatenate(
        [
            jnp.broadcast_to(pixels, (rows.shape[0], 4 * channels)),
            jnp.full((rows.shape[0], channels), local_images),
        ],
        axis=1,
    )
    counts_flat, means_flat, squares_flat = merge_rows(
        count_rows, rows[:, :width], rows[:, width : 2 * width]
    )
    vars_flat = squares_flat / counts_flat
    section_means = []
    section_vars = []
    offset = 0
    for width in [channels] * 5:
        section_means.append(means_flat[offset : offset + width])
        section_vars.append(vars_flat[offset : offset + width])
        offset += width
    pixel_count = counts_flat[0]
    fine_count = 16.0 * pixel_count
    fine_local = 16.0 * local_count
    gain_rows = [gains[0], gains[1], gains[2], gains[3], gains[4], low_gain]
    bias_rows = [biases[0], biases[1], biases[2], biases[3], biases[4], low_bias]
    kept = []
    activations = []
    for index in range(5):
        block_values, block_valid = blocks[index]
        result = normalize(
            block_values,
            block_valid,
            section_means[index],
            section_vars[index],
            gain_rows[index],
            bias_rows[index],
        )
        kept.append(result[1:])
        activations.append(result[0].astype(jnp.bfloat16))
    spread = jnp.einsum(
        "nwk,nkd->nwd", member_low, activations[4], preferred_element_type=jnp.float32
    ).astype(jnp.bfloat16)
    spread = jnp.broadcast_to(spread[:, None], (canvases, height, columns, channels))
    joined_coarse = jnp.concatenate(activations[:4] + [spread], axis=-1)
    proj_z = jnp.einsum(
        "nhwc,cd->nhwd", joined_coarse, proj_full, preferred_element_type=jnp.float32
    )
    proj_moments = local_moments(proj_z, valid_coarse, local_count)
    joint_mean, joint_var = merged(
        jnp.stack(
            [
                jnp.concatenate([proj_moments[0], low_stats[0, :extra]]),
                jnp.concatenate([proj_moments[1], low_stats[1, :extra] / 16.0]),
            ]
        ),
        local_count,
        pixel_count,
    )
    proj_mean, low_mean = joint_mean[:channels], joint_mean[channels:]
    proj_var, low_var = joint_var[:channels], joint_var[channels:]
    proj_act, proj_centered, proj_shaped, proj_scale = normalize(
        proj_z, valid_coarse, proj_mean, proj_var, gains[5], biases[5]
    )
    proj_act = proj_act.astype(jnp.bfloat16).astype(jnp.float32)
    cols_table = column_table(ids_coarse)[0].astype(jnp.bfloat16)
    low_vectors = widen(norm_vectors(low_mean, low_var, low_gain, low_bias))
    decode_z, decode_stats, upsampled = decode_forward(
        proj_act[0],
        jnp.concatenate([cols_table, cols_table], axis=1),
        low_flat,
        low_wide,
        low_vectors,
        masks,
        decode_full,
    )
    decode_mean, decode_var = merged(decode_stats, fine_local, fine_count)
    decode_vectors = norm_vectors(decode_mean, decode_var, gains[6], biases[6])
    refine_z, refine_stats = refine_forward(decode_z, decode_vectors, masks, refine_full)
    refine_mean, refine_var = merged(refine_stats, fine_local, fine_count)
    refine_vectors = norm_vectors(refine_mean, refine_var, gains[7], biases[7])
    logits, refine_sums, cls_weight_grad, cls_bias_grad = classify(
        refine_z, grad_flat, refine_vectors, masks, w_cls, b_cls.reshape(1, -1)
    )
    logits = logits.reshape(logit_grad.shape)
    cls_bias_grad = cls_bias_grad[0]
    devices = device_count()
    cls_flat = jnp.concatenate([cls_bias_grad, cls_weight_grad.reshape(-1)])
    share = -(-cls_flat.shape[0] // devices)
    cls_rows = jnp.pad(cls_flat, (0, share * devices - cls_flat.shape[0])).reshape(devices, share)
    own = jnp.concatenate([refine_sums[0], refine_sums[1]])
    own = jnp.broadcast_to(own[None], (devices, 2 * channels))
    summed = jnp.sum(hand_out(jnp.concatenate([own, cls_rows], axis=1)), axis=0)
    refine_gain, refine_bias = summed[:channels], summed[channels : 2 * channels]
    cls_share = summed[2 * channels :]
    refine_vectors = norm_vectors(
        refine_mean,
        refine_var,
        gains[7],
        biases[7],
        refine_gain / fine_count,
        refine_bias / fine_count,
    )
    decode_local, decode_sums, refine_kernel_grad = refine_backward(
        refine_z, grad_flat, refine_vectors, w_cls, decode_z, decode_vectors, masks, refine_full
    )
    rows = from_all(jnp.concatenate([decode_sums[0], decode_sums[1], cls_share]))
    summed = jnp.sum(rows[:, : 2 * channels], axis=0)
    decode_gain, decode_bias = summed[:channels], summed[channels:]
    cls_flat = rows[:, 2 * channels :].reshape(-1)[: cls_flat.shape[0]]
    classes = cls_bias_grad.shape[0]
    cls_bias_grad = cls_flat[:classes]
    cls_weight_grad = cls_flat[classes:].reshape(cls_weight_grad.shape).T
    decode_vectors = norm_vectors(
        decode_mean,
        decode_var,
        gains[6],
        biases[6],
        decode_gain / fine_count,
        decode_bias / fine_count,
    )
    proj_up, reduce_local, reduce_sums, decode_kernel_grad, low_kernel_grad = decode_backward(
        decode_local,
        decode_z,
        decode_vectors,
        upsampled,
        low_flat,
        low_wide,
        low_vectors,
        jnp.concatenate([cols_table.T, cols_table.T], axis=1),
        masks,
        decode_full,
        coarse_shape,
    )
    proj_up = proj_up[None]
    reduce_gain, reduce_bias = reduce_sums[0, :extra], reduce_sums[1, :extra]

    proj_local, proj_gain, proj_bias = norm_grad_terms(
        proj_up, valid_coarse, proj_centered, proj_shaped
    )
    summed_pairs = gradient_sums([(proj_gain, proj_bias), (reduce_gain, reduce_bias)])
    proj_gain, proj_bias = summed_pairs[0]
    reduce_gain, reduce_bias = summed_pairs[1]
    proj_dz = norm_grad_finish(
        proj_local,
        valid_coarse,
        proj_centered,
        proj_scale,
        gains[5],
        proj_gain,
        proj_bias,
        pixel_count,
    )
    proj_kernel_grad = jnp.einsum(
        "nhwc,nhwd->cd", joined_coarse, proj_dz, preferred_element_type=jnp.float32
    )
    concat_grad = jnp.einsum(
        "nhwd,cd->nhwc", proj_dz, proj_full, preferred_element_type=jnp.float32
    )
    branch_terms = []
    for index in range(4):
        upstream = concat_grad[..., index * channels : (index + 1) * channels]
        branch_terms.append(norm_grad_terms(upstream, valid_coarse, kept[index][0], kept[index][1]))
    pool_up = jnp.einsum(
        "nhwd,nwk->nkd", concat_grad[..., 4 * channels :], member, precision=highest
    )
    branch_terms.append(norm_grad_terms(pool_up, all_ones, kept[4][0], kept[4][1]))
    local_pairs = [(term_item[1], term_item[2]) for term_item in branch_terms]
    last_pairs = gradient_sums(local_pairs)
    valid_list = [valid_coarse, valid_coarse, valid_coarse, valid_coarse, all_ones]
    count_list = [pixel_count, pixel_count, pixel_count, pixel_count, images_total]
    branch_dz = [
        norm_grad_finish(
            branch_terms[index][0],
            valid_list[index],
            kept[index][0],
            kept[index][2],
            gains[index],
            last_pairs[index][0],
            last_pairs[index][1],
            count_list[index],
        )
        for index in range(5)
    ]
    flat_dz = [item.reshape(height * columns, channels) for item in branch_dz[:4]]
    pool_dz = jnp.pad(branch_dz[4][0], ((0, 8 - images), (0, 0)))
    low_vectors = widen(
        norm_vectors(
            low_mean,
            low_var,
            low_gain,
            low_bias,
            reduce_gain / fine_count,
            reduce_bias / fine_count,
        )
    )

    def low_late(tie):
        return low_backward(reduce_local, low_flat, low_wide, low_vectors, masks, tie)

    def input_late(tie):
        side_dz = [
            side_grads(branch_dz[branch + 1], ids_coarse, dilations[branch]).reshape(
                height * columns, -1
            )
            for branch in range(3)
        ]
        return coarse_input(
            flat_dz[0],
            pool_dz,
            member_rows * sizes_inverse.reshape(1, 8),
            side_dz,
            chunks,
            coarse_shape,
            features.shape[3],
            tie,
        )

    def weight_part(part, grads, tie=None):
        return coarse_weight(
            part,
            sides,
            grads[1:4],
            coarse_shape,
            (grads[0], pooled, grads[4]) if POINT_CHUNK in PARTS[part] else None,
            tie,
        )

    owned, small_owned, low_level_grad, features_grad = scatter_taps(
        flat_dz + [pool_dz],
        [item.shape for item in small],
        [functools.partial(weight_part, part) for part in range(3)],
        (proj_kernel_grad, decode_kernel_grad, low_kernel_grad, refine_kernel_grad),
        [low_late, input_late],
    )
    low_level_grad = low_level_grad.reshape(low_level.shape)
    features_grad = features_grad.reshape(features.shape)
    proj_owned, reduce_owned, decode_owned, refine_owned = small_owned
    point_owned, atrous_owned = restore_taps(owned, w_atrous.shape)
    gains_grad = jnp.stack(
        [
            last_pairs[0][0],
            last_pairs[1][0],
            last_pairs[2][0],
            last_pairs[3][0],
            last_pairs[4][0],
            proj_gain,
            decode_gain,
            refine_gain,
        ]
    )
    biases_grad = jnp.stack(
        [
            last_pairs[0][1],
            last_pairs[1][1],
            last_pairs[2][1],
            last_pairs[3][1],
            last_pairs[4][1],
            proj_bias,
            decode_bias,
            refine_bias,
        ]
    )
    return (
        logits,
        features_grad,
        low_level_grad,
        point_owned,
        atrous_owned,
        proj_owned,
        reduce_owned,
        decode_owned,
        refine_owned,
        cls_weight_grad,
        cls_bias_grad,
        gains_grad,
        biases_grad,
        reduce_gain,
        reduce_bias,
    )


def solution(mesh):
    in_specs = (
        P(("wide", "narrow"), None, None, None),
        P(("wide", "narrow"), None, None, None),
        P(("wide", "narrow"), None),
        P(None, "wide", "narrow"),
        P(None, None, "wide", "narrow"),
        P("wide", "narrow"),
        P("wide", "narrow"),
        P(None, "narrow", "wide"),
        P(None, "wide", "narrow"),
        P(),
        P(),
        P(),
        P(),
        P(),
        P(),
        P(("wide", "narrow"), None, None, None),
    )
    out_specs = (
        P(("wide", "narrow"), None, None, None),
        P(("wide", "narrow"), None, None, None),
        P(("wide", "narrow"), None, None, None),
        P(None, "wide", "narrow"),
        P(None, None, "wide", "narrow"),
        P("wide", "narrow"),
        P("wide", "narrow"),
        P(None, "narrow", "wide"),
        P(None, "wide", "narrow"),
        P(),
        P(),
        P(),
        P(),
        P(),
        P(),
    )
    return jax.shard_map(
        per_device, mesh=mesh, in_specs=in_specs, out_specs=out_specs, check_vma=False
    )
```

```python
import functools

import jax
import jax.numpy as jnp
from jax import lax
from jax.experimental import pallas as pl
from jax.experimental.pallas import tpu as pltpu
from jax.sharding import PartitionSpec as P

epsilon = 1e-05
highest = lax.Precision.HIGHEST
dilations = (6, 12, 18)
ROUNDS = 4
VMEM_BYTES = 48 * 1024 * 1024


class Layout:
    def __init__(self, chunks, point_chunk):
        self.chunks = chunks
        self.point_chunk = point_chunk
        self.parts = [(index, index + 1) for index in range(0, len(chunks), 2)]
        self.sizes = [[chunks[index] for index in part] for part in self.parts]
        places = []
        for chunk, size in enumerate(chunks):
            places += [(chunk, tap) for tap in range(2 if chunk == point_chunk else 0, size)]
        self.rows = [
            [(line,) + places[9 * branch + 3 * line] for line in range(3)] for branch in range(3)
        ]

    def part_of(self, chunk):
        return chunk // 2

    def place(self, chunk, tap):
        return tap + (self.chunks[chunk - 1] if chunk % 2 else 0)

    def part_rows(self, part):
        return [
            (branch, line, chunk, tap)
            for branch, rows in enumerate(self.rows)
            for line, chunk, tap in rows
            if chunk in self.parts[part]
        ]

    def has_point(self, part):
        return self.point_chunk in self.parts[part]

    def order(self, point, atrous):
        flat = atrous.reshape((-1,) + atrous.shape[2:])
        before = sum(self.chunks[: self.point_chunk])
        parts = []
        start = 0
        for part, sizes in enumerate(self.sizes):
            size = sum(sizes)
            if self.has_point(part):
                pieces = [flat[start:before], point, flat[before : start + size - 2]]
                parts.append(jnp.concatenate([item for item in pieces if item.shape[0]]))
                start += size - 2
            else:
                parts.append(flat[start : start + size])
                start += size
        return parts

    def restore(self, parts, shape):
        flat = jnp.concatenate(parts)
        before = sum(self.chunks[: self.point_chunk])
        atrous = jnp.concatenate([flat[:before], flat[before + 2 :]])
        return (flat[before : before + 2], atrous.reshape(shape))


GATHER = Layout((5, 6, 9, 9), 0)
SCATTER = Layout((3, 3, 5, 6, 6, 6), 2)


def exchange(values, axis, bit):
    size = lax.axis_size(axis)
    return lax.ppermute(values, axis, [(place, place ^ bit) for place in range(size)])


def rotate(values, axis, step, stride):
    size = lax.axis_size(axis)
    rounds = size // stride
    pairs = []
    for place in range(size):
        outer, inner = place // stride, place % stride
        pairs.append((place, ((outer + step) % rounds) * stride + inner))
    return lax.ppermute(values, axis, pairs)


def device_count():
    return lax.axis_size("wide") * lax.axis_size("narrow")


def hand_out(rows):
    return lax.all_to_all(rows, ("wide", "narrow"), 0, 0, tiled=True)


def from_all(values):
    return hand_out(jnp.broadcast_to(values[None], (device_count(),) + values.shape))


def merge_rows(counts, means, squares):
    total = jnp.sum(counts, axis=0)
    mean = jnp.sum(counts * means, axis=0) / total
    gap = means - mean[None]
    return (total, mean, jnp.sum(squares + counts * gap * gap, axis=0))


def local_moments(values, valid_map, count):
    axes = tuple(range(values.ndim - 1))
    mean = jnp.sum(values * valid_map, axis=axes) / count
    centered = values - mean
    return (mean, jnp.sum(centered * centered * valid_map, axis=axes))


def place():
    wide = lax.axis_index("wide")
    narrow = lax.axis_index("narrow")
    return (wide // 2, wide % 2, narrow // 2, narrow % 2)


def share_core(shard):
    core = place()[3]
    half = shard.shape[1] // 2
    parts = shard.reshape(shard.shape[0], 2, half, shard.shape[2])
    kept = lax.dynamic_index_in_dim(parts, core, 1, keepdims=False)
    given = lax.dynamic_index_in_dim(parts, 1 - core, 1, keepdims=False)
    got = exchange(given, "narrow", 1)
    lower = jnp.where(core == 0, kept, got)
    upper = jnp.where(core == 0, got, kept)
    return jnp.concatenate([lower, upper], axis=2)


def tuned():
    return lax.axis_size("wide") == 2 * ROUNDS and lax.axis_size("narrow") == 4


def kernel_place():
    values = jnp.stack(place()).astype(jnp.int32)
    return values if tuned() else jnp.zeros_like(values)


def tied(values, earlier):
    mark = earlier[(0,) * earlier.ndim]
    return jnp.where(mark == mark, values, jnp.zeros_like(values))


def one_step(body, outs, args, specs=None, tie=None):
    def whole_spec(array):
        return pl.BlockSpec(array.shape, lambda step: (0,) * len(array.shape))

    specs = list(specs or [None] * len(args))
    run = body
    if tie is not None:
        args = [tie] + list(args)
        specs = [pl.BlockSpec(memory_space=pl.ANY)] + specs

        def run(tie_ref, *refs):
            body(*refs)

    return pl.pallas_call(
        run,
        out_shape=outs,
        grid=(1,),
        in_specs=[spec or whole_spec(arg) for spec, arg in zip(specs, args)],
        out_specs=[whole_spec(out) for out in outs],
        compiler_params=pltpu.CompilerParams(vmem_limit_bytes=VMEM_BYTES),
        cost_estimate=cost(0, args),
        name="move",
    )(*args)


def entry_spec(array, index):
    block = (1,) + array.shape[1:]
    return pl.BlockSpec(block, lambda step: (index,) + (0,) * (len(block) - 1))


def cut(sizes):
    return [slice(sum(sizes[:index]), sum(sizes[: index + 1])) for index in range(len(sizes))]


def pass_on(values, tie):
    def body(source, target):
        target[...] = source[...]

    outs = [jax.ShapeDtypeStruct(values.shape, values.dtype)]
    return one_step(body, outs, [values], None, tie)[0]


def gather_depth(values):
    return [exchange(values, "wide", 2 * flip) for flip in range(1, ROUNDS)]


def lay_out(sizes, own, others, tie=None):
    shape = own.shape[1:]
    outs = [jax.ShapeDtypeStruct((ROUNDS, size) + shape, own.dtype) for size in sizes]

    def body(*refs):
        for target, taps in zip(refs[ROUNDS:], cut(sizes)):
            for slot, source in enumerate(refs[:ROUNDS]):
                target[slot] = source[taps]

    return one_step(body, outs, [own] + list(others), tie=tie)


def pair_up(values, others, tie=None):
    outs = [jax.ShapeDtypeStruct((2,) + item.shape, item.dtype) for item in values]
    count = len(outs)

    def body(*refs):
        for index in range(count):
            refs[2 * count + index][0] = refs[index][...]
            refs[2 * count + index][1] = refs[count + index][...]

    return one_step(body, outs, list(values) + list(others), tie=tie)


def pair_all(values, others, tie=None):
    count = len(values)
    shape = values[0].shape
    sizes = [item.shape[2] for item in values]
    outs = [jax.ShapeDtypeStruct((2,) + shape[:2] + (sum(sizes),) + shape[3:], values[0].dtype)]

    def body(*refs):
        target = refs[2 * count]
        for index, taps in enumerate(cut(sizes)):
            target[0, :, :, taps] = refs[index][...]
            target[1, :, :, taps] = refs[count + index][...]

    return one_step(body, outs, list(values) + list(others), tie=tie)[0]


def first_sums(sizes, keep, got, tie=None):
    tail = keep.shape[4:]
    outs = [jax.ShapeDtypeStruct((2, ROUNDS, size) + tail, jnp.bfloat16) for size in sizes]

    def body(keep_ref, got_ref, *targets):
        for target, taps in zip(targets, cut(sizes)):
            total = keep_ref[0, :, :, taps].astype(jnp.float32)
            total = total + got_ref[0, :, :, taps].astype(jnp.float32)
            target[...] = total.astype(jnp.bfloat16)

    return one_step(body, outs, [keep, got], [entry_spec(keep, 1), entry_spec(got, 1)], tie)


def second_sums(sizes, keep, got, values, tie=None):
    tail = keep.shape[4:]
    outs = [jax.ShapeDtypeStruct((ROUNDS, sum(sizes)) + tail, jnp.float32)]
    outs += [jax.ShapeDtypeStruct((ROUNDS, size) + tail, jnp.bfloat16) for size in sizes]
    count = len(sizes)

    def body(keep_ref, got_ref, *refs):
        kept = refs[count]
        for index, taps in enumerate(cut(sizes)):
            for half in range(2):
                total = keep_ref[0, half, :, taps].astype(jnp.float32)
                total = total + got_ref[0, half, :, taps].astype(jnp.float32)
                total = total + refs[index][half].astype(jnp.float32)
                if half:
                    refs[count + 1 + index][...] = total.astype(jnp.bfloat16)
                else:
                    kept[:, taps] = total

    specs = [entry_spec(keep, 0), entry_spec(got, 0)] + [None] * count
    results = one_step(body, outs, [keep, got] + list(values), specs, tie)
    return (results[0], results[1:])


def deep_sums(sizes, kept, values, tie=None):
    shape = (2,) + kept.shape[1:]
    outs = [jax.ShapeDtypeStruct(shape, dtype) for dtype in (jnp.float32, jnp.bfloat16)]
    count = len(sizes)

    def body(kept_ref, *refs):
        for slot in range(ROUNDS):
            target = refs[count + slot // 2]
            for value, taps in zip(refs, cut(sizes)):
                total = kept_ref[slot, taps] + value[slot].astype(jnp.float32)
                target[slot % 2, taps] = total.astype(target.dtype)

    return one_step(body, outs, [kept] + list(values), None, tie)


def near_sums(kept, far, tie=None):
    shape = kept.shape[1:]
    outs = [jax.ShapeDtypeStruct(shape, dtype) for dtype in (jnp.float32, jnp.bfloat16)]

    def body(kept_ref, far_ref, *targets):
        for slot, target in enumerate(targets):
            total = kept_ref[slot] + far_ref[slot].astype(jnp.float32)
            target[...] = total.astype(target.dtype)

    return one_step(body, outs, [kept, far], None, tie)


def last_sums(kept, near, tie=None):
    def body(kept_ref, near_ref, target):
        target[...] = kept_ref[...] + near_ref[...].astype(jnp.float32)

    outs = [jax.ShapeDtypeStruct(kept.shape, jnp.float32)]
    return one_step(body, outs, [kept, near], None, tie)[0]


def chunk_order(index):
    return [("wide", 1), ("narrow", 2)] if index % 2 == 0 else [("narrow", 2), ("wide", 1)]


def gather_taps(weights, small, fillers, kernels):
    rounds = ROUNDS
    sizes = GATHER.sizes
    shapes = [item.shape for item in small]
    if not tuned():
        parts = []
        for part, values in zip(GATHER.parts, weights):
            full = lax.all_gather(values, "narrow", axis=2, tiled=True)
            full = lax.all_gather(full, "wide", axis=1, tiled=True)
            rows = full.shape[1] // (4 * rounds)
            full = full.reshape(full.shape[0], rounds, 2, 2, rows, 2, full.shape[2] // 2)
            start = 0
            pieces = []
            for index in part:
                piece = full[start : start + GATHER.chunks[index]]
                start += GATHER.chunks[index]
                order = (3, 5, 2, 1, 0, 4, 6) if index % 2 == 0 else (3, 2, 5, 1, 0, 4, 6)
                pieces.append(piece.transpose(order))
            joined = jnp.concatenate(pieces, axis=4)
            parts.append((joined[0], joined[1]))
        flat = pack_small(small)
        everything = lax.all_gather(flat, ("wide", "narrow"))
        everything = everything.reshape(lax.axis_size("wide"), lax.axis_size("narrow"), -1)
        unpacked = unpack_small(everything, small)
        ready = fillers[0]()
        results = fillers[1](*unpacked)
        result = None
        for pair, kernel in zip(parts, kernels):
            result = kernel(ready, pair, result)
        return (parts, unpacked, ready, results, result)

    def along(part, stacks, turn):
        return [
            exchange(stack, *chunk_order(index)[turn]) for stack, index in zip(stacks, GATHER.parts[part])
        ]

    def across(values):
        return (values, exchange(values, "narrow", 1))

    shared = [share_core(values) for values in weights]
    z0 = gather_depth(shared[0])
    small = small_block(small)
    xs = exchange(small, "wide", 1)
    small = pair_up([small], [xs], shared[1])[0]
    ys = exchange(small, "narrow", 2)
    s0 = lay_out(sizes[0], shared[0], z0, small)
    f0 = along(0, s0, 0)
    z1 = gather_depth(shared[1])
    s0 = pair_up(s0, f0, z1[0])
    g0 = along(0, s0, 1)
    ready = fillers[0]()
    small = pair_up([small], [ys], s0[0])[0]
    zs = gather_depth(small)
    s1 = lay_out(sizes[1], shared[1], z1, small)
    f1 = along(1, s1, 0)
    p0 = across(pair_all(s0, g0, s1[0]))
    s1 = pair_up(s1, f1, p0[0])
    g1 = along(1, s1, 1)
    result = kernels[0](ready, p0, None, s1[0])
    small = lay_out([2], small, zs, result[0][0])[0]
    cs = exchange(small, "narrow", 1)
    p1 = across(pair_all(s1, g1, small))
    unpacked = unpack_block(small, cs, shapes=shapes)
    results = fillers[1](*unpacked)
    result = kernels[1](ready, p1, result)
    return ([p0, p1], unpacked, ready, results, result)


def scatter_taps(grads, shapes, kernels, pack, fillers):
    rounds = ROUNDS
    if not tuned():
        owned = []
        for part, kernel in zip(SCATTER.parts, kernels):
            joined = jnp.stack(kernel(grads))
            pieces = []
            for index, taps in zip(part, cut([SCATTER.chunks[index] for index in part])):
                piece = joined[:, :, :, :, taps]
                order = (4, 3, 1, 0, 5, 2, 6) if index % 2 == 0 else (4, 3, 2, 0, 5, 1, 6)
                piece = piece.transpose(order)
                pieces.append(piece.reshape(piece.shape[0], -1, 2 * piece.shape[6]))
            full = jnp.concatenate(pieces)
            full = lax.psum_scatter(full, "wide", scatter_dimension=1, tiled=True)
            full = lax.psum_scatter(full, "narrow", scatter_dimension=2, tiled=True)
            owned.append(full.astype(jnp.float32))
        low, low_weight = fillers[0](grads[0])
        small = pack_grads(low_weight, *pack, shapes)
        small = lax.psum_scatter(small, "wide", scatter_dimension=0, tiled=True)
        small = lax.psum_scatter(small, "narrow", scatter_dimension=1, tiled=True)
        small = unpack_grads(small[0, 0].astype(jnp.float32), shapes)
        return (owned, small, low, fillers[1](None))

    sizes = SCATTER.sizes

    def across(pair):
        return (pair[0], exchange(pair[1], "narrow", 1))

    def along(indices, values, turn):
        return [
            exchange(value, *chunk_order(index)[turn]) for value, index in zip(values, indices)
        ]

    def far(sent):
        return exchange(sent, "wide", 4)

    def near(sent):
        return exchange(sent, "wide", 2)

    a, b, c = 2, 1, 0
    pair_a = across(kernels[a](grads))
    pair_b = across(kernels[b](grads, tie=pair_a[0]))
    sent = first_sums(sizes[a], *pair_a, pair_b[0])
    first_a = along(SCATTER.parts[a], sent, 0)
    low, low_weight = fillers[0](sent[0])
    pair_s = across(pack_block(pack[0], low_weight, *pack[1:], shapes=shapes, tie=low_weight))
    sizes_s = [pair_s[0].shape[3]]
    pair_c = across(kernels[c](grads, tie=pair_s[0]))
    kept_a, sent = second_sums(sizes[a], *pair_a, first_a, pair_c[0])
    second_a = along(SCATTER.parts[a], sent, 1)
    sent = first_sums(sizes[b], *pair_b, sent[0])
    first_b = along(SCATTER.parts[b], sent, 0)
    kept_a, sent = deep_sums(sizes[a], kept_a, second_a, sent[0])
    far_a = far(sent)
    sent = first_sums(sizes_s, *pair_s, sent)
    first_s = along((0,), sent, 0)
    filled = fillers[1](sent[0])
    kept_b, sent = second_sums(sizes[b], *pair_b, first_b, filled)
    second_b = along(SCATTER.parts[b], sent, 1)
    sent = first_sums(sizes[c], *pair_c, sent[0])
    first_c = along(SCATTER.parts[c], sent, 0)
    kept_s, sent = second_sums(sizes_s, *pair_s, first_s, sent[0])
    second_s = along((0,), sent, 1)
    total_a, sent = near_sums(kept_a, far_a, sent[0])
    near_a = near(sent)
    kept_b, sent = deep_sums(sizes[b], kept_b, second_b, sent)
    far_b = far(sent)
    kept_c, sent = second_sums(sizes[c], *pair_c, first_c, sent)
    second_c = along(SCATTER.parts[c], sent, 1)
    kept_s, sent = deep_sums(sizes_s, kept_s, second_s, sent[0])
    far_s = far(sent)
    total_a = last_sums(total_a, near_a, sent)
    kept_c, sent = deep_sums(sizes[c], kept_c, second_c, total_a)
    far_c = far(sent)
    total_b, sent = near_sums(kept_b, far_b, sent)
    near_b = near(sent)
    total_s, sent = near_sums(kept_s, far_s, sent)
    near_s = near(sent)
    total_c, sent = near_sums(kept_c, far_c, sent)
    near_c = near(sent)
    total_b = last_sums(total_b, near_b, sent)
    total_s = last_sums(total_s, near_s, total_b)
    total_c = last_sums(total_c, near_c, total_s)
    owned = [settle_core(total) for total in (total_c, total_b, total_a)]
    small = settle_small(total_s, shapes)
    return (owned, small, low, filled)


def row_span(dilation, row, height):
    step = (row - 1) * dilation
    return (max(step, 0), max(-step, 0), height - abs(step))


def tap_matrix(pair, chunk, tap, place_ref):
    row, core = place_ref[2], place_ref[3]
    flip = lax.rem(pl.program_id(0) + place_ref[1], 2)
    place = GATHER.place(chunk, tap)

    def half(ref):
        if chunk % 2 == 0:
            sides = [ref[y, flip, 0, place] for y in (row, 1 - row)]
        else:
            sides = [ref[flip, y, 0, place] for y in (row, 1 - row)]
        return jnp.concatenate(sides, axis=1)

    mine = half(pair[0])
    other = half(pair[1])
    lower = jnp.where(core == 0, mine, other)
    upper = jnp.where(core == 0, other, mine)
    return jnp.concatenate([lower, upper], axis=0)


def part_spec(array):
    def index_map(step, place_ref):
        return (0, 0, lax.bitwise_xor(step // 2, place_ref[0]), 0, 0, 0)

    return pl.BlockSpec((2, 2, 1) + array.shape[3:], index_map)


def whole_cost(flops, arrays):
    total = 0
    for array in arrays:
        size = array.dtype.itemsize
        for extent in array.shape:
            size *= extent
        total += size
    return pl.CostEstimate(flops=int(flops), bytes_accessed=total, transcendentals=0)


def cost(flops, arrays):
    return pl.CostEstimate(flops=1, bytes_accessed=1, transcendentals=0)


def coarse_flops(rows, shape, width):
    height, columns, channels = shape
    extents = sum(row_span(dilations[branch], line, height)[2] for branch, line in rows)
    return 2 * 3 * extents * columns * channels * width


def full_spec(array):
    return pl.BlockSpec(array.shape, lambda step, place_ref: (0,) * array.ndim)


def lane_spec(array):
    return pl.BlockSpec(
        (array.shape[0], array.shape[1] // (2 * ROUNDS)), lambda step, place_ref: (0, step)
    )


def store_moments(z_ref, mask_ref, stats_ref):
    mask = mask_ref[...]
    count = jnp.sum(mask)
    values = z_ref[...]
    mean = jnp.sum(values * mask, axis=0, keepdims=True) / count
    centered = (values - mean) * mask
    stats_ref[0:1, :] = mean
    stats_ref[1:2, :] = jnp.sum(centered * centered, axis=0, keepdims=True)


def behind_tie(kernel):
    def run(place_ref, tie_ref, *refs):
        kernel(place_ref, *refs)

    return run


def coarse_forward_kernel(plan, place_ref, *refs):
    refs = list(refs)
    mask_ref = refs.pop(0)
    center = refs.pop(0)
    outer = {branch: (refs.pop(0), refs.pop(0)) for branch in plan["branches"]}
    before = {branch: refs.pop(0) for branch in plan["begun"]}
    if plan["pool"]:
        member_ref = refs.pop(0)
        sizes_ref = refs.pop(0)
    pair = (refs.pop(0), refs.pop(0))
    results = {branch: refs.pop(0) for branch in plan["branches"]}
    stats = {branch: refs.pop(0) for branch in plan["done"]}
    step = pl.program_id(0)

    @pl.when(step == 0)
    def _():
        for branch in plan["branches"]:
            if branch in before:
                results[branch][...] = before[branch][...]
            else:
                results[branch][...] = jnp.zeros_like(results[branch])

    columns = plan["columns"]
    for branch, row, chunk, tap in plan["rows"]:
        source, target, extent = row_span(dilations[branch], row, plan["height"])
        matrix = jnp.concatenate(
            [tap_matrix(pair, chunk, tap + k, place_ref) for k in range(3)],
            axis=0,
        )
        rows_in = pl.ds(source * columns, extent * columns)
        rows_out = pl.ds(target * columns, extent * columns)
        sides = (outer[branch][0], center, outer[branch][1])
        values = jnp.concatenate([side[rows_in, :] for side in sides], axis=1)
        results[branch][rows_out, :] += jnp.dot(
            values, matrix, preferred_element_type=jnp.float32
        )
    if plan["pool"]:
        point_ref, point_stats_ref, pool_ref, pooled_ref = refs

        @pl.when(step == 0)
        def _():
            point_ref[...] = jnp.zeros_like(point_ref)
            pool_ref[...] = jnp.zeros_like(pool_ref)

        values = center[...]
        point_ref[...] += jnp.dot(
            values, tap_matrix(pair, GATHER.point_chunk, 0, place_ref), preferred_element_type=jnp.float32
        )
        pooled = jnp.dot(member_ref[...], values, preferred_element_type=jnp.float32)
        pooled = (pooled * sizes_ref[...]).astype(jnp.bfloat16)
        pooled_ref[...] = pooled
        pool_ref[...] += jnp.dot(
            pooled, tap_matrix(pair, GATHER.point_chunk, 1, place_ref), preferred_element_type=jnp.float32
        )

    @pl.when(step == 2 * ROUNDS - 1)
    def _():
        for branch in plan["done"]:
            store_moments(results[branch], mask_ref, stats[branch])
        if plan["pool"]:
            store_moments(point_ref, mask_ref, point_stats_ref)


def coarse_forward(part, mask, sides, pair, shape, begun, pool=None, tie=None):
    height, columns, channels = shape
    positions = height * columns
    rows = GATHER.part_rows(part)
    branches = sorted({row[0] for row in rows})
    done = [branch for branch in branches if GATHER.rows[branch][-1][1] in GATHER.parts[part]]
    plan = {
        "pool": pool is not None,
        "chunks": GATHER.parts[part],
        "branches": branches,
        "begun": [branch for branch in branches if branch in begun],
        "done": done,
        "columns": columns,
        "height": height,
        "rows": rows,
    }
    center = sides[0][1]
    args = [mask, center]
    specs = [full_spec(mask), lane_spec(center)]
    for branch in branches:
        args += [sides[branch][0], sides[branch][2]]
        specs += [lane_spec(center)] * 2
    for branch in plan["begun"]:
        args.append(begun[branch])
        specs.append(full_spec(begun[branch]))
    if pool:
        args += list(pool)
        specs += [full_spec(item) for item in pool]
    args += list(pair)
    specs += [part_spec(item) for item in pair]
    kernel = functools.partial(coarse_forward_kernel, plan)
    if tie is not None:
        kernel = behind_tie(kernel)
        args.insert(0, tie)
        specs.insert(0, pl.BlockSpec(memory_space=pl.ANY))
    flat = jax.ShapeDtypeStruct((positions, channels), jnp.float32)
    small = jax.ShapeDtypeStruct((8, channels), jnp.float32)
    outs = [flat] * len(branches) + [small] * len(done)
    if pool:
        outs += [flat, small, small, jax.ShapeDtypeStruct((8, center.shape[1]), jnp.bfloat16)]
    out_specs = [full_spec(item) for item in outs]
    if pool:
        out_specs[-1] = lane_spec(outs[-1])
    results = pl.pallas_call(
        kernel,
        out_shape=outs,
        grid_spec=pltpu.PrefetchScalarGridSpec(
            num_scalar_prefetch=1, grid=(2 * ROUNDS,), in_specs=specs, out_specs=out_specs
        ),
        compiler_params=pltpu.CompilerParams(vmem_limit_bytes=VMEM_BYTES),
        cost_estimate=cost(
            coarse_flops([row[:2] for row in rows], shape, center.shape[1])
            + (2 * positions * channels * center.shape[1] if pool else 0),
            args + outs,
        ),
        name="coarse_forward",
    )(kernel_place(), *args)
    sums = dict(zip(branches, results))
    stats = dict(zip(done, results[len(branches) :]))
    return (sums, stats, results[len(branches) + len(done) :])


def coarse_weight_kernel(plan, place_ref, *refs):
    refs = list(refs)
    center = refs.pop(0)
    outer = {branch: (refs.pop(0), refs.pop(0)) for branch in plan["branches"]}
    grads = {branch: refs.pop(0) for branch in plan["branches"]}
    if plan["pool"]:
        point_ref, pooled_ref, pool_ref = refs.pop(0), refs.pop(0), refs.pop(0)
    outs = (refs.pop(0), refs.pop(0))
    row, core = place_ref[2], place_ref[3]
    flip = lax.rem(pl.program_id(0) + place_ref[1], 2)
    rows, cols = outs[0].shape[-2:]
    columns = plan["columns"]

    def store(chunk, tap, value):
        value = value.astype(jnp.bfloat16)
        lower, upper = value[:rows], value[rows:]
        mine = jnp.where(core == 0, lower, upper)
        other = jnp.where(core == 0, upper, lower)
        place = SCATTER.place(chunk, tap)
        for ref, part in zip(outs, (mine, other)):
            for side, lane_part in ((row, part[:, :cols]), (1 - row, part[:, cols:])):
                if chunk % 2 == 0:
                    ref[flip, side, 0, place] = lane_part
                else:
                    ref[side, flip, 0, place] = lane_part

    across = (((0,), (0,)), ((), ()))
    for branch, line, chunk, tap in plan["rows"]:
        source, target, extent = row_span(dilations[branch], line, plan["height"])
        sides = (outer[branch][0], center, outer[branch][1])
        values = jnp.concatenate(
            [side[pl.ds(source * columns, extent * columns), :] for side in sides], axis=1
        )
        result = lax.dot_general(
            values,
            grads[branch][pl.ds(target * columns, extent * columns), :],
            across,
            preferred_element_type=jnp.float32,
        )
        for k in range(3):
            store(chunk, tap + k, result[2 * rows * k : 2 * rows * (k + 1)])
    if plan["pool"]:
        for tap, left, right in ((0, center, point_ref), (1, pooled_ref, pool_ref)):
            store(
                SCATTER.point_chunk,
                tap,
                lax.dot_general(
                    left[...], right[...], across, preferred_element_type=jnp.float32
                ),
            )


def coarse_weight(part, sides, grads, shape, pool=None, tie=None):
    height, columns, channels = shape
    rows = SCATTER.part_rows(part)
    branches = sorted({row[0] for row in rows})
    plan = {
        "pool": pool is not None,
        "branches": branches,
        "chunks": SCATTER.parts[part],
        "rows": rows,
        "columns": columns,
        "height": height,
    }
    center = sides[0][1]
    args = [center]
    specs = [lane_spec(center)]
    for branch in branches:
        args += [sides[branch][0], sides[branch][2]]
        specs += [lane_spec(center)] * 2
    for branch in branches:
        args.append(grads[branch])
        specs.append(full_spec(grads[branch]))
    if pool:
        args += list(pool)
        specs += [full_spec(pool[0]), lane_spec(pool[1]), full_spec(pool[2])]
    kernel = functools.partial(coarse_weight_kernel, plan)
    if tie is not None:
        kernel = behind_tie(kernel)
        args.insert(0, tie)
        specs.insert(0, pl.BlockSpec(memory_space=pl.ANY))
    total = sum(SCATTER.sizes[part])
    tail = (total, center.shape[1] // (4 * ROUNDS), channels // 2)
    outs = [jax.ShapeDtypeStruct((2, 2, ROUNDS) + tail, jnp.bfloat16)] * 2
    out_specs = [part_spec(item) for item in outs]
    results = pl.pallas_call(
        kernel,
        out_shape=outs,
        grid_spec=pltpu.PrefetchScalarGridSpec(
            num_scalar_prefetch=1, grid=(2 * ROUNDS,), in_specs=specs, out_specs=out_specs
        ),
        compiler_params=pltpu.CompilerParams(vmem_limit_bytes=VMEM_BYTES),
        cost_estimate=cost(
            coarse_flops([row[:2] for row in rows], shape, center.shape[1])
            + (2 * height * columns * channels * center.shape[1] if pool else 0),
            args + outs,
        ),
        name="coarse_weight",
    )(kernel_place(), *args)
    return (results[0], results[1])


def coarse_input_kernel(plan, place_ref, *refs):
    refs = list(refs)
    point_ref, pool_ref, spread_ref = refs.pop(0), refs.pop(0), refs.pop(0)
    grads = [refs.pop(0) for _ in range(3)]
    pairs = [(refs.pop(0), refs.pop(0)) for _ in GATHER.parts]
    point_pair = pairs[GATHER.part_of(GATHER.point_chunk)]
    out_ref, total_ref = refs
    columns = plan["columns"]
    turned = (((1,), (1,)), ((), ()))
    total_ref[...] = lax.dot_general(
        point_ref[...],
        tap_matrix(point_pair, GATHER.point_chunk, 0, place_ref),
        turned,
        preferred_element_type=jnp.float32,
    )
    pooled = lax.dot_general(
        pool_ref[...],
        tap_matrix(point_pair, GATHER.point_chunk, 1, place_ref),
        turned,
        preferred_element_type=jnp.float32,
    )
    total_ref[...] += jnp.dot(
        spread_ref[...], pooled, preferred_element_type=jnp.float32, precision=highest
    )
    for branch, rows in enumerate(plan["rows"]):
        for line, chunk, tap in rows:
            source, target, extent = row_span(dilations[branch], line, plan["height"])
            matrix = jnp.concatenate(
                [
                    tap_matrix(pairs[GATHER.part_of(chunk)], chunk, tap + k, place_ref)
                    for k in range(3)
                ],
                axis=1,
            )
            total_ref[pl.ds(source * columns, extent * columns), :] += lax.dot_general(
                grads[branch][pl.ds(target * columns, extent * columns), :],
                matrix,
                turned,
                preferred_element_type=jnp.float32,
            )
    out_ref[...] = total_ref[...].astype(jnp.bfloat16)


def coarse_input(point_dz, pool_dz, spread, grads, parts, shape, width, tie=None):
    height, columns, channels = shape
    plan = {
        "columns": columns,
        "height": height,
        "rows": GATHER.rows,
    }
    args = [point_dz, pool_dz, spread] + list(grads)
    specs = [full_spec(item) for item in args]
    for pair in parts:
        args += list(pair)
        specs += [part_spec(item) for item in pair]
    kernel = functools.partial(coarse_input_kernel, plan)
    if tie is not None:
        kernel = behind_tie(kernel)
        args.insert(0, tie)
        specs.insert(0, pl.BlockSpec(memory_space=pl.ANY))
    out = jax.ShapeDtypeStruct((height * columns, width), jnp.bfloat16)
    return pl.pallas_call(
        kernel,
        out_shape=out,
        grid_spec=pltpu.PrefetchScalarGridSpec(
            num_scalar_prefetch=1,
            grid=(2 * ROUNDS,),
            in_specs=specs,
            out_specs=lane_spec(out),
            scratch_shapes=[pltpu.VMEM((height * columns, width // (2 * ROUNDS)), jnp.float32)],
        ),
        compiler_params=pltpu.CompilerParams(vmem_limit_bytes=VMEM_BYTES),
        cost_estimate=cost(
            coarse_flops([(b, k) for b in range(3) for k in range(3)], shape, width)
            + 2 * height * columns * channels * width,
            args + [out],
        ),
        name="coarse_input",
    )(kernel_place(), *args)


STRIP = 8


def norm_vectors(mean, variance, gain, bias, *more):
    rows = [mean, lax.rsqrt(variance + epsilon), gain, bias] + list(more)
    rows += [jnp.zeros_like(mean)] * (8 - len(rows))
    return jnp.stack(rows)


def sigmoid(values):
    return 0.5 * jnp.tanh(0.5 * values) + 0.5


def vector(ref, index):
    return ref[index : index + 1, :]


def shaped_of(values, vector_ref):
    centered = (values - vector(vector_ref, 0)) * vector(vector_ref, 1)
    return (centered, centered * vector(vector_ref, 2) + vector(vector_ref, 3))


def slope_of(shaped, gate):
    return gate * (1.0 + shaped * (1.0 - gate))


def merge_vectors(rows_ref, params_ref, vector_ref, sums_ref=None):
    width = vector_ref.shape[1]
    means = rows_ref[:, :width]
    squares = rows_ref[:, width : 2 * width]
    counts = rows_ref[:, 2 * width : 2 * width + 1]
    total = jnp.sum(counts, axis=0, keepdims=True)
    mean = jnp.sum(counts * means, axis=0, keepdims=True) / total
    gap = means - mean
    variance = jnp.sum(squares + counts * gap * gap, axis=0, keepdims=True) / total
    vector_ref[0:1, :] = mean
    vector_ref[1:2, :] = lax.rsqrt(variance + epsilon)
    vector_ref[2:4, :] = params_ref[...]
    if sums_ref is not None:
        for index in range(2):
            part = sums_ref[:, index * width : (index + 1) * width]
            vector_ref[6 + index : 7 + index, :] = jnp.sum(part, axis=0, keepdims=True)
            vector_ref[4 + index : 5 + index, :] = vector_ref[6 + index : 7 + index, :] / total


def send_rows(rows_ref, pieces):
    joined = jnp.concatenate(pieces, axis=1)
    rows_ref[...] = jnp.broadcast_to(joined, rows_ref.shape)


def send_moments(rows_ref, stats_ref, masks_ref, steps):
    count = jnp.sum(masks_ref[:, 0:1]) * steps
    send_rows(
        rows_ref,
        [stats_ref[0:1, :], stats_ref[1:2, :], jnp.full((1, 128), 1.0, jnp.float32) * count],
    )


def lag_specs(steps):
    def ahead(array, block):
        return pl.BlockSpec(block, lambda step: (jnp.minimum(step, steps - 1), 0))

    def behind(array, block):
        return pl.BlockSpec(block, lambda step: (jnp.maximum(step - 1, 0), 0))

    return (ahead, behind)


def whole(array):
    return pl.BlockSpec(array.shape, lambda step: (0,) * len(array.shape))


def window(ref, start, step, columns):
    return ref[pl.ds(pl.multiple_of((start + step) * columns, columns), STRIP * columns), :]


def run_moments(values, mask, stats_ref, step):
    count = jnp.sum(mask)
    mean = jnp.sum(values * mask, axis=0, keepdims=True) / count
    centered = (values - mean) * mask
    squares = jnp.sum(centered * centered, axis=0, keepdims=True)
    done = (step - 1).astype(jnp.float32)
    old_mean = jnp.where(step > 1, stats_ref[0:1, :], mean)
    old_squares = jnp.where(step > 1, stats_ref[1:2, :], 0.0)
    gap = mean - old_mean
    stats_ref[0:1, :] = old_mean + gap / (done + 1.0)
    stats_ref[1:2, :] = old_squares + squares + gap * gap * (count * done / (done + 1.0))


def spread_columns(products, masks_ref):
    size = products.shape[0]
    width = products.shape[1] // 3
    result = products[:, width : 2 * width]
    result = result + masks_ref[:, 1:2] * pltpu.roll(products[:, :width], 1, 0)
    return result + masks_ref[:, 2:3] * pltpu.roll(products[:, 2 * width :], size - 1, 0)


def clear_edges(ref, columns):
    ref[:columns, :] = jnp.zeros((columns, ref.shape[1]), ref.dtype)
    ref[ref.shape[0] - columns :, :] = jnp.zeros((columns, ref.shape[1]), ref.dtype)


def row_taps(w_ref, row, start, stop):
    return jnp.concatenate([w_ref[3 * row + k, start:stop, :] for k in range(3)], axis=1)


def low_lanes(width):
    return lax.broadcasted_iota(jnp.int32, (1, width), 1)


def decode_forward_kernel(
    steps, act_ref, table_ref, low_ref, wide_ref, vector_ref, masks_ref, w_ref, z_ref, rows_ref,
    up_ref, joined_ref, reduced_ref, stats_ref
):
    step = pl.program_id(0)
    columns = table_ref.shape[0]
    channels = act_ref.shape[2]
    rows = act_ref.shape[0]

    @pl.when(step == 0)
    def _():
        clear_edges(joined_ref, columns)
        clear_edges(reduced_ref, columns)

    @pl.when(step < steps)
    def _():
        for offset in range(STRIP):
            base = step * (STRIP // 4) + offset // 4 + (offset % 4 - 2) // 2
            fraction = ((2 * (offset % 4) - 3) % 8) / 8.0
            lower = act_ref[jnp.maximum(base, 0)]
            upper = act_ref[jnp.minimum(base + 1, rows - 1)]
            mixed = (1.0 - fraction) * lower + fraction * upper
            coarse = mixed.astype(jnp.bfloat16)
            fine = (mixed - coarse.astype(jnp.float32)).astype(jnp.bfloat16)
            value = jnp.dot(
                table_ref[...],
                jnp.concatenate([coarse, fine], axis=0),
                preferred_element_type=jnp.float32,
            ).astype(jnp.bfloat16)
            up_ref[offset * columns : (offset + 1) * columns, :] = value
            start = pl.multiple_of((step * STRIP + offset + 1) * columns, columns)
            joined_ref[pl.ds(start, columns), :] = value
        reduced = jnp.dot(low_ref[...], wide_ref[...], preferred_element_type=jnp.float32)
        _, shaped = shaped_of(reduced, vector_ref)
        value = masks_ref[:, 0:1] * (shaped * sigmoid(shaped))
        start = pl.multiple_of((step * STRIP + 1) * columns, columns)
        reduced_ref[pl.ds(start, STRIP * columns), :] = value.astype(jnp.bfloat16)

    @pl.when(step > 0)
    def _():
        start = (step - 1) * STRIP
        lane = low_lanes(reduced_ref.shape[1])
        lows = [window(reduced_ref, start, k, columns) for k in range(3)]
        low = jnp.where(lane < 64, lows[0], jnp.where(lane < 128, lows[1], lows[2]))
        values = jnp.concatenate(
            [window(joined_ref, start, k, columns) for k in range(3)] + [low], axis=1
        )
        extra = w_ref.shape[1] - channels
        parts = [row_taps(w_ref, k, 0, channels) for k in range(3)]
        for k in range(3):
            parts.append(row_taps(w_ref, k, channels, channels + extra))
            parts.append(jnp.zeros((64 - extra, 3 * channels), jnp.bfloat16))
        parts.append(jnp.zeros((64, 3 * channels), jnp.bfloat16))
        products = jnp.dot(
            values, jnp.concatenate(parts, axis=0), preferred_element_type=jnp.float32
        )
        result = spread_columns(products, masks_ref)
        z_ref[...] = result
        run_moments(result, masks_ref[:, 0:1], stats_ref, step)

    @pl.when(step == steps)
    def _():
        send_moments(rows_ref, stats_ref, masks_ref, steps)


def decode_forward(act, table, low, wide, vectors, masks, weights, devices):
    positions = low.shape[0]
    columns = table.shape[0]
    block = STRIP * columns
    steps = positions // block
    channels = act.shape[2]
    ahead, behind = lag_specs(steps)
    flat = jax.ShapeDtypeStruct((positions, channels), jnp.float32)
    stats = jax.ShapeDtypeStruct((devices, 2 * channels + 128), jnp.float32)
    up = jax.ShapeDtypeStruct((positions, channels), jnp.bfloat16)
    return pl.pallas_call(
        functools.partial(decode_forward_kernel, steps),
        out_shape=[flat, stats, up],
        grid=(steps + 1,),
        in_specs=[
            whole(act),
            whole(table),
            ahead(low, (block, low.shape[1])),
            whole(wide),
            whole(vectors),
            whole(masks),
            whole(weights),
        ],
        out_specs=[
            behind(flat, (block, channels)),
            whole(stats),
            ahead(up, (block, channels)),
        ],
        scratch_shapes=[
            pltpu.VMEM((positions + 2 * columns, channels), jnp.bfloat16),
            pltpu.VMEM((positions + 2 * columns, wide.shape[1]), jnp.bfloat16),
            pltpu.VMEM((8, channels), jnp.float32),
        ],
        compiler_params=pltpu.CompilerParams(vmem_limit_bytes=VMEM_BYTES),
        cost_estimate=cost(2 * positions * 3 * channels * 4 * channels, [low, flat, up]),
        name="decode_forward",
    )(act, table, low, wide, vectors, masks, weights)


def refine_forward_kernel(
    steps, columns, z_in_ref, rows_in_ref, params_ref, masks_ref, w_ref, z_ref, rows_ref, act_ref,
    vector_ref, stats_ref
):
    step = pl.program_id(0)
    channels = w_ref.shape[1]

    @pl.when(step == 0)
    def _():
        clear_edges(act_ref, columns)
        merge_vectors(rows_in_ref, params_ref, vector_ref)

    @pl.when(step < steps)
    def _():
        _, shaped = shaped_of(z_in_ref[...], vector_ref)
        value = masks_ref[:, 0:1] * (shaped * sigmoid(shaped))
        start = pl.multiple_of((step * STRIP + 1) * columns, columns)
        act_ref[pl.ds(start, STRIP * columns), :] = value.astype(jnp.bfloat16)

    @pl.when(step > 0)
    def _():
        start = (step - 1) * STRIP
        values = jnp.concatenate([window(act_ref, start, k, columns) for k in range(3)], axis=1)
        matrix = jnp.concatenate([row_taps(w_ref, k, 0, channels) for k in range(3)], axis=0)
        products = jnp.dot(values, matrix, preferred_element_type=jnp.float32)
        result = spread_columns(products, masks_ref)
        z_ref[...] = result
        run_moments(result, masks_ref[:, 0:1], stats_ref, step)

    @pl.when(step == steps)
    def _():
        send_moments(rows_ref, stats_ref, masks_ref, steps)


def refine_forward(z_in, rows, params, masks, weights):
    positions, channels = z_in.shape
    block = masks.shape[0]
    columns = block // STRIP
    steps = positions // block
    ahead, behind = lag_specs(steps)
    flat = jax.ShapeDtypeStruct((positions, channels), jnp.float32)
    stats = jax.ShapeDtypeStruct(rows.shape, jnp.float32)
    return pl.pallas_call(
        functools.partial(refine_forward_kernel, steps, columns),
        out_shape=[flat, stats],
        grid=(steps + 1,),
        in_specs=[
            ahead(z_in, (block, channels)),
            whole(rows),
            whole(params),
            whole(masks),
            whole(weights),
        ],
        out_specs=[behind(flat, (block, channels)), whole(stats)],
        scratch_shapes=[
            pltpu.VMEM((positions + 2 * columns, channels), jnp.bfloat16),
            pltpu.VMEM((8, channels), jnp.float32),
            pltpu.VMEM((8, channels), jnp.float32),
        ],
        compiler_params=pltpu.CompilerParams(vmem_limit_bytes=VMEM_BYTES),
        cost_estimate=cost(2 * positions * 9 * channels * channels, [z_in, flat]),
        name="refine_forward",
    )(z_in, rows, params, masks, weights)


def class_kernel(
    steps, z_ref, grad_ref, rows_ref, params_ref, masks_ref, w_ref, b_ref, logits_ref, out_ref,
    vector_ref, sums_ref, weight_ref, bias_ref
):
    step = pl.program_id(0)

    @pl.when(step == 0)
    def _():
        merge_vectors(rows_ref, params_ref, vector_ref)
        sums_ref[...] = jnp.zeros_like(sums_ref)
        weight_ref[...] = jnp.zeros_like(weight_ref)
        bias_ref[...] = jnp.zeros_like(bias_ref)

    mask = masks_ref[:, 0:1]
    centered, shaped = shaped_of(z_ref[...], vector_ref)
    gate = sigmoid(shaped)
    act = (mask * (shaped * gate)).astype(jnp.bfloat16)
    logits = jnp.dot(act, w_ref[...], preferred_element_type=jnp.float32) + b_ref[...]
    logits_ref[...] = (mask * logits).astype(jnp.bfloat16)
    grad = (mask * grad_ref[...].astype(jnp.float32)).astype(jnp.bfloat16)
    upstream = lax.dot_general(
        grad, w_ref[...], (((1,), (1,)), ((), ())), preferred_element_type=jnp.float32
    )
    local = mask * upstream * slope_of(shaped, gate)
    sums_ref[0:1, :] += jnp.sum(local * centered, axis=0, keepdims=True)
    sums_ref[1:2, :] += jnp.sum(local, axis=0, keepdims=True)
    weight_ref[...] += lax.dot_general(
        grad, act, (((0,), (0,)), ((), ())), preferred_element_type=jnp.float32
    )
    bias_ref[...] += jnp.sum(grad.astype(jnp.float32), axis=0, keepdims=True)

    @pl.when(step == steps - 1)
    def _():
        width = vector_ref.shape[1]
        classes = bias_ref.shape[1]
        shape = (classes, width)
        place = lax.broadcasted_iota(jnp.int32, shape, 0) == lax.broadcasted_iota(jnp.int32, shape, 1)
        wide_bias = jnp.dot(
            bias_ref[...],
            jnp.where(place, 1.0, 0.0),
            preferred_element_type=jnp.float32,
            precision=highest,
        )
        out_ref[...] = jnp.zeros_like(out_ref)
        send_rows(out_ref.at[:, : 2 * width], [sums_ref[0:1, :], sums_ref[1:2, :]])
        out_ref[:classes, 2 * width :] = weight_ref[...]
        out_ref[classes : classes + 1, 2 * width :] = wide_bias


def classify(z, grad, rows, params, masks, weights, bias):
    positions, channels = z.shape
    block = masks.shape[0]
    classes = grad.shape[1]
    steps = positions // block
    outs = [
        jax.ShapeDtypeStruct((positions, classes), jnp.bfloat16),
        jax.ShapeDtypeStruct((rows.shape[0], 3 * channels), jnp.float32),
    ]

    def strip(width):
        return pl.BlockSpec((block, width), lambda step: (step, 0))

    return pl.pallas_call(
        functools.partial(class_kernel, steps),
        out_shape=outs,
        grid=(steps,),
        in_specs=[
            strip(channels),
            strip(classes),
            whole(rows),
            whole(params),
            whole(masks),
            whole(weights),
            whole(bias),
        ],
        out_specs=[strip(classes), whole(outs[1])],
        scratch_shapes=[
            pltpu.VMEM((8, channels), jnp.float32),
            pltpu.VMEM((8, channels), jnp.float32),
            pltpu.VMEM((classes, channels), jnp.float32),
            pltpu.VMEM((1, classes), jnp.float32),
        ],
        compiler_params=pltpu.CompilerParams(vmem_limit_bytes=VMEM_BYTES),
        cost_estimate=cost(6 * positions * channels * 128, [z, grad, grad]),
        name="classify",
    )(z, grad, rows, params, masks, weights, bias)


def finish_grad(local, centered, mask, vector_ref):
    inner = local - vector(vector_ref, 5) - centered * vector(vector_ref, 4)
    return mask * vector(vector_ref, 2) * vector(vector_ref, 1) * inner


def store_sides(grad, masks_ref, side_ref, start):
    size, width = grad.shape
    grad = grad.astype(jnp.bfloat16).astype(jnp.float32)
    rows = pl.ds(start, size)
    side_ref[rows, :width] = pltpu.roll(masks_ref[:, 1:2] * grad, size - 1, 0).astype(jnp.bfloat16)
    side_ref[rows, width : 2 * width] = grad.astype(jnp.bfloat16)
    side_ref[rows, 2 * width :] = pltpu.roll(masks_ref[:, 2:3] * grad, 1, 0).astype(jnp.bfloat16)


def refine_backward_kernel(
    steps, columns, z_ref, grad_ref, rows_ref, sums_in_ref, params_ref, cls_ref, z_in_ref,
    rows_in_ref, params_in_ref, masks_ref, w_ref, local_ref, out_ref, totals_ref, weight_ref,
    side_ref, vector_ref, vector_in_ref, sums_ref
):
    step = pl.program_id(0)
    channels = w_ref.shape[1]
    mask = masks_ref[:, 0:1]

    @pl.when(step == 0)
    def _():
        clear_edges(side_ref, columns)
        merge_vectors(rows_ref, params_ref, vector_ref, sums_in_ref)
        merge_vectors(rows_in_ref, params_in_ref, vector_in_ref)
        totals_ref[...] = vector_ref[...]
        sums_ref[...] = jnp.zeros_like(sums_ref)
        weight_ref[...] = jnp.zeros_like(weight_ref)

    @pl.when(step < steps)
    def _():
        centered, shaped = shaped_of(z_ref[...], vector_ref)
        grad = (mask * grad_ref[...].astype(jnp.float32)).astype(jnp.bfloat16)
        upstream = lax.dot_general(
            grad, cls_ref[...], (((1,), (1,)), ((), ())), preferred_element_type=jnp.float32
        )
        local = mask * upstream * slope_of(shaped, sigmoid(shaped))
        start = pl.multiple_of((step * STRIP + 1) * columns, columns)
        store_sides(finish_grad(local, centered, mask, vector_ref), masks_ref, side_ref, start)

    @pl.when(step > 0)
    def _():
        start = (step - 1) * STRIP
        centered, shaped = shaped_of(z_in_ref[...], vector_in_ref)
        gate = sigmoid(shaped)
        act = (mask * (shaped * gate)).astype(jnp.bfloat16)
        sides = [window(side_ref, start, 2 - k, columns) for k in range(3)]
        upstream = lax.dot_general(
            jnp.concatenate(sides, axis=1),
            jnp.concatenate([w_ref[tap] for tap in range(9)], axis=1),
            (((1,), (1,)), ((), ())),
            preferred_element_type=jnp.float32,
        )
        local = mask * upstream * slope_of(shaped, gate)
        local_ref[...] = local
        sums_ref[0:1, :] += jnp.sum(local * centered, axis=0, keepdims=True)
        sums_ref[1:2, :] += jnp.sum(local, axis=0, keepdims=True)
        turned = act.T
        for k in range(3):
            weight_ref[k] += jnp.dot(turned, sides[k], preferred_element_type=jnp.float32)

    @pl.when(step == steps)
    def _():
        share = jnp.sum(sums_in_ref[:, 2 * channels :], axis=0, keepdims=True)
        send_rows(out_ref, [sums_ref[0:1, :], sums_ref[1:2, :], share])


def refine_backward(
    z, grad, rows, sums, params, classes, z_in, rows_in, params_in, masks, weights
):
    positions, channels = z.shape
    block = masks.shape[0]
    columns = block // STRIP
    steps = positions // block
    ahead, behind = lag_specs(steps)
    outs = [
        jax.ShapeDtypeStruct((positions, channels), jnp.float32),
        jax.ShapeDtypeStruct(sums.shape, jnp.float32),
        jax.ShapeDtypeStruct((8, channels), jnp.float32),
        jax.ShapeDtypeStruct((3, channels, 3 * channels), jnp.float32),
    ]
    return pl.pallas_call(
        functools.partial(refine_backward_kernel, steps, columns),
        out_shape=outs,
        grid=(steps + 1,),
        in_specs=[
            ahead(z, (block, channels)),
            ahead(grad, (block, grad.shape[1])),
            whole(rows),
            whole(sums),
            whole(params),
            whole(classes),
            behind(z_in, (block, channels)),
            whole(rows_in),
            whole(params_in),
            whole(masks),
            whole(weights),
        ],
        out_specs=[behind(z, (block, channels))] + [whole(item) for item in outs[1:]],
        scratch_shapes=[
            pltpu.VMEM((positions + 2 * columns, 3 * channels), jnp.bfloat16),
            pltpu.VMEM((8, channels), jnp.float32),
            pltpu.VMEM((8, channels), jnp.float32),
            pltpu.VMEM((8, channels), jnp.float32),
        ],
        compiler_params=pltpu.CompilerParams(vmem_limit_bytes=VMEM_BYTES),
        cost_estimate=cost(4 * positions * 9 * channels * channels, [z, z_in, grad, outs[0], weights]),
        name="refine_backward",
    )(z, grad, rows, sums, params, classes, z_in, rows_in, params_in, masks, weights)


def decode_backward_kernel(
    steps, columns, local_ref, z_ref, rows_ref, sums_in_ref, params_ref, up_ref, low_ref, wide_ref,
    low_vector_ref, table_ref, masks_ref, w_ref, coarse_ref, low_local_ref, sums_ref, totals_ref,
    weight_ref, low_weight_ref, side_ref, total_ref, vector_ref
):
    step = pl.program_id(0)
    channels = w_ref.shape[2]
    extra = w_ref.shape[1] - channels
    mask = masks_ref[:, 0:1]

    @pl.when(step == 0)
    def _():
        clear_edges(side_ref, columns)
        merge_vectors(rows_ref, params_ref, vector_ref, sums_in_ref)
        totals_ref[...] = vector_ref[...]
        sums_ref[...] = jnp.zeros_like(sums_ref)
        weight_ref[...] = jnp.zeros_like(weight_ref)
        low_weight_ref[...] = jnp.zeros_like(low_weight_ref)
        total_ref[...] = jnp.zeros_like(total_ref)

    @pl.when(step < steps)
    def _():
        centered, _ = shaped_of(z_ref[...], vector_ref)
        start = pl.multiple_of((step * STRIP + 1) * columns, columns)
        grad = finish_grad(local_ref[...], centered, mask, vector_ref)
        store_sides(grad, masks_ref, side_ref, start)

    @pl.when(step > 0)
    def _():
        start = (step - 1) * STRIP
        sides = [window(side_ref, start, 2 - k, columns) for k in range(3)]
        pieces = []
        for tap in range(9):
            pieces.append(
                jnp.concatenate(
                    [w_ref[tap], jnp.zeros((64 - extra, channels), jnp.bfloat16)], axis=0
                )
            )
        upstream = lax.dot_general(
            jnp.concatenate(sides, axis=1),
            jnp.concatenate(pieces, axis=1),
            (((1,), (1,)), ((), ())),
            preferred_element_type=jnp.float32,
        )
        for offset in range(STRIP):
            base = (step - 1) * (STRIP // 4) + offset // 4 + (offset % 4 - 2) // 2
            fraction = ((2 * (offset % 4) - 3) % 8) / 8.0
            value = upstream[offset * columns : (offset + 1) * columns, :channels]
            value = value.astype(jnp.bfloat16).astype(jnp.float32)
            total_ref[base + 1] += (1.0 - fraction) * value
            total_ref[base + 2] += fraction * value
        reduced = jnp.dot(low_ref[...], wide_ref[...], preferred_element_type=jnp.float32)
        centered, shaped = shaped_of(reduced, low_vector_ref)
        gate = sigmoid(shaped)
        low_act = (mask * (shaped * gate)).astype(jnp.bfloat16)
        low_up = upstream[:, channels:]
        local = mask * low_up * slope_of(shaped, gate)[:, :64]
        low_local_ref[...] = local
        sums_ref[0:1, :64] += jnp.sum(local * centered[:, :64], axis=0, keepdims=True)
        sums_ref[1:2, :64] += jnp.sum(local, axis=0, keepdims=True)
        turned = up_ref[...].T
        low_turned = low_act[:, :128].T[:64]
        for k in range(3):
            weight_ref[k] += jnp.dot(turned, sides[k], preferred_element_type=jnp.float32)
            low_weight_ref[k] += jnp.dot(low_turned, sides[k], preferred_element_type=jnp.float32)

    @pl.when(step == steps)
    def _():
        rows = coarse_ref.shape[0]
        total_ref[1] += total_ref[0]
        total_ref[rows] += total_ref[rows + 1]
        for row in range(rows):
            value = total_ref[row + 1]
            upper = value.astype(jnp.bfloat16)
            lower = (value - upper.astype(jnp.float32)).astype(jnp.bfloat16)
            coarse_ref[row] = jnp.dot(
                table_ref[...],
                jnp.concatenate([upper, lower], axis=0),
                preferred_element_type=jnp.float32,
            )


def decode_backward(
    local, z, rows, sums, params, up, low, wide, low_vectors, table, masks, weights, shape
):
    positions, channels = z.shape
    block = masks.shape[0]
    columns = block // STRIP
    steps = positions // block
    height, coarse_columns, _ = shape
    ahead, behind = lag_specs(steps)
    outs = [
        jax.ShapeDtypeStruct((height, coarse_columns, channels), jnp.float32),
        jax.ShapeDtypeStruct((positions, 64), jnp.float32),
        jax.ShapeDtypeStruct((8, channels), jnp.float32),
        jax.ShapeDtypeStruct((8, channels), jnp.float32),
        jax.ShapeDtypeStruct((3, channels, 3 * channels), jnp.float32),
        jax.ShapeDtypeStruct((3, 64, 3 * channels), jnp.float32),
    ]
    return pl.pallas_call(
        functools.partial(decode_backward_kernel, steps, columns),
        out_shape=outs,
        grid=(steps + 1,),
        in_specs=[
            ahead(local, (block, channels)),
            ahead(z, (block, channels)),
            whole(rows),
            whole(sums),
            whole(params),
            behind(up, (block, channels)),
            behind(low, (block, low.shape[1])),
            whole(wide),
            whole(low_vectors),
            whole(table),
            whole(masks),
            whole(weights),
        ],
        out_specs=[whole(outs[0]), behind(outs[1], (block, 64))]
        + [whole(item) for item in outs[2:]],
        scratch_shapes=[
            pltpu.VMEM((positions + 2 * columns, 3 * channels), jnp.bfloat16),
            pltpu.VMEM((height + 2, columns, channels), jnp.float32),
            pltpu.VMEM((8, channels), jnp.float32),
        ],
        compiler_params=pltpu.CompilerParams(vmem_limit_bytes=VMEM_BYTES),
        cost_estimate=cost(4 * positions * 9 * channels * (channels + 64), [local, z, up, low, outs[1], weights]),
        name="decode_backward",
    )(local, z, rows, sums, params, up, low, wide, low_vectors, table, masks, weights)


def low_backward_kernel(
    vector_ref, local_ref, low_ref, wide_ref, masks_ref, out_ref, weight_ref
):
    @pl.when(pl.program_id(0) == 0)
    def _():
        weight_ref[...] = jnp.zeros_like(weight_ref)

    low = low_ref[...]
    weights = wide_ref[:, :128]
    reduced = jnp.dot(low, weights, preferred_element_type=jnp.float32)
    mean, scale, gain = (vector_ref[k : k + 1, :64] for k in range(3))
    centered = (reduced[:, :64] - mean) * scale
    inner = local_ref[...] - vector_ref[5:6, :64] - centered * vector_ref[4:5, :64]
    grad = (masks_ref[:, 0:1] * gain * scale * inner).astype(jnp.bfloat16)
    out_ref[...] = lax.dot_general(
        grad, weights[:, :64], (((1,), (1,)), ((), ())), preferred_element_type=jnp.float32
    ).astype(jnp.bfloat16)
    weight_ref[...] += lax.dot_general(
        grad, low, (((0,), (0,)), ((), ())), preferred_element_type=jnp.float32
    )


def low_backward(local, low, wide, vectors, masks, tie):
    positions, width = low.shape
    block = masks.shape[0]
    outs = [
        jax.ShapeDtypeStruct((positions, width), jnp.bfloat16),
        jax.ShapeDtypeStruct((64, width), jnp.float32),
    ]
    return pl.pallas_call(
        behind_tie(low_backward_kernel),
        out_shape=outs,
        grid=(positions // block,),
        in_specs=[
            whole(vectors),
            pl.BlockSpec(memory_space=pl.ANY),
            pl.BlockSpec((block, 64), lambda step: (step, 0)),
            pl.BlockSpec((block, width), lambda step: (step, 0)),
            whole(wide),
            whole(masks),
        ],
        out_specs=[pl.BlockSpec((block, width), lambda step: (step, 0)), whole(outs[1])],
        compiler_params=pltpu.CompilerParams(vmem_limit_bytes=VMEM_BYTES),
        cost_estimate=whole_cost(6 * positions * width * 128, [local, low, low]),
        name="low_backward",
    )(vectors, tie, local, low, wide, masks)


def side_values(values, image_ids, dilation):
    result = []
    for step in (-dilation, dilation):
        mask = tap_mask(image_ids, values.shape[1], 0, step).astype(values.dtype)
        result.append(mask * shifted(values, 0, step))
    return [result[0], values, result[1]]


def side_grads(values, image_ids, dilation):
    result = []
    for step in (-dilation, 0, dilation):
        masked = tap_mask(image_ids, values.shape[1], 0, step).astype(values.dtype) * values
        result.append(shifted(masked, 0, -step))
    return jnp.concatenate(result, axis=-1)


def settle_core(values):
    core = place()[3]
    taps, rows, cols = values.shape
    parts = values.reshape(taps, rows, 2, cols // 2)
    kept = lax.dynamic_index_in_dim(parts, core, 2, keepdims=False)
    given = lax.dynamic_index_in_dim(parts, 1 - core, 2, keepdims=False).astype(jnp.bfloat16)
    got = exchange(given, "narrow", 1).astype(jnp.float32)
    lower = jnp.where(core == 0, kept, got)
    upper = jnp.where(core == 0, got, kept)
    return jnp.concatenate([lower, upper], axis=1)


def band_ids(widths, columns):
    ends_all = jnp.cumsum(widths, axis=1)
    position = jnp.arange(columns, dtype=jnp.int32)
    band_index = jnp.sum(
        (position[None, :, None] >= ends_all[:, None, :]).astype(jnp.int32), axis=2
    )
    return jnp.where(band_index < widths.shape[1] - 1, band_index, -1)


def shifted(values, row_shift, col_shift):
    height = values.shape[1]
    columns = values.shape[2]
    padded = jnp.pad(
        values, ((0, 0), (abs(row_shift), abs(row_shift)), (abs(col_shift), abs(col_shift)), (0, 0))
    )
    row_start = abs(row_shift) + row_shift
    col_start = abs(col_shift) + col_shift
    return padded[:, row_start : row_start + height, col_start : col_start + columns, :]


def tap_mask(image_ids, height, row_shift, col_shift):
    columns = image_ids.shape[1]
    padded = jnp.pad(image_ids, ((0, 0), (abs(col_shift), abs(col_shift))), constant_values=-2)
    col_start = abs(col_shift) + col_shift
    other_ids = padded[:, col_start : col_start + columns]
    same_image = (other_ids == image_ids).astype(jnp.float32)
    row_place = jnp.arange(height) + row_shift
    inside = ((row_place >= 0) & (row_place < height)).astype(jnp.float32)
    return (inside[None, :, None] * same_image[:, None, :])[..., None]


def tap_offsets(dilation):
    return [
        ((tap_index // 3 - 1) * dilation, (tap_index % 3 - 1) * dilation) for tap_index in range(9)
    ]


def linear_weights(out_count, in_count):
    position = jnp.arange(out_count, dtype=jnp.int32)
    scaled = 2 * position - 3
    left_index = jnp.floor_divide(scaled, 8)
    fraction = (scaled - 8 * left_index).astype(jnp.float32) / 8.0
    lower_index = jnp.clip(left_index, 0, in_count - 1)
    upper_index = jnp.clip(left_index + 1, 0, in_count - 1)
    return (position, lower_index, upper_index, fraction)


def column_table(image_ids):
    columns = image_ids.shape[1]
    position, lower_index, upper_index, fraction = linear_weights(4 * columns, columns)
    source = jnp.arange(columns, dtype=jnp.int32)[None, :]

    def picker(index_row):
        return (source == index_row[:, None]).astype(jnp.int32)

    def lookup(index_row):
        return jnp.sum(image_ids[:, None, :] * picker(index_row)[None], axis=2)

    own_index = position // 4
    own_id = lookup(own_index)
    weight_lower = (1.0 - fraction)[None, :] * (lookup(lower_index) == own_id).astype(jnp.float32)
    weight_upper = fraction[None, :] * (lookup(upper_index) == own_id).astype(jnp.float32)
    weight_own = 1.0 - weight_lower - weight_upper
    table = weight_lower[:, :, None] * picker(lower_index)[None].astype(jnp.float32)
    table = table + weight_upper[:, :, None] * picker(upper_index)[None].astype(jnp.float32)
    table = table + weight_own[:, :, None] * picker(own_index)[None].astype(jnp.float32)
    return table


def normalize(values, valid_map, mean_row, variance, gain_row, bias_row):
    norm_scale = lax.rsqrt(variance + epsilon)
    centered = (values - mean_row) * norm_scale
    shaped = centered * gain_row + bias_row
    return (valid_map * jax.nn.silu(shaped), centered, shaped, norm_scale)


def norm_grad_terms(upstream, valid_map, centered, shaped):
    sigmoid_value = jax.nn.sigmoid(shaped)
    local_term = valid_map * upstream * sigmoid_value * (1.0 + shaped * (1.0 - sigmoid_value))
    axes = tuple(range(local_term.ndim - 1))
    return (local_term, jnp.sum(local_term * centered, axis=axes), jnp.sum(local_term, axis=axes))


def norm_grad_finish(
    local_term, valid_map, centered, norm_scale, gain_row, gain_sum, bias_sum, count_all
):
    inner = local_term - bias_sum / count_all - centered * gain_sum / count_all
    return (valid_map * gain_row * norm_scale * inner).astype(jnp.bfloat16)


def moments(values, valid_map, local_count, count_all):
    mean, squares = local_moments(values, valid_map, local_count)
    return merged(jnp.stack([mean, squares]), local_count, count_all)


def merged(stats, local_count, count_all):
    width = stats.shape[1]
    own = jnp.concatenate([stats[0], stats[1], jnp.full((1,), 1.0) * local_count])
    rows = from_all(own)
    counts, means, squares = merge_rows(
        rows[:, 2 * width :], rows[:, :width], rows[:, width : 2 * width]
    )
    return (means, squares / count_all)


def pack_pairs(pairs):
    return jnp.concatenate(
        [pair_item[0] for pair_item in pairs] + [pair_item[1] for pair_item in pairs]
    )


def unpack_pairs(flat, pairs):
    lengths = [pair_item[0].shape[0] for pair_item in pairs]
    half_point = sum(lengths)
    result_pairs = []
    offset = 0
    for length_now in lengths:
        result_pairs.append(
            (
                flat[offset : offset + length_now],
                flat[half_point + offset : half_point + offset + length_now],
            )
        )
        offset = offset + length_now
    return result_pairs


def gradient_sums(pairs):
    return unpack_pairs(jnp.sum(from_all(pack_pairs(pairs)), axis=0), pairs)


def small_block(items):
    proj, reduce, decode, refine = items
    taps, rows, cols = refine.shape
    count = proj.shape[0] // rows
    proj = proj.reshape(2, count, rows // 2, cols).swapaxes(0, 1).reshape(count, rows, cols)
    reduce = jnp.pad(reduce, ((0, 0), (0, cols - reduce.shape[1])))[None]
    shared = share_core(jnp.concatenate([refine, proj, reduce]))
    lanes = shared.shape[2]
    decode = decode.swapaxes(1, 2)
    decode = jnp.pad(decode, ((0, 0), (0, 0), (0, lanes - decode.shape[2])))
    return jnp.concatenate([shared, decode.reshape(-1, shared.shape[1], lanes)])


def settle_small(owned, shapes):
    shape_p, shape_r, shape_d, shape_f = shapes
    taps, rows, cols = shape_f
    count = shape_p[0] // rows
    first = taps + count + 1
    settled = settle_core(owned[:first])
    proj = settled[taps : taps + count].reshape(count, 2, rows // 2, cols)
    proj = proj.swapaxes(0, 1).reshape(shape_p)
    reduce = settled[taps + count, :, : shape_r[1]]
    decode = owned[first:].reshape(taps, shape_d[2], -1)[:, :, : shape_d[1]].swapaxes(1, 2)
    return (proj, reduce, decode, settled[:taps])


def reduce_lanes(width, row, core, half):
    start = (2 * row + core) * width
    return start, core * half


def unpack_kernel(shapes, place_ref, own_ref, other_ref, proj_ref, wide_ref, decode_ref, refine_ref):
    deep, side, row, core = (place_ref[index] for index in range(4))
    shape_p, shape_r, shape_d, shape_f = shapes
    taps = shape_f[0]
    rows = shape_f[1] // 2
    count = shape_p[0] // (2 * rows)
    lanes = own_ref.shape[-1]

    def load(ref, z, x, y, start, size):
        slot = lax.bitwise_xor(deep, z)
        return ref[slot, lax.rem(y + row, 2), lax.rem(x + side, 2), start : start + size]

    def both(z, x, y, start, size):
        mine = load(own_ref, z, x, y, start, size)
        others = load(other_ref, z, x, y, start, size)
        return (jnp.where(core == 0, mine, others), jnp.where(core == 0, others, mine))

    lane = lax.broadcasted_iota(jnp.int32, (1, lanes), 1)
    for z in range(ROUNDS):
        for x in range(2):
            wide = 2 * z + x
            halves = [both(z, x, y, 0, taps + count + 1) for y in range(2)]
            for h in range(2):
                joined = jnp.concatenate([halves[0][h], halves[1][h]], axis=-1)
                base = (2 * wide + h) * rows
                refine_ref[:, base : base + rows, :] = joined[:taps]
                base = (2 * wide + h) * rows * count
                proj_ref[base : base + rows * count, :] = joined[taps : taps + count].reshape(
                    rows * count, 2 * lanes
                )
                total = jnp.zeros((rows, lanes), jnp.float32)
                for y in range(2):
                    value = halves[y][h][taps + count].astype(jnp.float32)
                    for c in range(2):
                        start, held = reduce_lanes(shape_r[1], y, c, lanes // 2)
                        moved = pltpu.roll(value, (start - held) % lanes, 1)
                        inside = (lane >= start) & (lane < start + shape_r[1])
                        total = total + jnp.where(inside, moved, 0.0)
                base = (2 * wide + h) * rows
                left = total + pltpu.roll(total, 64, 1)
                wide_ref[base : base + rows, :] = jnp.concatenate([left, total], axis=1).astype(
                    jnp.bfloat16
                )
    height, width = shape_d[1], shape_d[2]
    blocks = width // rows
    for tap in range(taps):
        start = taps + count + 1 + tap * blocks
        pieces = []
        for y in range(2):
            columns = ([], [])
            for z in range(ROUNDS):
                for x in range(2):
                    for c, value in enumerate(both(z, x, y, start, blocks)):
                        columns[c].append(value.reshape(width, lanes))
            for c in range(2):
                joined = jnp.concatenate(columns[c], axis=0).astype(jnp.float32)
                pieces.append(joined.T[:height])
        decode_ref[tap] = jnp.concatenate(pieces, axis=0).astype(jnp.bfloat16)


def unpack_block(own, other, shapes):
    wide = 2 * ROUNDS
    shape_p, shape_r, shape_d, shape_f = shapes
    outs = [
        jax.ShapeDtypeStruct((wide * shape_p[0], 4 * shape_p[1]), jnp.bfloat16),
        jax.ShapeDtypeStruct((wide * shape_r[0], 256), jnp.bfloat16),
        jax.ShapeDtypeStruct((shape_d[0], 4 * shape_d[1], wide * shape_d[2]), jnp.bfloat16),
        jax.ShapeDtypeStruct((shape_f[0], wide * shape_f[1], 4 * shape_f[2]), jnp.bfloat16),
    ]
    return pl.pallas_call(
        functools.partial(unpack_kernel, shapes),
        out_shape=outs,
        in_specs=[pl.BlockSpec(memory_space=pltpu.SMEM)]
        + [pl.BlockSpec(memory_space=pltpu.VMEM)] * 2,
        out_specs=[pl.BlockSpec(memory_space=pltpu.VMEM)] * 4,
        compiler_params=pltpu.CompilerParams(vmem_limit_bytes=VMEM_BYTES),
        cost_estimate=whole_cost(0, [own, other] + outs + outs),
        name="unpack_weights",
    )(kernel_place(), own, other)


def pack_kernel(
    shapes, place_ref, proj_ref, reduce_ref, decode_ref, low_ref, refine_ref, keep_ref, give_ref
):
    deep, side, row, core = (place_ref[index] for index in range(4))
    shape_p, shape_r, shape_d, shape_f = shapes
    taps = shape_f[0]
    rows = shape_f[1] // 2
    count = shape_p[0] // (2 * rows)
    lanes = keep_ref.shape[-1]
    channels = 2 * lanes

    def store(z, x, y, start, size, values):
        values = [value.astype(jnp.bfloat16) for value in values]
        index = (
            lax.rem(x + side, 2),
            lax.rem(y + row, 2),
            lax.bitwise_xor(deep, z),
            pl.ds(start, size),
        )
        keep_ref[index] = jnp.where(core == 0, values[0], values[1])
        give_ref[index] = jnp.where(core == 0, values[1], values[0])

    lane = lax.broadcasted_iota(jnp.int32, (1, lanes), 1)
    reduce = jnp.concatenate(
        [reduce_ref[...], jnp.zeros((lanes - reduce_ref.shape[0], reduce_ref.shape[1]), jnp.float32)]
    ).T
    moved = []
    for y in range(2):
        total = jnp.zeros_like(reduce)
        for c in range(2):
            start, held = reduce_lanes(shape_r[1], y, c, lanes // 2)
            inside = (lane >= held) & (lane < held + shape_r[1])
            total = total + jnp.where(inside, pltpu.roll(reduce, (held - start) % lanes, 1), 0.0)
        moved.append(total)
    for z in range(ROUNDS):
        for x in range(2):
            wide = 2 * z + x
            for y in range(2):
                columns = slice(y * lanes, (y + 1) * lanes)
                for tap in range(taps):
                    line, k = tap // 3, tap % 3
                    left = k * channels + y * lanes
                    values = []
                    for h in range(2):
                        base = (2 * wide + h) * rows
                        values.append(
                            refine_ref[line, base : base + rows, left : left + lanes][None]
                        )
                    store(z, x, y, tap, 1, values)
                values = []
                for h in range(2):
                    base = (2 * wide + h) * rows * count
                    values.append(
                        proj_ref[base : base + rows * count, columns].reshape(count, rows, lanes)
                    )
                store(z, x, y, taps, count, values)
                values = [
                    moved[y][(2 * wide + h) * rows : (2 * wide + h + 1) * rows][None]
                    for h in range(2)
                ]
                store(z, x, y, taps + count, 1, values)
    height, width = shape_d[1], shape_d[2]
    blocks = width // rows
    for tap in range(taps):
        line, k = tap // 3, tap % 3
        columns = slice(k * channels, (k + 1) * channels)
        whole_tap = jnp.concatenate(
            [
                decode_ref[line, :, columns],
                low_ref[line, :, columns],
                jnp.zeros((lanes, channels), jnp.float32),
            ],
            axis=0,
        )
        turned = [whole_tap[n * height : n * height + lanes].T for n in range(4)]
        for z in range(ROUNDS):
            for x in range(2):
                base = (2 * z + x) * width
                for y in range(2):
                    values = [
                        turned[2 * y + c][base : base + width].reshape(blocks, rows, lanes)
                        for c in range(2)
                    ]
                    store(z, x, y, taps + count + 1 + tap * blocks, blocks, values)


def pack_block(proj, reduce, decode, low, refine, shapes, tie):
    shape_p, shape_r, shape_d, shape_f = shapes
    rows = shape_f[1] // 2
    total = shape_f[0] + shape_p[0] // (2 * rows) + 1 + shape_d[0] * shape_d[2] // rows
    out = jax.ShapeDtypeStruct((2, 2, ROUNDS, total, rows, 2 * shape_f[2]), jnp.bfloat16)
    return pl.pallas_call(
        behind_tie(functools.partial(pack_kernel, shapes)),
        out_shape=[out, out],
        in_specs=[pl.BlockSpec(memory_space=pltpu.SMEM), pl.BlockSpec(memory_space=pl.ANY)]
        + [pl.BlockSpec(memory_space=pltpu.VMEM)] * 5,
        out_specs=[pl.BlockSpec(memory_space=pltpu.VMEM)] * 2,
        compiler_params=pltpu.CompilerParams(vmem_limit_bytes=VMEM_BYTES),
        cost_estimate=whole_cost(0, [proj, decode, low, refine, out, out, out]),
        name="pack_gradients",
    )(kernel_place(), tie, proj, reduce, decode, low, refine)


def low_moments_kernel(low_ref, wide_ref, masks_ref, stats_ref):
    reduced = jnp.dot(low_ref[...], wide_ref[...], preferred_element_type=jnp.float32)
    run_moments(reduced, masks_ref[:, 0:1], stats_ref, pl.program_id(0) + 1)


def low_moments(low, wide, masks):
    block = masks.shape[0]
    out = jax.ShapeDtypeStruct((8, wide.shape[1]), jnp.float32)
    return pl.pallas_call(
        low_moments_kernel,
        out_shape=out,
        grid=(low.shape[0] // block,),
        in_specs=[
            pl.BlockSpec((block, low.shape[1]), lambda step: (step, 0)),
            whole(wide),
            whole(masks),
        ],
        out_specs=whole(out),
        compiler_params=pltpu.CompilerParams(vmem_limit_bytes=VMEM_BYTES),
        cost_estimate=whole_cost(2 * low.shape[0] * low.shape[1] * 256, [low]),
        name="low_moments",
    )(low, wide, masks)


def by_tap(values):
    width = values.shape[2] // 3
    split = values.reshape(3, values.shape[1], 3, width)
    return split.transpose(0, 2, 1, 3).reshape(9, values.shape[1], width)


def widen(values):
    padded = jnp.pad(values, ((0, 0), (0, 64 - values.shape[1])))
    return jnp.concatenate([padded, padded, padded, jnp.zeros_like(padded)], axis=1)


def pack_small(items):
    total = sum(item.size for item in items)
    padded = -(-total // 2048) * 2048
    flats = [item.reshape(-1) for item in items]
    return jnp.concatenate(flats + [jnp.zeros((padded - total,), jnp.bfloat16)]).reshape(-1, 128)


def unpack_small(everything, items):
    wide, narrow = everything.shape[:2]
    everything = everything.reshape(wide, narrow, -1)
    pieces = []
    start = 0
    for item in items:
        pieces.append(
            everything[:, :, start : start + item.size].reshape((wide, narrow) + item.shape)
        )
        start += item.size
    proj, reduce, decode, refine = pieces
    proj = proj.transpose(0, 2, 1, 3).reshape(wide * proj.shape[2], -1)
    reduce = reduce.transpose(0, 2, 1, 3).reshape(wide * reduce.shape[2], -1)
    decode = decode.transpose(2, 1, 3, 0, 4).reshape(decode.shape[2], narrow * decode.shape[3], -1)
    refine = refine.transpose(2, 0, 3, 1, 4).reshape(refine.shape[2], wide * refine.shape[3], -1)
    return (proj, widen(reduce), decode, refine)


def pack_grads(reduce, proj, decode, low, refine, shapes):
    wide = lax.axis_size("wide")
    narrow = lax.axis_size("narrow")
    extra = narrow * shapes[1][1]
    reduce = reduce[:extra].T
    decode = jnp.concatenate([by_tap(decode), by_tap(low)[:, :extra]], axis=1)
    refine = by_tap(refine)
    shape_p, shape_r, shape_d, shape_f = shapes
    proj = proj.reshape(wide, shape_p[0], narrow, shape_p[1]).transpose(0, 2, 1, 3)
    reduce = reduce.reshape(wide, shape_r[0], narrow, shape_r[1]).transpose(0, 2, 1, 3)
    decode = decode.reshape(shape_d[0], narrow, shape_d[1], wide, shape_d[2]).transpose(3, 1, 0, 2, 4)
    refine = refine.reshape(shape_f[0], wide, shape_f[1], narrow, shape_f[2]).transpose(1, 3, 0, 2, 4)
    flats = [
        item.astype(jnp.bfloat16).reshape(wide, narrow, -1)
        for item in (proj, reduce, decode, refine)
    ]
    total = sum(item.shape[2] for item in flats)
    padded = -(-total // 2048) * 2048
    flats.append(jnp.zeros((wide, narrow, padded - total), jnp.bfloat16))
    return jnp.concatenate(flats, axis=2).reshape(wide, narrow, -1, 128)


def unpack_grads(owned, shapes):
    owned = owned.reshape(-1)
    pieces = []
    start = 0
    for shape in shapes:
        size = 1
        for extent in shape:
            size *= extent
        pieces.append(owned[start : start + size].reshape(shape))
        start += size
    return pieces


def per_device(
    features,
    low_level,
    widths,
    w_point,
    w_atrous,
    w_proj,
    w_low,
    w_dec1,
    w_dec2,
    w_cls,
    b_cls,
    gains,
    biases,
    low_gain,
    low_bias,
    logit_grad,
):
    canvases = features.shape[0]
    height = features.shape[1]
    columns = features.shape[2]
    fine_columns = low_level.shape[2]
    images = widths.shape[1] - 1
    channels = gains.shape[1]
    images_total = float(canvases * lax.axis_size("wide") * lax.axis_size("narrow") * images)
    small = [w_proj, w_low, w_dec1, w_dec2]
    ids_coarse = band_ids(widths, columns)
    ids_fine = band_ids(4 * widths, fine_columns)
    valid_coarse = (ids_coarse >= 0).astype(jnp.float32)[:, None, :, None]
    valid_fine = (ids_fine >= 0).astype(jnp.float32)[:, None, :, None]
    all_ones = jnp.ones((1, 1, 1), jnp.float32)
    local_count = (height * jnp.sum(widths[:, :images])).astype(jnp.float32)
    member = (ids_coarse[:, :, None] == jnp.arange(images, dtype=jnp.int32)[None, None, :]).astype(
        jnp.float32
    )
    member_low = member.astype(jnp.bfloat16)
    image_sizes = (height * widths[:, :images]).astype(jnp.float32)
    positions = low_level.shape[1] * fine_columns
    low_flat = low_level.reshape(positions, -1)
    extra = low_gain.shape[0]
    side_masks = [tap_mask(ids_fine, STRIP, 0, step) for step in (-1, 1)]
    masks = jnp.concatenate([valid_fine * jnp.ones((1, STRIP, 1, 1))] + side_masks, axis=-1)
    masks = masks.reshape(STRIP * fine_columns, 3)
    coarse_shape = (height, columns, channels)
    mask_column = jnp.broadcast_to(valid_coarse, (1, height, columns, 1)).reshape(-1, 1)
    member_wide = jnp.pad(member[0], ((0, 0), (0, 8 - images)))
    member_rows = jnp.tile(member_wide, (height, 1))
    sizes_inverse = jnp.pad(1.0 / image_sizes[0], (0, 8 - images)).reshape(8, 1)
    pool_inputs = (member_rows.T.astype(jnp.bfloat16), sizes_inverse)

    def all_sides():
        sides = [
            [
                item.reshape(height * columns, -1)
                for item in side_values(features, ids_coarse, dilation)
            ]
            for dilation in dilations
        ]
        return (sides, logit_grad.reshape(-1, logit_grad.shape[-1]))

    def low_part(proj, wide, decode, refine):
        return low_moments(low_flat, wide, masks)

    def forward(part, ready, pair, before, tie=None):
        sums, stats, pooling = ({}, {}, ()) if before is None else before
        more, more_stats, more_pooling = coarse_forward(
            part,
            mask_column,
            ready[0],
            pair,
            coarse_shape,
            sums,
            pool_inputs if GATHER.has_point(part) else None,
            tie,
        )
        return ({**sums, **more}, {**stats, **more_stats}, tuple(pooling) + tuple(more_pooling))

    parts, unpacked, ready, low_stats, coarse = gather_taps(
        GATHER.order(w_point, w_atrous),
        small,
        [all_sides, low_part],
        [functools.partial(forward, part) for part in range(len(GATHER.parts))],
    )
    proj_full, low_wide, decode_full, refine_full = unpacked
    sides, grad_flat = ready
    sums, stats, pool_results = coarse
    point_z, point_stats, pool_z, pooled = pool_results
    pool_z = pool_z[None, :images]
    coarse_stats = [point_stats, stats[0], stats[1], stats[2]]
    coarse_z = [
        item.reshape(1, height, columns, channels) for item in (point_z, sums[0], sums[1], sums[2])
    ]
    blocks = [(item_z, valid_coarse) for item_z in coarse_z] + [(pool_z, all_ones)]
    local_images = float(canvases * images)
    states = [(item[0], item[1]) for item in coarse_stats] + [
        local_moments(pool_z, all_ones, local_images),
    ]
    own = [state[item] for item in range(2) for state in states]
    rows = from_all(jnp.concatenate(own + [jnp.full((1,), 1.0) * local_count]))
    width = 5 * channels
    pixels = rows[:, 2 * width :]
    count_rows = jnp.concatenate(
        [
            jnp.broadcast_to(pixels, (rows.shape[0], 4 * channels)),
            jnp.full((rows.shape[0], channels), local_images),
        ],
        axis=1,
    )
    counts_flat, means_flat, squares_flat = merge_rows(
        count_rows, rows[:, :width], rows[:, width : 2 * width]
    )
    vars_flat = squares_flat / counts_flat
    section_means = []
    section_vars = []
    offset = 0
    for width in [channels] * 5:
        section_means.append(means_flat[offset : offset + width])
        section_vars.append(vars_flat[offset : offset + width])
        offset += width
    pixel_count = counts_flat[0]
    fine_count = 16.0 * pixel_count
    gain_rows = [gains[0], gains[1], gains[2], gains[3], gains[4], low_gain]
    bias_rows = [biases[0], biases[1], biases[2], biases[3], biases[4], low_bias]
    kept = []
    activations = []
    for index in range(5):
        block_values, block_valid = blocks[index]
        result = normalize(
            block_values,
            block_valid,
            section_means[index],
            section_vars[index],
            gain_rows[index],
            bias_rows[index],
        )
        kept.append(result[1:])
        activations.append(result[0].astype(jnp.bfloat16))
    spread = jnp.einsum(
        "nwk,nkd->nwd", member_low, activations[4], preferred_element_type=jnp.float32
    ).astype(jnp.bfloat16)
    spread = jnp.broadcast_to(spread[:, None], (canvases, height, columns, channels))
    joined_coarse = jnp.concatenate(activations[:4] + [spread], axis=-1)
    proj_z = jnp.einsum(
        "nhwc,cd->nhwd", joined_coarse, proj_full, preferred_element_type=jnp.float32
    )
    proj_moments = local_moments(proj_z, valid_coarse, local_count)
    joint_mean, joint_var = merged(
        jnp.stack(
            [
                jnp.concatenate([proj_moments[0], low_stats[0, :extra]]),
                jnp.concatenate([proj_moments[1], low_stats[1, :extra] / 16.0]),
            ]
        ),
        local_count,
        pixel_count,
    )
    proj_mean, low_mean = joint_mean[:channels], joint_mean[channels:]
    proj_var, low_var = joint_var[:channels], joint_var[channels:]
    proj_act, proj_centered, proj_shaped, proj_scale = normalize(
        proj_z, valid_coarse, proj_mean, proj_var, gains[5], biases[5]
    )
    proj_act = proj_act.astype(jnp.bfloat16).astype(jnp.float32)
    cols_table = column_table(ids_coarse)[0].astype(jnp.bfloat16)
    low_vectors = widen(norm_vectors(low_mean, low_var, low_gain, low_bias))
    devices = device_count()
    decode_params = jnp.stack([gains[6], biases[6]])
    refine_params = jnp.stack([gains[7], biases[7]])
    decode_z, rows, upsampled = decode_forward(
        proj_act[0],
        jnp.concatenate([cols_table, cols_table], axis=1),
        low_flat,
        low_wide,
        low_vectors,
        masks,
        decode_full,
        devices,
    )
    decode_rows = hand_out(rows)
    refine_z, rows = refine_forward(decode_z, decode_rows, decode_params, masks, refine_full)
    refine_rows = hand_out(rows)
    logits, rows = classify(
        refine_z, grad_flat, refine_rows, refine_params, masks, w_cls, b_cls.reshape(1, -1)
    )
    logits = logits.reshape(logit_grad.shape)
    refine_sums = hand_out(rows)
    decode_local, rows, refine_totals, refine_kernel_grad = refine_backward(
        refine_z,
        grad_flat,
        refine_rows,
        refine_sums,
        refine_params,
        w_cls,
        decode_z,
        decode_rows,
        decode_params,
        masks,
        refine_full,
    )
    decode_sums = hand_out(rows)
    classes = w_cls.shape[1]
    cls_weight_grad = decode_sums[:classes, 2 * channels :].T
    cls_bias_grad = decode_sums[classes, 2 * channels : 2 * channels + classes]
    refine_gain, refine_bias = refine_totals[6], refine_totals[7]
    (
        proj_up,
        reduce_local,
        reduce_sums,
        decode_totals,
        decode_kernel_grad,
        low_kernel_grad,
    ) = decode_backward(
        decode_local,
        decode_z,
        decode_rows,
        decode_sums,
        decode_params,
        upsampled,
        low_flat,
        low_wide,
        low_vectors,
        jnp.concatenate([cols_table.T, cols_table.T], axis=1),
        masks,
        decode_full,
        coarse_shape,
    )
    decode_gain, decode_bias = decode_totals[6], decode_totals[7]
    proj_up = proj_up[None]
    reduce_gain, reduce_bias = reduce_sums[0, :extra], reduce_sums[1, :extra]

    proj_local, proj_gain, proj_bias = norm_grad_terms(
        proj_up, valid_coarse, proj_centered, proj_shaped
    )
    summed_pairs = gradient_sums([(proj_gain, proj_bias), (reduce_gain, reduce_bias)])
    proj_gain, proj_bias = summed_pairs[0]
    reduce_gain, reduce_bias = summed_pairs[1]
    proj_dz = norm_grad_finish(
        proj_local,
        valid_coarse,
        proj_centered,
        proj_scale,
        gains[5],
        proj_gain,
        proj_bias,
        pixel_count,
    )
    proj_kernel_grad = jnp.einsum(
        "nhwc,nhwd->cd", joined_coarse, proj_dz, preferred_element_type=jnp.float32
    )
    concat_grad = jnp.einsum(
        "nhwd,cd->nhwc", proj_dz, proj_full, preferred_element_type=jnp.float32
    )
    branch_terms = []
    for index in range(4):
        upstream = concat_grad[..., index * channels : (index + 1) * channels]
        branch_terms.append(norm_grad_terms(upstream, valid_coarse, kept[index][0], kept[index][1]))
    pool_up = jnp.einsum(
        "nhwd,nwk->nkd", concat_grad[..., 4 * channels :], member, precision=highest
    )
    branch_terms.append(norm_grad_terms(pool_up, all_ones, kept[4][0], kept[4][1]))
    local_pairs = [(term_item[1], term_item[2]) for term_item in branch_terms]
    last_pairs = gradient_sums(local_pairs)
    valid_list = [valid_coarse, valid_coarse, valid_coarse, valid_coarse, all_ones]
    count_list = [pixel_count, pixel_count, pixel_count, pixel_count, images_total]
    branch_dz = [
        norm_grad_finish(
            branch_terms[index][0],
            valid_list[index],
            kept[index][0],
            kept[index][2],
            gains[index],
            last_pairs[index][0],
            last_pairs[index][1],
            count_list[index],
        )
        for index in range(5)
    ]
    flat_dz = [item.reshape(height * columns, channels) for item in branch_dz[:4]]
    pool_dz = jnp.pad(branch_dz[4][0], ((0, 8 - images), (0, 0)))
    low_vectors = widen(
        norm_vectors(
            low_mean,
            low_var,
            low_gain,
            low_bias,
            reduce_gain / fine_count,
            reduce_bias / fine_count,
        )
    )

    def low_late(tie):
        return low_backward(reduce_local, low_flat, low_wide, low_vectors, masks, tie)

    def input_late(tie):
        side_dz = [
            side_grads(branch_dz[branch + 1], ids_coarse, dilations[branch]).reshape(
                height * columns, -1
            )
            for branch in range(3)
        ]
        return coarse_input(
            flat_dz[0],
            pool_dz,
            member_rows * sizes_inverse.reshape(1, 8),
            side_dz,
            parts,
            coarse_shape,
            features.shape[3],
            tie,
        )

    def weight_part(part, grads, tie=None):
        return coarse_weight(
            part,
            sides,
            grads[1:4],
            coarse_shape,
            (grads[0], pooled, grads[4]) if SCATTER.has_point(part) else None,
            tie,
        )

    owned, small_owned, low_level_grad, features_grad = scatter_taps(
        flat_dz + [pool_dz],
        [item.shape for item in small],
        [functools.partial(weight_part, part) for part in range(len(SCATTER.parts))],
        (proj_kernel_grad, decode_kernel_grad, low_kernel_grad, refine_kernel_grad),
        [low_late, input_late],
    )
    low_level_grad = low_level_grad.reshape(low_level.shape)
    features_grad = features_grad.reshape(features.shape)
    proj_owned, reduce_owned, decode_owned, refine_owned = small_owned
    point_owned, atrous_owned = SCATTER.restore(owned, w_atrous.shape)
    gains_grad = jnp.stack(
        [
            last_pairs[0][0],
            last_pairs[1][0],
            last_pairs[2][0],
            last_pairs[3][0],
            last_pairs[4][0],
            proj_gain,
            decode_gain,
            refine_gain,
        ]
    )
    biases_grad = jnp.stack(
        [
            last_pairs[0][1],
            last_pairs[1][1],
            last_pairs[2][1],
            last_pairs[3][1],
            last_pairs[4][1],
            proj_bias,
            decode_bias,
            refine_bias,
        ]
    )
    return (
        logits,
        features_grad,
        low_level_grad,
        point_owned,
        atrous_owned,
        proj_owned,
        reduce_owned,
        decode_owned,
        refine_owned,
        cls_weight_grad,
        cls_bias_grad,
        gains_grad,
        biases_grad,
        reduce_gain,
        reduce_bias,
    )


def solution(mesh):
    in_specs = (
        P(("wide", "narrow"), None, None, None),
        P(("wide", "narrow"), None, None, None),
        P(("wide", "narrow"), None),
        P(None, "wide", "narrow"),
        P(None, None, "wide", "narrow"),
        P("wide", "narrow"),
        P("wide", "narrow"),
        P(None, "narrow", "wide"),
        P(None, "wide", "narrow"),
        P(),
        P(),
        P(),
        P(),
        P(),
        P(),
        P(("wide", "narrow"), None, None, None),
    )
    out_specs = (
        P(("wide", "narrow"), None, None, None),
        P(("wide", "narrow"), None, None, None),
        P(("wide", "narrow"), None, None, None),
        P(None, "wide", "narrow"),
        P(None, None, "wide", "narrow"),
        P("wide", "narrow"),
        P("wide", "narrow"),
        P(None, "narrow", "wide"),
        P(None, "wide", "narrow"),
        P(),
        P(),
        P(),
        P(),
        P(),
        P(),
    )
    return jax.shard_map(
        per_device, mesh=mesh, in_specs=in_specs, out_specs=out_specs, check_vma=False
    )
```

```python
import functools

import jax
import jax.numpy as jnp
from jax import lax
from jax.experimental import pallas as pl
from jax.experimental.pallas import tpu as pltpu
from jax.sharding import PartitionSpec as P

epsilon = 1e-05
highest = lax.Precision.HIGHEST
dilations = (6, 12, 18)
ROUNDS = 4
VMEM_BYTES = 48 * 1024 * 1024


class Layout:
    def __init__(self, chunks, point_chunk):
        self.chunks = chunks
        self.point_chunk = point_chunk
        self.parts = [(index, index + 1) for index in range(0, len(chunks), 2)]
        self.sizes = [[chunks[index] for index in part] for part in self.parts]
        places = []
        for chunk, size in enumerate(chunks):
            places += [(chunk, tap) for tap in range(2 if chunk == point_chunk else 0, size)]
        self.rows = [
            [(line,) + places[9 * branch + 3 * line] for line in range(3)] for branch in range(3)
        ]

    def part_of(self, chunk):
        return chunk // 2

    def place(self, chunk, tap):
        return tap + (self.chunks[chunk - 1] if chunk % 2 else 0)

    def part_rows(self, part):
        return [
            (branch, line, chunk, tap)
            for branch, rows in enumerate(self.rows)
            for line, chunk, tap in rows
            if chunk in self.parts[part]
        ]

    def has_point(self, part):
        return self.point_chunk in self.parts[part]

    def order(self, point, atrous):
        flat = atrous.reshape((-1,) + atrous.shape[2:])
        before = sum(self.chunks[: self.point_chunk])
        parts = []
        start = 0
        for part, sizes in enumerate(self.sizes):
            size = sum(sizes)
            if self.has_point(part):
                pieces = [flat[start:before], point, flat[before : start + size - 2]]
                parts.append(jnp.concatenate([item for item in pieces if item.shape[0]]))
                start += size - 2
            else:
                parts.append(flat[start : start + size])
                start += size
        return parts

    def restore(self, parts, shape):
        flat = jnp.concatenate(parts)
        before = sum(self.chunks[: self.point_chunk])
        atrous = jnp.concatenate([flat[:before], flat[before + 2 :]])
        return (flat[before : before + 2], atrous.reshape(shape))


GATHER = Layout((5, 6, 6, 3, 3, 6), 0)
SCATTER = Layout((3, 3, 5, 6, 6, 6), 2)


def exchange(values, axis, bit):
    size = lax.axis_size(axis)
    return lax.ppermute(values, axis, [(place, place ^ bit) for place in range(size)])


def rotate(values, axis, step, stride):
    size = lax.axis_size(axis)
    rounds = size // stride
    pairs = []
    for place in range(size):
        outer, inner = place // stride, place % stride
        pairs.append((place, ((outer + step) % rounds) * stride + inner))
    return lax.ppermute(values, axis, pairs)


def device_count():
    return lax.axis_size("wide") * lax.axis_size("narrow")


def hand_out(rows):
    return lax.all_to_all(rows, ("wide", "narrow"), 0, 0, tiled=True)


def from_all(values):
    return hand_out(jnp.broadcast_to(values[None], (device_count(),) + values.shape))


def merge_rows(counts, means, squares):
    total = jnp.sum(counts, axis=0)
    mean = jnp.sum(counts * means, axis=0) / total
    gap = means - mean[None]
    return (total, mean, jnp.sum(squares + counts * gap * gap, axis=0))


def local_moments(values, valid_map, count):
    axes = tuple(range(values.ndim - 1))
    mean = jnp.sum(values * valid_map, axis=axes) / count
    centered = values - mean
    return (mean, jnp.sum(centered * centered * valid_map, axis=axes))


def place():
    wide = lax.axis_index("wide")
    narrow = lax.axis_index("narrow")
    return (wide // 2, wide % 2, narrow // 2, narrow % 2)


def share_core(shard):
    core = place()[3]
    half = shard.shape[1] // 2
    parts = shard.reshape(shard.shape[0], 2, half, shard.shape[2])
    kept = lax.dynamic_index_in_dim(parts, core, 1, keepdims=False)
    given = lax.dynamic_index_in_dim(parts, 1 - core, 1, keepdims=False)
    got = exchange(given, "narrow", 1)
    lower = jnp.where(core == 0, kept, got)
    upper = jnp.where(core == 0, got, kept)
    return jnp.concatenate([lower, upper], axis=2)


def tuned():
    return lax.axis_size("wide") == 2 * ROUNDS and lax.axis_size("narrow") == 4


def kernel_place():
    values = jnp.stack(place()).astype(jnp.int32)
    return values if tuned() else jnp.zeros_like(values)


def tied(values, earlier):
    mark = earlier[(0,) * earlier.ndim]
    return jnp.where(mark == mark, values, jnp.zeros_like(values))


def one_step(body, outs, args, specs=None, tie=None, vmem=32 * 1024 * 1024):
    def whole_spec(array):
        return pl.BlockSpec(array.shape, lambda step: (0,) * len(array.shape))

    specs = list(specs or [None] * len(args))
    run = body
    if tie is not None:
        ties = tie if isinstance(tie, list) else [tie]
        args = ties + list(args)
        specs = [pl.BlockSpec(memory_space=pl.ANY)] * len(ties) + specs

        def run(*refs):
            body(*refs[len(ties) :])

    return pl.pallas_call(
        run,
        out_shape=outs,
        grid=(1,),
        in_specs=[spec or whole_spec(arg) for spec, arg in zip(specs, args)],
        out_specs=[whole_spec(out) for out in outs],
        compiler_params=pltpu.CompilerParams(vmem_limit_bytes=vmem),
        cost_estimate=cost(0, args),
        name="move",
    )(*args)


def entry_spec(array, index):
    block = (1,) + array.shape[1:]
    return pl.BlockSpec(block, lambda step: (index,) + (0,) * (len(block) - 1))


def cut(sizes):
    return [slice(sum(sizes[:index]), sum(sizes[: index + 1])) for index in range(len(sizes))]


def pass_on(values, tie):
    def body(source, target):
        target[...] = source[...]

    outs = [jax.ShapeDtypeStruct(values.shape, values.dtype)]
    return one_step(body, outs, [values], None, tie)[0]


def gather_depth(values):
    return [exchange(values, "wide", 2 * flip) for flip in range(1, ROUNDS)]


def lay_out(sizes, own, others, tie=None):
    shape = own.shape[1:]
    outs = [jax.ShapeDtypeStruct((ROUNDS, size) + shape, own.dtype) for size in sizes]

    def body(*refs):
        for target, taps in zip(refs[ROUNDS:], cut(sizes)):
            for slot, source in enumerate(refs[:ROUNDS]):
                target[slot] = source[taps]

    return one_step(body, outs, [own] + list(others), tie=tie)


def pair_up(values, others, tie=None):
    outs = [jax.ShapeDtypeStruct((2,) + item.shape, item.dtype) for item in values]
    count = len(outs)

    def body(*refs):
        for index in range(count):
            refs[2 * count + index][0] = refs[index][...]
            refs[2 * count + index][1] = refs[count + index][...]

    return one_step(body, outs, list(values) + list(others), tie=tie)


def pair_cut(sizes, values, others, tie=None):
    count = len(values)
    outs = [
        jax.ShapeDtypeStruct((2, ROUNDS, size) + values[0].shape[2:], values[0].dtype)
        for part in sizes
        for size in part
    ]

    def body(*refs):
        for index in range(count):
            taps = cut([part[index] for part in sizes])
            for part in range(len(sizes)):
                target = refs[2 * count + part * count + index]
                for half in range(2):
                    target[half] = refs[half * count + index][:, taps[part]]

    results = one_step(body, outs, list(values) + list(others), tie=tie)
    return [results[part * count : (part + 1) * count] for part in range(len(sizes))]


def pair_all(values, others, tie=None):
    count = len(values)
    shape = values[0].shape
    sizes = [item.shape[2] for item in values]
    outs = [jax.ShapeDtypeStruct((2,) + shape[:2] + (sum(sizes),) + shape[3:], values[0].dtype)]

    def body(*refs):
        target = refs[2 * count]
        for index, taps in enumerate(cut(sizes)):
            target[0, :, :, taps] = refs[index][...]
            target[1, :, :, taps] = refs[count + index][...]

    return one_step(body, outs, list(values) + list(others), tie=tie)[0]


def first_sums(sizes, keep, got, tie=None):
    tail = keep.shape[4:]
    outs = [jax.ShapeDtypeStruct((2, ROUNDS, size) + tail, jnp.bfloat16) for size in sizes]

    def body(keep_ref, got_ref, *targets):
        for target, taps in zip(targets, cut(sizes)):
            total = keep_ref[0, :, :, taps].astype(jnp.float32)
            total = total + got_ref[0, :, :, taps].astype(jnp.float32)
            target[...] = total.astype(jnp.bfloat16)

    return one_step(body, outs, [keep, got], [entry_spec(keep, 1), entry_spec(got, 1)], tie)


def second_sums(sizes, keep, got, values, tie=None):
    tail = keep.shape[4:]
    outs = [jax.ShapeDtypeStruct((ROUNDS, sum(sizes)) + tail, jnp.float32)]
    outs += [jax.ShapeDtypeStruct((ROUNDS, size) + tail, jnp.bfloat16) for size in sizes]
    count = len(sizes)

    def body(keep_ref, got_ref, *refs):
        kept = refs[count]
        for index, taps in enumerate(cut(sizes)):
            for half in range(2):
                total = keep_ref[0, half, :, taps].astype(jnp.float32)
                total = total + got_ref[0, half, :, taps].astype(jnp.float32)
                total = total + refs[index][half].astype(jnp.float32)
                if half:
                    refs[count + 1 + index][...] = total.astype(jnp.bfloat16)
                else:
                    kept[:, taps] = total

    specs = [entry_spec(keep, 0), entry_spec(got, 0)] + [None] * count
    results = one_step(body, outs, [keep, got] + list(values), specs, tie)
    return (results[0], results[1:])


def deep_sums(sizes, kept, values, tie=None):
    shape = (2,) + kept.shape[1:]
    outs = [jax.ShapeDtypeStruct(shape, dtype) for dtype in (jnp.float32, jnp.bfloat16)]
    count = len(sizes)

    def body(kept_ref, *refs):
        for slot in range(ROUNDS):
            target = refs[count + slot // 2]
            for value, taps in zip(refs, cut(sizes)):
                total = kept_ref[slot, taps] + value[slot].astype(jnp.float32)
                target[slot % 2, taps] = total.astype(target.dtype)

    return one_step(body, outs, [kept] + list(values), None, tie)


def near_sums(kept, far, tie=None):
    shape = kept.shape[1:]
    outs = [jax.ShapeDtypeStruct(shape, dtype) for dtype in (jnp.float32, jnp.bfloat16)]

    def body(kept_ref, far_ref, *targets):
        for slot, target in enumerate(targets):
            total = kept_ref[slot] + far_ref[slot].astype(jnp.float32)
            target[...] = total.astype(target.dtype)

    return one_step(body, outs, [kept, far], None, tie)


def last_sums(kept, near, tie=None):
    def body(kept_ref, near_ref, target):
        target[...] = kept_ref[...] + near_ref[...].astype(jnp.float32)

    outs = [jax.ShapeDtypeStruct(kept.shape, jnp.float32)]
    return one_step(body, outs, [kept, near], None, tie)[0]


def chunk_order(index):
    return [("wide", 1), ("narrow", 2)] if index % 2 == 0 else [("narrow", 2), ("wide", 1)]


def gather_taps(weights, small, fillers, kernels, prepared):
    rounds = ROUNDS
    sizes = GATHER.sizes
    shapes = [item.shape for item in small]
    if not tuned():
        parts = []
        for part, values in zip(GATHER.parts, weights):
            full = lax.all_gather(values, "narrow", axis=2, tiled=True)
            full = lax.all_gather(full, "wide", axis=1, tiled=True)
            rows = full.shape[1] // (4 * rounds)
            full = full.reshape(full.shape[0], rounds, 2, 2, rows, 2, full.shape[2] // 2)
            start = 0
            pieces = []
            for index in part:
                piece = full[start : start + GATHER.chunks[index]]
                start += GATHER.chunks[index]
                order = (3, 5, 2, 1, 0, 4, 6) if index % 2 == 0 else (3, 2, 5, 1, 0, 4, 6)
                pieces.append(piece.transpose(order))
            joined = jnp.concatenate(pieces, axis=4)
            parts.append((joined[0], joined[1]))
        flat = pack_small(small)
        everything = lax.all_gather(flat, ("wide", "narrow"))
        everything = everything.reshape(lax.axis_size("wide"), lax.axis_size("narrow"), -1)
        unpacked = unpack_small(everything, small)
        ready = fillers[0]()
        results = fillers[1](*unpacked)
        result = None
        for pair, kernel in zip(parts, kernels):
            result = kernel(ready, pair, result)
        return (parts, unpacked, ready, results, result)

    def along(part, stacks, turn):
        return [
            exchange(stack, *chunk_order(index)[turn]) for stack, index in zip(stacks, GATHER.parts[part])
        ]

    def across(values):
        return (values, exchange(values, "narrow", 1))

    first, second = sizes[1], sizes[2]
    weights = [
        weights[0],
        jnp.concatenate(
            [
                weights[1][: first[0]],
                weights[2][: second[0]],
                weights[1][first[0] :],
                weights[2][second[0] :],
            ]
        ),
    ]
    joint = [first[0] + second[0], first[1] + second[1]]
    shared = [share_core(values) for values in weights]
    z0 = gather_depth(shared[0])
    small = small_block(small)
    xs = exchange(small, "wide", 1)
    small = pair_up([small], [xs], shared[1])[0]
    ys = exchange(small, "narrow", 2)
    small = pair_up([small], [ys])[0]
    s0 = lay_out(sizes[0], shared[0], z0, small)
    f0 = along(0, s0, 0)
    z1 = gather_depth(shared[1])
    s0 = pair_up(s0, f0, [z1[1]] + prepared)
    g0 = along(0, s0, 1)
    ready = fillers[0]()
    s1 = lay_out(joint, shared[1], z1, s0[0])
    f1 = along(0, s1, 0)
    small = pass_on(small, s1[0])
    zs = gather_depth(small)
    p0 = across(pair_all(s0, g0, s1[0]))
    s1, s2 = pair_cut([first, second], s1, f1, zs[0])
    g1 = along(0, s1, 1)
    g2 = along(0, s2, 1)
    result = kernels[0](ready, p0, None, s1[0])
    small = lay_out([2], small, zs, result[0][0])[0]
    cs = exchange(small, "narrow", 1)
    p1 = across(pair_all(s1, g1, small))
    unpacked = unpack_block(small, cs, shapes=shapes)
    results = fillers[1](*unpacked)
    result = kernels[1](ready, p1, result)
    p2 = across(pair_all(s2, g2, p1[0]))
    result = kernels[2](ready, p2, result)
    return ([p0, p1, p2], unpacked, ready, results, result)


def scatter_taps(grads, shapes, kernels, pack, fillers):
    rounds = ROUNDS
    if not tuned():
        owned = []
        for part, kernel in zip(SCATTER.parts, kernels):
            joined = jnp.stack(kernel(grads))
            pieces = []
            for index, taps in zip(part, cut([SCATTER.chunks[index] for index in part])):
                piece = joined[:, :, :, :, taps]
                order = (4, 3, 1, 0, 5, 2, 6) if index % 2 == 0 else (4, 3, 2, 0, 5, 1, 6)
                piece = piece.transpose(order)
                pieces.append(piece.reshape(piece.shape[0], -1, 2 * piece.shape[6]))
            full = jnp.concatenate(pieces)
            full = lax.psum_scatter(full, "wide", scatter_dimension=1, tiled=True)
            full = lax.psum_scatter(full, "narrow", scatter_dimension=2, tiled=True)
            owned.append(full.astype(jnp.float32))
        low, low_weight = fillers[0](grads[0])
        small = pack_grads(low_weight, *pack, shapes)
        small = lax.psum_scatter(small, "wide", scatter_dimension=0, tiled=True)
        small = lax.psum_scatter(small, "narrow", scatter_dimension=1, tiled=True)
        small = unpack_grads(small[0, 0].astype(jnp.float32), shapes)
        return (owned, small, low, fillers[1](None))

    sizes = SCATTER.sizes

    def across(pair):
        return (pair[0], exchange(pair[1], "narrow", 1))

    def along(indices, values, turn):
        return [
            exchange(value, *chunk_order(index)[turn]) for value, index in zip(values, indices)
        ]

    def far(sent):
        return exchange(sent, "wide", 4)

    def near(sent):
        return exchange(sent, "wide", 2)

    a, b, c = 2, 1, 0
    pair_a = across(kernels[a](grads))
    pair_b = across(kernels[b](grads, tie=pair_a[0]))
    sent = first_sums(sizes[a], *pair_a, pair_b[0])
    first_a = along(SCATTER.parts[a], sent, 0)
    low, low_weight = fillers[0](sent[0])
    pair_s = across(pack_block(pack[0], low_weight, *pack[1:], shapes=shapes, tie=low_weight))
    sizes_s = [pair_s[0].shape[3]]
    pair_c = across(kernels[c](grads, tie=pair_s[0]))
    kept_a, sent = second_sums(sizes[a], *pair_a, first_a, pair_c[0])
    second_a = along(SCATTER.parts[a], sent, 1)
    sent = first_sums(sizes[b], *pair_b, sent[0])
    first_b = along(SCATTER.parts[b], sent, 0)
    kept_a, sent = deep_sums(sizes[a], kept_a, second_a, sent[0])
    far_a = far(sent)
    sent = first_sums(sizes_s, *pair_s, sent)
    first_s = along((0,), sent, 0)
    filled = fillers[1](sent[0])
    kept_b, sent = second_sums(sizes[b], *pair_b, first_b, filled)
    second_b = along(SCATTER.parts[b], sent, 1)
    sent = first_sums(sizes[c], *pair_c, sent[0])
    first_c = along(SCATTER.parts[c], sent, 0)
    kept_s, sent = second_sums(sizes_s, *pair_s, first_s, sent[0])
    second_s = along((0,), sent, 1)
    total_a, sent = near_sums(kept_a, far_a, sent[0])
    near_a = near(sent)
    kept_b, sent = deep_sums(sizes[b], kept_b, second_b, sent)
    far_b = far(sent)
    kept_c, sent = second_sums(sizes[c], *pair_c, first_c, sent)
    second_c = along(SCATTER.parts[c], sent, 1)
    kept_s, sent = deep_sums(sizes_s, kept_s, second_s, sent[0])
    far_s = far(sent)
    total_a = last_sums(total_a, near_a, sent)
    kept_c, sent = deep_sums(sizes[c], kept_c, second_c, total_a)
    far_c = far(sent)
    total_b, sent = near_sums(kept_b, far_b, sent)
    near_b = near(sent)
    total_s, sent = near_sums(kept_s, far_s, sent)
    near_s = near(sent)
    total_c, sent = near_sums(kept_c, far_c, sent)
    near_c = near(sent)
    total_b = last_sums(total_b, near_b, sent)
    total_s = last_sums(total_s, near_s, total_b)
    total_c = last_sums(total_c, near_c, total_s)
    owned = [settle_core(total) for total in (total_c, total_b, total_a)]
    small = settle_small(total_s, shapes)
    return (owned, small, low, filled)


def row_span(dilation, row, height):
    step = (row - 1) * dilation
    return (max(step, 0), max(-step, 0), height - abs(step))


def tap_matrix(pair, chunk, tap, place_ref):
    row, core = place_ref[2], place_ref[3]
    flip = lax.rem(pl.program_id(0) + place_ref[1], 2)
    place = GATHER.place(chunk, tap)

    def half(ref):
        if chunk % 2 == 0:
            sides = [ref[y, flip, 0, place] for y in (row, 1 - row)]
        else:
            sides = [ref[flip, y, 0, place] for y in (row, 1 - row)]
        return jnp.concatenate(sides, axis=1)

    mine = half(pair[0])
    other = half(pair[1])
    lower = jnp.where(core == 0, mine, other)
    upper = jnp.where(core == 0, other, mine)
    return jnp.concatenate([lower, upper], axis=0)


def part_spec(array):
    def index_map(step, place_ref):
        return (0, 0, lax.bitwise_xor(step // 2, place_ref[0]), 0, 0, 0)

    return pl.BlockSpec((2, 2, 1) + array.shape[3:], index_map)


def whole_cost(flops, arrays):
    total = 0
    for array in arrays:
        size = array.dtype.itemsize
        for extent in array.shape:
            size *= extent
        total += size
    return pl.CostEstimate(flops=int(flops), bytes_accessed=total, transcendentals=0)


def cost(flops, arrays):
    return pl.CostEstimate(flops=1, bytes_accessed=1, transcendentals=0)


def coarse_flops(rows, shape, width):
    height, columns, channels = shape
    extents = sum(row_span(dilations[branch], line, height)[2] for branch, line in rows)
    return 2 * 3 * extents * columns * channels * width


def full_spec(array):
    return pl.BlockSpec(array.shape, lambda step, place_ref: (0,) * array.ndim)


def lane_spec(array):
    return pl.BlockSpec(
        (array.shape[0], array.shape[1] // (2 * ROUNDS)), lambda step, place_ref: (0, step)
    )


def store_moments(z_ref, mask_ref, stats_ref):
    mask = mask_ref[...]
    count = jnp.sum(mask)
    values = z_ref[...]
    mean = jnp.sum(values * mask, axis=0, keepdims=True) / count
    centered = (values - mean) * mask
    stats_ref[0:1, :] = mean
    stats_ref[1:2, :] = jnp.sum(centered * centered, axis=0, keepdims=True)


def behind_tie(kernel):
    def run(place_ref, tie_ref, *refs):
        kernel(place_ref, *refs)

    return run


def coarse_forward_kernel(plan, place_ref, *refs):
    refs = list(refs)
    mask_ref = refs.pop(0)
    center = refs.pop(0)
    outer = {branch: (refs.pop(0), refs.pop(0)) for branch in plan["branches"]}
    before = {branch: refs.pop(0) for branch in plan["begun"]}
    if plan["pool"]:
        member_ref = refs.pop(0)
        sizes_ref = refs.pop(0)
    pair = (refs.pop(0), refs.pop(0))
    results = {branch: refs.pop(0) for branch in plan["branches"]}
    stats = {branch: refs.pop(0) for branch in plan["done"]}
    step = pl.program_id(0)

    @pl.when(step == 0)
    def _():
        for branch in plan["branches"]:
            if branch in before:
                results[branch][...] = before[branch][...]
            else:
                results[branch][...] = jnp.zeros_like(results[branch])

    columns = plan["columns"]
    for branch, row, chunk, tap in plan["rows"]:
        source, target, extent = row_span(dilations[branch], row, plan["height"])
        matrix = jnp.concatenate(
            [tap_matrix(pair, chunk, tap + k, place_ref) for k in range(3)],
            axis=0,
        )
        rows_in = pl.ds(source * columns, extent * columns)
        rows_out = pl.ds(target * columns, extent * columns)
        sides = (outer[branch][0], center, outer[branch][1])
        values = jnp.concatenate([side[rows_in, :] for side in sides], axis=1)
        results[branch][rows_out, :] += jnp.dot(
            values, matrix, preferred_element_type=jnp.float32
        )
    if plan["pool"]:
        point_ref, point_stats_ref, pool_ref, pooled_ref = refs

        @pl.when(step == 0)
        def _():
            point_ref[...] = jnp.zeros_like(point_ref)
            pool_ref[...] = jnp.zeros_like(pool_ref)

        values = center[...]
        point_ref[...] += jnp.dot(
            values, tap_matrix(pair, GATHER.point_chunk, 0, place_ref), preferred_element_type=jnp.float32
        )
        pooled = jnp.dot(member_ref[...], values, preferred_element_type=jnp.float32)
        pooled = (pooled * sizes_ref[...]).astype(jnp.bfloat16)
        pooled_ref[...] = pooled
        pool_ref[...] += jnp.dot(
            pooled, tap_matrix(pair, GATHER.point_chunk, 1, place_ref), preferred_element_type=jnp.float32
        )

    @pl.when(step == 2 * ROUNDS - 1)
    def _():
        for branch in plan["done"]:
            store_moments(results[branch], mask_ref, stats[branch])
        if plan["pool"]:
            store_moments(point_ref, mask_ref, point_stats_ref)


def coarse_forward(part, mask, sides, pair, shape, begun, pool=None, tie=None):
    height, columns, channels = shape
    positions = height * columns
    rows = GATHER.part_rows(part)
    branches = sorted({row[0] for row in rows})
    done = [branch for branch in branches if GATHER.rows[branch][-1][1] in GATHER.parts[part]]
    plan = {
        "pool": pool is not None,
        "chunks": GATHER.parts[part],
        "branches": branches,
        "begun": [branch for branch in branches if branch in begun],
        "done": done,
        "columns": columns,
        "height": height,
        "rows": rows,
    }
    center = sides[0][1]
    args = [mask, center]
    specs = [full_spec(mask), lane_spec(center)]
    for branch in branches:
        args += [sides[branch][0], sides[branch][2]]
        specs += [lane_spec(center)] * 2
    for branch in plan["begun"]:
        args.append(begun[branch])
        specs.append(full_spec(begun[branch]))
    if pool:
        args += list(pool)
        specs += [full_spec(item) for item in pool]
    args += list(pair)
    specs += [part_spec(item) for item in pair]
    kernel = functools.partial(coarse_forward_kernel, plan)
    if tie is not None:
        kernel = behind_tie(kernel)
        args.insert(0, tie)
        specs.insert(0, pl.BlockSpec(memory_space=pl.ANY))
    flat = jax.ShapeDtypeStruct((positions, channels), jnp.float32)
    small = jax.ShapeDtypeStruct((8, channels), jnp.float32)
    outs = [flat] * len(branches) + [small] * len(done)
    if pool:
        outs += [flat, small, small, jax.ShapeDtypeStruct((8, center.shape[1]), jnp.bfloat16)]
    out_specs = [full_spec(item) for item in outs]
    if pool:
        out_specs[-1] = lane_spec(outs[-1])
    results = pl.pallas_call(
        kernel,
        out_shape=outs,
        grid_spec=pltpu.PrefetchScalarGridSpec(
            num_scalar_prefetch=1, grid=(2 * ROUNDS,), in_specs=specs, out_specs=out_specs
        ),
        compiler_params=pltpu.CompilerParams(vmem_limit_bytes=VMEM_BYTES),
        cost_estimate=cost(
            coarse_flops([row[:2] for row in rows], shape, center.shape[1])
            + (2 * positions * channels * center.shape[1] if pool else 0),
            args + outs,
        ),
        name="coarse_forward",
    )(kernel_place(), *args)
    sums = dict(zip(branches, results))
    stats = dict(zip(done, results[len(branches) :]))
    return (sums, stats, results[len(branches) + len(done) :])


def coarse_weight_kernel(plan, place_ref, *refs):
    refs = list(refs)
    center = refs.pop(0)
    outer = {branch: (refs.pop(0), refs.pop(0)) for branch in plan["branches"]}
    grads = {branch: refs.pop(0) for branch in plan["branches"]}
    if plan["pool"]:
        point_ref, pooled_ref, pool_ref = refs.pop(0), refs.pop(0), refs.pop(0)
    outs = (refs.pop(0), refs.pop(0))
    row, core = place_ref[2], place_ref[3]
    flip = lax.rem(pl.program_id(0) + place_ref[1], 2)
    rows, cols = outs[0].shape[-2:]
    columns = plan["columns"]

    def store(chunk, tap, value):
        value = value.astype(jnp.bfloat16)
        lower, upper = value[:rows], value[rows:]
        mine = jnp.where(core == 0, lower, upper)
        other = jnp.where(core == 0, upper, lower)
        place = SCATTER.place(chunk, tap)
        for ref, part in zip(outs, (mine, other)):
            for side, lane_part in ((row, part[:, :cols]), (1 - row, part[:, cols:])):
                if chunk % 2 == 0:
                    ref[flip, side, 0, place] = lane_part
                else:
                    ref[side, flip, 0, place] = lane_part

    across = (((0,), (0,)), ((), ()))
    for branch, line, chunk, tap in plan["rows"]:
        source, target, extent = row_span(dilations[branch], line, plan["height"])
        sides = (outer[branch][0], center, outer[branch][1])
        values = jnp.concatenate(
            [side[pl.ds(source * columns, extent * columns), :] for side in sides], axis=1
        )
        result = lax.dot_general(
            values,
            grads[branch][pl.ds(target * columns, extent * columns), :],
            across,
            preferred_element_type=jnp.float32,
        )
        for k in range(3):
            store(chunk, tap + k, result[2 * rows * k : 2 * rows * (k + 1)])
    if plan["pool"]:
        for tap, left, right in ((0, center, point_ref), (1, pooled_ref, pool_ref)):
            store(
                SCATTER.point_chunk,
                tap,
                lax.dot_general(
                    left[...], right[...], across, preferred_element_type=jnp.float32
                ),
            )


def coarse_weight(part, sides, grads, shape, pool=None, tie=None):
    height, columns, channels = shape
    rows = SCATTER.part_rows(part)
    branches = sorted({row[0] for row in rows})
    plan = {
        "pool": pool is not None,
        "branches": branches,
        "chunks": SCATTER.parts[part],
        "rows": rows,
        "columns": columns,
        "height": height,
    }
    center = sides[0][1]
    args = [center]
    specs = [lane_spec(center)]
    for branch in branches:
        args += [sides[branch][0], sides[branch][2]]
        specs += [lane_spec(center)] * 2
    for branch in branches:
        args.append(grads[branch])
        specs.append(full_spec(grads[branch]))
    if pool:
        args += list(pool)
        specs += [full_spec(pool[0]), lane_spec(pool[1]), full_spec(pool[2])]
    kernel = functools.partial(coarse_weight_kernel, plan)
    if tie is not None:
        kernel = behind_tie(kernel)
        args.insert(0, tie)
        specs.insert(0, pl.BlockSpec(memory_space=pl.ANY))
    total = sum(SCATTER.sizes[part])
    tail = (total, center.shape[1] // (4 * ROUNDS), channels // 2)
    outs = [jax.ShapeDtypeStruct((2, 2, ROUNDS) + tail, jnp.bfloat16)] * 2
    out_specs = [part_spec(item) for item in outs]
    results = pl.pallas_call(
        kernel,
        out_shape=outs,
        grid_spec=pltpu.PrefetchScalarGridSpec(
            num_scalar_prefetch=1, grid=(2 * ROUNDS,), in_specs=specs, out_specs=out_specs
        ),
        compiler_params=pltpu.CompilerParams(vmem_limit_bytes=VMEM_BYTES),
        cost_estimate=cost(
            coarse_flops([row[:2] for row in rows], shape, center.shape[1])
            + (2 * height * columns * channels * center.shape[1] if pool else 0),
            args + outs,
        ),
        name="coarse_weight",
    )(kernel_place(), *args)
    return (results[0], results[1])


def coarse_input_kernel(plan, place_ref, *refs):
    refs = list(refs)
    point_ref, pool_ref, spread_ref = refs.pop(0), refs.pop(0), refs.pop(0)
    grads = [refs.pop(0) for _ in range(3)]
    pairs = [(refs.pop(0), refs.pop(0)) for _ in GATHER.parts]
    point_pair = pairs[GATHER.part_of(GATHER.point_chunk)]
    out_ref, total_ref = refs
    columns = plan["columns"]
    turned = (((1,), (1,)), ((), ()))
    total_ref[...] = lax.dot_general(
        point_ref[...],
        tap_matrix(point_pair, GATHER.point_chunk, 0, place_ref),
        turned,
        preferred_element_type=jnp.float32,
    )
    pooled = lax.dot_general(
        pool_ref[...],
        tap_matrix(point_pair, GATHER.point_chunk, 1, place_ref),
        turned,
        preferred_element_type=jnp.float32,
    )
    total_ref[...] += jnp.dot(
        spread_ref[...], pooled, preferred_element_type=jnp.float32, precision=highest
    )
    for branch, rows in enumerate(plan["rows"]):
        for line, chunk, tap in rows:
            source, target, extent = row_span(dilations[branch], line, plan["height"])
            matrix = jnp.concatenate(
                [
                    tap_matrix(pairs[GATHER.part_of(chunk)], chunk, tap + k, place_ref)
                    for k in range(3)
                ],
                axis=1,
            )
            total_ref[pl.ds(source * columns, extent * columns), :] += lax.dot_general(
                grads[branch][pl.ds(target * columns, extent * columns), :],
                matrix,
                turned,
                preferred_element_type=jnp.float32,
            )
    out_ref[...] = total_ref[...].astype(jnp.bfloat16)


def coarse_input(point_dz, pool_dz, spread, grads, parts, shape, width, tie=None):
    height, columns, channels = shape
    plan = {
        "columns": columns,
        "height": height,
        "rows": GATHER.rows,
    }
    args = [point_dz, pool_dz, spread] + list(grads)
    specs = [full_spec(item) for item in args]
    for pair in parts:
        args += list(pair)
        specs += [part_spec(item) for item in pair]
    kernel = functools.partial(coarse_input_kernel, plan)
    if tie is not None:
        kernel = behind_tie(kernel)
        args.insert(0, tie)
        specs.insert(0, pl.BlockSpec(memory_space=pl.ANY))
    out = jax.ShapeDtypeStruct((height * columns, width), jnp.bfloat16)
    return pl.pallas_call(
        kernel,
        out_shape=out,
        grid_spec=pltpu.PrefetchScalarGridSpec(
            num_scalar_prefetch=1,
            grid=(2 * ROUNDS,),
            in_specs=specs,
            out_specs=lane_spec(out),
            scratch_shapes=[pltpu.VMEM((height * columns, width // (2 * ROUNDS)), jnp.float32)],
        ),
        compiler_params=pltpu.CompilerParams(vmem_limit_bytes=VMEM_BYTES),
        cost_estimate=cost(
            coarse_flops([(b, k) for b in range(3) for k in range(3)], shape, width)
            + 2 * height * columns * channels * width,
            args + [out],
        ),
        name="coarse_input",
    )(kernel_place(), *args)


STRIP = 8


def norm_vectors(mean, variance, gain, bias, *more):
    rows = [mean, lax.rsqrt(variance + epsilon), gain, bias] + list(more)
    rows += [jnp.zeros_like(mean)] * (8 - len(rows))
    return jnp.stack(rows)


def sigmoid(values):
    return 0.5 * jnp.tanh(0.5 * values) + 0.5


def vector(ref, index):
    return ref[index : index + 1, :]


def shaped_of(values, vector_ref):
    centered = (values - vector(vector_ref, 0)) * vector(vector_ref, 1)
    return (centered, centered * vector(vector_ref, 2) + vector(vector_ref, 3))


def slope_of(shaped, gate):
    return gate * (1.0 + shaped * (1.0 - gate))


def merge_vectors(rows_ref, params_ref, vector_ref, sums_ref=None):
    width = vector_ref.shape[1]
    means = rows_ref[:, :width]
    squares = rows_ref[:, width : 2 * width]
    counts = rows_ref[:, 2 * width : 2 * width + 1]
    total = jnp.sum(counts, axis=0, keepdims=True)
    mean = jnp.sum(counts * means, axis=0, keepdims=True) / total
    gap = means - mean
    variance = jnp.sum(squares + counts * gap * gap, axis=0, keepdims=True) / total
    vector_ref[0:1, :] = mean
    vector_ref[1:2, :] = lax.rsqrt(variance + epsilon)
    vector_ref[2:4, :] = params_ref[...]
    if sums_ref is not None:
        for index in range(2):
            part = sums_ref[:, index * width : (index + 1) * width]
            vector_ref[6 + index : 7 + index, :] = jnp.sum(part, axis=0, keepdims=True)
            vector_ref[4 + index : 5 + index, :] = vector_ref[6 + index : 7 + index, :] / total


def send_rows(rows_ref, pieces):
    joined = jnp.concatenate(pieces, axis=1)
    rows_ref[...] = jnp.broadcast_to(joined, rows_ref.shape)


def send_moments(rows_ref, stats_ref, masks_ref, steps):
    count = jnp.sum(masks_ref[:, 0:1]) * steps
    send_rows(
        rows_ref,
        [stats_ref[0:1, :], stats_ref[1:2, :], jnp.full((1, 128), 1.0, jnp.float32) * count],
    )


def lag_specs(steps):
    def ahead(array, block):
        return pl.BlockSpec(block, lambda step: (jnp.minimum(step, steps - 1), 0))

    def behind(array, block):
        return pl.BlockSpec(block, lambda step: (jnp.maximum(step - 1, 0), 0))

    return (ahead, behind)


def whole(array):
    return pl.BlockSpec(array.shape, lambda step: (0,) * len(array.shape))


def window(ref, start, step, columns):
    return ref[pl.ds(pl.multiple_of((start + step) * columns, columns), STRIP * columns), :]


def run_moments(values, mask, stats_ref, step):
    count = jnp.sum(mask)
    mean = jnp.sum(values * mask, axis=0, keepdims=True) / count
    centered = (values - mean) * mask
    squares = jnp.sum(centered * centered, axis=0, keepdims=True)
    done = (step - 1).astype(jnp.float32)
    old_mean = jnp.where(step > 1, stats_ref[0:1, :], mean)
    old_squares = jnp.where(step > 1, stats_ref[1:2, :], 0.0)
    gap = mean - old_mean
    stats_ref[0:1, :] = old_mean + gap / (done + 1.0)
    stats_ref[1:2, :] = old_squares + squares + gap * gap * (count * done / (done + 1.0))


def spread_columns(products, masks_ref):
    size = products.shape[0]
    width = products.shape[1] // 3
    result = products[:, width : 2 * width]
    result = result + masks_ref[:, 1:2] * pltpu.roll(products[:, :width], 1, 0)
    return result + masks_ref[:, 2:3] * pltpu.roll(products[:, 2 * width :], size - 1, 0)


def clear_edges(ref, columns):
    ref[:columns, :] = jnp.zeros((columns, ref.shape[1]), ref.dtype)
    ref[ref.shape[0] - columns :, :] = jnp.zeros((columns, ref.shape[1]), ref.dtype)


def row_taps(w_ref, row, start, stop):
    return jnp.concatenate([w_ref[3 * row + k, start:stop, :] for k in range(3)], axis=1)


def low_lanes(width):
    return lax.broadcasted_iota(jnp.int32, (1, width), 1)


def decode_forward_kernel(
    steps, act_ref, table_ref, low_ref, wide_ref, vector_ref, masks_ref, w_ref, z_ref, rows_ref,
    up_ref, joined_ref, reduced_ref, stats_ref
):
    step = pl.program_id(0)
    columns = table_ref.shape[0]
    channels = act_ref.shape[2]
    rows = act_ref.shape[0]

    @pl.when(step == 0)
    def _():
        clear_edges(joined_ref, columns)
        clear_edges(reduced_ref, columns)

    @pl.when(step < steps)
    def _():
        for offset in range(STRIP):
            base = step * (STRIP // 4) + offset // 4 + (offset % 4 - 2) // 2
            fraction = ((2 * (offset % 4) - 3) % 8) / 8.0
            lower = act_ref[jnp.maximum(base, 0)]
            upper = act_ref[jnp.minimum(base + 1, rows - 1)]
            mixed = (1.0 - fraction) * lower + fraction * upper
            coarse = mixed.astype(jnp.bfloat16)
            fine = (mixed - coarse.astype(jnp.float32)).astype(jnp.bfloat16)
            value = jnp.dot(
                table_ref[...],
                jnp.concatenate([coarse, fine], axis=0),
                preferred_element_type=jnp.float32,
            ).astype(jnp.bfloat16)
            up_ref[offset * columns : (offset + 1) * columns, :] = value
            start = pl.multiple_of((step * STRIP + offset + 1) * columns, columns)
            joined_ref[pl.ds(start, columns), :] = value
        reduced = jnp.dot(low_ref[...], wide_ref[...], preferred_element_type=jnp.float32)
        _, shaped = shaped_of(reduced, vector_ref)
        value = masks_ref[:, 0:1] * (shaped * sigmoid(shaped))
        start = pl.multiple_of((step * STRIP + 1) * columns, columns)
        reduced_ref[pl.ds(start, STRIP * columns), :] = value.astype(jnp.bfloat16)

    @pl.when(step > 0)
    def _():
        start = (step - 1) * STRIP
        lane = low_lanes(reduced_ref.shape[1])
        lows = [window(reduced_ref, start, k, columns) for k in range(3)]
        low = jnp.where(lane < 64, lows[0], jnp.where(lane < 128, lows[1], lows[2]))
        values = jnp.concatenate(
            [window(joined_ref, start, k, columns) for k in range(3)] + [low], axis=1
        )
        extra = w_ref.shape[1] - channels
        parts = [row_taps(w_ref, k, 0, channels) for k in range(3)]
        for k in range(3):
            parts.append(row_taps(w_ref, k, channels, channels + extra))
            parts.append(jnp.zeros((64 - extra, 3 * channels), jnp.bfloat16))
        parts.append(jnp.zeros((64, 3 * channels), jnp.bfloat16))
        products = jnp.dot(
            values, jnp.concatenate(parts, axis=0), preferred_element_type=jnp.float32
        )
        result = spread_columns(products, masks_ref)
        z_ref[...] = result
        run_moments(result, masks_ref[:, 0:1], stats_ref, step)

    @pl.when(step == steps)
    def _():
        send_moments(rows_ref, stats_ref, masks_ref, steps)


def decode_forward(act, table, low, wide, vectors, masks, weights, devices):
    positions = low.shape[0]
    columns = table.shape[0]
    block = STRIP * columns
    steps = positions // block
    channels = act.shape[2]
    ahead, behind = lag_specs(steps)
    flat = jax.ShapeDtypeStruct((positions, channels), jnp.float32)
    stats = jax.ShapeDtypeStruct((devices, 2 * channels + 128), jnp.float32)
    up = jax.ShapeDtypeStruct((positions, channels), jnp.bfloat16)
    return pl.pallas_call(
        functools.partial(decode_forward_kernel, steps),
        out_shape=[flat, stats, up],
        grid=(steps + 1,),
        in_specs=[
            whole(act),
            whole(table),
            ahead(low, (block, low.shape[1])),
            whole(wide),
            whole(vectors),
            whole(masks),
            whole(weights),
        ],
        out_specs=[
            behind(flat, (block, channels)),
            whole(stats),
            ahead(up, (block, channels)),
        ],
        scratch_shapes=[
            pltpu.VMEM((positions + 2 * columns, channels), jnp.bfloat16),
            pltpu.VMEM((positions + 2 * columns, wide.shape[1]), jnp.bfloat16),
            pltpu.VMEM((8, channels), jnp.float32),
        ],
        compiler_params=pltpu.CompilerParams(vmem_limit_bytes=VMEM_BYTES),
        cost_estimate=cost(2 * positions * 3 * channels * 4 * channels, [low, flat, up]),
        name="decode_forward",
    )(act, table, low, wide, vectors, masks, weights)


def refine_forward_kernel(
    steps, columns, z_in_ref, rows_in_ref, params_ref, masks_ref, w_ref, z_ref, rows_ref, act_ref,
    vector_ref, stats_ref
):
    step = pl.program_id(0)
    channels = w_ref.shape[1]

    @pl.when(step == 0)
    def _():
        clear_edges(act_ref, columns)
        merge_vectors(rows_in_ref, params_ref, vector_ref)

    @pl.when(step < steps)
    def _():
        _, shaped = shaped_of(z_in_ref[...], vector_ref)
        value = masks_ref[:, 0:1] * (shaped * sigmoid(shaped))
        start = pl.multiple_of((step * STRIP + 1) * columns, columns)
        act_ref[pl.ds(start, STRIP * columns), :] = value.astype(jnp.bfloat16)

    @pl.when(step > 0)
    def _():
        start = (step - 1) * STRIP
        values = jnp.concatenate([window(act_ref, start, k, columns) for k in range(3)], axis=1)
        matrix = jnp.concatenate([row_taps(w_ref, k, 0, channels) for k in range(3)], axis=0)
        products = jnp.dot(values, matrix, preferred_element_type=jnp.float32)
        result = spread_columns(products, masks_ref)
        z_ref[...] = result
        run_moments(result, masks_ref[:, 0:1], stats_ref, step)

    @pl.when(step == steps)
    def _():
        send_moments(rows_ref, stats_ref, masks_ref, steps)


def refine_forward(z_in, rows, params, masks, weights):
    positions, channels = z_in.shape
    block = masks.shape[0]
    columns = block // STRIP
    steps = positions // block
    ahead, behind = lag_specs(steps)
    flat = jax.ShapeDtypeStruct((positions, channels), jnp.float32)
    stats = jax.ShapeDtypeStruct(rows.shape, jnp.float32)
    return pl.pallas_call(
        functools.partial(refine_forward_kernel, steps, columns),
        out_shape=[flat, stats],
        grid=(steps + 1,),
        in_specs=[
            ahead(z_in, (block, channels)),
            whole(rows),
            whole(params),
            whole(masks),
            whole(weights),
        ],
        out_specs=[behind(flat, (block, channels)), whole(stats)],
        scratch_shapes=[
            pltpu.VMEM((positions + 2 * columns, channels), jnp.bfloat16),
            pltpu.VMEM((8, channels), jnp.float32),
            pltpu.VMEM((8, channels), jnp.float32),
        ],
        compiler_params=pltpu.CompilerParams(vmem_limit_bytes=VMEM_BYTES),
        cost_estimate=cost(2 * positions * 9 * channels * channels, [z_in, flat]),
        name="refine_forward",
    )(z_in, rows, params, masks, weights)


def class_kernel(
    steps, z_ref, grad_ref, rows_ref, params_ref, masks_ref, w_ref, b_ref, logits_ref, out_ref,
    vector_ref, sums_ref, weight_ref, bias_ref
):
    step = pl.program_id(0)

    @pl.when(step == 0)
    def _():
        merge_vectors(rows_ref, params_ref, vector_ref)
        sums_ref[...] = jnp.zeros_like(sums_ref)
        weight_ref[...] = jnp.zeros_like(weight_ref)
        bias_ref[...] = jnp.zeros_like(bias_ref)

    mask = masks_ref[:, 0:1]
    centered, shaped = shaped_of(z_ref[...], vector_ref)
    gate = sigmoid(shaped)
    act = (mask * (shaped * gate)).astype(jnp.bfloat16)
    logits = jnp.dot(act, w_ref[...], preferred_element_type=jnp.float32) + b_ref[...]
    logits_ref[...] = (mask * logits).astype(jnp.bfloat16)
    grad = (mask * grad_ref[...].astype(jnp.float32)).astype(jnp.bfloat16)
    upstream = lax.dot_general(
        grad, w_ref[...], (((1,), (1,)), ((), ())), preferred_element_type=jnp.float32
    )
    local = mask * upstream * slope_of(shaped, gate)
    sums_ref[0:1, :] += jnp.sum(local * centered, axis=0, keepdims=True)
    sums_ref[1:2, :] += jnp.sum(local, axis=0, keepdims=True)
    weight_ref[...] += lax.dot_general(
        grad, act, (((0,), (0,)), ((), ())), preferred_element_type=jnp.float32
    )
    bias_ref[...] += jnp.sum(grad.astype(jnp.float32), axis=0, keepdims=True)

    @pl.when(step == steps - 1)
    def _():
        width = vector_ref.shape[1]
        classes = bias_ref.shape[1]
        shape = (classes, width)
        place = lax.broadcasted_iota(jnp.int32, shape, 0) == lax.broadcasted_iota(jnp.int32, shape, 1)
        wide_bias = jnp.dot(
            bias_ref[...],
            jnp.where(place, 1.0, 0.0),
            preferred_element_type=jnp.float32,
            precision=highest,
        )
        out_ref[...] = jnp.zeros_like(out_ref)
        send_rows(out_ref.at[:, : 2 * width], [sums_ref[0:1, :], sums_ref[1:2, :]])
        out_ref[:classes, 2 * width :] = weight_ref[...]
        out_ref[classes : classes + 1, 2 * width :] = wide_bias


def classify(z, grad, rows, params, masks, weights, bias):
    positions, channels = z.shape
    block = masks.shape[0]
    classes = grad.shape[1]
    steps = positions // block
    outs = [
        jax.ShapeDtypeStruct((positions, classes), jnp.bfloat16),
        jax.ShapeDtypeStruct((rows.shape[0], 3 * channels), jnp.float32),
    ]

    def strip(width):
        return pl.BlockSpec((block, width), lambda step: (step, 0))

    return pl.pallas_call(
        functools.partial(class_kernel, steps),
        out_shape=outs,
        grid=(steps,),
        in_specs=[
            strip(channels),
            strip(classes),
            whole(rows),
            whole(params),
            whole(masks),
            whole(weights),
            whole(bias),
        ],
        out_specs=[strip(classes), whole(outs[1])],
        scratch_shapes=[
            pltpu.VMEM((8, channels), jnp.float32),
            pltpu.VMEM((8, channels), jnp.float32),
            pltpu.VMEM((classes, channels), jnp.float32),
            pltpu.VMEM((1, classes), jnp.float32),
        ],
        compiler_params=pltpu.CompilerParams(vmem_limit_bytes=VMEM_BYTES),
        cost_estimate=cost(6 * positions * channels * 128, [z, grad, grad]),
        name="classify",
    )(z, grad, rows, params, masks, weights, bias)


def finish_grad(local, centered, mask, vector_ref):
    inner = local - vector(vector_ref, 5) - centered * vector(vector_ref, 4)
    return mask * vector(vector_ref, 2) * vector(vector_ref, 1) * inner


def store_sides(grad, masks_ref, side_ref, start):
    size, width = grad.shape
    grad = grad.astype(jnp.bfloat16).astype(jnp.float32)
    rows = pl.ds(start, size)
    side_ref[rows, :width] = pltpu.roll(masks_ref[:, 1:2] * grad, size - 1, 0).astype(jnp.bfloat16)
    side_ref[rows, width : 2 * width] = grad.astype(jnp.bfloat16)
    side_ref[rows, 2 * width :] = pltpu.roll(masks_ref[:, 2:3] * grad, 1, 0).astype(jnp.bfloat16)


def refine_backward_kernel(
    steps, columns, z_ref, grad_ref, rows_ref, sums_in_ref, params_ref, cls_ref, z_in_ref,
    rows_in_ref, params_in_ref, masks_ref, w_ref, local_ref, out_ref, totals_ref, weight_ref,
    side_ref, vector_ref, vector_in_ref, sums_ref
):
    step = pl.program_id(0)
    channels = w_ref.shape[1]
    mask = masks_ref[:, 0:1]

    @pl.when(step == 0)
    def _():
        clear_edges(side_ref, columns)
        merge_vectors(rows_ref, params_ref, vector_ref, sums_in_ref)
        merge_vectors(rows_in_ref, params_in_ref, vector_in_ref)
        totals_ref[...] = vector_ref[...]
        sums_ref[...] = jnp.zeros_like(sums_ref)
        weight_ref[...] = jnp.zeros_like(weight_ref)

    @pl.when(step < steps)
    def _():
        centered, shaped = shaped_of(z_ref[...], vector_ref)
        grad = (mask * grad_ref[...].astype(jnp.float32)).astype(jnp.bfloat16)
        upstream = lax.dot_general(
            grad, cls_ref[...], (((1,), (1,)), ((), ())), preferred_element_type=jnp.float32
        )
        local = mask * upstream * slope_of(shaped, sigmoid(shaped))
        start = pl.multiple_of((step * STRIP + 1) * columns, columns)
        store_sides(finish_grad(local, centered, mask, vector_ref), masks_ref, side_ref, start)

    @pl.when(step > 0)
    def _():
        start = (step - 1) * STRIP
        centered, shaped = shaped_of(z_in_ref[...], vector_in_ref)
        gate = sigmoid(shaped)
        act = (mask * (shaped * gate)).astype(jnp.bfloat16)
        sides = [window(side_ref, start, 2 - k, columns) for k in range(3)]
        upstream = lax.dot_general(
            jnp.concatenate(sides, axis=1),
            jnp.concatenate([w_ref[tap] for tap in range(9)], axis=1),
            (((1,), (1,)), ((), ())),
            preferred_element_type=jnp.float32,
        )
        local = mask * upstream * slope_of(shaped, gate)
        local_ref[...] = local
        sums_ref[0:1, :] += jnp.sum(local * centered, axis=0, keepdims=True)
        sums_ref[1:2, :] += jnp.sum(local, axis=0, keepdims=True)
        turned = act.T
        for k in range(3):
            weight_ref[k] += jnp.dot(turned, sides[k], preferred_element_type=jnp.float32)

    @pl.when(step == steps)
    def _():
        share = jnp.sum(sums_in_ref[:, 2 * channels :], axis=0, keepdims=True)
        send_rows(out_ref, [sums_ref[0:1, :], sums_ref[1:2, :], share])


def refine_backward(
    z, grad, rows, sums, params, classes, z_in, rows_in, params_in, masks, weights
):
    positions, channels = z.shape
    block = masks.shape[0]
    columns = block // STRIP
    steps = positions // block
    ahead, behind = lag_specs(steps)
    outs = [
        jax.ShapeDtypeStruct((positions, channels), jnp.float32),
        jax.ShapeDtypeStruct(sums.shape, jnp.float32),
        jax.ShapeDtypeStruct((8, channels), jnp.float32),
        jax.ShapeDtypeStruct((3, channels, 3 * channels), jnp.float32),
    ]
    return pl.pallas_call(
        functools.partial(refine_backward_kernel, steps, columns),
        out_shape=outs,
        grid=(steps + 1,),
        in_specs=[
            ahead(z, (block, channels)),
            ahead(grad, (block, grad.shape[1])),
            whole(rows),
            whole(sums),
            whole(params),
            whole(classes),
            behind(z_in, (block, channels)),
            whole(rows_in),
            whole(params_in),
            whole(masks),
            whole(weights),
        ],
        out_specs=[behind(z, (block, channels))] + [whole(item) for item in outs[1:]],
        scratch_shapes=[
            pltpu.VMEM((positions + 2 * columns, 3 * channels), jnp.bfloat16),
            pltpu.VMEM((8, channels), jnp.float32),
            pltpu.VMEM((8, channels), jnp.float32),
            pltpu.VMEM((8, channels), jnp.float32),
        ],
        compiler_params=pltpu.CompilerParams(vmem_limit_bytes=VMEM_BYTES),
        cost_estimate=cost(4 * positions * 9 * channels * channels, [z, z_in, grad, outs[0], weights]),
        name="refine_backward",
    )(z, grad, rows, sums, params, classes, z_in, rows_in, params_in, masks, weights)


def decode_backward_kernel(
    steps, columns, local_ref, z_ref, rows_ref, sums_in_ref, params_ref, up_ref, low_ref, wide_ref,
    low_vector_ref, table_ref, masks_ref, w_ref, coarse_ref, low_local_ref, sums_ref, totals_ref,
    weight_ref, low_weight_ref, side_ref, total_ref, vector_ref
):
    step = pl.program_id(0)
    channels = w_ref.shape[2]
    extra = w_ref.shape[1] - channels
    mask = masks_ref[:, 0:1]

    @pl.when(step == 0)
    def _():
        clear_edges(side_ref, columns)
        merge_vectors(rows_ref, params_ref, vector_ref, sums_in_ref)
        totals_ref[...] = vector_ref[...]
        sums_ref[...] = jnp.zeros_like(sums_ref)
        weight_ref[...] = jnp.zeros_like(weight_ref)
        low_weight_ref[...] = jnp.zeros_like(low_weight_ref)
        total_ref[...] = jnp.zeros_like(total_ref)

    @pl.when(step < steps)
    def _():
        centered, _ = shaped_of(z_ref[...], vector_ref)
        start = pl.multiple_of((step * STRIP + 1) * columns, columns)
        grad = finish_grad(local_ref[...], centered, mask, vector_ref)
        store_sides(grad, masks_ref, side_ref, start)

    @pl.when(step > 0)
    def _():
        start = (step - 1) * STRIP
        sides = [window(side_ref, start, 2 - k, columns) for k in range(3)]
        pieces = []
        for tap in range(9):
            pieces.append(
                jnp.concatenate(
                    [w_ref[tap], jnp.zeros((64 - extra, channels), jnp.bfloat16)], axis=0
                )
            )
        upstream = lax.dot_general(
            jnp.concatenate(sides, axis=1),
            jnp.concatenate(pieces, axis=1),
            (((1,), (1,)), ((), ())),
            preferred_element_type=jnp.float32,
        )
        for offset in range(STRIP):
            base = (step - 1) * (STRIP // 4) + offset // 4 + (offset % 4 - 2) // 2
            fraction = ((2 * (offset % 4) - 3) % 8) / 8.0
            value = upstream[offset * columns : (offset + 1) * columns, :channels]
            value = value.astype(jnp.bfloat16).astype(jnp.float32)
            total_ref[base + 1] += (1.0 - fraction) * value
            total_ref[base + 2] += fraction * value
        reduced = jnp.dot(low_ref[...], wide_ref[...], preferred_element_type=jnp.float32)
        centered, shaped = shaped_of(reduced, low_vector_ref)
        gate = sigmoid(shaped)
        low_act = (mask * (shaped * gate)).astype(jnp.bfloat16)
        low_up = upstream[:, channels:]
        local = mask * low_up * slope_of(shaped, gate)[:, :64]
        low_local_ref[...] = local
        sums_ref[0:1, :64] += jnp.sum(local * centered[:, :64], axis=0, keepdims=True)
        sums_ref[1:2, :64] += jnp.sum(local, axis=0, keepdims=True)
        turned = up_ref[...].T
        low_turned = low_act[:, :128].T[:64]
        for k in range(3):
            weight_ref[k] += jnp.dot(turned, sides[k], preferred_element_type=jnp.float32)
            low_weight_ref[k] += jnp.dot(low_turned, sides[k], preferred_element_type=jnp.float32)

    @pl.when(step == steps)
    def _():
        rows = coarse_ref.shape[0]
        total_ref[1] += total_ref[0]
        total_ref[rows] += total_ref[rows + 1]
        for row in range(rows):
            value = total_ref[row + 1]
            upper = value.astype(jnp.bfloat16)
            lower = (value - upper.astype(jnp.float32)).astype(jnp.bfloat16)
            coarse_ref[row] = jnp.dot(
                table_ref[...],
                jnp.concatenate([upper, lower], axis=0),
                preferred_element_type=jnp.float32,
            )


def decode_backward(
    local, z, rows, sums, params, up, low, wide, low_vectors, table, masks, weights, shape
):
    positions, channels = z.shape
    block = masks.shape[0]
    columns = block // STRIP
    steps = positions // block
    height, coarse_columns, _ = shape
    ahead, behind = lag_specs(steps)
    outs = [
        jax.ShapeDtypeStruct((height, coarse_columns, channels), jnp.float32),
        jax.ShapeDtypeStruct((positions, 64), jnp.float32),
        jax.ShapeDtypeStruct((8, channels), jnp.float32),
        jax.ShapeDtypeStruct((8, channels), jnp.float32),
        jax.ShapeDtypeStruct((3, channels, 3 * channels), jnp.float32),
        jax.ShapeDtypeStruct((3, 64, 3 * channels), jnp.float32),
    ]
    return pl.pallas_call(
        functools.partial(decode_backward_kernel, steps, columns),
        out_shape=outs,
        grid=(steps + 1,),
        in_specs=[
            ahead(local, (block, channels)),
            ahead(z, (block, channels)),
            whole(rows),
            whole(sums),
            whole(params),
            behind(up, (block, channels)),
            behind(low, (block, low.shape[1])),
            whole(wide),
            whole(low_vectors),
            whole(table),
            whole(masks),
            whole(weights),
        ],
        out_specs=[whole(outs[0]), behind(outs[1], (block, 64))]
        + [whole(item) for item in outs[2:]],
        scratch_shapes=[
            pltpu.VMEM((positions + 2 * columns, 3 * channels), jnp.bfloat16),
            pltpu.VMEM((height + 2, columns, channels), jnp.float32),
            pltpu.VMEM((8, channels), jnp.float32),
        ],
        compiler_params=pltpu.CompilerParams(vmem_limit_bytes=VMEM_BYTES),
        cost_estimate=cost(4 * positions * 9 * channels * (channels + 64), [local, z, up, low, outs[1], weights]),
        name="decode_backward",
    )(local, z, rows, sums, params, up, low, wide, low_vectors, table, masks, weights)


def branch_back(
    upstream, z, vectors, joined, weights, branch_z, pool_z, branch_vectors, mask, pool_mask, member,
    devices
):
    positions, channels = z.shape
    width = joined.shape[1]
    count = len(branch_z)
    outs = [
        jax.ShapeDtypeStruct((width, channels), jnp.float32),
        jax.ShapeDtypeStruct((positions, count * channels), jnp.float32),
        jax.ShapeDtypeStruct(pool_z.shape, jnp.float32),
        jax.ShapeDtypeStruct((devices, 2 * width), jnp.float32),
    ]
    args = [upstream, z, vectors, joined, weights, pool_z, branch_vectors, mask, pool_mask, member]
    args += list(branch_z)

    def body(*refs):
        (up_ref, z_ref, vector_ref, joined_ref, w_ref, pool_ref, branch_ref, mask_ref) = refs[:8]
        pool_mask_ref, member_ref = refs[8:10]
        z_refs = refs[10 : 10 + count]
        weight_ref, local_ref, pool_local_ref, rows_ref = refs[10 + count :]
        valid = mask_ref[...]
        centered, shaped = shaped_of(z_ref[...], vector_ref)
        local = valid * up_ref[...] * slope_of(shaped, sigmoid(shaped))
        grad = finish_grad(local, centered, valid, vector_ref).astype(jnp.bfloat16)
        weight_ref[...] = lax.dot_general(
            joined_ref[...], grad, (((0,), (0,)), ((), ())), preferred_element_type=jnp.float32
        )
        spread = lax.dot_general(
            grad, w_ref[...], (((1,), (1,)), ((), ())), preferred_element_type=jnp.float32
        )
        gains = []
        biases = []
        for index in range(count + 1):
            lanes = slice(index * channels, (index + 1) * channels)
            values = spread[:, lanes]
            if index < count:
                source, allowed = z_refs[index], valid
            else:
                source, allowed = pool_ref, pool_mask_ref[...]
                upper = values.astype(jnp.bfloat16)
                lower = (values - upper.astype(jnp.float32)).astype(jnp.bfloat16)
                values = jnp.dot(member_ref[...], upper, preferred_element_type=jnp.float32)
                values += jnp.dot(member_ref[...], lower, preferred_element_type=jnp.float32)
            centered, shaped = shaped_of(source[...], branch_ref.at[:, lanes])
            term = allowed * values * slope_of(shaped, sigmoid(shaped))
            if index < count:
                local_ref[:, lanes] = term
            else:
                pool_local_ref[...] = term
            gains.append(jnp.sum(term * centered, axis=0, keepdims=True))
            biases.append(jnp.sum(term, axis=0, keepdims=True))
        send_rows(rows_ref, gains + biases)

    return one_step(body, outs, args, vmem=60 * 1024 * 1024)


def branch_grads(rows, local, pool_local, branch_z, pool_z, branch_vectors, counts, mask, pool_mask):
    positions, channels = branch_z[0].shape
    count = len(branch_z)
    width = (count + 1) * channels
    outs = [jax.ShapeDtypeStruct((positions, channels), jnp.bfloat16)] * count
    outs += [jax.ShapeDtypeStruct(pool_z.shape, jnp.bfloat16)]
    outs += [jax.ShapeDtypeStruct((8, width), jnp.float32)]
    args = [rows, local, pool_local, pool_z, branch_vectors, counts, mask, pool_mask]
    args += list(branch_z)

    def body(*refs):
        rows_ref, local_ref, pool_local_ref, pool_ref, branch_ref, counts_ref = refs[:6]
        mask_ref, pool_mask_ref = refs[6:8]
        z_refs = refs[8 : 8 + count]
        grad_refs, totals_ref = refs[8 + count : -1], refs[-1]
        totals_ref[...] = jnp.zeros_like(totals_ref)
        totals_ref[0:1, :] = jnp.sum(rows_ref[:, :width], axis=0, keepdims=True)
        totals_ref[1:2, :] = jnp.sum(rows_ref[:, width:], axis=0, keepdims=True)
        for index in range(count + 1):
            lanes = slice(index * channels, (index + 1) * channels)
            vectors = branch_ref.at[:, lanes]
            source = z_refs[index] if index < count else pool_ref
            allowed = mask_ref[...] if index < count else pool_mask_ref[...]
            term = local_ref[:, lanes] if index < count else pool_local_ref[...]
            centered, _ = shaped_of(source[...], vectors)
            share = 1.0 / counts_ref[:, lanes]
            inner = term - totals_ref[1:2, lanes] * share
            inner = inner - centered * (totals_ref[0:1, lanes] * share)
            grad = allowed * vector(vectors, 2) * vector(vectors, 1) * inner
            grad_refs[index][...] = grad.astype(jnp.bfloat16)

    return one_step(body, outs, args, vmem=60 * 1024 * 1024)


def low_backward_kernel(
    vector_ref, local_ref, low_ref, wide_ref, masks_ref, out_ref, weight_ref
):
    @pl.when(pl.program_id(0) == 0)
    def _():
        weight_ref[...] = jnp.zeros_like(weight_ref)

    low = low_ref[...]
    weights = wide_ref[:, :128]
    reduced = jnp.dot(low, weights, preferred_element_type=jnp.float32)
    mean, scale, gain = (vector_ref[k : k + 1, :64] for k in range(3))
    centered = (reduced[:, :64] - mean) * scale
    inner = local_ref[...] - vector_ref[5:6, :64] - centered * vector_ref[4:5, :64]
    grad = (masks_ref[:, 0:1] * gain * scale * inner).astype(jnp.bfloat16)
    out_ref[...] = lax.dot_general(
        grad, weights[:, :64], (((1,), (1,)), ((), ())), preferred_element_type=jnp.float32
    ).astype(jnp.bfloat16)
    weight_ref[...] += lax.dot_general(
        grad, low, (((0,), (0,)), ((), ())), preferred_element_type=jnp.float32
    )


def low_backward(local, low, wide, vectors, masks, tie):
    positions, width = low.shape
    block = masks.shape[0]
    outs = [
        jax.ShapeDtypeStruct((positions, width), jnp.bfloat16),
        jax.ShapeDtypeStruct((64, width), jnp.float32),
    ]
    return pl.pallas_call(
        behind_tie(low_backward_kernel),
        out_shape=outs,
        grid=(positions // block,),
        in_specs=[
            whole(vectors),
            pl.BlockSpec(memory_space=pl.ANY),
            pl.BlockSpec((block, 64), lambda step: (step, 0)),
            pl.BlockSpec((block, width), lambda step: (step, 0)),
            whole(wide),
            whole(masks),
        ],
        out_specs=[pl.BlockSpec((block, width), lambda step: (step, 0)), whole(outs[1])],
        compiler_params=pltpu.CompilerParams(vmem_limit_bytes=VMEM_BYTES),
        cost_estimate=whole_cost(6 * positions * width * 128, [local, low, low]),
        name="low_backward",
    )(vectors, tie, local, low, wide, masks)


def side_values(values, image_ids, dilation):
    result = []
    for step in (-dilation, dilation):
        mask = tap_mask(image_ids, values.shape[1], 0, step).astype(values.dtype)
        result.append(mask * shifted(values, 0, step))
    return [result[0], values, result[1]]


def side_grads(values, image_ids, dilation):
    result = []
    for step in (-dilation, 0, dilation):
        masked = tap_mask(image_ids, values.shape[1], 0, step).astype(values.dtype) * values
        result.append(shifted(masked, 0, -step))
    return jnp.concatenate(result, axis=-1)


def settle_core(values):
    core = place()[3]
    taps, rows, cols = values.shape
    parts = values.reshape(taps, rows, 2, cols // 2)
    kept = lax.dynamic_index_in_dim(parts, core, 2, keepdims=False)
    given = lax.dynamic_index_in_dim(parts, 1 - core, 2, keepdims=False).astype(jnp.bfloat16)
    got = exchange(given, "narrow", 1).astype(jnp.float32)
    lower = jnp.where(core == 0, kept, got)
    upper = jnp.where(core == 0, got, kept)
    return jnp.concatenate([lower, upper], axis=1)


def band_ids(widths, columns):
    ends_all = jnp.cumsum(widths, axis=1)
    position = jnp.arange(columns, dtype=jnp.int32)
    band_index = jnp.sum(
        (position[None, :, None] >= ends_all[:, None, :]).astype(jnp.int32), axis=2
    )
    return jnp.where(band_index < widths.shape[1] - 1, band_index, -1)


def shifted(values, row_shift, col_shift):
    height = values.shape[1]
    columns = values.shape[2]
    padded = jnp.pad(
        values, ((0, 0), (abs(row_shift), abs(row_shift)), (abs(col_shift), abs(col_shift)), (0, 0))
    )
    row_start = abs(row_shift) + row_shift
    col_start = abs(col_shift) + col_shift
    return padded[:, row_start : row_start + height, col_start : col_start + columns, :]


def tap_mask(image_ids, height, row_shift, col_shift):
    columns = image_ids.shape[1]
    padded = jnp.pad(image_ids, ((0, 0), (abs(col_shift), abs(col_shift))), constant_values=-2)
    col_start = abs(col_shift) + col_shift
    other_ids = padded[:, col_start : col_start + columns]
    same_image = (other_ids == image_ids).astype(jnp.float32)
    row_place = jnp.arange(height) + row_shift
    inside = ((row_place >= 0) & (row_place < height)).astype(jnp.float32)
    return (inside[None, :, None] * same_image[:, None, :])[..., None]


def tap_offsets(dilation):
    return [
        ((tap_index // 3 - 1) * dilation, (tap_index % 3 - 1) * dilation) for tap_index in range(9)
    ]


def linear_weights(out_count, in_count):
    position = jnp.arange(out_count, dtype=jnp.int32)
    scaled = 2 * position - 3
    left_index = jnp.floor_divide(scaled, 8)
    fraction = (scaled - 8 * left_index).astype(jnp.float32) / 8.0
    lower_index = jnp.clip(left_index, 0, in_count - 1)
    upper_index = jnp.clip(left_index + 1, 0, in_count - 1)
    return (position, lower_index, upper_index, fraction)


def column_table(image_ids):
    columns = image_ids.shape[1]
    position, lower_index, upper_index, fraction = linear_weights(4 * columns, columns)
    source = jnp.arange(columns, dtype=jnp.int32)[None, :]

    def picker(index_row):
        return (source == index_row[:, None]).astype(jnp.int32)

    def lookup(index_row):
        return jnp.sum(image_ids[:, None, :] * picker(index_row)[None], axis=2)

    own_index = position // 4
    own_id = lookup(own_index)
    weight_lower = (1.0 - fraction)[None, :] * (lookup(lower_index) == own_id).astype(jnp.float32)
    weight_upper = fraction[None, :] * (lookup(upper_index) == own_id).astype(jnp.float32)
    weight_own = 1.0 - weight_lower - weight_upper
    table = weight_lower[:, :, None] * picker(lower_index)[None].astype(jnp.float32)
    table = table + weight_upper[:, :, None] * picker(upper_index)[None].astype(jnp.float32)
    table = table + weight_own[:, :, None] * picker(own_index)[None].astype(jnp.float32)
    return table


def normalize(values, valid_map, mean_row, variance, gain_row, bias_row):
    norm_scale = lax.rsqrt(variance + epsilon)
    centered = (values - mean_row) * norm_scale
    shaped = centered * gain_row + bias_row
    return (valid_map * jax.nn.silu(shaped), centered, shaped, norm_scale)


def norm_grad_terms(upstream, valid_map, centered, shaped):
    sigmoid_value = jax.nn.sigmoid(shaped)
    local_term = valid_map * upstream * sigmoid_value * (1.0 + shaped * (1.0 - sigmoid_value))
    axes = tuple(range(local_term.ndim - 1))
    return (local_term, jnp.sum(local_term * centered, axis=axes), jnp.sum(local_term, axis=axes))


def moments(values, valid_map, local_count, count_all):
    mean, squares = local_moments(values, valid_map, local_count)
    return merged(jnp.stack([mean, squares]), local_count, count_all)


def merged(stats, local_count, count_all):
    width = stats.shape[1]
    own = jnp.concatenate([stats[0], stats[1], jnp.full((1,), 1.0) * local_count])
    rows = from_all(own)
    counts, means, squares = merge_rows(
        rows[:, 2 * width :], rows[:, :width], rows[:, width : 2 * width]
    )
    return (means, squares / count_all)


def pack_pairs(pairs):
    return jnp.concatenate(
        [pair_item[0] for pair_item in pairs] + [pair_item[1] for pair_item in pairs]
    )


def unpack_pairs(flat, pairs):
    lengths = [pair_item[0].shape[0] for pair_item in pairs]
    half_point = sum(lengths)
    result_pairs = []
    offset = 0
    for length_now in lengths:
        result_pairs.append(
            (
                flat[offset : offset + length_now],
                flat[half_point + offset : half_point + offset + length_now],
            )
        )
        offset = offset + length_now
    return result_pairs


def gradient_sums(pairs):
    return unpack_pairs(jnp.sum(from_all(pack_pairs(pairs)), axis=0), pairs)


def small_block(items):
    proj, reduce, decode, refine = items
    taps, rows, cols = refine.shape
    count = proj.shape[0] // rows
    proj = proj.reshape(2, count, rows // 2, cols).swapaxes(0, 1).reshape(count, rows, cols)
    reduce = jnp.pad(reduce, ((0, 0), (0, cols - reduce.shape[1])))[None]
    shared = share_core(jnp.concatenate([refine, proj, reduce]))
    lanes = shared.shape[2]
    decode = decode.swapaxes(1, 2)
    decode = jnp.pad(decode, ((0, 0), (0, 0), (0, lanes - decode.shape[2])))
    return jnp.concatenate([shared, decode.reshape(-1, shared.shape[1], lanes)])


def settle_small(owned, shapes):
    shape_p, shape_r, shape_d, shape_f = shapes
    taps, rows, cols = shape_f
    count = shape_p[0] // rows
    first = taps + count + 1
    settled = settle_core(owned[:first])
    proj = settled[taps : taps + count].reshape(count, 2, rows // 2, cols)
    proj = proj.swapaxes(0, 1).reshape(shape_p)
    reduce = settled[taps + count, :, : shape_r[1]]
    decode = owned[first:].reshape(taps, shape_d[2], -1)[:, :, : shape_d[1]].swapaxes(1, 2)
    return (proj, reduce, decode, settled[:taps])


def reduce_lanes(width, row, core, half):
    start = (2 * row + core) * width
    return start, core * half


def unpack_kernel(shapes, place_ref, own_ref, other_ref, proj_ref, wide_ref, decode_ref, refine_ref):
    deep, side, row, core = (place_ref[index] for index in range(4))
    shape_p, shape_r, shape_d, shape_f = shapes
    taps = shape_f[0]
    rows = shape_f[1] // 2
    count = shape_p[0] // (2 * rows)
    lanes = own_ref.shape[-1]

    def load(ref, z, x, y, start, size):
        slot = lax.bitwise_xor(deep, z)
        return ref[slot, lax.rem(y + row, 2), lax.rem(x + side, 2), start : start + size]

    def both(z, x, y, start, size):
        mine = load(own_ref, z, x, y, start, size)
        others = load(other_ref, z, x, y, start, size)
        return (jnp.where(core == 0, mine, others), jnp.where(core == 0, others, mine))

    lane = lax.broadcasted_iota(jnp.int32, (1, lanes), 1)
    for z in range(ROUNDS):
        for x in range(2):
            wide = 2 * z + x
            halves = [both(z, x, y, 0, taps + count + 1) for y in range(2)]
            for h in range(2):
                joined = jnp.concatenate([halves[0][h], halves[1][h]], axis=-1)
                base = (2 * wide + h) * rows
                refine_ref[:, base : base + rows, :] = joined[:taps]
                base = (2 * wide + h) * rows * count
                proj_ref[base : base + rows * count, :] = joined[taps : taps + count].reshape(
                    rows * count, 2 * lanes
                )
                total = jnp.zeros((rows, lanes), jnp.float32)
                for y in range(2):
                    value = halves[y][h][taps + count].astype(jnp.float32)
                    for c in range(2):
                        start, held = reduce_lanes(shape_r[1], y, c, lanes // 2)
                        moved = pltpu.roll(value, (start - held) % lanes, 1)
                        inside = (lane >= start) & (lane < start + shape_r[1])
                        total = total + jnp.where(inside, moved, 0.0)
                base = (2 * wide + h) * rows
                left = total + pltpu.roll(total, 64, 1)
                wide_ref[base : base + rows, :] = jnp.concatenate([left, total], axis=1).astype(
                    jnp.bfloat16
                )
    height, width = shape_d[1], shape_d[2]
    blocks = width // rows
    for tap in range(taps):
        start = taps + count + 1 + tap * blocks
        pieces = []
        for y in range(2):
            columns = ([], [])
            for z in range(ROUNDS):
                for x in range(2):
                    for c, value in enumerate(both(z, x, y, start, blocks)):
                        columns[c].append(value.reshape(width, lanes))
            for c in range(2):
                joined = jnp.concatenate(columns[c], axis=0).astype(jnp.float32)
                pieces.append(joined.T[:height])
        decode_ref[tap] = jnp.concatenate(pieces, axis=0).astype(jnp.bfloat16)


def unpack_block(own, other, shapes):
    wide = 2 * ROUNDS
    shape_p, shape_r, shape_d, shape_f = shapes
    outs = [
        jax.ShapeDtypeStruct((wide * shape_p[0], 4 * shape_p[1]), jnp.bfloat16),
        jax.ShapeDtypeStruct((wide * shape_r[0], 256), jnp.bfloat16),
        jax.ShapeDtypeStruct((shape_d[0], 4 * shape_d[1], wide * shape_d[2]), jnp.bfloat16),
        jax.ShapeDtypeStruct((shape_f[0], wide * shape_f[1], 4 * shape_f[2]), jnp.bfloat16),
    ]
    return pl.pallas_call(
        functools.partial(unpack_kernel, shapes),
        out_shape=outs,
        in_specs=[pl.BlockSpec(memory_space=pltpu.SMEM)]
        + [pl.BlockSpec(memory_space=pltpu.VMEM)] * 2,
        out_specs=[pl.BlockSpec(memory_space=pltpu.VMEM)] * 4,
        compiler_params=pltpu.CompilerParams(vmem_limit_bytes=VMEM_BYTES),
        cost_estimate=whole_cost(0, [own, other] + outs + outs),
        name="unpack_weights",
    )(kernel_place(), own, other)


def pack_kernel(
    shapes, place_ref, proj_ref, reduce_ref, decode_ref, low_ref, refine_ref, keep_ref, give_ref
):
    deep, side, row, core = (place_ref[index] for index in range(4))
    shape_p, shape_r, shape_d, shape_f = shapes
    taps = shape_f[0]
    rows = shape_f[1] // 2
    count = shape_p[0] // (2 * rows)
    lanes = keep_ref.shape[-1]
    channels = 2 * lanes

    def store(z, x, y, start, size, values):
        values = [value.astype(jnp.bfloat16) for value in values]
        index = (
            lax.rem(x + side, 2),
            lax.rem(y + row, 2),
            lax.bitwise_xor(deep, z),
            pl.ds(start, size),
        )
        keep_ref[index] = jnp.where(core == 0, values[0], values[1])
        give_ref[index] = jnp.where(core == 0, values[1], values[0])

    lane = lax.broadcasted_iota(jnp.int32, (1, lanes), 1)
    reduce = jnp.concatenate(
        [reduce_ref[...], jnp.zeros((lanes - reduce_ref.shape[0], reduce_ref.shape[1]), jnp.float32)]
    ).T
    moved = []
    for y in range(2):
        total = jnp.zeros_like(reduce)
        for c in range(2):
            start, held = reduce_lanes(shape_r[1], y, c, lanes // 2)
            inside = (lane >= held) & (lane < held + shape_r[1])
            total = total + jnp.where(inside, pltpu.roll(reduce, (held - start) % lanes, 1), 0.0)
        moved.append(total)
    for z in range(ROUNDS):
        for x in range(2):
            wide = 2 * z + x
            for y in range(2):
                columns = slice(y * lanes, (y + 1) * lanes)
                for tap in range(taps):
                    line, k = tap // 3, tap % 3
                    left = k * channels + y * lanes
                    values = []
                    for h in range(2):
                        base = (2 * wide + h) * rows
                        values.append(
                            refine_ref[line, base : base + rows, left : left + lanes][None]
                        )
                    store(z, x, y, tap, 1, values)
                values = []
                for h in range(2):
                    base = (2 * wide + h) * rows * count
                    values.append(
                        proj_ref[base : base + rows * count, columns].reshape(count, rows, lanes)
                    )
                store(z, x, y, taps, count, values)
                values = [
                    moved[y][(2 * wide + h) * rows : (2 * wide + h + 1) * rows][None]
                    for h in range(2)
                ]
                store(z, x, y, taps + count, 1, values)
    height, width = shape_d[1], shape_d[2]
    blocks = width // rows
    for tap in range(taps):
        line, k = tap // 3, tap % 3
        columns = slice(k * channels, (k + 1) * channels)
        whole_tap = jnp.concatenate(
            [
                decode_ref[line, :, columns],
                low_ref[line, :, columns],
                jnp.zeros((lanes, channels), jnp.float32),
            ],
            axis=0,
        )
        turned = [whole_tap[n * height : n * height + lanes].T for n in range(4)]
        for z in range(ROUNDS):
            for x in range(2):
                base = (2 * z + x) * width
                for y in range(2):
                    values = [
                        turned[2 * y + c][base : base + width].reshape(blocks, rows, lanes)
                        for c in range(2)
                    ]
                    store(z, x, y, taps + count + 1 + tap * blocks, blocks, values)


def pack_block(proj, reduce, decode, low, refine, shapes, tie):
    shape_p, shape_r, shape_d, shape_f = shapes
    rows = shape_f[1] // 2
    total = shape_f[0] + shape_p[0] // (2 * rows) + 1 + shape_d[0] * shape_d[2] // rows
    out = jax.ShapeDtypeStruct((2, 2, ROUNDS, total, rows, 2 * shape_f[2]), jnp.bfloat16)
    return pl.pallas_call(
        behind_tie(functools.partial(pack_kernel, shapes)),
        out_shape=[out, out],
        in_specs=[pl.BlockSpec(memory_space=pltpu.SMEM), pl.BlockSpec(memory_space=pl.ANY)]
        + [pl.BlockSpec(memory_space=pltpu.VMEM)] * 5,
        out_specs=[pl.BlockSpec(memory_space=pltpu.VMEM)] * 2,
        compiler_params=pltpu.CompilerParams(vmem_limit_bytes=VMEM_BYTES),
        cost_estimate=whole_cost(0, [proj, decode, low, refine, out, out, out]),
        name="pack_gradients",
    )(kernel_place(), tie, proj, reduce, decode, low, refine)


def low_moments_kernel(low_ref, wide_ref, masks_ref, stats_ref):
    reduced = jnp.dot(low_ref[...], wide_ref[...], preferred_element_type=jnp.float32)
    run_moments(reduced, masks_ref[:, 0:1], stats_ref, pl.program_id(0) + 1)


def low_moments(low, wide, masks):
    block = masks.shape[0]
    out = jax.ShapeDtypeStruct((8, wide.shape[1]), jnp.float32)
    return pl.pallas_call(
        low_moments_kernel,
        out_shape=out,
        grid=(low.shape[0] // block,),
        in_specs=[
            pl.BlockSpec((block, low.shape[1]), lambda step: (step, 0)),
            whole(wide),
            whole(masks),
        ],
        out_specs=whole(out),
        compiler_params=pltpu.CompilerParams(vmem_limit_bytes=VMEM_BYTES),
        cost_estimate=whole_cost(2 * low.shape[0] * low.shape[1] * 256, [low]),
        name="low_moments",
    )(low, wide, masks)


def by_tap(values):
    width = values.shape[2] // 3
    split = values.reshape(3, values.shape[1], 3, width)
    return split.transpose(0, 2, 1, 3).reshape(9, values.shape[1], width)


def widen(values):
    padded = jnp.pad(values, ((0, 0), (0, 64 - values.shape[1])))
    return jnp.concatenate([padded, padded, padded, jnp.zeros_like(padded)], axis=1)


def pack_small(items):
    total = sum(item.size for item in items)
    padded = -(-total // 2048) * 2048
    flats = [item.reshape(-1) for item in items]
    return jnp.concatenate(flats + [jnp.zeros((padded - total,), jnp.bfloat16)]).reshape(-1, 128)


def unpack_small(everything, items):
    wide, narrow = everything.shape[:2]
    everything = everything.reshape(wide, narrow, -1)
    pieces = []
    start = 0
    for item in items:
        pieces.append(
            everything[:, :, start : start + item.size].reshape((wide, narrow) + item.shape)
        )
        start += item.size
    proj, reduce, decode, refine = pieces
    proj = proj.transpose(0, 2, 1, 3).reshape(wide * proj.shape[2], -1)
    reduce = reduce.transpose(0, 2, 1, 3).reshape(wide * reduce.shape[2], -1)
    decode = decode.transpose(2, 1, 3, 0, 4).reshape(decode.shape[2], narrow * decode.shape[3], -1)
    refine = refine.transpose(2, 0, 3, 1, 4).reshape(refine.shape[2], wide * refine.shape[3], -1)
    return (proj, widen(reduce), decode, refine)


def pack_grads(reduce, proj, decode, low, refine, shapes):
    wide = lax.axis_size("wide")
    narrow = lax.axis_size("narrow")
    extra = narrow * shapes[1][1]
    reduce = reduce[:extra].T
    decode = jnp.concatenate([by_tap(decode), by_tap(low)[:, :extra]], axis=1)
    refine = by_tap(refine)
    shape_p, shape_r, shape_d, shape_f = shapes
    proj = proj.reshape(wide, shape_p[0], narrow, shape_p[1]).transpose(0, 2, 1, 3)
    reduce = reduce.reshape(wide, shape_r[0], narrow, shape_r[1]).transpose(0, 2, 1, 3)
    decode = decode.reshape(shape_d[0], narrow, shape_d[1], wide, shape_d[2]).transpose(3, 1, 0, 2, 4)
    refine = refine.reshape(shape_f[0], wide, shape_f[1], narrow, shape_f[2]).transpose(1, 3, 0, 2, 4)
    flats = [
        item.astype(jnp.bfloat16).reshape(wide, narrow, -1)
        for item in (proj, reduce, decode, refine)
    ]
    total = sum(item.shape[2] for item in flats)
    padded = -(-total // 2048) * 2048
    flats.append(jnp.zeros((wide, narrow, padded - total), jnp.bfloat16))
    return jnp.concatenate(flats, axis=2).reshape(wide, narrow, -1, 128)


def unpack_grads(owned, shapes):
    owned = owned.reshape(-1)
    pieces = []
    start = 0
    for shape in shapes:
        size = 1
        for extent in shape:
            size *= extent
        pieces.append(owned[start : start + size].reshape(shape))
        start += size
    return pieces


def per_device(
    features,
    low_level,
    widths,
    w_point,
    w_atrous,
    w_proj,
    w_low,
    w_dec1,
    w_dec2,
    w_cls,
    b_cls,
    gains,
    biases,
    low_gain,
    low_bias,
    logit_grad,
):
    canvases = features.shape[0]
    height = features.shape[1]
    columns = features.shape[2]
    fine_columns = low_level.shape[2]
    images = widths.shape[1] - 1
    channels = gains.shape[1]
    images_total = float(canvases * lax.axis_size("wide") * lax.axis_size("narrow") * images)
    small = [w_proj, w_low, w_dec1, w_dec2]
    ids_coarse = band_ids(widths, columns)
    ids_fine = band_ids(4 * widths, fine_columns)
    valid_coarse = (ids_coarse >= 0).astype(jnp.float32)[:, None, :, None]
    valid_fine = (ids_fine >= 0).astype(jnp.float32)[:, None, :, None]
    all_ones = jnp.ones((1, 1, 1), jnp.float32)
    local_count = (height * jnp.sum(widths[:, :images])).astype(jnp.float32)
    member = (ids_coarse[:, :, None] == jnp.arange(images, dtype=jnp.int32)[None, None, :]).astype(
        jnp.float32
    )
    member_low = member.astype(jnp.bfloat16)
    image_sizes = (height * widths[:, :images]).astype(jnp.float32)
    positions = low_level.shape[1] * fine_columns
    low_flat = low_level.reshape(positions, -1)
    extra = low_gain.shape[0]
    side_masks = [tap_mask(ids_fine, STRIP, 0, step) for step in (-1, 1)]
    masks = jnp.concatenate([valid_fine * jnp.ones((1, STRIP, 1, 1))] + side_masks, axis=-1)
    masks = masks.reshape(STRIP * fine_columns, 3)
    coarse_shape = (height, columns, channels)
    mask_column = jnp.broadcast_to(valid_coarse, (1, height, columns, 1)).reshape(-1, 1)
    member_wide = jnp.pad(member[0], ((0, 0), (0, 8 - images)))
    member_rows = jnp.tile(member_wide, (height, 1))
    sizes_inverse = jnp.pad(1.0 / image_sizes[0], (0, 8 - images)).reshape(8, 1)
    pool_inputs = (member_rows.T.astype(jnp.bfloat16), sizes_inverse)

    cols_table = column_table(ids_coarse)[0].astype(jnp.bfloat16)
    up_table = jnp.concatenate([cols_table, cols_table], axis=1)
    down_table = jnp.concatenate([cols_table.T, cols_table.T], axis=1)
    decode_params = jnp.stack([gains[6], biases[6]])
    refine_params = jnp.stack([gains[7], biases[7]])
    pool_mask = (jnp.arange(8) < images).astype(jnp.float32).reshape(8, 1)
    grad_flat = logit_grad.reshape(-1, logit_grad.shape[-1])
    spread_rows = member_rows * sizes_inverse.reshape(1, 8)
    prepared = [
        masks,
        mask_column,
        sizes_inverse,
        pool_inputs[0],
        up_table,
        down_table,
        decode_params,
        refine_params,
        pool_mask,
        grad_flat,
        w_cls,
        spread_rows,
    ]

    def all_sides():
        sides = [
            [
                item.reshape(height * columns, -1)
                for item in side_values(features, ids_coarse, dilation)
            ]
            for dilation in dilations
        ]
        return (sides, grad_flat)

    def low_part(proj, wide, decode, refine):
        return low_moments(low_flat, wide, masks)

    def forward(part, ready, pair, before, tie=None):
        sums, stats, pooling = ({}, {}, ()) if before is None else before
        more, more_stats, more_pooling = coarse_forward(
            part,
            mask_column,
            ready[0],
            pair,
            coarse_shape,
            sums,
            pool_inputs if GATHER.has_point(part) else None,
            tie,
        )
        return ({**sums, **more}, {**stats, **more_stats}, tuple(pooling) + tuple(more_pooling))

    parts, unpacked, ready, low_stats, coarse = gather_taps(
        GATHER.order(w_point, w_atrous),
        small,
        [all_sides, low_part],
        [functools.partial(forward, part) for part in range(len(GATHER.parts))],
        prepared,
    )
    proj_full, low_wide, decode_full, refine_full = unpacked
    sides, grad_flat = ready
    sums, stats, pool_results = coarse
    point_z, point_stats, pool_z, pooled = pool_results
    pool_wide = pool_z
    pool_z = pool_z[None, :images]
    coarse_stats = [point_stats, stats[0], stats[1], stats[2]]
    coarse_z = [
        item.reshape(1, height, columns, channels) for item in (point_z, sums[0], sums[1], sums[2])
    ]
    blocks = [(item_z, valid_coarse) for item_z in coarse_z] + [(pool_z, all_ones)]
    local_images = float(canvases * images)
    states = [(item[0], item[1]) for item in coarse_stats] + [
        local_moments(pool_z, all_ones, local_images),
    ]
    own = [state[item] for item in range(2) for state in states]
    rows = from_all(jnp.concatenate(own + [jnp.full((1,), 1.0) * local_count]))
    width = 5 * channels
    pixels = rows[:, 2 * width :]
    count_rows = jnp.concatenate(
        [
            jnp.broadcast_to(pixels, (rows.shape[0], 4 * channels)),
            jnp.full((rows.shape[0], channels), local_images),
        ],
        axis=1,
    )
    counts_flat, means_flat, squares_flat = merge_rows(
        count_rows, rows[:, :width], rows[:, width : 2 * width]
    )
    vars_flat = squares_flat / counts_flat
    section_means = []
    section_vars = []
    offset = 0
    for width in [channels] * 5:
        section_means.append(means_flat[offset : offset + width])
        section_vars.append(vars_flat[offset : offset + width])
        offset += width
    pixel_count = counts_flat[0]
    fine_count = 16.0 * pixel_count
    gain_rows = [gains[0], gains[1], gains[2], gains[3], gains[4], low_gain]
    bias_rows = [biases[0], biases[1], biases[2], biases[3], biases[4], low_bias]
    kept = []
    activations = []
    for index in range(5):
        block_values, block_valid = blocks[index]
        result = normalize(
            block_values,
            block_valid,
            section_means[index],
            section_vars[index],
            gain_rows[index],
            bias_rows[index],
        )
        kept.append(result[1:])
        activations.append(result[0].astype(jnp.bfloat16))
    spread = jnp.einsum(
        "nwk,nkd->nwd", member_low, activations[4], preferred_element_type=jnp.float32
    ).astype(jnp.bfloat16)
    spread = jnp.broadcast_to(spread[:, None], (canvases, height, columns, channels))
    joined_coarse = jnp.concatenate(activations[:4] + [spread], axis=-1)
    proj_z = jnp.einsum(
        "nhwc,cd->nhwd", joined_coarse, proj_full, preferred_element_type=jnp.float32
    )
    proj_moments = local_moments(proj_z, valid_coarse, local_count)
    joint_mean, joint_var = merged(
        jnp.stack(
            [
                jnp.concatenate([proj_moments[0], low_stats[0, :extra]]),
                jnp.concatenate([proj_moments[1], low_stats[1, :extra] / 16.0]),
            ]
        ),
        local_count,
        pixel_count,
    )
    proj_mean, low_mean = joint_mean[:channels], joint_mean[channels:]
    proj_var, low_var = joint_var[:channels], joint_var[channels:]
    proj_act, proj_centered, proj_shaped, proj_scale = normalize(
        proj_z, valid_coarse, proj_mean, proj_var, gains[5], biases[5]
    )
    proj_act = proj_act.astype(jnp.bfloat16).astype(jnp.float32)
    low_vectors = widen(norm_vectors(low_mean, low_var, low_gain, low_bias))
    devices = device_count()
    decode_z, rows, upsampled = decode_forward(
        proj_act[0],
        up_table,
        low_flat,
        low_wide,
        low_vectors,
        masks,
        decode_full,
        devices,
    )
    decode_rows = hand_out(rows)
    refine_z, rows = refine_forward(decode_z, decode_rows, decode_params, masks, refine_full)
    refine_rows = hand_out(rows)
    logits, rows = classify(
        refine_z, grad_flat, refine_rows, refine_params, masks, w_cls, b_cls.reshape(1, -1)
    )
    logits = logits.reshape(logit_grad.shape)
    refine_sums = hand_out(rows)
    decode_local, rows, refine_totals, refine_kernel_grad = refine_backward(
        refine_z,
        grad_flat,
        refine_rows,
        refine_sums,
        refine_params,
        w_cls,
        decode_z,
        decode_rows,
        decode_params,
        masks,
        refine_full,
    )
    decode_sums = hand_out(rows)
    classes = w_cls.shape[1]
    cls_weight_grad = decode_sums[:classes, 2 * channels :].T
    cls_bias_grad = decode_sums[classes, 2 * channels : 2 * channels + classes]
    refine_gain, refine_bias = refine_totals[6], refine_totals[7]
    (
        proj_up,
        reduce_local,
        reduce_sums,
        decode_totals,
        decode_kernel_grad,
        low_kernel_grad,
    ) = decode_backward(
        decode_local,
        decode_z,
        decode_rows,
        decode_sums,
        decode_params,
        upsampled,
        low_flat,
        low_wide,
        low_vectors,
        down_table,
        masks,
        decode_full,
        coarse_shape,
    )
    decode_gain, decode_bias = decode_totals[6], decode_totals[7]
    proj_up = proj_up[None]
    reduce_gain, reduce_bias = reduce_sums[0, :extra], reduce_sums[1, :extra]

    proj_local, proj_gain, proj_bias = norm_grad_terms(
        proj_up, valid_coarse, proj_centered, proj_shaped
    )
    summed_pairs = gradient_sums([(proj_gain, proj_bias), (reduce_gain, reduce_bias)])
    proj_gain, proj_bias = summed_pairs[0]
    reduce_gain, reduce_bias = summed_pairs[1]
    flat_z = [item.reshape(height * columns, channels) for item in coarse_z]
    branch_vectors = jnp.concatenate(
        [
            norm_vectors(section_means[index], section_vars[index], gains[index], biases[index])
            for index in range(5)
        ],
        axis=1,
    )
    branch_counts = jnp.concatenate(
        [
            jnp.full((1, 4 * channels), 1.0) * pixel_count,
            jnp.full((1, channels), images_total, jnp.float32),
        ],
        axis=1,
    )
    proj_kernel_grad, branch_local, pool_local, rows = branch_back(
        proj_up.reshape(height * columns, channels),
        proj_z.reshape(height * columns, channels),
        norm_vectors(
            proj_mean,
            proj_var,
            gains[5],
            biases[5],
            proj_gain / pixel_count,
            proj_bias / pixel_count,
        ),
        joined_coarse.reshape(height * columns, -1),
        proj_full,
        flat_z,
        pool_wide,
        branch_vectors,
        mask_column,
        pool_mask,
        pool_inputs[0],
        devices,
    )
    rows = hand_out(rows)
    branch_dz = branch_grads(
        rows,
        branch_local,
        pool_local,
        flat_z,
        pool_wide,
        branch_vectors,
        branch_counts,
        mask_column,
        pool_mask,
    )
    flat_dz, pool_dz, branch_totals = list(branch_dz[:4]), branch_dz[4], branch_dz[5]
    last_pairs = [
        (
            branch_totals[0, index * channels : (index + 1) * channels],
            branch_totals[1, index * channels : (index + 1) * channels],
        )
        for index in range(5)
    ]
    low_vectors = widen(
        norm_vectors(
            low_mean,
            low_var,
            low_gain,
            low_bias,
            reduce_gain / fine_count,
            reduce_bias / fine_count,
        )
    )

    def low_late(tie):
        return low_backward(reduce_local, low_flat, low_wide, low_vectors, masks, tie)

    def input_late(tie):
        side_dz = [
            side_grads(
                flat_dz[branch + 1].reshape(1, height, columns, channels),
                ids_coarse,
                dilations[branch],
            ).reshape(height * columns, -1)
            for branch in range(3)
        ]
        return coarse_input(
            flat_dz[0],
            pool_dz,
            spread_rows,
            side_dz,
            parts,
            coarse_shape,
            features.shape[3],
            tie,
        )

    def weight_part(part, grads, tie=None):
        return coarse_weight(
            part,
            sides,
            grads[1:4],
            coarse_shape,
            (grads[0], pooled, grads[4]) if SCATTER.has_point(part) else None,
            tie,
        )

    owned, small_owned, low_level_grad, features_grad = scatter_taps(
        flat_dz + [pool_dz],
        [item.shape for item in small],
        [functools.partial(weight_part, part) for part in range(len(SCATTER.parts))],
        (proj_kernel_grad, decode_kernel_grad, low_kernel_grad, refine_kernel_grad),
        [low_late, input_late],
    )
    low_level_grad = low_level_grad.reshape(low_level.shape)
    features_grad = features_grad.reshape(features.shape)
    proj_owned, reduce_owned, decode_owned, refine_owned = small_owned
    point_owned, atrous_owned = SCATTER.restore(owned, w_atrous.shape)
    gains_grad = jnp.stack(
        [
            last_pairs[0][0],
            last_pairs[1][0],
            last_pairs[2][0],
            last_pairs[3][0],
            last_pairs[4][0],
            proj_gain,
            decode_gain,
            refine_gain,
        ]
    )
    biases_grad = jnp.stack(
        [
            last_pairs[0][1],
            last_pairs[1][1],
            last_pairs[2][1],
            last_pairs[3][1],
            last_pairs[4][1],
            proj_bias,
            decode_bias,
            refine_bias,
        ]
    )
    return (
        logits,
        features_grad,
        low_level_grad,
        point_owned,
        atrous_owned,
        proj_owned,
        reduce_owned,
        decode_owned,
        refine_owned,
        cls_weight_grad,
        cls_bias_grad,
        gains_grad,
        biases_grad,
        reduce_gain,
        reduce_bias,
    )


def solution(mesh):
    in_specs = (
        P(("wide", "narrow"), None, None, None),
        P(("wide", "narrow"), None, None, None),
        P(("wide", "narrow"), None),
        P(None, "wide", "narrow"),
        P(None, None, "wide", "narrow"),
        P("wide", "narrow"),
        P("wide", "narrow"),
        P(None, "narrow", "wide"),
        P(None, "wide", "narrow"),
        P(),
        P(),
        P(),
        P(),
        P(),
        P(),
        P(("wide", "narrow"), None, None, None),
    )
    out_specs = (
        P(("wide", "narrow"), None, None, None),
        P(("wide", "narrow"), None, None, None),
        P(("wide", "narrow"), None, None, None),
        P(None, "wide", "narrow"),
        P(None, None, "wide", "narrow"),
        P("wide", "narrow"),
        P("wide", "narrow"),
        P(None, "narrow", "wide"),
        P(None, "wide", "narrow"),
        P(),
        P(),
        P(),
        P(),
        P(),
        P(),
    )
    return jax.shard_map(
        per_device, mesh=mesh, in_specs=in_specs, out_specs=out_specs, check_vma=False
    )
```

```python
import functools

import jax
import jax.numpy as jnp
from jax import lax
from jax.experimental import pallas as pl
from jax.experimental.pallas import tpu as pltpu
from jax.sharding import PartitionSpec as P

epsilon = 1e-05
highest = lax.Precision.HIGHEST
dilations = (6, 12, 18)
ROUNDS = 4
VMEM_BYTES = 48 * 1024 * 1024


class Layout:
    def __init__(self, chunks, point_chunk):
        self.chunks = chunks
        self.point_chunk = point_chunk
        self.parts = [(index, index + 1) for index in range(0, len(chunks), 2)]
        self.sizes = [[chunks[index] for index in part] for part in self.parts]
        places = []
        for chunk, size in enumerate(chunks):
            places += [(chunk, tap) for tap in range(2 if chunk == point_chunk else 0, size)]
        self.rows = [
            [(line,) + places[9 * branch + 3 * line] for line in range(3)] for branch in range(3)
        ]

    def part_of(self, chunk):
        return chunk // 2

    def place(self, chunk, tap):
        return tap + (self.chunks[chunk - 1] if chunk % 2 else 0)

    def part_rows(self, part):
        return [
            (branch, line, chunk, tap)
            for branch, rows in enumerate(self.rows)
            for line, chunk, tap in rows
            if chunk in self.parts[part]
        ]

    def has_point(self, part):
        return self.point_chunk in self.parts[part]

    def order(self, point, atrous):
        flat = atrous.reshape((-1,) + atrous.shape[2:])
        before = sum(self.chunks[: self.point_chunk])
        parts = []
        start = 0
        for part, sizes in enumerate(self.sizes):
            size = sum(sizes)
            if self.has_point(part):
                pieces = [flat[start:before], point, flat[before : start + size - 2]]
                parts.append(jnp.concatenate([item for item in pieces if item.shape[0]]))
                start += size - 2
            else:
                parts.append(flat[start : start + size])
                start += size
        return parts

    def restore(self, parts, shape):
        flat = jnp.concatenate(parts)
        before = sum(self.chunks[: self.point_chunk])
        atrous = jnp.concatenate([flat[:before], flat[before + 2 :]])
        return (flat[before : before + 2], atrous.reshape(shape))


GATHER = Layout((5, 6, 6, 3, 3, 6), 0)
SCATTER = Layout((3, 3, 5, 6, 6, 6), 2)


def exchange(values, axis, bit):
    size = lax.axis_size(axis)
    return lax.ppermute(values, axis, [(place, place ^ bit) for place in range(size)])


def rotate(values, axis, step, stride):
    size = lax.axis_size(axis)
    rounds = size // stride
    pairs = []
    for place in range(size):
        outer, inner = place // stride, place % stride
        pairs.append((place, ((outer + step) % rounds) * stride + inner))
    return lax.ppermute(values, axis, pairs)


def device_count():
    return lax.axis_size("wide") * lax.axis_size("narrow")


def hand_out(rows):
    return lax.all_to_all(rows, ("wide", "narrow"), 0, 0, tiled=True)


def from_all(values):
    return hand_out(jnp.broadcast_to(values[None], (device_count(),) + values.shape))


def merge_rows(counts, means, squares):
    total = jnp.sum(counts, axis=0)
    mean = jnp.sum(counts * means, axis=0) / total
    gap = means - mean[None]
    return (total, mean, jnp.sum(squares + counts * gap * gap, axis=0))


def local_moments(values, valid_map, count):
    axes = tuple(range(values.ndim - 1))
    mean = jnp.sum(values * valid_map, axis=axes) / count
    centered = values - mean
    return (mean, jnp.sum(centered * centered * valid_map, axis=axes))


def place():
    wide = lax.axis_index("wide")
    narrow = lax.axis_index("narrow")
    return (wide // 2, wide % 2, narrow // 2, narrow % 2)


def share_core(shard):
    core = place()[3]
    half = shard.shape[1] // 2
    parts = shard.reshape(shard.shape[0], 2, half, shard.shape[2])
    kept = lax.dynamic_index_in_dim(parts, core, 1, keepdims=False)
    given = lax.dynamic_index_in_dim(parts, 1 - core, 1, keepdims=False)
    got = exchange(given, "narrow", 1)
    lower = jnp.where(core == 0, kept, got)
    upper = jnp.where(core == 0, got, kept)
    return jnp.concatenate([lower, upper], axis=2)


def tuned():
    return lax.axis_size("wide") == 2 * ROUNDS and lax.axis_size("narrow") == 4


def kernel_place():
    values = jnp.stack(place()).astype(jnp.int32)
    return values if tuned() else jnp.zeros_like(values)


def tied(values, earlier):
    mark = earlier[(0,) * earlier.ndim]
    return jnp.where(mark == mark, values, jnp.zeros_like(values))


def one_step(body, outs, args, specs=None, tie=None, vmem=32 * 1024 * 1024):
    def whole_spec(array):
        return pl.BlockSpec(array.shape, lambda step: (0,) * len(array.shape))

    specs = list(specs or [None] * len(args))
    run = body
    if tie is not None:
        ties = tie if isinstance(tie, list) else [tie]
        args = ties + list(args)
        specs = [pl.BlockSpec(memory_space=pl.ANY)] * len(ties) + specs

        def run(*refs):
            body(*refs[len(ties) :])

    return pl.pallas_call(
        run,
        out_shape=outs,
        grid=(1,),
        in_specs=[spec or whole_spec(arg) for spec, arg in zip(specs, args)],
        out_specs=[whole_spec(out) for out in outs],
        compiler_params=pltpu.CompilerParams(vmem_limit_bytes=vmem),
        cost_estimate=cost(0, args),
        name="move",
    )(*args)


def entry_spec(array, index):
    block = (1,) + array.shape[1:]
    return pl.BlockSpec(block, lambda step: (index,) + (0,) * (len(block) - 1))


def cut(sizes):
    return [slice(sum(sizes[:index]), sum(sizes[: index + 1])) for index in range(len(sizes))]


def pass_on(values, tie):
    def body(source, target):
        target[...] = source[...]

    outs = [jax.ShapeDtypeStruct(values.shape, values.dtype)]
    return one_step(body, outs, [values], None, tie)[0]


def gather_depth(values):
    return [exchange(values, "wide", 2 * flip) for flip in range(1, ROUNDS)]


def lay_out(sizes, own, others, tie=None):
    shape = own.shape[1:]
    outs = [jax.ShapeDtypeStruct((ROUNDS, size) + shape, own.dtype) for size in sizes]

    def body(*refs):
        for target, taps in zip(refs[ROUNDS:], cut(sizes)):
            for slot, source in enumerate(refs[:ROUNDS]):
                target[slot] = source[taps]

    return one_step(body, outs, [own] + list(others), tie=tie)


def pair_up(values, others, tie=None):
    outs = [jax.ShapeDtypeStruct((2,) + item.shape, item.dtype) for item in values]
    count = len(outs)

    def body(*refs):
        for index in range(count):
            refs[2 * count + index][0] = refs[index][...]
            refs[2 * count + index][1] = refs[count + index][...]

    return one_step(body, outs, list(values) + list(others), tie=tie)


def pair_cut(sizes, values, others, tie=None):
    count = len(values)
    outs = [
        jax.ShapeDtypeStruct((2, ROUNDS, size) + values[0].shape[2:], values[0].dtype)
        for part in sizes
        for size in part
    ]

    def body(*refs):
        for index in range(count):
            taps = cut([part[index] for part in sizes])
            for part in range(len(sizes)):
                target = refs[2 * count + part * count + index]
                for half in range(2):
                    target[half] = refs[half * count + index][:, taps[part]]

    results = one_step(body, outs, list(values) + list(others), tie=tie)
    return [results[part * count : (part + 1) * count] for part in range(len(sizes))]


def pair_all(values, others, tie=None):
    count = len(values)
    shape = values[0].shape
    sizes = [item.shape[2] for item in values]
    outs = [jax.ShapeDtypeStruct((2,) + shape[:2] + (sum(sizes),) + shape[3:], values[0].dtype)]

    def body(*refs):
        target = refs[2 * count]
        for index, taps in enumerate(cut(sizes)):
            target[0, :, :, taps] = refs[index][...]
            target[1, :, :, taps] = refs[count + index][...]

    return one_step(body, outs, list(values) + list(others), tie=tie)[0]


def first_sums(sizes, keep, got, tie=None):
    tail = keep.shape[4:]
    outs = [jax.ShapeDtypeStruct((2, ROUNDS, size) + tail, jnp.bfloat16) for size in sizes]

    def body(keep_ref, got_ref, *targets):
        for target, taps in zip(targets, cut(sizes)):
            total = keep_ref[0, :, :, taps].astype(jnp.float32)
            total = total + got_ref[0, :, :, taps].astype(jnp.float32)
            target[...] = total.astype(jnp.bfloat16)

    return one_step(body, outs, [keep, got], [entry_spec(keep, 1), entry_spec(got, 1)], tie)


def second_sums(sizes, keep, got, values, tie=None):
    tail = keep.shape[4:]
    outs = [jax.ShapeDtypeStruct((ROUNDS, sum(sizes)) + tail, jnp.float32)]
    outs += [jax.ShapeDtypeStruct((ROUNDS, size) + tail, jnp.bfloat16) for size in sizes]
    count = len(sizes)

    def body(keep_ref, got_ref, *refs):
        kept = refs[count]
        for index, taps in enumerate(cut(sizes)):
            for half in range(2):
                total = keep_ref[0, half, :, taps].astype(jnp.float32)
                total = total + got_ref[0, half, :, taps].astype(jnp.float32)
                total = total + refs[index][half].astype(jnp.float32)
                if half:
                    refs[count + 1 + index][...] = total.astype(jnp.bfloat16)
                else:
                    kept[:, taps] = total

    specs = [entry_spec(keep, 0), entry_spec(got, 0)] + [None] * count
    results = one_step(body, outs, [keep, got] + list(values), specs, tie)
    return (results[0], results[1:])


def deep_sums(sizes, kept, values, tie=None):
    shape = (2,) + kept.shape[1:]
    outs = [jax.ShapeDtypeStruct(shape, dtype) for dtype in (jnp.float32, jnp.bfloat16)]
    count = len(sizes)

    def body(kept_ref, *refs):
        for slot in range(ROUNDS):
            target = refs[count + slot // 2]
            for value, taps in zip(refs, cut(sizes)):
                total = kept_ref[slot, taps] + value[slot].astype(jnp.float32)
                target[slot % 2, taps] = total.astype(target.dtype)

    return one_step(body, outs, [kept] + list(values), None, tie)


def near_sums(kept, far, tie=None):
    shape = kept.shape[1:]
    outs = [jax.ShapeDtypeStruct(shape, dtype) for dtype in (jnp.float32, jnp.bfloat16)]

    def body(kept_ref, far_ref, *targets):
        for slot, target in enumerate(targets):
            total = kept_ref[slot] + far_ref[slot].astype(jnp.float32)
            target[...] = total.astype(target.dtype)

    return one_step(body, outs, [kept, far], None, tie)


def last_sums(kept, near, tie=None):
    def body(kept_ref, near_ref, target):
        target[...] = kept_ref[...] + near_ref[...].astype(jnp.float32)

    outs = [jax.ShapeDtypeStruct(kept.shape, jnp.float32)]
    return one_step(body, outs, [kept, near], None, tie)[0]


def chunk_order(index):
    return [("wide", 1), ("narrow", 2)] if index % 2 == 0 else [("narrow", 2), ("wide", 1)]


def gather_taps(weights, small, fillers, kernels, prepared):
    rounds = ROUNDS
    sizes = GATHER.sizes
    shapes = [item.shape for item in small]
    if not tuned():
        parts = []
        for part, values in zip(GATHER.parts, weights):
            full = lax.all_gather(values, "narrow", axis=2, tiled=True)
            full = lax.all_gather(full, "wide", axis=1, tiled=True)
            rows = full.shape[1] // (4 * rounds)
            full = full.reshape(full.shape[0], rounds, 2, 2, rows, 2, full.shape[2] // 2)
            start = 0
            pieces = []
            for index in part:
                piece = full[start : start + GATHER.chunks[index]]
                start += GATHER.chunks[index]
                order = (3, 5, 2, 1, 0, 4, 6) if index % 2 == 0 else (3, 2, 5, 1, 0, 4, 6)
                pieces.append(piece.transpose(order))
            joined = jnp.concatenate(pieces, axis=4)
            parts.append((joined[0], joined[1]))
        flat = pack_small(small)
        everything = lax.all_gather(flat, ("wide", "narrow"))
        everything = everything.reshape(lax.axis_size("wide"), lax.axis_size("narrow"), -1)
        unpacked = unpack_small(everything, small)
        ready = fillers[0]()
        results = fillers[1](*unpacked)
        result = None
        for pair, kernel in zip(parts, kernels):
            result = kernel(ready, pair, result)
        return (parts, unpacked, ready, results, result)

    def along(part, stacks, turn):
        return [
            exchange(stack, *chunk_order(index)[turn]) for stack, index in zip(stacks, GATHER.parts[part])
        ]

    def across(values):
        return (values, exchange(values, "narrow", 1))

    first, second = sizes[1], sizes[2]
    weights = [
        weights[0],
        jnp.concatenate(
            [
                weights[1][: first[0]],
                weights[2][: second[0]],
                weights[1][first[0] :],
                weights[2][second[0] :],
            ]
        ),
    ]
    joint = [first[0] + second[0], first[1] + second[1]]
    shared = [share_core(values) for values in weights]
    z0 = gather_depth(shared[0])
    small = small_block(small)
    xs = exchange(small, "wide", 1)
    small = pair_up([small], [xs], shared[1])[0]
    ys = exchange(small, "narrow", 2)
    small = pair_up([small], [ys])[0]
    s0 = lay_out(sizes[0], shared[0], z0, small)
    f0 = along(0, s0, 0)
    z1 = gather_depth(shared[1])
    s0 = pair_up(s0, f0, [z1[1]] + prepared)
    g0 = along(0, s0, 1)
    ready = fillers[0]()
    s1 = lay_out(joint, shared[1], z1, s0[0])
    f1 = along(0, s1, 0)
    small = pass_on(small, s1[0])
    zs = gather_depth(small)
    p0 = across(pair_all(s0, g0, s1[0]))
    s1, s2 = pair_cut([first, second], s1, f1, zs[0])
    g1 = along(0, s1, 1)
    g2 = along(0, s2, 1)
    result = kernels[0](ready, p0, None, s1[0])
    small = lay_out([2], small, zs, result[0][0])[0]
    cs = exchange(small, "narrow", 1)
    p1 = across(pair_all(s1, g1, small))
    unpacked = unpack_block(small, cs, shapes=shapes)
    results = fillers[1](*unpacked)
    result = kernels[1](ready, p1, result)
    p2 = across(pair_all(s2, g2, p1[0]))
    result = kernels[2](ready, p2, result)
    return ([p0, p1, p2], unpacked, ready, results, result)


def scatter_taps(grads, shapes, kernels, pack, fillers):
    rounds = ROUNDS
    if not tuned():
        owned = []
        for part, kernel in zip(SCATTER.parts, kernels):
            joined = jnp.stack(kernel(grads))
            pieces = []
            for index, taps in zip(part, cut([SCATTER.chunks[index] for index in part])):
                piece = joined[:, :, :, :, taps]
                order = (4, 3, 1, 0, 5, 2, 6) if index % 2 == 0 else (4, 3, 2, 0, 5, 1, 6)
                piece = piece.transpose(order)
                pieces.append(piece.reshape(piece.shape[0], -1, 2 * piece.shape[6]))
            full = jnp.concatenate(pieces)
            full = lax.psum_scatter(full, "wide", scatter_dimension=1, tiled=True)
            full = lax.psum_scatter(full, "narrow", scatter_dimension=2, tiled=True)
            owned.append(full.astype(jnp.float32))
        low, low_weight = fillers[0](grads[0])
        small = pack_grads(low_weight, *pack, shapes)
        small = lax.psum_scatter(small, "wide", scatter_dimension=0, tiled=True)
        small = lax.psum_scatter(small, "narrow", scatter_dimension=1, tiled=True)
        small = unpack_grads(small[0, 0].astype(jnp.float32), shapes)
        return (owned, small, low, fillers[1](None))

    sizes = SCATTER.sizes

    def across(pair):
        return (pair[0], exchange(pair[1], "narrow", 1))

    def along(indices, values, turn):
        return [
            exchange(value, *chunk_order(index)[turn]) for value, index in zip(values, indices)
        ]

    def far(sent):
        return exchange(sent, "wide", 4)

    def near(sent):
        return exchange(sent, "wide", 2)

    a, b, c = 2, 1, 0
    pair_a = across(kernels[a](grads))
    pair_b = across(kernels[b](grads, tie=pair_a[0]))
    sent = first_sums(sizes[a], *pair_a, pair_b[0])
    first_a = along(SCATTER.parts[a], sent, 0)
    low, low_weight = fillers[0](sent[0])
    pair_s = across(pack_block(pack[0], low_weight, *pack[1:], shapes=shapes, tie=low_weight))
    sizes_s = [pair_s[0].shape[3]]
    pair_c = across(kernels[c](grads, tie=pair_s[0]))
    kept_a, sent = second_sums(sizes[a], *pair_a, first_a, pair_c[0])
    second_a = along(SCATTER.parts[a], sent, 1)
    sent = first_sums(sizes[b], *pair_b, sent[0])
    first_b = along(SCATTER.parts[b], sent, 0)
    kept_a, sent = deep_sums(sizes[a], kept_a, second_a, sent[0])
    far_a = far(sent)
    sent = first_sums(sizes_s, *pair_s, sent)
    first_s = along((0,), sent, 0)
    filled = fillers[1](sent[0])
    kept_b, sent = second_sums(sizes[b], *pair_b, first_b, filled)
    second_b = along(SCATTER.parts[b], sent, 1)
    sent = first_sums(sizes[c], *pair_c, sent[0])
    first_c = along(SCATTER.parts[c], sent, 0)
    kept_s, sent = second_sums(sizes_s, *pair_s, first_s, sent[0])
    second_s = along((0,), sent, 1)
    total_a, sent = near_sums(kept_a, far_a, sent[0])
    near_a = near(sent)
    kept_b, sent = deep_sums(sizes[b], kept_b, second_b, sent)
    far_b = far(sent)
    kept_c, sent = second_sums(sizes[c], *pair_c, first_c, sent)
    second_c = along(SCATTER.parts[c], sent, 1)
    kept_s, sent = deep_sums(sizes_s, kept_s, second_s, sent[0])
    far_s = far(sent)
    total_a = last_sums(total_a, near_a, sent)
    kept_c, sent = deep_sums(sizes[c], kept_c, second_c, total_a)
    far_c = far(sent)
    total_b, sent = near_sums(kept_b, far_b, sent)
    near_b = near(sent)
    total_s, sent = near_sums(kept_s, far_s, sent)
    near_s = near(sent)
    total_c, sent = near_sums(kept_c, far_c, sent)
    near_c = near(sent)
    total_b = last_sums(total_b, near_b, sent)
    total_s = last_sums(total_s, near_s, total_b)
    total_c = last_sums(total_c, near_c, total_s)
    owned = [settle_core(total) for total in (total_c, total_b, total_a)]
    small = settle_small(total_s, shapes)
    return (owned, small, low, filled)


def row_span(dilation, row, height):
    step = (row - 1) * dilation
    return (max(step, 0), max(-step, 0), height - abs(step))


def tap_matrix(pair, chunk, tap, place_ref):
    row, core = place_ref[2], place_ref[3]
    flip = lax.rem(pl.program_id(0) + place_ref[1], 2)
    place = GATHER.place(chunk, tap)

    def half(ref):
        if chunk % 2 == 0:
            sides = [ref[y, flip, 0, place] for y in (row, 1 - row)]
        else:
            sides = [ref[flip, y, 0, place] for y in (row, 1 - row)]
        return jnp.concatenate(sides, axis=1)

    mine = half(pair[0])
    other = half(pair[1])
    lower = jnp.where(core == 0, mine, other)
    upper = jnp.where(core == 0, other, mine)
    return jnp.concatenate([lower, upper], axis=0)


def part_spec(array):
    def index_map(step, place_ref):
        return (0, 0, lax.bitwise_xor(step // 2, place_ref[0]), 0, 0, 0)

    return pl.BlockSpec((2, 2, 1) + array.shape[3:], index_map)


def whole_cost(flops, arrays):
    total = 0
    for array in arrays:
        size = array.dtype.itemsize
        for extent in array.shape:
            size *= extent
        total += size
    return pl.CostEstimate(flops=int(flops), bytes_accessed=total, transcendentals=0)


def cost(flops, arrays):
    return pl.CostEstimate(flops=1, bytes_accessed=1, transcendentals=0)


def coarse_flops(rows, shape, width):
    height, columns, channels = shape
    extents = sum(row_span(dilations[branch], line, height)[2] for branch, line in rows)
    return 2 * 3 * extents * columns * channels * width


def full_spec(array):
    return pl.BlockSpec(array.shape, lambda step, place_ref: (0,) * array.ndim)


def lane_spec(array):
    return pl.BlockSpec(
        (array.shape[0], array.shape[1] // (2 * ROUNDS)), lambda step, place_ref: (0, step)
    )


def store_moments(z_ref, mask_ref, stats_ref):
    mask = mask_ref[...]
    count = jnp.sum(mask)
    values = z_ref[...]
    mean = jnp.sum(values * mask, axis=0, keepdims=True) / count
    centered = (values - mean) * mask
    stats_ref[0:1, :] = mean
    stats_ref[1:2, :] = jnp.sum(centered * centered, axis=0, keepdims=True)


def behind_tie(kernel):
    def run(place_ref, tie_ref, *refs):
        kernel(place_ref, *refs)

    return run


def coarse_forward_kernel(plan, place_ref, *refs):
    refs = list(refs)
    mask_ref = refs.pop(0)
    center = refs.pop(0)
    outer = {branch: (refs.pop(0), refs.pop(0)) for branch in plan["branches"]}
    before = {branch: refs.pop(0) for branch in plan["begun"]}
    if plan["pool"]:
        member_ref = refs.pop(0)
        sizes_ref = refs.pop(0)
    pair = (refs.pop(0), refs.pop(0))
    results = {branch: refs.pop(0) for branch in plan["branches"]}
    stats = {branch: refs.pop(0) for branch in plan["done"]}
    step = pl.program_id(0)

    @pl.when(step == 0)
    def _():
        for branch in plan["branches"]:
            if branch in before:
                results[branch][...] = before[branch][...]
            else:
                results[branch][...] = jnp.zeros_like(results[branch])

    columns = plan["columns"]
    for branch, row, chunk, tap in plan["rows"]:
        source, target, extent = row_span(dilations[branch], row, plan["height"])
        matrix = jnp.concatenate(
            [tap_matrix(pair, chunk, tap + k, place_ref) for k in range(3)],
            axis=0,
        )
        rows_in = pl.ds(source * columns, extent * columns)
        rows_out = pl.ds(target * columns, extent * columns)
        sides = (outer[branch][0], center, outer[branch][1])
        values = jnp.concatenate([side[rows_in, :] for side in sides], axis=1)
        results[branch][rows_out, :] += jnp.dot(
            values, matrix, preferred_element_type=jnp.float32
        )
    if plan["pool"]:
        point_ref, point_stats_ref, pool_ref, pooled_ref = refs

        @pl.when(step == 0)
        def _():
            point_ref[...] = jnp.zeros_like(point_ref)
            pool_ref[...] = jnp.zeros_like(pool_ref)

        values = center[...]
        point_ref[...] += jnp.dot(
            values, tap_matrix(pair, GATHER.point_chunk, 0, place_ref), preferred_element_type=jnp.float32
        )
        pooled = jnp.dot(member_ref[...], values, preferred_element_type=jnp.float32)
        pooled = (pooled * sizes_ref[...]).astype(jnp.bfloat16)
        pooled_ref[...] = pooled
        pool_ref[...] += jnp.dot(
            pooled, tap_matrix(pair, GATHER.point_chunk, 1, place_ref), preferred_element_type=jnp.float32
        )

    @pl.when(step == 2 * ROUNDS - 1)
    def _():
        for branch in plan["done"]:
            store_moments(results[branch], mask_ref, stats[branch])
        if plan["pool"]:
            store_moments(point_ref, mask_ref, point_stats_ref)


def coarse_forward(part, mask, sides, pair, shape, begun, pool=None, tie=None):
    height, columns, channels = shape
    positions = height * columns
    rows = GATHER.part_rows(part)
    branches = sorted({row[0] for row in rows})
    done = [branch for branch in branches if GATHER.rows[branch][-1][1] in GATHER.parts[part]]
    plan = {
        "pool": pool is not None,
        "chunks": GATHER.parts[part],
        "branches": branches,
        "begun": [branch for branch in branches if branch in begun],
        "done": done,
        "columns": columns,
        "height": height,
        "rows": rows,
    }
    center = sides[0][1]
    args = [mask, center]
    specs = [full_spec(mask), lane_spec(center)]
    for branch in branches:
        args += [sides[branch][0], sides[branch][2]]
        specs += [lane_spec(center)] * 2
    for branch in plan["begun"]:
        args.append(begun[branch])
        specs.append(full_spec(begun[branch]))
    if pool:
        args += list(pool)
        specs += [full_spec(item) for item in pool]
    args += list(pair)
    specs += [part_spec(item) for item in pair]
    kernel = functools.partial(coarse_forward_kernel, plan)
    if tie is not None:
        kernel = behind_tie(kernel)
        args.insert(0, tie)
        specs.insert(0, pl.BlockSpec(memory_space=pl.ANY))
    flat = jax.ShapeDtypeStruct((positions, channels), jnp.float32)
    small = jax.ShapeDtypeStruct((8, channels), jnp.float32)
    outs = [flat] * len(branches) + [small] * len(done)
    if pool:
        outs += [flat, small, small, jax.ShapeDtypeStruct((8, center.shape[1]), jnp.bfloat16)]
    out_specs = [full_spec(item) for item in outs]
    if pool:
        out_specs[-1] = lane_spec(outs[-1])
    results = pl.pallas_call(
        kernel,
        out_shape=outs,
        grid_spec=pltpu.PrefetchScalarGridSpec(
            num_scalar_prefetch=1, grid=(2 * ROUNDS,), in_specs=specs, out_specs=out_specs
        ),
        compiler_params=pltpu.CompilerParams(vmem_limit_bytes=VMEM_BYTES),
        cost_estimate=cost(
            coarse_flops([row[:2] for row in rows], shape, center.shape[1])
            + (2 * positions * channels * center.shape[1] if pool else 0),
            args + outs,
        ),
        name="coarse_forward",
    )(kernel_place(), *args)
    sums = dict(zip(branches, results))
    stats = dict(zip(done, results[len(branches) :]))
    return (sums, stats, results[len(branches) + len(done) :])


def coarse_weight_kernel(plan, place_ref, *refs):
    refs = list(refs)
    center = refs.pop(0)
    outer = {branch: (refs.pop(0), refs.pop(0)) for branch in plan["branches"]}
    grads = {branch: refs.pop(0) for branch in plan["branches"]}
    if plan["pool"]:
        point_ref, pooled_ref, pool_ref = refs.pop(0), refs.pop(0), refs.pop(0)
    outs = (refs.pop(0), refs.pop(0))
    row, core = place_ref[2], place_ref[3]
    flip = lax.rem(pl.program_id(0) + place_ref[1], 2)
    rows, cols = outs[0].shape[-2:]
    columns = plan["columns"]

    def store(chunk, tap, value):
        value = value.astype(jnp.bfloat16)
        lower, upper = value[:rows], value[rows:]
        mine = jnp.where(core == 0, lower, upper)
        other = jnp.where(core == 0, upper, lower)
        place = SCATTER.place(chunk, tap)
        for ref, part in zip(outs, (mine, other)):
            for side, lane_part in ((row, part[:, :cols]), (1 - row, part[:, cols:])):
                if chunk % 2 == 0:
                    ref[flip, side, 0, place] = lane_part
                else:
                    ref[side, flip, 0, place] = lane_part

    across = (((0,), (0,)), ((), ()))
    for branch, line, chunk, tap in plan["rows"]:
        source, target, extent = row_span(dilations[branch], line, plan["height"])
        sides = (outer[branch][0], center, outer[branch][1])
        values = jnp.concatenate(
            [side[pl.ds(source * columns, extent * columns), :] for side in sides], axis=1
        )
        result = lax.dot_general(
            values,
            grads[branch][pl.ds(target * columns, extent * columns), :],
            across,
            preferred_element_type=jnp.float32,
        )
        for k in range(3):
            store(chunk, tap + k, result[2 * rows * k : 2 * rows * (k + 1)])
    if plan["pool"]:
        for tap, left, right in ((0, center, point_ref), (1, pooled_ref, pool_ref)):
            store(
                SCATTER.point_chunk,
                tap,
                lax.dot_general(
                    left[...], right[...], across, preferred_element_type=jnp.float32
                ),
            )


def coarse_weight(part, sides, grads, shape, pool=None, tie=None):
    height, columns, channels = shape
    rows = SCATTER.part_rows(part)
    branches = sorted({row[0] for row in rows})
    plan = {
        "pool": pool is not None,
        "branches": branches,
        "chunks": SCATTER.parts[part],
        "rows": rows,
        "columns": columns,
        "height": height,
    }
    center = sides[0][1]
    args = [center]
    specs = [lane_spec(center)]
    for branch in branches:
        args += [sides[branch][0], sides[branch][2]]
        specs += [lane_spec(center)] * 2
    for branch in branches:
        args.append(grads[branch])
        specs.append(full_spec(grads[branch]))
    if pool:
        args += list(pool)
        specs += [full_spec(pool[0]), lane_spec(pool[1]), full_spec(pool[2])]
    kernel = functools.partial(coarse_weight_kernel, plan)
    if tie is not None:
        kernel = behind_tie(kernel)
        args.insert(0, tie)
        specs.insert(0, pl.BlockSpec(memory_space=pl.ANY))
    total = sum(SCATTER.sizes[part])
    tail = (total, center.shape[1] // (4 * ROUNDS), channels // 2)
    outs = [jax.ShapeDtypeStruct((2, 2, ROUNDS) + tail, jnp.bfloat16)] * 2
    out_specs = [part_spec(item) for item in outs]
    results = pl.pallas_call(
        kernel,
        out_shape=outs,
        grid_spec=pltpu.PrefetchScalarGridSpec(
            num_scalar_prefetch=1, grid=(2 * ROUNDS,), in_specs=specs, out_specs=out_specs
        ),
        compiler_params=pltpu.CompilerParams(vmem_limit_bytes=VMEM_BYTES),
        cost_estimate=cost(
            coarse_flops([row[:2] for row in rows], shape, center.shape[1])
            + (2 * height * columns * channels * center.shape[1] if pool else 0),
            args + outs,
        ),
        name="coarse_weight",
    )(kernel_place(), *args)
    return (results[0], results[1])


def coarse_input_kernel(plan, place_ref, *refs):
    refs = list(refs)
    point_ref, pool_ref, spread_ref = refs.pop(0), refs.pop(0), refs.pop(0)
    grads = [refs.pop(0) for _ in range(3)]
    pairs = [(refs.pop(0), refs.pop(0)) for _ in GATHER.parts]
    point_pair = pairs[GATHER.part_of(GATHER.point_chunk)]
    out_ref, total_ref = refs
    columns = plan["columns"]
    turned = (((1,), (1,)), ((), ()))
    total_ref[...] = lax.dot_general(
        point_ref[...],
        tap_matrix(point_pair, GATHER.point_chunk, 0, place_ref),
        turned,
        preferred_element_type=jnp.float32,
    )
    pooled = lax.dot_general(
        pool_ref[...],
        tap_matrix(point_pair, GATHER.point_chunk, 1, place_ref),
        turned,
        preferred_element_type=jnp.float32,
    )
    total_ref[...] += jnp.dot(
        spread_ref[...], pooled, preferred_element_type=jnp.float32, precision=highest
    )
    for branch, rows in enumerate(plan["rows"]):
        for line, chunk, tap in rows:
            source, target, extent = row_span(dilations[branch], line, plan["height"])
            matrix = jnp.concatenate(
                [
                    tap_matrix(pairs[GATHER.part_of(chunk)], chunk, tap + k, place_ref)
                    for k in range(3)
                ],
                axis=1,
            )
            total_ref[pl.ds(source * columns, extent * columns), :] += lax.dot_general(
                grads[branch][pl.ds(target * columns, extent * columns), :],
                matrix,
                turned,
                preferred_element_type=jnp.float32,
            )
    out_ref[...] = total_ref[...].astype(jnp.bfloat16)


def coarse_input(point_dz, pool_dz, spread, grads, parts, shape, width, tie=None):
    height, columns, channels = shape
    plan = {
        "columns": columns,
        "height": height,
        "rows": GATHER.rows,
    }
    args = [point_dz, pool_dz, spread] + list(grads)
    specs = [full_spec(item) for item in args]
    for pair in parts:
        args += list(pair)
        specs += [part_spec(item) for item in pair]
    kernel = functools.partial(coarse_input_kernel, plan)
    if tie is not None:
        kernel = behind_tie(kernel)
        args.insert(0, tie)
        specs.insert(0, pl.BlockSpec(memory_space=pl.ANY))
    out = jax.ShapeDtypeStruct((height * columns, width), jnp.bfloat16)
    return pl.pallas_call(
        kernel,
        out_shape=out,
        grid_spec=pltpu.PrefetchScalarGridSpec(
            num_scalar_prefetch=1,
            grid=(2 * ROUNDS,),
            in_specs=specs,
            out_specs=lane_spec(out),
            scratch_shapes=[pltpu.VMEM((height * columns, width // (2 * ROUNDS)), jnp.float32)],
        ),
        compiler_params=pltpu.CompilerParams(vmem_limit_bytes=VMEM_BYTES),
        cost_estimate=cost(
            coarse_flops([(b, k) for b in range(3) for k in range(3)], shape, width)
            + 2 * height * columns * channels * width,
            args + [out],
        ),
        name="coarse_input",
    )(kernel_place(), *args)


STRIP = 16


def norm_vectors(mean, variance, gain, bias, *more):
    rows = [mean, lax.rsqrt(variance + epsilon), gain, bias] + list(more)
    rows += [jnp.zeros_like(mean)] * (8 - len(rows))
    return jnp.stack(rows)


def sigmoid(values):
    return 0.5 * jnp.tanh(0.5 * values) + 0.5


def vector(ref, index):
    return ref[index : index + 1, :]


def shaped_of(values, vector_ref):
    centered = (values - vector(vector_ref, 0)) * vector(vector_ref, 1)
    return (centered, centered * vector(vector_ref, 2) + vector(vector_ref, 3))


def slope_of(shaped, gate):
    return gate * (1.0 + shaped * (1.0 - gate))


def merge_vectors(rows_ref, params_ref, vector_ref, sums_ref=None):
    width = vector_ref.shape[1]
    means = rows_ref[:, :width]
    squares = rows_ref[:, width : 2 * width]
    counts = rows_ref[:, 2 * width : 2 * width + 1]
    total = jnp.sum(counts, axis=0, keepdims=True)
    mean = jnp.sum(counts * means, axis=0, keepdims=True) / total
    gap = means - mean
    variance = jnp.sum(squares + counts * gap * gap, axis=0, keepdims=True) / total
    vector_ref[0:1, :] = mean
    vector_ref[1:2, :] = lax.rsqrt(variance + epsilon)
    vector_ref[2:4, :] = params_ref[...]
    if sums_ref is not None:
        for index in range(2):
            part = sums_ref[:, index * width : (index + 1) * width]
            vector_ref[6 + index : 7 + index, :] = jnp.sum(part, axis=0, keepdims=True)
            vector_ref[4 + index : 5 + index, :] = vector_ref[6 + index : 7 + index, :] / total


def send_rows(rows_ref, pieces):
    joined = jnp.concatenate(pieces, axis=1)
    rows_ref[...] = jnp.broadcast_to(joined, rows_ref.shape)


def send_moments(rows_ref, stats_ref, masks_ref, steps):
    count = jnp.sum(masks_ref[:, 0:1]) * steps
    send_rows(
        rows_ref,
        [stats_ref[0:1, :], stats_ref[1:2, :], jnp.full((1, 128), 1.0, jnp.float32) * count],
    )


def lag_specs(steps):
    def ahead(array, block):
        return pl.BlockSpec(block, lambda step: (jnp.minimum(step, steps - 1), 0))

    def behind(array, block):
        return pl.BlockSpec(block, lambda step: (jnp.maximum(step - 1, 0), 0))

    return (ahead, behind)


def whole(array):
    return pl.BlockSpec(array.shape, lambda step: (0,) * len(array.shape))


def window(ref, start, step, columns):
    return ref[pl.ds(pl.multiple_of((start + step) * columns, columns), STRIP * columns), :]


def run_moments(values, mask, stats_ref, step):
    count = jnp.sum(mask)
    mean = jnp.sum(values * mask, axis=0, keepdims=True) / count
    centered = (values - mean) * mask
    squares = jnp.sum(centered * centered, axis=0, keepdims=True)
    done = (step - 1).astype(jnp.float32)
    old_mean = jnp.where(step > 1, stats_ref[0:1, :], mean)
    old_squares = jnp.where(step > 1, stats_ref[1:2, :], 0.0)
    gap = mean - old_mean
    stats_ref[0:1, :] = old_mean + gap / (done + 1.0)
    stats_ref[1:2, :] = old_squares + squares + gap * gap * (count * done / (done + 1.0))


def spread_columns(products, masks_ref):
    size = products.shape[0]
    width = products.shape[1] // 3
    result = products[:, width : 2 * width]
    result = result + masks_ref[:, 1:2] * pltpu.roll(products[:, :width], 1, 0)
    return result + masks_ref[:, 2:3] * pltpu.roll(products[:, 2 * width :], size - 1, 0)


def clear_edges(ref, columns):
    ref[:columns, :] = jnp.zeros((columns, ref.shape[1]), ref.dtype)
    ref[ref.shape[0] - columns :, :] = jnp.zeros((columns, ref.shape[1]), ref.dtype)


def row_taps(w_ref, row, start, stop):
    return jnp.concatenate([w_ref[3 * row + k, start:stop, :] for k in range(3)], axis=1)


def low_lanes(width):
    return lax.broadcasted_iota(jnp.int32, (1, width), 1)


def decode_forward_kernel(
    steps, act_ref, table_ref, low_ref, wide_ref, vector_ref, masks_ref, w_ref, z_ref, rows_ref,
    up_ref, joined_ref, reduced_ref, stats_ref
):
    step = pl.program_id(0)
    columns = table_ref.shape[0]
    channels = act_ref.shape[2]
    rows = act_ref.shape[0]

    @pl.when(step == 0)
    def _():
        clear_edges(joined_ref, columns)
        clear_edges(reduced_ref, columns)

    @pl.when(step < steps)
    def _():
        for offset in range(STRIP):
            base = step * (STRIP // 4) + offset // 4 + (offset % 4 - 2) // 2
            fraction = ((2 * (offset % 4) - 3) % 8) / 8.0
            lower = act_ref[jnp.maximum(base, 0)]
            upper = act_ref[jnp.minimum(base + 1, rows - 1)]
            mixed = (1.0 - fraction) * lower + fraction * upper
            coarse = mixed.astype(jnp.bfloat16)
            fine = (mixed - coarse.astype(jnp.float32)).astype(jnp.bfloat16)
            value = jnp.dot(
                table_ref[...],
                jnp.concatenate([coarse, fine], axis=0),
                preferred_element_type=jnp.float32,
            ).astype(jnp.bfloat16)
            up_ref[offset * columns : (offset + 1) * columns, :] = value
            start = pl.multiple_of((step * STRIP + offset + 1) * columns, columns)
            joined_ref[pl.ds(start, columns), :] = value
        reduced = jnp.dot(low_ref[...], wide_ref[...], preferred_element_type=jnp.float32)
        _, shaped = shaped_of(reduced, vector_ref)
        value = masks_ref[:, 0:1] * (shaped * sigmoid(shaped))
        start = pl.multiple_of((step * STRIP + 1) * columns, columns)
        reduced_ref[pl.ds(start, STRIP * columns), :] = value.astype(jnp.bfloat16)

    @pl.when(step > 0)
    def _():
        start = (step - 1) * STRIP
        lane = low_lanes(reduced_ref.shape[1])
        lows = [window(reduced_ref, start, k, columns) for k in range(3)]
        low = jnp.where(lane < 64, lows[0], jnp.where(lane < 128, lows[1], lows[2]))
        values = jnp.concatenate(
            [window(joined_ref, start, k, columns) for k in range(3)] + [low], axis=1
        )
        extra = w_ref.shape[1] - channels
        parts = [row_taps(w_ref, k, 0, channels) for k in range(3)]
        for k in range(3):
            parts.append(row_taps(w_ref, k, channels, channels + extra))
            parts.append(jnp.zeros((64 - extra, 3 * channels), jnp.bfloat16))
        parts.append(jnp.zeros((64, 3 * channels), jnp.bfloat16))
        products = jnp.dot(
            values, jnp.concatenate(parts, axis=0), preferred_element_type=jnp.float32
        )
        result = spread_columns(products, masks_ref)
        z_ref[...] = result
        run_moments(result, masks_ref[:, 0:1], stats_ref, step)

    @pl.when(step == steps)
    def _():
        send_moments(rows_ref, stats_ref, masks_ref, steps)


def decode_forward(act, table, low, wide, vectors, masks, weights, devices):
    positions = low.shape[0]
    columns = table.shape[0]
    block = STRIP * columns
    steps = positions // block
    channels = act.shape[2]
    ahead, behind = lag_specs(steps)
    flat = jax.ShapeDtypeStruct((positions, channels), jnp.float32)
    stats = jax.ShapeDtypeStruct((devices, 2 * channels + 128), jnp.float32)
    up = jax.ShapeDtypeStruct((positions, channels), jnp.bfloat16)
    return pl.pallas_call(
        functools.partial(decode_forward_kernel, steps),
        out_shape=[flat, stats, up],
        grid=(steps + 1,),
        in_specs=[
            whole(act),
            whole(table),
            ahead(low, (block, low.shape[1])),
            whole(wide),
            whole(vectors),
            whole(masks),
            whole(weights),
        ],
        out_specs=[
            behind(flat, (block, channels)),
            whole(stats),
            ahead(up, (block, channels)),
        ],
        scratch_shapes=[
            pltpu.VMEM((positions + 2 * columns, channels), jnp.bfloat16),
            pltpu.VMEM((positions + 2 * columns, wide.shape[1]), jnp.bfloat16),
            pltpu.VMEM((8, channels), jnp.float32),
        ],
        compiler_params=pltpu.CompilerParams(vmem_limit_bytes=VMEM_BYTES),
        cost_estimate=cost(2 * positions * 3 * channels * 4 * channels, [low, flat, up]),
        name="decode_forward",
    )(act, table, low, wide, vectors, masks, weights)


def refine_forward_kernel(
    steps, columns, z_in_ref, rows_in_ref, params_ref, masks_ref, w_ref, z_ref, rows_ref, act_ref,
    vector_ref, stats_ref
):
    step = pl.program_id(0)
    channels = w_ref.shape[1]

    @pl.when(step == 0)
    def _():
        clear_edges(act_ref, columns)
        merge_vectors(rows_in_ref, params_ref, vector_ref)

    @pl.when(step < steps)
    def _():
        _, shaped = shaped_of(z_in_ref[...], vector_ref)
        value = masks_ref[:, 0:1] * (shaped * sigmoid(shaped))
        start = pl.multiple_of((step * STRIP + 1) * columns, columns)
        act_ref[pl.ds(start, STRIP * columns), :] = value.astype(jnp.bfloat16)

    @pl.when(step > 0)
    def _():
        start = (step - 1) * STRIP
        values = jnp.concatenate([window(act_ref, start, k, columns) for k in range(3)], axis=1)
        matrix = jnp.concatenate([row_taps(w_ref, k, 0, channels) for k in range(3)], axis=0)
        products = jnp.dot(values, matrix, preferred_element_type=jnp.float32)
        result = spread_columns(products, masks_ref)
        z_ref[...] = result
        run_moments(result, masks_ref[:, 0:1], stats_ref, step)

    @pl.when(step == steps)
    def _():
        send_moments(rows_ref, stats_ref, masks_ref, steps)


def refine_forward(z_in, rows, params, masks, weights):
    positions, channels = z_in.shape
    block = masks.shape[0]
    columns = block // STRIP
    steps = positions // block
    ahead, behind = lag_specs(steps)
    flat = jax.ShapeDtypeStruct((positions, channels), jnp.float32)
    stats = jax.ShapeDtypeStruct(rows.shape, jnp.float32)
    return pl.pallas_call(
        functools.partial(refine_forward_kernel, steps, columns),
        out_shape=[flat, stats],
        grid=(steps + 1,),
        in_specs=[
            ahead(z_in, (block, channels)),
            whole(rows),
            whole(params),
            whole(masks),
            whole(weights),
        ],
        out_specs=[behind(flat, (block, channels)), whole(stats)],
        scratch_shapes=[
            pltpu.VMEM((positions + 2 * columns, channels), jnp.bfloat16),
            pltpu.VMEM((8, channels), jnp.float32),
            pltpu.VMEM((8, channels), jnp.float32),
        ],
        compiler_params=pltpu.CompilerParams(vmem_limit_bytes=VMEM_BYTES),
        cost_estimate=cost(2 * positions * 9 * channels * channels, [z_in, flat]),
        name="refine_forward",
    )(z_in, rows, params, masks, weights)


def class_kernel(
    steps, z_ref, grad_ref, rows_ref, params_ref, masks_ref, w_ref, b_ref, logits_ref, out_ref,
    vector_ref, sums_ref, weight_ref, bias_ref
):
    step = pl.program_id(0)

    @pl.when(step == 0)
    def _():
        merge_vectors(rows_ref, params_ref, vector_ref)
        sums_ref[...] = jnp.zeros_like(sums_ref)
        weight_ref[...] = jnp.zeros_like(weight_ref)
        bias_ref[...] = jnp.zeros_like(bias_ref)

    mask = masks_ref[:, 0:1]
    centered, shaped = shaped_of(z_ref[...], vector_ref)
    gate = sigmoid(shaped)
    act = (mask * (shaped * gate)).astype(jnp.bfloat16)
    logits = jnp.dot(act, w_ref[...], preferred_element_type=jnp.float32) + b_ref[...]
    logits_ref[...] = (mask * logits).astype(jnp.bfloat16)
    grad = (mask * grad_ref[...].astype(jnp.float32)).astype(jnp.bfloat16)
    upstream = lax.dot_general(
        grad, w_ref[...], (((1,), (1,)), ((), ())), preferred_element_type=jnp.float32
    )
    local = mask * upstream * slope_of(shaped, gate)
    sums_ref[0:1, :] += jnp.sum(local * centered, axis=0, keepdims=True)
    sums_ref[1:2, :] += jnp.sum(local, axis=0, keepdims=True)
    weight_ref[...] += lax.dot_general(
        grad, act, (((0,), (0,)), ((), ())), preferred_element_type=jnp.float32
    )
    bias_ref[...] += jnp.sum(grad.astype(jnp.float32), axis=0, keepdims=True)

    @pl.when(step == steps - 1)
    def _():
        width = vector_ref.shape[1]
        classes = bias_ref.shape[1]
        shape = (classes, width)
        place = lax.broadcasted_iota(jnp.int32, shape, 0) == lax.broadcasted_iota(jnp.int32, shape, 1)
        wide_bias = jnp.dot(
            bias_ref[...],
            jnp.where(place, 1.0, 0.0),
            preferred_element_type=jnp.float32,
            precision=highest,
        )
        out_ref[...] = jnp.zeros_like(out_ref)
        send_rows(out_ref.at[:, : 2 * width], [sums_ref[0:1, :], sums_ref[1:2, :]])
        out_ref[:classes, 2 * width :] = weight_ref[...]
        out_ref[classes : classes + 1, 2 * width :] = wide_bias


def classify(z, grad, rows, params, masks, weights, bias):
    positions, channels = z.shape
    block = masks.shape[0]
    classes = grad.shape[1]
    steps = positions // block
    outs = [
        jax.ShapeDtypeStruct((positions, classes), jnp.bfloat16),
        jax.ShapeDtypeStruct((rows.shape[0], 3 * channels), jnp.float32),
    ]

    def strip(width):
        return pl.BlockSpec((block, width), lambda step: (step, 0))

    return pl.pallas_call(
        functools.partial(class_kernel, steps),
        out_shape=outs,
        grid=(steps,),
        in_specs=[
            strip(channels),
            strip(classes),
            whole(rows),
            whole(params),
            whole(masks),
            whole(weights),
            whole(bias),
        ],
        out_specs=[strip(classes), whole(outs[1])],
        scratch_shapes=[
            pltpu.VMEM((8, channels), jnp.float32),
            pltpu.VMEM((8, channels), jnp.float32),
            pltpu.VMEM((classes, channels), jnp.float32),
            pltpu.VMEM((1, classes), jnp.float32),
        ],
        compiler_params=pltpu.CompilerParams(vmem_limit_bytes=VMEM_BYTES),
        cost_estimate=cost(6 * positions * channels * 128, [z, grad, grad]),
        name="classify",
    )(z, grad, rows, params, masks, weights, bias)


def finish_grad(local, centered, mask, vector_ref):
    inner = local - vector(vector_ref, 5) - centered * vector(vector_ref, 4)
    return mask * vector(vector_ref, 2) * vector(vector_ref, 1) * inner


def store_sides(grad, masks_ref, side_ref, start):
    size, width = grad.shape
    grad = grad.astype(jnp.bfloat16).astype(jnp.float32)
    rows = pl.ds(start, size)
    side_ref[rows, :width] = pltpu.roll(masks_ref[:, 1:2] * grad, size - 1, 0).astype(jnp.bfloat16)
    side_ref[rows, width : 2 * width] = grad.astype(jnp.bfloat16)
    side_ref[rows, 2 * width :] = pltpu.roll(masks_ref[:, 2:3] * grad, 1, 0).astype(jnp.bfloat16)


def refine_backward_kernel(
    steps, columns, z_ref, grad_ref, rows_ref, sums_in_ref, params_ref, cls_ref, z_in_ref,
    rows_in_ref, params_in_ref, masks_ref, w_ref, local_ref, out_ref, totals_ref, weight_ref,
    side_ref, vector_ref, vector_in_ref, sums_ref
):
    step = pl.program_id(0)
    channels = w_ref.shape[1]
    mask = masks_ref[:, 0:1]

    @pl.when(step == 0)
    def _():
        clear_edges(side_ref, columns)
        merge_vectors(rows_ref, params_ref, vector_ref, sums_in_ref)
        merge_vectors(rows_in_ref, params_in_ref, vector_in_ref)
        totals_ref[...] = vector_ref[...]
        sums_ref[...] = jnp.zeros_like(sums_ref)
        weight_ref[...] = jnp.zeros_like(weight_ref)

    @pl.when(step < steps)
    def _():
        centered, shaped = shaped_of(z_ref[...], vector_ref)
        grad = (mask * grad_ref[...].astype(jnp.float32)).astype(jnp.bfloat16)
        upstream = lax.dot_general(
            grad, cls_ref[...], (((1,), (1,)), ((), ())), preferred_element_type=jnp.float32
        )
        local = mask * upstream * slope_of(shaped, sigmoid(shaped))
        start = pl.multiple_of((step * STRIP + 1) * columns, columns)
        store_sides(finish_grad(local, centered, mask, vector_ref), masks_ref, side_ref, start)

    @pl.when(step > 0)
    def _():
        start = (step - 1) * STRIP
        centered, shaped = shaped_of(z_in_ref[...], vector_in_ref)
        gate = sigmoid(shaped)
        act = (mask * (shaped * gate)).astype(jnp.bfloat16)
        sides = [window(side_ref, start, 2 - k, columns) for k in range(3)]
        upstream = lax.dot_general(
            jnp.concatenate(sides, axis=1),
            jnp.concatenate([w_ref[tap] for tap in range(9)], axis=1),
            (((1,), (1,)), ((), ())),
            preferred_element_type=jnp.float32,
        )
        local = mask * upstream * slope_of(shaped, gate)
        local_ref[...] = local
        sums_ref[0:1, :] += jnp.sum(local * centered, axis=0, keepdims=True)
        sums_ref[1:2, :] += jnp.sum(local, axis=0, keepdims=True)
        turned = act.T
        for k in range(3):
            weight_ref[k] += jnp.dot(turned, sides[k], preferred_element_type=jnp.float32)

    @pl.when(step == steps)
    def _():
        share = jnp.sum(sums_in_ref[:, 2 * channels :], axis=0, keepdims=True)
        send_rows(out_ref, [sums_ref[0:1, :], sums_ref[1:2, :], share])


def refine_backward(
    z, grad, rows, sums, params, classes, z_in, rows_in, params_in, masks, weights
):
    positions, channels = z.shape
    block = masks.shape[0]
    columns = block // STRIP
    steps = positions // block
    ahead, behind = lag_specs(steps)
    outs = [
        jax.ShapeDtypeStruct((positions, channels), jnp.float32),
        jax.ShapeDtypeStruct(sums.shape, jnp.float32),
        jax.ShapeDtypeStruct((8, channels), jnp.float32),
        jax.ShapeDtypeStruct((3, channels, 3 * channels), jnp.float32),
    ]
    return pl.pallas_call(
        functools.partial(refine_backward_kernel, steps, columns),
        out_shape=outs,
        grid=(steps + 1,),
        in_specs=[
            ahead(z, (block, channels)),
            ahead(grad, (block, grad.shape[1])),
            whole(rows),
            whole(sums),
            whole(params),
            whole(classes),
            behind(z_in, (block, channels)),
            whole(rows_in),
            whole(params_in),
            whole(masks),
            whole(weights),
        ],
        out_specs=[behind(z, (block, channels))] + [whole(item) for item in outs[1:]],
        scratch_shapes=[
            pltpu.VMEM((positions + 2 * columns, 3 * channels), jnp.bfloat16),
            pltpu.VMEM((8, channels), jnp.float32),
            pltpu.VMEM((8, channels), jnp.float32),
            pltpu.VMEM((8, channels), jnp.float32),
        ],
        compiler_params=pltpu.CompilerParams(vmem_limit_bytes=VMEM_BYTES),
        cost_estimate=cost(4 * positions * 9 * channels * channels, [z, z_in, grad, outs[0], weights]),
        name="refine_backward",
    )(z, grad, rows, sums, params, classes, z_in, rows_in, params_in, masks, weights)


def decode_backward_kernel(
    steps, columns, local_ref, z_ref, rows_ref, sums_in_ref, params_ref, up_ref, low_ref, wide_ref,
    low_vector_ref, table_ref, masks_ref, w_ref, coarse_ref, low_local_ref, sums_ref, totals_ref,
    weight_ref, low_weight_ref, side_ref, total_ref, vector_ref
):
    step = pl.program_id(0)
    channels = w_ref.shape[2]
    extra = w_ref.shape[1] - channels
    mask = masks_ref[:, 0:1]

    @pl.when(step == 0)
    def _():
        clear_edges(side_ref, columns)
        merge_vectors(rows_ref, params_ref, vector_ref, sums_in_ref)
        totals_ref[...] = vector_ref[...]
        sums_ref[...] = jnp.zeros_like(sums_ref)
        weight_ref[...] = jnp.zeros_like(weight_ref)
        low_weight_ref[...] = jnp.zeros_like(low_weight_ref)
        total_ref[...] = jnp.zeros_like(total_ref)

    @pl.when(step < steps)
    def _():
        centered, _ = shaped_of(z_ref[...], vector_ref)
        start = pl.multiple_of((step * STRIP + 1) * columns, columns)
        grad = finish_grad(local_ref[...], centered, mask, vector_ref)
        store_sides(grad, masks_ref, side_ref, start)

    @pl.when(step > 0)
    def _():
        start = (step - 1) * STRIP
        sides = [window(side_ref, start, 2 - k, columns) for k in range(3)]
        pieces = []
        for tap in range(9):
            pieces.append(
                jnp.concatenate(
                    [w_ref[tap], jnp.zeros((64 - extra, channels), jnp.bfloat16)], axis=0
                )
            )
        upstream = lax.dot_general(
            jnp.concatenate(sides, axis=1),
            jnp.concatenate(pieces, axis=1),
            (((1,), (1,)), ((), ())),
            preferred_element_type=jnp.float32,
        )
        for offset in range(STRIP):
            base = (step - 1) * (STRIP // 4) + offset // 4 + (offset % 4 - 2) // 2
            fraction = ((2 * (offset % 4) - 3) % 8) / 8.0
            value = upstream[offset * columns : (offset + 1) * columns, :channels]
            value = value.astype(jnp.bfloat16).astype(jnp.float32)
            total_ref[base + 1] += (1.0 - fraction) * value
            total_ref[base + 2] += fraction * value
        reduced = jnp.dot(low_ref[...], wide_ref[...], preferred_element_type=jnp.float32)
        centered, shaped = shaped_of(reduced, low_vector_ref)
        gate = sigmoid(shaped)
        low_act = (mask * (shaped * gate)).astype(jnp.bfloat16)
        low_up = upstream[:, channels:]
        local = mask * low_up * slope_of(shaped, gate)[:, :64]
        low_local_ref[...] = local
        sums_ref[0:1, :64] += jnp.sum(local * centered[:, :64], axis=0, keepdims=True)
        sums_ref[1:2, :64] += jnp.sum(local, axis=0, keepdims=True)
        turned = up_ref[...].T
        low_turned = low_act[:, :128].T[:64]
        for k in range(3):
            weight_ref[k] += jnp.dot(turned, sides[k], preferred_element_type=jnp.float32)
            low_weight_ref[k] += jnp.dot(low_turned, sides[k], preferred_element_type=jnp.float32)

    @pl.when(step == steps)
    def _():
        rows = coarse_ref.shape[0]
        total_ref[1] += total_ref[0]
        total_ref[rows] += total_ref[rows + 1]
        for row in range(rows):
            value = total_ref[row + 1]
            upper = value.astype(jnp.bfloat16)
            lower = (value - upper.astype(jnp.float32)).astype(jnp.bfloat16)
            coarse_ref[row] = jnp.dot(
                table_ref[...],
                jnp.concatenate([upper, lower], axis=0),
                preferred_element_type=jnp.float32,
            )


def decode_backward(
    local, z, rows, sums, params, up, low, wide, low_vectors, table, masks, weights, shape
):
    positions, channels = z.shape
    block = masks.shape[0]
    columns = block // STRIP
    steps = positions // block
    height, coarse_columns, _ = shape
    ahead, behind = lag_specs(steps)
    outs = [
        jax.ShapeDtypeStruct((height, coarse_columns, channels), jnp.float32),
        jax.ShapeDtypeStruct((positions, 64), jnp.float32),
        jax.ShapeDtypeStruct((8, channels), jnp.float32),
        jax.ShapeDtypeStruct((8, channels), jnp.float32),
        jax.ShapeDtypeStruct((3, channels, 3 * channels), jnp.float32),
        jax.ShapeDtypeStruct((3, 64, 3 * channels), jnp.float32),
    ]
    return pl.pallas_call(
        functools.partial(decode_backward_kernel, steps, columns),
        out_shape=outs,
        grid=(steps + 1,),
        in_specs=[
            ahead(local, (block, channels)),
            ahead(z, (block, channels)),
            whole(rows),
            whole(sums),
            whole(params),
            behind(up, (block, channels)),
            behind(low, (block, low.shape[1])),
            whole(wide),
            whole(low_vectors),
            whole(table),
            whole(masks),
            whole(weights),
        ],
        out_specs=[whole(outs[0]), behind(outs[1], (block, 64))]
        + [whole(item) for item in outs[2:]],
        scratch_shapes=[
            pltpu.VMEM((positions + 2 * columns, 3 * channels), jnp.bfloat16),
            pltpu.VMEM((height + 2, columns, channels), jnp.float32),
            pltpu.VMEM((8, channels), jnp.float32),
        ],
        compiler_params=pltpu.CompilerParams(vmem_limit_bytes=VMEM_BYTES),
        cost_estimate=cost(4 * positions * 9 * channels * (channels + 64), [local, z, up, low, outs[1], weights]),
        name="decode_backward",
    )(local, z, rows, sums, params, up, low, wide, low_vectors, table, masks, weights)


def branch_back(
    upstream, z, vectors, joined, weights, branch_z, pool_z, branch_vectors, mask, pool_mask, member,
    devices
):
    positions, channels = z.shape
    width = joined.shape[1]
    count = len(branch_z)
    outs = [
        jax.ShapeDtypeStruct((width, channels), jnp.float32),
        jax.ShapeDtypeStruct((positions, count * channels), jnp.float32),
        jax.ShapeDtypeStruct(pool_z.shape, jnp.float32),
        jax.ShapeDtypeStruct((devices, 2 * width), jnp.float32),
    ]
    args = [upstream, z, vectors, joined, weights, pool_z, branch_vectors, mask, pool_mask, member]
    args += list(branch_z)

    def body(*refs):
        (up_ref, z_ref, vector_ref, joined_ref, w_ref, pool_ref, branch_ref, mask_ref) = refs[:8]
        pool_mask_ref, member_ref = refs[8:10]
        z_refs = refs[10 : 10 + count]
        weight_ref, local_ref, pool_local_ref, rows_ref = refs[10 + count :]
        valid = mask_ref[...]
        centered, shaped = shaped_of(z_ref[...], vector_ref)
        local = valid * up_ref[...] * slope_of(shaped, sigmoid(shaped))
        grad = finish_grad(local, centered, valid, vector_ref).astype(jnp.bfloat16)
        weight_ref[...] = lax.dot_general(
            joined_ref[...], grad, (((0,), (0,)), ((), ())), preferred_element_type=jnp.float32
        )
        spread = lax.dot_general(
            grad, w_ref[...], (((1,), (1,)), ((), ())), preferred_element_type=jnp.float32
        )
        gains = []
        biases = []
        for index in range(count + 1):
            lanes = slice(index * channels, (index + 1) * channels)
            values = spread[:, lanes]
            if index < count:
                source, allowed = z_refs[index], valid
            else:
                source, allowed = pool_ref, pool_mask_ref[...]
                upper = values.astype(jnp.bfloat16)
                lower = (values - upper.astype(jnp.float32)).astype(jnp.bfloat16)
                values = jnp.dot(member_ref[...], upper, preferred_element_type=jnp.float32)
                values += jnp.dot(member_ref[...], lower, preferred_element_type=jnp.float32)
            centered, shaped = shaped_of(source[...], branch_ref.at[:, lanes])
            term = allowed * values * slope_of(shaped, sigmoid(shaped))
            if index < count:
                local_ref[:, lanes] = term
            else:
                pool_local_ref[...] = term
            gains.append(jnp.sum(term * centered, axis=0, keepdims=True))
            biases.append(jnp.sum(term, axis=0, keepdims=True))
        send_rows(rows_ref, gains + biases)

    return one_step(body, outs, args, vmem=60 * 1024 * 1024)


def branch_grads(rows, local, pool_local, branch_z, pool_z, branch_vectors, counts, mask, pool_mask):
    positions, channels = branch_z[0].shape
    count = len(branch_z)
    width = (count + 1) * channels
    outs = [jax.ShapeDtypeStruct((positions, channels), jnp.bfloat16)] * count
    outs += [jax.ShapeDtypeStruct(pool_z.shape, jnp.bfloat16)]
    outs += [jax.ShapeDtypeStruct((8, width), jnp.float32)]
    args = [rows, local, pool_local, pool_z, branch_vectors, counts, mask, pool_mask]
    args += list(branch_z)

    def body(*refs):
        rows_ref, local_ref, pool_local_ref, pool_ref, branch_ref, counts_ref = refs[:6]
        mask_ref, pool_mask_ref = refs[6:8]
        z_refs = refs[8 : 8 + count]
        grad_refs, totals_ref = refs[8 + count : -1], refs[-1]
        totals_ref[...] = jnp.zeros_like(totals_ref)
        totals_ref[0:1, :] = jnp.sum(rows_ref[:, :width], axis=0, keepdims=True)
        totals_ref[1:2, :] = jnp.sum(rows_ref[:, width:], axis=0, keepdims=True)
        for index in range(count + 1):
            lanes = slice(index * channels, (index + 1) * channels)
            vectors = branch_ref.at[:, lanes]
            source = z_refs[index] if index < count else pool_ref
            allowed = mask_ref[...] if index < count else pool_mask_ref[...]
            term = local_ref[:, lanes] if index < count else pool_local_ref[...]
            centered, _ = shaped_of(source[...], vectors)
            share = 1.0 / counts_ref[:, lanes]
            inner = term - totals_ref[1:2, lanes] * share
            inner = inner - centered * (totals_ref[0:1, lanes] * share)
            grad = allowed * vector(vectors, 2) * vector(vectors, 1) * inner
            grad_refs[index][...] = grad.astype(jnp.bfloat16)

    return one_step(body, outs, args, vmem=60 * 1024 * 1024)


def low_backward_kernel(
    vector_ref, local_ref, low_ref, wide_ref, masks_ref, out_ref, weight_ref
):
    @pl.when(pl.program_id(0) == 0)
    def _():
        weight_ref[...] = jnp.zeros_like(weight_ref)

    low = low_ref[...]
    weights = wide_ref[:, :128]
    reduced = jnp.dot(low, weights, preferred_element_type=jnp.float32)
    mean, scale, gain = (vector_ref[k : k + 1, :64] for k in range(3))
    centered = (reduced[:, :64] - mean) * scale
    inner = local_ref[...] - vector_ref[5:6, :64] - centered * vector_ref[4:5, :64]
    grad = (masks_ref[:, 0:1] * gain * scale * inner).astype(jnp.bfloat16)
    out_ref[...] = lax.dot_general(
        grad, weights[:, :64], (((1,), (1,)), ((), ())), preferred_element_type=jnp.float32
    ).astype(jnp.bfloat16)
    weight_ref[...] += lax.dot_general(
        grad, low, (((0,), (0,)), ((), ())), preferred_element_type=jnp.float32
    )


def low_backward(local, low, wide, vectors, masks, tie):
    positions, width = low.shape
    block = masks.shape[0]
    outs = [
        jax.ShapeDtypeStruct((positions, width), jnp.bfloat16),
        jax.ShapeDtypeStruct((64, width), jnp.float32),
    ]
    return pl.pallas_call(
        behind_tie(low_backward_kernel),
        out_shape=outs,
        grid=(positions // block,),
        in_specs=[
            whole(vectors),
            pl.BlockSpec(memory_space=pl.ANY),
            pl.BlockSpec((block, 64), lambda step: (step, 0)),
            pl.BlockSpec((block, width), lambda step: (step, 0)),
            whole(wide),
            whole(masks),
        ],
        out_specs=[pl.BlockSpec((block, width), lambda step: (step, 0)), whole(outs[1])],
        compiler_params=pltpu.CompilerParams(vmem_limit_bytes=VMEM_BYTES),
        cost_estimate=whole_cost(6 * positions * width * 128, [local, low, low]),
        name="low_backward",
    )(vectors, tie, local, low, wide, masks)


def side_values(values, image_ids, dilation):
    result = []
    for step in (-dilation, dilation):
        mask = tap_mask(image_ids, values.shape[1], 0, step).astype(values.dtype)
        result.append(mask * shifted(values, 0, step))
    return [result[0], values, result[1]]


def side_grads(values, image_ids, dilation):
    result = []
    for step in (-dilation, 0, dilation):
        masked = tap_mask(image_ids, values.shape[1], 0, step).astype(values.dtype) * values
        result.append(shifted(masked, 0, -step))
    return jnp.concatenate(result, axis=-1)


def settle_core(values):
    core = place()[3]
    taps, rows, cols = values.shape
    parts = values.reshape(taps, rows, 2, cols // 2)
    kept = lax.dynamic_index_in_dim(parts, core, 2, keepdims=False)
    given = lax.dynamic_index_in_dim(parts, 1 - core, 2, keepdims=False).astype(jnp.bfloat16)
    got = exchange(given, "narrow", 1).astype(jnp.float32)
    lower = jnp.where(core == 0, kept, got)
    upper = jnp.where(core == 0, got, kept)
    return jnp.concatenate([lower, upper], axis=1)


def band_ids(widths, columns):
    ends_all = jnp.cumsum(widths, axis=1)
    position = jnp.arange(columns, dtype=jnp.int32)
    band_index = jnp.sum(
        (position[None, :, None] >= ends_all[:, None, :]).astype(jnp.int32), axis=2
    )
    return jnp.where(band_index < widths.shape[1] - 1, band_index, -1)


def shifted(values, row_shift, col_shift):
    height = values.shape[1]
    columns = values.shape[2]
    padded = jnp.pad(
        values, ((0, 0), (abs(row_shift), abs(row_shift)), (abs(col_shift), abs(col_shift)), (0, 0))
    )
    row_start = abs(row_shift) + row_shift
    col_start = abs(col_shift) + col_shift
    return padded[:, row_start : row_start + height, col_start : col_start + columns, :]


def tap_mask(image_ids, height, row_shift, col_shift):
    columns = image_ids.shape[1]
    padded = jnp.pad(image_ids, ((0, 0), (abs(col_shift), abs(col_shift))), constant_values=-2)
    col_start = abs(col_shift) + col_shift
    other_ids = padded[:, col_start : col_start + columns]
    same_image = (other_ids == image_ids).astype(jnp.float32)
    row_place = jnp.arange(height) + row_shift
    inside = ((row_place >= 0) & (row_place < height)).astype(jnp.float32)
    return (inside[None, :, None] * same_image[:, None, :])[..., None]


def tap_offsets(dilation):
    return [
        ((tap_index // 3 - 1) * dilation, (tap_index % 3 - 1) * dilation) for tap_index in range(9)
    ]


def linear_weights(out_count, in_count):
    position = jnp.arange(out_count, dtype=jnp.int32)
    scaled = 2 * position - 3
    left_index = jnp.floor_divide(scaled, 8)
    fraction = (scaled - 8 * left_index).astype(jnp.float32) / 8.0
    lower_index = jnp.clip(left_index, 0, in_count - 1)
    upper_index = jnp.clip(left_index + 1, 0, in_count - 1)
    return (position, lower_index, upper_index, fraction)


def column_table(image_ids):
    columns = image_ids.shape[1]
    position, lower_index, upper_index, fraction = linear_weights(4 * columns, columns)
    source = jnp.arange(columns, dtype=jnp.int32)[None, :]

    def picker(index_row):
        return (source == index_row[:, None]).astype(jnp.int32)

    def lookup(index_row):
        return jnp.sum(image_ids[:, None, :] * picker(index_row)[None], axis=2)

    own_index = position // 4
    own_id = lookup(own_index)
    weight_lower = (1.0 - fraction)[None, :] * (lookup(lower_index) == own_id).astype(jnp.float32)
    weight_upper = fraction[None, :] * (lookup(upper_index) == own_id).astype(jnp.float32)
    weight_own = 1.0 - weight_lower - weight_upper
    table = weight_lower[:, :, None] * picker(lower_index)[None].astype(jnp.float32)
    table = table + weight_upper[:, :, None] * picker(upper_index)[None].astype(jnp.float32)
    table = table + weight_own[:, :, None] * picker(own_index)[None].astype(jnp.float32)
    return table


def normalize(values, valid_map, mean_row, variance, gain_row, bias_row):
    norm_scale = lax.rsqrt(variance + epsilon)
    centered = (values - mean_row) * norm_scale
    shaped = centered * gain_row + bias_row
    return (valid_map * jax.nn.silu(shaped), centered, shaped, norm_scale)


def norm_grad_terms(upstream, valid_map, centered, shaped):
    sigmoid_value = jax.nn.sigmoid(shaped)
    local_term = valid_map * upstream * sigmoid_value * (1.0 + shaped * (1.0 - sigmoid_value))
    axes = tuple(range(local_term.ndim - 1))
    return (local_term, jnp.sum(local_term * centered, axis=axes), jnp.sum(local_term, axis=axes))


def moments(values, valid_map, local_count, count_all):
    mean, squares = local_moments(values, valid_map, local_count)
    return merged(jnp.stack([mean, squares]), local_count, count_all)


def merged(stats, local_count, count_all):
    width = stats.shape[1]
    own = jnp.concatenate([stats[0], stats[1], jnp.full((1,), 1.0) * local_count])
    rows = from_all(own)
    counts, means, squares = merge_rows(
        rows[:, 2 * width :], rows[:, :width], rows[:, width : 2 * width]
    )
    return (means, squares / count_all)


def pack_pairs(pairs):
    return jnp.concatenate(
        [pair_item[0] for pair_item in pairs] + [pair_item[1] for pair_item in pairs]
    )


def unpack_pairs(flat, pairs):
    lengths = [pair_item[0].shape[0] for pair_item in pairs]
    half_point = sum(lengths)
    result_pairs = []
    offset = 0
    for length_now in lengths:
        result_pairs.append(
            (
                flat[offset : offset + length_now],
                flat[half_point + offset : half_point + offset + length_now],
            )
        )
        offset = offset + length_now
    return result_pairs


def gradient_sums(pairs):
    return unpack_pairs(jnp.sum(from_all(pack_pairs(pairs)), axis=0), pairs)


def small_block(items):
    proj, reduce, decode, refine = items
    taps, rows, cols = refine.shape
    count = proj.shape[0] // rows
    proj = proj.reshape(2, count, rows // 2, cols).swapaxes(0, 1).reshape(count, rows, cols)
    reduce = jnp.pad(reduce, ((0, 0), (0, cols - reduce.shape[1])))[None]
    shared = share_core(jnp.concatenate([refine, proj, reduce]))
    lanes = shared.shape[2]
    decode = decode.swapaxes(1, 2)
    decode = jnp.pad(decode, ((0, 0), (0, 0), (0, lanes - decode.shape[2])))
    return jnp.concatenate([shared, decode.reshape(-1, shared.shape[1], lanes)])


def settle_small(owned, shapes):
    shape_p, shape_r, shape_d, shape_f = shapes
    taps, rows, cols = shape_f
    count = shape_p[0] // rows
    first = taps + count + 1
    settled = settle_core(owned[:first])
    proj = settled[taps : taps + count].reshape(count, 2, rows // 2, cols)
    proj = proj.swapaxes(0, 1).reshape(shape_p)
    reduce = settled[taps + count, :, : shape_r[1]]
    decode = owned[first:].reshape(taps, shape_d[2], -1)[:, :, : shape_d[1]].swapaxes(1, 2)
    return (proj, reduce, decode, settled[:taps])


def reduce_lanes(width, row, core, half):
    start = (2 * row + core) * width
    return start, core * half


def unpack_kernel(shapes, place_ref, own_ref, other_ref, proj_ref, wide_ref, decode_ref, refine_ref):
    deep, side, row, core = (place_ref[index] for index in range(4))
    shape_p, shape_r, shape_d, shape_f = shapes
    taps = shape_f[0]
    rows = shape_f[1] // 2
    count = shape_p[0] // (2 * rows)
    lanes = own_ref.shape[-1]

    def load(ref, z, x, y, start, size):
        slot = lax.bitwise_xor(deep, z)
        return ref[slot, lax.rem(y + row, 2), lax.rem(x + side, 2), start : start + size]

    def both(z, x, y, start, size):
        mine = load(own_ref, z, x, y, start, size)
        others = load(other_ref, z, x, y, start, size)
        return (jnp.where(core == 0, mine, others), jnp.where(core == 0, others, mine))

    lane = lax.broadcasted_iota(jnp.int32, (1, lanes), 1)
    for z in range(ROUNDS):
        for x in range(2):
            wide = 2 * z + x
            halves = [both(z, x, y, 0, taps + count + 1) for y in range(2)]
            for h in range(2):
                joined = jnp.concatenate([halves[0][h], halves[1][h]], axis=-1)
                base = (2 * wide + h) * rows
                refine_ref[:, base : base + rows, :] = joined[:taps]
                base = (2 * wide + h) * rows * count
                proj_ref[base : base + rows * count, :] = joined[taps : taps + count].reshape(
                    rows * count, 2 * lanes
                )
                total = jnp.zeros((rows, lanes), jnp.float32)
                for y in range(2):
                    value = halves[y][h][taps + count].astype(jnp.float32)
                    for c in range(2):
                        start, held = reduce_lanes(shape_r[1], y, c, lanes // 2)
                        moved = pltpu.roll(value, (start - held) % lanes, 1)
                        inside = (lane >= start) & (lane < start + shape_r[1])
                        total = total + jnp.where(inside, moved, 0.0)
                base = (2 * wide + h) * rows
                left = total + pltpu.roll(total, 64, 1)
                wide_ref[base : base + rows, :] = jnp.concatenate([left, total], axis=1).astype(
                    jnp.bfloat16
                )
    height, width = shape_d[1], shape_d[2]
    blocks = width // rows
    for tap in range(taps):
        start = taps + count + 1 + tap * blocks
        pieces = []
        for y in range(2):
            columns = ([], [])
            for z in range(ROUNDS):
                for x in range(2):
                    for c, value in enumerate(both(z, x, y, start, blocks)):
                        columns[c].append(value.reshape(width, lanes))
            for c in range(2):
                joined = jnp.concatenate(columns[c], axis=0).astype(jnp.float32)
                pieces.append(joined.T[:height])
        decode_ref[tap] = jnp.concatenate(pieces, axis=0).astype(jnp.bfloat16)


def unpack_block(own, other, shapes):
    wide = 2 * ROUNDS
    shape_p, shape_r, shape_d, shape_f = shapes
    outs = [
        jax.ShapeDtypeStruct((wide * shape_p[0], 4 * shape_p[1]), jnp.bfloat16),
        jax.ShapeDtypeStruct((wide * shape_r[0], 256), jnp.bfloat16),
        jax.ShapeDtypeStruct((shape_d[0], 4 * shape_d[1], wide * shape_d[2]), jnp.bfloat16),
        jax.ShapeDtypeStruct((shape_f[0], wide * shape_f[1], 4 * shape_f[2]), jnp.bfloat16),
    ]
    return pl.pallas_call(
        functools.partial(unpack_kernel, shapes),
        out_shape=outs,
        in_specs=[pl.BlockSpec(memory_space=pltpu.SMEM)]
        + [pl.BlockSpec(memory_space=pltpu.VMEM)] * 2,
        out_specs=[pl.BlockSpec(memory_space=pltpu.VMEM)] * 4,
        compiler_params=pltpu.CompilerParams(vmem_limit_bytes=VMEM_BYTES),
        cost_estimate=whole_cost(0, [own, other] + outs + outs),
        name="unpack_weights",
    )(kernel_place(), own, other)


def pack_kernel(
    shapes, place_ref, proj_ref, reduce_ref, decode_ref, low_ref, refine_ref, keep_ref, give_ref
):
    deep, side, row, core = (place_ref[index] for index in range(4))
    shape_p, shape_r, shape_d, shape_f = shapes
    taps = shape_f[0]
    rows = shape_f[1] // 2
    count = shape_p[0] // (2 * rows)
    lanes = keep_ref.shape[-1]
    channels = 2 * lanes

    def store(z, x, y, start, size, values):
        values = [value.astype(jnp.bfloat16) for value in values]
        index = (
            lax.rem(x + side, 2),
            lax.rem(y + row, 2),
            lax.bitwise_xor(deep, z),
            pl.ds(start, size),
        )
        keep_ref[index] = jnp.where(core == 0, values[0], values[1])
        give_ref[index] = jnp.where(core == 0, values[1], values[0])

    lane = lax.broadcasted_iota(jnp.int32, (1, lanes), 1)
    reduce = jnp.concatenate(
        [reduce_ref[...], jnp.zeros((lanes - reduce_ref.shape[0], reduce_ref.shape[1]), jnp.float32)]
    ).T
    moved = []
    for y in range(2):
        total = jnp.zeros_like(reduce)
        for c in range(2):
            start, held = reduce_lanes(shape_r[1], y, c, lanes // 2)
            inside = (lane >= held) & (lane < held + shape_r[1])
            total = total + jnp.where(inside, pltpu.roll(reduce, (held - start) % lanes, 1), 0.0)
        moved.append(total)
    for z in range(ROUNDS):
        for x in range(2):
            wide = 2 * z + x
            for y in range(2):
                columns = slice(y * lanes, (y + 1) * lanes)
                for tap in range(taps):
                    line, k = tap // 3, tap % 3
                    left = k * channels + y * lanes
                    values = []
                    for h in range(2):
                        base = (2 * wide + h) * rows
                        values.append(
                            refine_ref[line, base : base + rows, left : left + lanes][None]
                        )
                    store(z, x, y, tap, 1, values)
                values = []
                for h in range(2):
                    base = (2 * wide + h) * rows * count
                    values.append(
                        proj_ref[base : base + rows * count, columns].reshape(count, rows, lanes)
                    )
                store(z, x, y, taps, count, values)
                values = [
                    moved[y][(2 * wide + h) * rows : (2 * wide + h + 1) * rows][None]
                    for h in range(2)
                ]
                store(z, x, y, taps + count, 1, values)
    height, width = shape_d[1], shape_d[2]
    blocks = width // rows
    for tap in range(taps):
        line, k = tap // 3, tap % 3
        columns = slice(k * channels, (k + 1) * channels)
        whole_tap = jnp.concatenate(
            [
                decode_ref[line, :, columns],
                low_ref[line, :, columns],
                jnp.zeros((lanes, channels), jnp.float32),
            ],
            axis=0,
        )
        turned = [whole_tap[n * height : n * height + lanes].T for n in range(4)]
        for z in range(ROUNDS):
            for x in range(2):
                base = (2 * z + x) * width
                for y in range(2):
                    values = [
                        turned[2 * y + c][base : base + width].reshape(blocks, rows, lanes)
                        for c in range(2)
                    ]
                    store(z, x, y, taps + count + 1 + tap * blocks, blocks, values)


def pack_block(proj, reduce, decode, low, refine, shapes, tie):
    shape_p, shape_r, shape_d, shape_f = shapes
    rows = shape_f[1] // 2
    total = shape_f[0] + shape_p[0] // (2 * rows) + 1 + shape_d[0] * shape_d[2] // rows
    out = jax.ShapeDtypeStruct((2, 2, ROUNDS, total, rows, 2 * shape_f[2]), jnp.bfloat16)
    return pl.pallas_call(
        behind_tie(functools.partial(pack_kernel, shapes)),
        out_shape=[out, out],
        in_specs=[pl.BlockSpec(memory_space=pltpu.SMEM), pl.BlockSpec(memory_space=pl.ANY)]
        + [pl.BlockSpec(memory_space=pltpu.VMEM)] * 5,
        out_specs=[pl.BlockSpec(memory_space=pltpu.VMEM)] * 2,
        compiler_params=pltpu.CompilerParams(vmem_limit_bytes=VMEM_BYTES),
        cost_estimate=whole_cost(0, [proj, decode, low, refine, out, out, out]),
        name="pack_gradients",
    )(kernel_place(), tie, proj, reduce, decode, low, refine)


def low_moments_kernel(low_ref, wide_ref, masks_ref, stats_ref):
    reduced = jnp.dot(low_ref[...], wide_ref[...], preferred_element_type=jnp.float32)
    run_moments(reduced, masks_ref[:, 0:1], stats_ref, pl.program_id(0) + 1)


def low_moments(low, wide, masks):
    block = masks.shape[0]
    out = jax.ShapeDtypeStruct((8, wide.shape[1]), jnp.float32)
    return pl.pallas_call(
        low_moments_kernel,
        out_shape=out,
        grid=(low.shape[0] // block,),
        in_specs=[
            pl.BlockSpec((block, low.shape[1]), lambda step: (step, 0)),
            whole(wide),
            whole(masks),
        ],
        out_specs=whole(out),
        compiler_params=pltpu.CompilerParams(vmem_limit_bytes=VMEM_BYTES),
        cost_estimate=whole_cost(2 * low.shape[0] * low.shape[1] * 256, [low]),
        name="low_moments",
    )(low, wide, masks)


def by_tap(values):
    width = values.shape[2] // 3
    split = values.reshape(3, values.shape[1], 3, width)
    return split.transpose(0, 2, 1, 3).reshape(9, values.shape[1], width)


def widen(values):
    padded = jnp.pad(values, ((0, 0), (0, 64 - values.shape[1])))
    return jnp.concatenate([padded, padded, padded, jnp.zeros_like(padded)], axis=1)


def pack_small(items):
    total = sum(item.size for item in items)
    padded = -(-total // 2048) * 2048
    flats = [item.reshape(-1) for item in items]
    return jnp.concatenate(flats + [jnp.zeros((padded - total,), jnp.bfloat16)]).reshape(-1, 128)


def unpack_small(everything, items):
    wide, narrow = everything.shape[:2]
    everything = everything.reshape(wide, narrow, -1)
    pieces = []
    start = 0
    for item in items:
        pieces.append(
            everything[:, :, start : start + item.size].reshape((wide, narrow) + item.shape)
        )
        start += item.size
    proj, reduce, decode, refine = pieces
    proj = proj.transpose(0, 2, 1, 3).reshape(wide * proj.shape[2], -1)
    reduce = reduce.transpose(0, 2, 1, 3).reshape(wide * reduce.shape[2], -1)
    decode = decode.transpose(2, 1, 3, 0, 4).reshape(decode.shape[2], narrow * decode.shape[3], -1)
    refine = refine.transpose(2, 0, 3, 1, 4).reshape(refine.shape[2], wide * refine.shape[3], -1)
    return (proj, widen(reduce), decode, refine)


def pack_grads(reduce, proj, decode, low, refine, shapes):
    wide = lax.axis_size("wide")
    narrow = lax.axis_size("narrow")
    extra = narrow * shapes[1][1]
    reduce = reduce[:extra].T
    decode = jnp.concatenate([by_tap(decode), by_tap(low)[:, :extra]], axis=1)
    refine = by_tap(refine)
    shape_p, shape_r, shape_d, shape_f = shapes
    proj = proj.reshape(wide, shape_p[0], narrow, shape_p[1]).transpose(0, 2, 1, 3)
    reduce = reduce.reshape(wide, shape_r[0], narrow, shape_r[1]).transpose(0, 2, 1, 3)
    decode = decode.reshape(shape_d[0], narrow, shape_d[1], wide, shape_d[2]).transpose(3, 1, 0, 2, 4)
    refine = refine.reshape(shape_f[0], wide, shape_f[1], narrow, shape_f[2]).transpose(1, 3, 0, 2, 4)
    flats = [
        item.astype(jnp.bfloat16).reshape(wide, narrow, -1)
        for item in (proj, reduce, decode, refine)
    ]
    total = sum(item.shape[2] for item in flats)
    padded = -(-total // 2048) * 2048
    flats.append(jnp.zeros((wide, narrow, padded - total), jnp.bfloat16))
    return jnp.concatenate(flats, axis=2).reshape(wide, narrow, -1, 128)


def unpack_grads(owned, shapes):
    owned = owned.reshape(-1)
    pieces = []
    start = 0
    for shape in shapes:
        size = 1
        for extent in shape:
            size *= extent
        pieces.append(owned[start : start + size].reshape(shape))
        start += size
    return pieces


def per_device(
    features,
    low_level,
    widths,
    w_point,
    w_atrous,
    w_proj,
    w_low,
    w_dec1,
    w_dec2,
    w_cls,
    b_cls,
    gains,
    biases,
    low_gain,
    low_bias,
    logit_grad,
):
    canvases = features.shape[0]
    height = features.shape[1]
    columns = features.shape[2]
    fine_columns = low_level.shape[2]
    images = widths.shape[1] - 1
    channels = gains.shape[1]
    images_total = float(canvases * lax.axis_size("wide") * lax.axis_size("narrow") * images)
    small = [w_proj, w_low, w_dec1, w_dec2]
    ids_coarse = band_ids(widths, columns)
    ids_fine = band_ids(4 * widths, fine_columns)
    valid_coarse = (ids_coarse >= 0).astype(jnp.float32)[:, None, :, None]
    valid_fine = (ids_fine >= 0).astype(jnp.float32)[:, None, :, None]
    all_ones = jnp.ones((1, 1, 1), jnp.float32)
    local_count = (height * jnp.sum(widths[:, :images])).astype(jnp.float32)
    member = (ids_coarse[:, :, None] == jnp.arange(images, dtype=jnp.int32)[None, None, :]).astype(
        jnp.float32
    )
    member_low = member.astype(jnp.bfloat16)
    image_sizes = (height * widths[:, :images]).astype(jnp.float32)
    positions = low_level.shape[1] * fine_columns
    low_flat = low_level.reshape(positions, -1)
    extra = low_gain.shape[0]
    side_masks = [tap_mask(ids_fine, STRIP, 0, step) for step in (-1, 1)]
    masks = jnp.concatenate([valid_fine * jnp.ones((1, STRIP, 1, 1))] + side_masks, axis=-1)
    masks = masks.reshape(STRIP * fine_columns, 3)
    coarse_shape = (height, columns, channels)
    mask_column = jnp.broadcast_to(valid_coarse, (1, height, columns, 1)).reshape(-1, 1)
    member_wide = jnp.pad(member[0], ((0, 0), (0, 8 - images)))
    member_rows = jnp.tile(member_wide, (height, 1))
    sizes_inverse = jnp.pad(1.0 / image_sizes[0], (0, 8 - images)).reshape(8, 1)
    pool_inputs = (member_rows.T.astype(jnp.bfloat16), sizes_inverse)

    cols_table = column_table(ids_coarse)[0].astype(jnp.bfloat16)
    up_table = jnp.concatenate([cols_table, cols_table], axis=1)
    down_table = jnp.concatenate([cols_table.T, cols_table.T], axis=1)
    decode_params = jnp.stack([gains[6], biases[6]])
    refine_params = jnp.stack([gains[7], biases[7]])
    pool_mask = (jnp.arange(8) < images).astype(jnp.float32).reshape(8, 1)
    grad_flat = logit_grad.reshape(-1, logit_grad.shape[-1])
    spread_rows = member_rows * sizes_inverse.reshape(1, 8)
    prepared = [
        masks,
        mask_column,
        sizes_inverse,
        pool_inputs[0],
        up_table,
        down_table,
        decode_params,
        refine_params,
        pool_mask,
        grad_flat,
        w_cls,
        spread_rows,
    ]

    def all_sides():
        sides = [
            [
                item.reshape(height * columns, -1)
                for item in side_values(features, ids_coarse, dilation)
            ]
            for dilation in dilations
        ]
        return (sides, grad_flat)

    def low_part(proj, wide, decode, refine):
        return low_moments(low_flat, wide, masks)

    def forward(part, ready, pair, before, tie=None):
        sums, stats, pooling = ({}, {}, ()) if before is None else before
        more, more_stats, more_pooling = coarse_forward(
            part,
            mask_column,
            ready[0],
            pair,
            coarse_shape,
            sums,
            pool_inputs if GATHER.has_point(part) else None,
            tie,
        )
        return ({**sums, **more}, {**stats, **more_stats}, tuple(pooling) + tuple(more_pooling))

    parts, unpacked, ready, low_stats, coarse = gather_taps(
        GATHER.order(w_point, w_atrous),
        small,
        [all_sides, low_part],
        [functools.partial(forward, part) for part in range(len(GATHER.parts))],
        prepared,
    )
    proj_full, low_wide, decode_full, refine_full = unpacked
    sides, grad_flat = ready
    sums, stats, pool_results = coarse
    point_z, point_stats, pool_z, pooled = pool_results
    pool_wide = pool_z
    pool_z = pool_z[None, :images]
    coarse_stats = [point_stats, stats[0], stats[1], stats[2]]
    coarse_z = [
        item.reshape(1, height, columns, channels) for item in (point_z, sums[0], sums[1], sums[2])
    ]
    blocks = [(item_z, valid_coarse) for item_z in coarse_z] + [(pool_z, all_ones)]
    local_images = float(canvases * images)
    states = [(item[0], item[1]) for item in coarse_stats] + [
        local_moments(pool_z, all_ones, local_images),
    ]
    own = [state[item] for item in range(2) for state in states]
    rows = from_all(jnp.concatenate(own + [jnp.full((1,), 1.0) * local_count]))
    width = 5 * channels
    pixels = rows[:, 2 * width :]
    count_rows = jnp.concatenate(
        [
            jnp.broadcast_to(pixels, (rows.shape[0], 4 * channels)),
            jnp.full((rows.shape[0], channels), local_images),
        ],
        axis=1,
    )
    counts_flat, means_flat, squares_flat = merge_rows(
        count_rows, rows[:, :width], rows[:, width : 2 * width]
    )
    vars_flat = squares_flat / counts_flat
    section_means = []
    section_vars = []
    offset = 0
    for width in [channels] * 5:
        section_means.append(means_flat[offset : offset + width])
        section_vars.append(vars_flat[offset : offset + width])
        offset += width
    pixel_count = counts_flat[0]
    fine_count = 16.0 * pixel_count
    gain_rows = [gains[0], gains[1], gains[2], gains[3], gains[4], low_gain]
    bias_rows = [biases[0], biases[1], biases[2], biases[3], biases[4], low_bias]
    kept = []
    activations = []
    for index in range(5):
        block_values, block_valid = blocks[index]
        result = normalize(
            block_values,
            block_valid,
            section_means[index],
            section_vars[index],
            gain_rows[index],
            bias_rows[index],
        )
        kept.append(result[1:])
        activations.append(result[0].astype(jnp.bfloat16))
    spread = jnp.einsum(
        "nwk,nkd->nwd", member_low, activations[4], preferred_element_type=jnp.float32
    ).astype(jnp.bfloat16)
    spread = jnp.broadcast_to(spread[:, None], (canvases, height, columns, channels))
    joined_coarse = jnp.concatenate(activations[:4] + [spread], axis=-1)
    proj_z = jnp.einsum(
        "nhwc,cd->nhwd", joined_coarse, proj_full, preferred_element_type=jnp.float32
    )
    proj_moments = local_moments(proj_z, valid_coarse, local_count)
    joint_mean, joint_var = merged(
        jnp.stack(
            [
                jnp.concatenate([proj_moments[0], low_stats[0, :extra]]),
                jnp.concatenate([proj_moments[1], low_stats[1, :extra] / 16.0]),
            ]
        ),
        local_count,
        pixel_count,
    )
    proj_mean, low_mean = joint_mean[:channels], joint_mean[channels:]
    proj_var, low_var = joint_var[:channels], joint_var[channels:]
    proj_act, proj_centered, proj_shaped, proj_scale = normalize(
        proj_z, valid_coarse, proj_mean, proj_var, gains[5], biases[5]
    )
    proj_act = proj_act.astype(jnp.bfloat16).astype(jnp.float32)
    low_vectors = widen(norm_vectors(low_mean, low_var, low_gain, low_bias))
    devices = device_count()
    decode_z, rows, upsampled = decode_forward(
        proj_act[0],
        up_table,
        low_flat,
        low_wide,
        low_vectors,
        masks,
        decode_full,
        devices,
    )
    decode_rows = hand_out(rows)
    refine_z, rows = refine_forward(decode_z, decode_rows, decode_params, masks, refine_full)
    refine_rows = hand_out(rows)
    logits, rows = classify(
        refine_z, grad_flat, refine_rows, refine_params, masks, w_cls, b_cls.reshape(1, -1)
    )
    logits = logits.reshape(logit_grad.shape)
    refine_sums = hand_out(rows)
    decode_local, rows, refine_totals, refine_kernel_grad = refine_backward(
        refine_z,
        grad_flat,
        refine_rows,
        refine_sums,
        refine_params,
        w_cls,
        decode_z,
        decode_rows,
        decode_params,
        masks,
        refine_full,
    )
    decode_sums = hand_out(rows)
    classes = w_cls.shape[1]
    cls_weight_grad = decode_sums[:classes, 2 * channels :].T
    cls_bias_grad = decode_sums[classes, 2 * channels : 2 * channels + classes]
    refine_gain, refine_bias = refine_totals[6], refine_totals[7]
    (
        proj_up,
        reduce_local,
        reduce_sums,
        decode_totals,
        decode_kernel_grad,
        low_kernel_grad,
    ) = decode_backward(
        decode_local,
        decode_z,
        decode_rows,
        decode_sums,
        decode_params,
        upsampled,
        low_flat,
        low_wide,
        low_vectors,
        down_table,
        masks,
        decode_full,
        coarse_shape,
    )
    decode_gain, decode_bias = decode_totals[6], decode_totals[7]
    proj_up = proj_up[None]
    reduce_gain, reduce_bias = reduce_sums[0, :extra], reduce_sums[1, :extra]

    proj_local, proj_gain, proj_bias = norm_grad_terms(
        proj_up, valid_coarse, proj_centered, proj_shaped
    )
    summed_pairs = gradient_sums([(proj_gain, proj_bias), (reduce_gain, reduce_bias)])
    proj_gain, proj_bias = summed_pairs[0]
    reduce_gain, reduce_bias = summed_pairs[1]
    flat_z = [item.reshape(height * columns, channels) for item in coarse_z]
    branch_vectors = jnp.concatenate(
        [
            norm_vectors(section_means[index], section_vars[index], gains[index], biases[index])
            for index in range(5)
        ],
        axis=1,
    )
    branch_counts = jnp.concatenate(
        [
            jnp.full((1, 4 * channels), 1.0) * pixel_count,
            jnp.full((1, channels), images_total, jnp.float32),
        ],
        axis=1,
    )
    proj_kernel_grad, branch_local, pool_local, rows = branch_back(
        proj_up.reshape(height * columns, channels),
        proj_z.reshape(height * columns, channels),
        norm_vectors(
            proj_mean,
            proj_var,
            gains[5],
            biases[5],
            proj_gain / pixel_count,
            proj_bias / pixel_count,
        ),
        joined_coarse.reshape(height * columns, -1),
        proj_full,
        flat_z,
        pool_wide,
        branch_vectors,
        mask_column,
        pool_mask,
        pool_inputs[0],
        devices,
    )
    rows = hand_out(rows)
    branch_dz = branch_grads(
        rows,
        branch_local,
        pool_local,
        flat_z,
        pool_wide,
        branch_vectors,
        branch_counts,
        mask_column,
        pool_mask,
    )
    flat_dz, pool_dz, branch_totals = list(branch_dz[:4]), branch_dz[4], branch_dz[5]
    last_pairs = [
        (
            branch_totals[0, index * channels : (index + 1) * channels],
            branch_totals[1, index * channels : (index + 1) * channels],
        )
        for index in range(5)
    ]
    low_vectors = widen(
        norm_vectors(
            low_mean,
            low_var,
            low_gain,
            low_bias,
            reduce_gain / fine_count,
            reduce_bias / fine_count,
        )
    )

    def low_late(tie):
        return low_backward(reduce_local, low_flat, low_wide, low_vectors, masks, tie)

    def input_late(tie):
        side_dz = [
            side_grads(
                flat_dz[branch + 1].reshape(1, height, columns, channels),
                ids_coarse,
                dilations[branch],
            ).reshape(height * columns, -1)
            for branch in range(3)
        ]
        return coarse_input(
            flat_dz[0],
            pool_dz,
            spread_rows,
            side_dz,
            parts,
            coarse_shape,
            features.shape[3],
            tie,
        )

    def weight_part(part, grads, tie=None):
        return coarse_weight(
            part,
            sides,
            grads[1:4],
            coarse_shape,
            (grads[0], pooled, grads[4]) if SCATTER.has_point(part) else None,
            tie,
        )

    owned, small_owned, low_level_grad, features_grad = scatter_taps(
        flat_dz + [pool_dz],
        [item.shape for item in small],
        [functools.partial(weight_part, part) for part in range(len(SCATTER.parts))],
        (proj_kernel_grad, decode_kernel_grad, low_kernel_grad, refine_kernel_grad),
        [low_late, input_late],
    )
    low_level_grad = low_level_grad.reshape(low_level.shape)
    features_grad = features_grad.reshape(features.shape)
    proj_owned, reduce_owned, decode_owned, refine_owned = small_owned
    point_owned, atrous_owned = SCATTER.restore(owned, w_atrous.shape)
    gains_grad = jnp.stack(
        [
            last_pairs[0][0],
            last_pairs[1][0],
            last_pairs[2][0],
            last_pairs[3][0],
            last_pairs[4][0],
            proj_gain,
            decode_gain,
            refine_gain,
        ]
    )
    biases_grad = jnp.stack(
        [
            last_pairs[0][1],
            last_pairs[1][1],
            last_pairs[2][1],
            last_pairs[3][1],
            last_pairs[4][1],
            proj_bias,
            decode_bias,
            refine_bias,
        ]
    )
    return (
        logits,
        features_grad,
        low_level_grad,
        point_owned,
        atrous_owned,
        proj_owned,
        reduce_owned,
        decode_owned,
        refine_owned,
        cls_weight_grad,
        cls_bias_grad,
        gains_grad,
        biases_grad,
        reduce_gain,
        reduce_bias,
    )


def solution(mesh):
    in_specs = (
        P(("wide", "narrow"), None, None, None),
        P(("wide", "narrow"), None, None, None),
        P(("wide", "narrow"), None),
        P(None, "wide", "narrow"),
        P(None, None, "wide", "narrow"),
        P("wide", "narrow"),
        P("wide", "narrow"),
        P(None, "narrow", "wide"),
        P(None, "wide", "narrow"),
        P(),
        P(),
        P(),
        P(),
        P(),
        P(),
        P(("wide", "narrow"), None, None, None),
    )
    out_specs = (
        P(("wide", "narrow"), None, None, None),
        P(("wide", "narrow"), None, None, None),
        P(("wide", "narrow"), None, None, None),
        P(None, "wide", "narrow"),
        P(None, None, "wide", "narrow"),
        P("wide", "narrow"),
        P("wide", "narrow"),
        P(None, "narrow", "wide"),
        P(None, "wide", "narrow"),
        P(),
        P(),
        P(),
        P(),
        P(),
        P(),
    )
    return jax.shard_map(
        per_device, mesh=mesh, in_specs=in_specs, out_specs=out_specs, check_vma=False
    )
```

```python
import functools

import jax
import jax.numpy as jnp
from jax import lax
from jax.experimental import pallas as pl
from jax.experimental.pallas import tpu as pltpu
from jax.sharding import PartitionSpec as P

epsilon = 1e-05
highest = lax.Precision.HIGHEST
dilations = (6, 12, 18)
ROUNDS = 4
VMEM_BYTES = 48 * 1024 * 1024


class Layout:
    def __init__(self, chunks, point_chunk):
        self.chunks = chunks
        self.point_chunk = point_chunk
        self.parts = [(index, index + 1) for index in range(0, len(chunks), 2)]
        self.sizes = [[chunks[index] for index in part] for part in self.parts]
        places = []
        for chunk, size in enumerate(chunks):
            places += [(chunk, tap) for tap in range(2 if chunk == point_chunk else 0, size)]
        self.rows = [
            [(line,) + places[9 * branch + 3 * line] for line in range(3)] for branch in range(3)
        ]

    def part_of(self, chunk):
        return chunk // 2

    def place(self, chunk, tap):
        return tap + (self.chunks[chunk - 1] if chunk % 2 else 0)

    def part_rows(self, part):
        return [
            (branch, line, chunk, tap)
            for branch, rows in enumerate(self.rows)
            for line, chunk, tap in rows
            if chunk in self.parts[part]
        ]

    def has_point(self, part):
        return self.point_chunk in self.parts[part]

    def order(self, point, atrous):
        flat = atrous.reshape((-1,) + atrous.shape[2:])
        before = sum(self.chunks[: self.point_chunk])
        parts = []
        start = 0
        for part, sizes in enumerate(self.sizes):
            size = sum(sizes)
            if self.has_point(part):
                pieces = [flat[start:before], point, flat[before : start + size - 2]]
                parts.append(jnp.concatenate([item for item in pieces if item.shape[0]]))
                start += size - 2
            else:
                parts.append(flat[start : start + size])
                start += size
        return parts

    def restore(self, parts, shape):
        flat = jnp.concatenate(parts)
        before = sum(self.chunks[: self.point_chunk])
        atrous = jnp.concatenate([flat[:before], flat[before + 2 :]])
        return (flat[before : before + 2], atrous.reshape(shape))


GATHER = Layout((5, 6, 6, 3, 3, 6), 0)
SCATTER = Layout((3, 3, 5, 6, 6, 6), 2)


def exchange(values, axis, bit):
    size = lax.axis_size(axis)
    return lax.ppermute(values, axis, [(place, place ^ bit) for place in range(size)])


def rotate(values, axis, step, stride):
    size = lax.axis_size(axis)
    rounds = size // stride
    pairs = []
    for place in range(size):
        outer, inner = place // stride, place % stride
        pairs.append((place, ((outer + step) % rounds) * stride + inner))
    return lax.ppermute(values, axis, pairs)


def device_count():
    return lax.axis_size("wide") * lax.axis_size("narrow")


def hand_out(rows):
    return lax.all_to_all(rows, ("wide", "narrow"), 0, 0, tiled=True)


def from_all(values):
    return hand_out(jnp.broadcast_to(values[None], (device_count(),) + values.shape))


def merge_rows(counts, means, squares):
    total = jnp.sum(counts, axis=0)
    mean = jnp.sum(counts * means, axis=0) / total
    gap = means - mean[None]
    return (total, mean, jnp.sum(squares + counts * gap * gap, axis=0))


def local_moments(values, valid_map, count):
    axes = tuple(range(values.ndim - 1))
    mean = jnp.sum(values * valid_map, axis=axes) / count
    centered = values - mean
    return (mean, jnp.sum(centered * centered * valid_map, axis=axes))


def place():
    wide = lax.axis_index("wide")
    narrow = lax.axis_index("narrow")
    return (wide // 2, wide % 2, narrow // 2, narrow % 2)


def share_core(shard):
    core = place()[3]
    half = shard.shape[1] // 2
    parts = shard.reshape(shard.shape[0], 2, half, shard.shape[2])
    kept = lax.dynamic_index_in_dim(parts, core, 1, keepdims=False)
    given = lax.dynamic_index_in_dim(parts, 1 - core, 1, keepdims=False)
    got = exchange(given, "narrow", 1)
    lower = jnp.where(core == 0, kept, got)
    upper = jnp.where(core == 0, got, kept)
    return jnp.concatenate([lower, upper], axis=2)


def tuned():
    return lax.axis_size("wide") == 2 * ROUNDS and lax.axis_size("narrow") == 4


def kernel_place():
    values = jnp.stack(place()).astype(jnp.int32)
    return values if tuned() else jnp.zeros_like(values)


def tied(values, earlier):
    mark = earlier[(0,) * earlier.ndim]
    return jnp.where(mark == mark, values, jnp.zeros_like(values))


def one_step(body, outs, args, specs=None, tie=None, vmem=32 * 1024 * 1024):
    def whole_spec(array):
        return pl.BlockSpec(array.shape, lambda step: (0,) * len(array.shape))

    specs = list(specs or [None] * len(args))
    run = body
    if tie is not None:
        ties = tie if isinstance(tie, list) else [tie]
        args = ties + list(args)
        specs = [pl.BlockSpec(memory_space=pl.ANY)] * len(ties) + specs

        def run(*refs):
            body(*refs[len(ties) :])

    return pl.pallas_call(
        run,
        out_shape=outs,
        grid=(1,),
        in_specs=[spec or whole_spec(arg) for spec, arg in zip(specs, args)],
        out_specs=[whole_spec(out) for out in outs],
        compiler_params=pltpu.CompilerParams(vmem_limit_bytes=vmem),
        cost_estimate=cost(0, args),
        name="move",
    )(*args)


def entry_spec(array, index):
    block = (1,) + array.shape[1:]
    return pl.BlockSpec(block, lambda step: (index,) + (0,) * (len(block) - 1))


def cut(sizes):
    return [slice(sum(sizes[:index]), sum(sizes[: index + 1])) for index in range(len(sizes))]


def pass_on(values, tie):
    def body(source, target):
        target[...] = source[...]

    outs = [jax.ShapeDtypeStruct(values.shape, values.dtype)]
    return one_step(body, outs, [values], None, tie)[0]


def gather_depth(values):
    return [exchange(values, "wide", 2 * flip) for flip in range(1, ROUNDS)]


def lay_out(sizes, own, others, tie=None):
    shape = own.shape[1:]
    outs = [jax.ShapeDtypeStruct((ROUNDS, size) + shape, own.dtype) for size in sizes]

    def body(*refs):
        for target, taps in zip(refs[ROUNDS:], cut(sizes)):
            for slot, source in enumerate(refs[:ROUNDS]):
                target[slot] = source[taps]

    return one_step(body, outs, [own] + list(others), tie=tie)


def pair_up(values, others, tie=None):
    outs = [jax.ShapeDtypeStruct((2,) + item.shape, item.dtype) for item in values]
    count = len(outs)

    def body(*refs):
        for index in range(count):
            refs[2 * count + index][0] = refs[index][...]
            refs[2 * count + index][1] = refs[count + index][...]

    return one_step(body, outs, list(values) + list(others), tie=tie)


def pair_cut(sizes, values, others, tie=None):
    count = len(values)
    outs = [
        jax.ShapeDtypeStruct((2, ROUNDS, size) + values[0].shape[2:], values[0].dtype)
        for part in sizes
        for size in part
    ]

    def body(*refs):
        for index in range(count):
            taps = cut([part[index] for part in sizes])
            for part in range(len(sizes)):
                target = refs[2 * count + part * count + index]
                for half in range(2):
                    target[half] = refs[half * count + index][:, taps[part]]

    results = one_step(body, outs, list(values) + list(others), tie=tie)
    return [results[part * count : (part + 1) * count] for part in range(len(sizes))]


def pair_all(values, others, tie=None):
    count = len(values)
    shape = values[0].shape
    sizes = [item.shape[2] for item in values]
    outs = [jax.ShapeDtypeStruct((2,) + shape[:2] + (sum(sizes),) + shape[3:], values[0].dtype)]

    def body(*refs):
        target = refs[2 * count]
        for index, taps in enumerate(cut(sizes)):
            target[0, :, :, taps] = refs[index][...]
            target[1, :, :, taps] = refs[count + index][...]

    return one_step(body, outs, list(values) + list(others), tie=tie)[0]


def first_sums(sizes, keep, got, tie=None):
    tail = keep.shape[4:]
    outs = [jax.ShapeDtypeStruct((2, ROUNDS, size) + tail, jnp.bfloat16) for size in sizes]

    def body(keep_ref, got_ref, *targets):
        for target, taps in zip(targets, cut(sizes)):
            total = keep_ref[0, :, :, taps].astype(jnp.float32)
            total = total + got_ref[0, :, :, taps].astype(jnp.float32)
            target[...] = total.astype(jnp.bfloat16)

    return one_step(body, outs, [keep, got], [entry_spec(keep, 1), entry_spec(got, 1)], tie)


def second_sums(sizes, keep, got, values, tie=None):
    tail = keep.shape[4:]
    outs = [jax.ShapeDtypeStruct((ROUNDS, sum(sizes)) + tail, jnp.float32)]
    outs += [jax.ShapeDtypeStruct((ROUNDS, size) + tail, jnp.bfloat16) for size in sizes]
    count = len(sizes)

    def body(keep_ref, got_ref, *refs):
        kept = refs[count]
        for index, taps in enumerate(cut(sizes)):
            for half in range(2):
                total = keep_ref[0, half, :, taps].astype(jnp.float32)
                total = total + got_ref[0, half, :, taps].astype(jnp.float32)
                total = total + refs[index][half].astype(jnp.float32)
                if half:
                    refs[count + 1 + index][...] = total.astype(jnp.bfloat16)
                else:
                    kept[:, taps] = total

    specs = [entry_spec(keep, 0), entry_spec(got, 0)] + [None] * count
    results = one_step(body, outs, [keep, got] + list(values), specs, tie)
    return (results[0], results[1:])


def deep_sums(sizes, kept, values, tie=None):
    shape = (2,) + kept.shape[1:]
    outs = [jax.ShapeDtypeStruct(shape, dtype) for dtype in (jnp.float32, jnp.bfloat16)]
    count = len(sizes)

    def body(kept_ref, *refs):
        for slot in range(ROUNDS):
            target = refs[count + slot // 2]
            for value, taps in zip(refs, cut(sizes)):
                total = kept_ref[slot, taps] + value[slot].astype(jnp.float32)
                target[slot % 2, taps] = total.astype(target.dtype)

    return one_step(body, outs, [kept] + list(values), None, tie)


def near_sums(kept, far, tie=None):
    shape = kept.shape[1:]
    outs = [jax.ShapeDtypeStruct(shape, dtype) for dtype in (jnp.float32, jnp.bfloat16)]

    def body(kept_ref, far_ref, *targets):
        for slot, target in enumerate(targets):
            total = kept_ref[slot] + far_ref[slot].astype(jnp.float32)
            target[...] = total.astype(target.dtype)

    return one_step(body, outs, [kept, far], None, tie)


def last_sums(kept, near, tie=None):
    def body(kept_ref, near_ref, target):
        target[...] = kept_ref[...] + near_ref[...].astype(jnp.float32)

    outs = [jax.ShapeDtypeStruct(kept.shape, jnp.float32)]
    return one_step(body, outs, [kept, near], None, tie)[0]


def chunk_order(index):
    return [("wide", 1), ("narrow", 2)] if index % 2 == 0 else [("narrow", 2), ("wide", 1)]


def gather_taps(weights, small, fillers, kernels, prepared):
    rounds = ROUNDS
    sizes = GATHER.sizes
    shapes = [item.shape for item in small]
    if not tuned():
        parts = []
        for part, values in zip(GATHER.parts, weights):
            full = lax.all_gather(values, "narrow", axis=2, tiled=True)
            full = lax.all_gather(full, "wide", axis=1, tiled=True)
            rows = full.shape[1] // (4 * rounds)
            full = full.reshape(full.shape[0], rounds, 2, 2, rows, 2, full.shape[2] // 2)
            start = 0
            pieces = []
            for index in part:
                piece = full[start : start + GATHER.chunks[index]]
                start += GATHER.chunks[index]
                order = (3, 5, 2, 1, 0, 4, 6) if index % 2 == 0 else (3, 2, 5, 1, 0, 4, 6)
                pieces.append(piece.transpose(order))
            joined = jnp.concatenate(pieces, axis=4)
            parts.append((joined[0], joined[1]))
        flat = pack_small(small)
        everything = lax.all_gather(flat, ("wide", "narrow"))
        everything = everything.reshape(lax.axis_size("wide"), lax.axis_size("narrow"), -1)
        unpacked = unpack_small(everything, small)
        ready = fillers[0]()
        results = fillers[1](*unpacked)
        result = None
        for pair, kernel in zip(parts, kernels):
            result = kernel(ready, pair, result)
        return (parts, unpacked, ready, results, result)

    def along(part, stacks, turn):
        return [
            exchange(stack, *chunk_order(index)[turn]) for stack, index in zip(stacks, GATHER.parts[part])
        ]

    def across(values):
        return (values, exchange(values, "narrow", 1))

    first, second = sizes[1], sizes[2]
    weights = [
        weights[0],
        jnp.concatenate(
            [
                weights[1][: first[0]],
                weights[2][: second[0]],
                weights[1][first[0] :],
                weights[2][second[0] :],
            ]
        ),
    ]
    joint = [first[0] + second[0], first[1] + second[1]]
    shared = [share_core(values) for values in weights]
    z0 = gather_depth(shared[0])
    small = small_block(small)
    xs = exchange(small, "wide", 1)
    small = pair_up([small], [xs], shared[1])[0]
    ys = exchange(small, "narrow", 2)
    small = pair_up([small], [ys])[0]
    s0 = lay_out(sizes[0], shared[0], z0, small)
    f0 = along(0, s0, 0)
    z1 = gather_depth(shared[1])
    s0 = pair_up(s0, f0, [z1[1]] + prepared)
    g0 = along(0, s0, 1)
    ready = fillers[0]()
    s1 = lay_out(joint, shared[1], z1, s0[0])
    f1 = along(0, s1, 0)
    small = pass_on(small, s1[0])
    zs = gather_depth(small)
    p0 = across(pair_all(s0, g0, s1[0]))
    s1, s2 = pair_cut([first, second], s1, f1, zs[0])
    g1 = along(0, s1, 1)
    g2 = along(0, s2, 1)
    result = kernels[0](ready, p0, None, s1[0])
    small = lay_out([2], small, zs, result[0][0])[0]
    cs = exchange(small, "narrow", 1)
    p1 = across(pair_all(s1, g1, small))
    unpacked = unpack_block(small, cs, shapes=shapes)
    results = fillers[1](*unpacked)
    result = kernels[1](ready, p1, result)
    p2 = across(pair_all(s2, g2, p1[0]))
    result = kernels[2](ready, p2, result)
    return ([p0, p1, p2], unpacked, ready, results, result)


def scatter_taps(grads, shapes, kernels, pack, fillers):
    rounds = ROUNDS
    if not tuned():
        owned = []
        for part, kernel in zip(SCATTER.parts, kernels):
            joined = jnp.stack(kernel(grads))
            pieces = []
            for index, taps in zip(part, cut([SCATTER.chunks[index] for index in part])):
                piece = joined[:, :, :, :, taps]
                order = (4, 3, 1, 0, 5, 2, 6) if index % 2 == 0 else (4, 3, 2, 0, 5, 1, 6)
                piece = piece.transpose(order)
                pieces.append(piece.reshape(piece.shape[0], -1, 2 * piece.shape[6]))
            full = jnp.concatenate(pieces)
            full = lax.psum_scatter(full, "wide", scatter_dimension=1, tiled=True)
            full = lax.psum_scatter(full, "narrow", scatter_dimension=2, tiled=True)
            owned.append(full.astype(jnp.float32))
        low, low_weight = fillers[0](grads[0])
        small = pack_grads(low_weight, *pack, shapes)
        small = lax.psum_scatter(small, "wide", scatter_dimension=0, tiled=True)
        small = lax.psum_scatter(small, "narrow", scatter_dimension=1, tiled=True)
        small = unpack_grads(small[0, 0].astype(jnp.float32), shapes)
        return (owned, small, low, fillers[1](None))

    sizes = SCATTER.sizes

    def across(pair):
        return (pair[0], exchange(pair[1], "narrow", 1))

    def along(indices, values, turn):
        return [
            exchange(value, *chunk_order(index)[turn]) for value, index in zip(values, indices)
        ]

    def far(sent):
        return exchange(sent, "wide", 4)

    def near(sent):
        return exchange(sent, "wide", 2)

    a, b, c = 2, 1, 0
    pair_a = across(kernels[a](grads))
    pair_b = across(kernels[b](grads, tie=pair_a[0]))
    sent = first_sums(sizes[a], *pair_a, pair_b[0])
    first_a = along(SCATTER.parts[a], sent, 0)
    low, low_weight = fillers[0](sent[0])
    pair_s = across(pack_block(pack[0], low_weight, *pack[1:], shapes=shapes, tie=low_weight))
    sizes_s = [pair_s[0].shape[3]]
    pair_c = across(kernels[c](grads, tie=pair_s[0]))
    kept_a, sent = second_sums(sizes[a], *pair_a, first_a, pair_c[0])
    second_a = along(SCATTER.parts[a], sent, 1)
    sent = first_sums(sizes[b], *pair_b, sent[0])
    first_b = along(SCATTER.parts[b], sent, 0)
    kept_a, sent = deep_sums(sizes[a], kept_a, second_a, sent[0])
    far_a = far(sent)
    sent = first_sums(sizes_s, *pair_s, sent)
    first_s = along((0,), sent, 0)
    filled = fillers[1](sent[0])
    kept_b, sent = second_sums(sizes[b], *pair_b, first_b, filled)
    second_b = along(SCATTER.parts[b], sent, 1)
    sent = first_sums(sizes[c], *pair_c, sent[0])
    first_c = along(SCATTER.parts[c], sent, 0)
    kept_s, sent = second_sums(sizes_s, *pair_s, first_s, sent[0])
    second_s = along((0,), sent, 1)
    total_a, sent = near_sums(kept_a, far_a, sent[0])
    near_a = near(sent)
    kept_b, sent = deep_sums(sizes[b], kept_b, second_b, sent)
    far_b = far(sent)
    kept_c, sent = second_sums(sizes[c], *pair_c, first_c, sent)
    second_c = along(SCATTER.parts[c], sent, 1)
    kept_s, sent = deep_sums(sizes_s, kept_s, second_s, sent[0])
    far_s = far(sent)
    total_a = last_sums(total_a, near_a, sent)
    kept_c, sent = deep_sums(sizes[c], kept_c, second_c, total_a)
    far_c = far(sent)
    total_b, sent = near_sums(kept_b, far_b, sent)
    near_b = near(sent)
    total_s, sent = near_sums(kept_s, far_s, sent)
    near_s = near(sent)
    total_c, sent = near_sums(kept_c, far_c, sent)
    near_c = near(sent)
    total_b = last_sums(total_b, near_b, sent)
    total_s = last_sums(total_s, near_s, total_b)
    total_c = last_sums(total_c, near_c, total_s)
    owned = [settle_core(total) for total in (total_c, total_b, total_a)]
    small = settle_small(total_s, shapes)
    return (owned, small, low, filled)


def row_span(dilation, row, height):
    step = (row - 1) * dilation
    return (max(step, 0), max(-step, 0), height - abs(step))


def tap_matrix(pair, chunk, tap, place_ref):
    row, core = place_ref[2], place_ref[3]
    flip = lax.rem(pl.program_id(0) + place_ref[1], 2)
    place = GATHER.place(chunk, tap)

    def half(ref):
        if chunk % 2 == 0:
            sides = [ref[y, flip, 0, place] for y in (row, 1 - row)]
        else:
            sides = [ref[flip, y, 0, place] for y in (row, 1 - row)]
        return jnp.concatenate(sides, axis=1)

    mine = half(pair[0])
    other = half(pair[1])
    lower = jnp.where(core == 0, mine, other)
    upper = jnp.where(core == 0, other, mine)
    return jnp.concatenate([lower, upper], axis=0)


def part_spec(array):
    def index_map(step, place_ref):
        return (0, 0, lax.bitwise_xor(step // 2, place_ref[0]), 0, 0, 0)

    return pl.BlockSpec((2, 2, 1) + array.shape[3:], index_map)


def whole_cost(flops, arrays):
    total = 0
    for array in arrays:
        size = array.dtype.itemsize
        for extent in array.shape:
            size *= extent
        total += size
    return pl.CostEstimate(flops=int(flops), bytes_accessed=total, transcendentals=0)


def cost(flops, arrays):
    return pl.CostEstimate(flops=1, bytes_accessed=1, transcendentals=0)


def coarse_flops(rows, shape, width):
    height, columns, channels = shape
    extents = sum(row_span(dilations[branch], line, height)[2] for branch, line in rows)
    return 2 * 3 * extents * columns * channels * width


def full_spec(array):
    return pl.BlockSpec(array.shape, lambda step, place_ref: (0,) * array.ndim)


def lane_spec(array):
    return pl.BlockSpec(
        (array.shape[0], array.shape[1] // (2 * ROUNDS)), lambda step, place_ref: (0, step)
    )


def store_moments(z_ref, mask_ref, stats_ref):
    mask = mask_ref[...]
    count = jnp.sum(mask)
    values = z_ref[...]
    mean = jnp.sum(values * mask, axis=0, keepdims=True) / count
    centered = (values - mean) * mask
    stats_ref[0:1, :] = mean
    stats_ref[1:2, :] = jnp.sum(centered * centered, axis=0, keepdims=True)


def behind_tie(kernel):
    def run(place_ref, tie_ref, *refs):
        kernel(place_ref, *refs)

    return run


def coarse_forward_kernel(plan, place_ref, *refs):
    refs = list(refs)
    mask_ref = refs.pop(0)
    center = refs.pop(0)
    outer = {branch: (refs.pop(0), refs.pop(0)) for branch in plan["branches"]}
    before = {branch: refs.pop(0) for branch in plan["begun"]}
    if plan["pool"]:
        member_ref = refs.pop(0)
        sizes_ref = refs.pop(0)
    pair = (refs.pop(0), refs.pop(0))
    results = {branch: refs.pop(0) for branch in plan["branches"]}
    stats = {branch: refs.pop(0) for branch in plan["done"]}
    step = pl.program_id(0)

    @pl.when(step == 0)
    def _():
        for branch in plan["branches"]:
            if branch in before:
                results[branch][...] = before[branch][...]
            else:
                results[branch][...] = jnp.zeros_like(results[branch])

    columns = plan["columns"]
    for branch, row, chunk, tap in plan["rows"]:
        source, target, extent = row_span(dilations[branch], row, plan["height"])
        matrix = jnp.concatenate(
            [tap_matrix(pair, chunk, tap + k, place_ref) for k in range(3)],
            axis=0,
        )
        rows_in = pl.ds(source * columns, extent * columns)
        rows_out = pl.ds(target * columns, extent * columns)
        sides = (outer[branch][0], center, outer[branch][1])
        values = jnp.concatenate([side[rows_in, :] for side in sides], axis=1)
        results[branch][rows_out, :] += jnp.dot(
            values, matrix, preferred_element_type=jnp.float32
        )
    if plan["pool"]:
        point_ref, point_stats_ref, pool_ref, pooled_ref = refs

        @pl.when(step == 0)
        def _():
            point_ref[...] = jnp.zeros_like(point_ref)
            pool_ref[...] = jnp.zeros_like(pool_ref)

        values = center[...]
        point_ref[...] += jnp.dot(
            values, tap_matrix(pair, GATHER.point_chunk, 0, place_ref), preferred_element_type=jnp.float32
        )
        pooled = jnp.dot(member_ref[...], values, preferred_element_type=jnp.float32)
        pooled = (pooled * sizes_ref[...]).astype(jnp.bfloat16)
        pooled_ref[...] = pooled
        pool_ref[...] += jnp.dot(
            pooled, tap_matrix(pair, GATHER.point_chunk, 1, place_ref), preferred_element_type=jnp.float32
        )

    @pl.when(step == 2 * ROUNDS - 1)
    def _():
        for branch in plan["done"]:
            store_moments(results[branch], mask_ref, stats[branch])
        if plan["pool"]:
            store_moments(point_ref, mask_ref, point_stats_ref)


def coarse_forward(part, mask, sides, pair, shape, begun, pool=None, tie=None):
    height, columns, channels = shape
    positions = height * columns
    rows = GATHER.part_rows(part)
    branches = sorted({row[0] for row in rows})
    done = [branch for branch in branches if GATHER.rows[branch][-1][1] in GATHER.parts[part]]
    plan = {
        "pool": pool is not None,
        "chunks": GATHER.parts[part],
        "branches": branches,
        "begun": [branch for branch in branches if branch in begun],
        "done": done,
        "columns": columns,
        "height": height,
        "rows": rows,
    }
    center = sides[0][1]
    args = [mask, center]
    specs = [full_spec(mask), lane_spec(center)]
    for branch in branches:
        args += [sides[branch][0], sides[branch][2]]
        specs += [lane_spec(center)] * 2
    for branch in plan["begun"]:
        args.append(begun[branch])
        specs.append(full_spec(begun[branch]))
    if pool:
        args += list(pool)
        specs += [full_spec(item) for item in pool]
    args += list(pair)
    specs += [part_spec(item) for item in pair]
    kernel = functools.partial(coarse_forward_kernel, plan)
    if tie is not None:
        kernel = behind_tie(kernel)
        args.insert(0, tie)
        specs.insert(0, pl.BlockSpec(memory_space=pl.ANY))
    flat = jax.ShapeDtypeStruct((positions, channels), jnp.float32)
    small = jax.ShapeDtypeStruct((8, channels), jnp.float32)
    outs = [flat] * len(branches) + [small] * len(done)
    if pool:
        outs += [flat, small, small, jax.ShapeDtypeStruct((8, center.shape[1]), jnp.bfloat16)]
    out_specs = [full_spec(item) for item in outs]
    if pool:
        out_specs[-1] = lane_spec(outs[-1])
    results = pl.pallas_call(
        kernel,
        out_shape=outs,
        grid_spec=pltpu.PrefetchScalarGridSpec(
            num_scalar_prefetch=1, grid=(2 * ROUNDS,), in_specs=specs, out_specs=out_specs
        ),
        compiler_params=pltpu.CompilerParams(vmem_limit_bytes=VMEM_BYTES),
        cost_estimate=cost(
            coarse_flops([row[:2] for row in rows], shape, center.shape[1])
            + (2 * positions * channels * center.shape[1] if pool else 0),
            args + outs,
        ),
        name="coarse_forward",
    )(kernel_place(), *args)
    sums = dict(zip(branches, results))
    stats = dict(zip(done, results[len(branches) :]))
    return (sums, stats, results[len(branches) + len(done) :])


def coarse_weight_kernel(plan, place_ref, *refs):
    refs = list(refs)
    center = refs.pop(0)
    outer = {branch: (refs.pop(0), refs.pop(0)) for branch in plan["branches"]}
    grads = {branch: refs.pop(0) for branch in plan["branches"]}
    if plan["pool"]:
        point_ref, pooled_ref, pool_ref = refs.pop(0), refs.pop(0), refs.pop(0)
    outs = (refs.pop(0), refs.pop(0))
    row, core = place_ref[2], place_ref[3]
    flip = lax.rem(pl.program_id(0) + place_ref[1], 2)
    rows, cols = outs[0].shape[-2:]
    columns = plan["columns"]

    def store(chunk, tap, value):
        value = value.astype(jnp.bfloat16)
        lower, upper = value[:rows], value[rows:]
        mine = jnp.where(core == 0, lower, upper)
        other = jnp.where(core == 0, upper, lower)
        place = SCATTER.place(chunk, tap)
        for ref, part in zip(outs, (mine, other)):
            for side, lane_part in ((row, part[:, :cols]), (1 - row, part[:, cols:])):
                if chunk % 2 == 0:
                    ref[flip, side, 0, place] = lane_part
                else:
                    ref[side, flip, 0, place] = lane_part

    across = (((0,), (0,)), ((), ()))
    for branch, line, chunk, tap in plan["rows"]:
        source, target, extent = row_span(dilations[branch], line, plan["height"])
        sides = (outer[branch][0], center, outer[branch][1])
        values = jnp.concatenate(
            [side[pl.ds(source * columns, extent * columns), :] for side in sides], axis=1
        )
        result = lax.dot_general(
            values,
            grads[branch][pl.ds(target * columns, extent * columns), :],
            across,
            preferred_element_type=jnp.float32,
        )
        for k in range(3):
            store(chunk, tap + k, result[2 * rows * k : 2 * rows * (k + 1)])
    if plan["pool"]:
        for tap, left, right in ((0, center, point_ref), (1, pooled_ref, pool_ref)):
            store(
                SCATTER.point_chunk,
                tap,
                lax.dot_general(
                    left[...], right[...], across, preferred_element_type=jnp.float32
                ),
            )


def coarse_weight(part, sides, grads, shape, pool=None, tie=None):
    height, columns, channels = shape
    rows = SCATTER.part_rows(part)
    branches = sorted({row[0] for row in rows})
    plan = {
        "pool": pool is not None,
        "branches": branches,
        "chunks": SCATTER.parts[part],
        "rows": rows,
        "columns": columns,
        "height": height,
    }
    center = sides[0][1]
    args = [center]
    specs = [lane_spec(center)]
    for branch in branches:
        args += [sides[branch][0], sides[branch][2]]
        specs += [lane_spec(center)] * 2
    for branch in branches:
        args.append(grads[branch])
        specs.append(full_spec(grads[branch]))
    if pool:
        args += list(pool)
        specs += [full_spec(pool[0]), lane_spec(pool[1]), full_spec(pool[2])]
    kernel = functools.partial(coarse_weight_kernel, plan)
    if tie is not None:
        kernel = behind_tie(kernel)
        args.insert(0, tie)
        specs.insert(0, pl.BlockSpec(memory_space=pl.ANY))
    total = sum(SCATTER.sizes[part])
    tail = (total, center.shape[1] // (4 * ROUNDS), channels // 2)
    outs = [jax.ShapeDtypeStruct((2, 2, ROUNDS) + tail, jnp.bfloat16)] * 2
    out_specs = [part_spec(item) for item in outs]
    results = pl.pallas_call(
        kernel,
        out_shape=outs,
        grid_spec=pltpu.PrefetchScalarGridSpec(
            num_scalar_prefetch=1, grid=(2 * ROUNDS,), in_specs=specs, out_specs=out_specs
        ),
        compiler_params=pltpu.CompilerParams(vmem_limit_bytes=VMEM_BYTES),
        cost_estimate=cost(
            coarse_flops([row[:2] for row in rows], shape, center.shape[1])
            + (2 * height * columns * channels * center.shape[1] if pool else 0),
            args + outs,
        ),
        name="coarse_weight",
    )(kernel_place(), *args)
    return (results[0], results[1])


def coarse_input_kernel(plan, place_ref, *refs):
    refs = list(refs)
    point_ref, pool_ref, spread_ref = refs.pop(0), refs.pop(0), refs.pop(0)
    grads = [refs.pop(0) for _ in range(3)]
    pairs = [(refs.pop(0), refs.pop(0)) for _ in GATHER.parts]
    point_pair = pairs[GATHER.part_of(GATHER.point_chunk)]
    out_ref, total_ref = refs
    columns = plan["columns"]
    turned = (((1,), (1,)), ((), ()))
    total_ref[...] = lax.dot_general(
        point_ref[...],
        tap_matrix(point_pair, GATHER.point_chunk, 0, place_ref),
        turned,
        preferred_element_type=jnp.float32,
    )
    pooled = lax.dot_general(
        pool_ref[...],
        tap_matrix(point_pair, GATHER.point_chunk, 1, place_ref),
        turned,
        preferred_element_type=jnp.float32,
    )
    total_ref[...] += jnp.dot(
        spread_ref[...], pooled, preferred_element_type=jnp.float32, precision=highest
    )
    for branch, rows in enumerate(plan["rows"]):
        for line, chunk, tap in rows:
            source, target, extent = row_span(dilations[branch], line, plan["height"])
            matrix = jnp.concatenate(
                [
                    tap_matrix(pairs[GATHER.part_of(chunk)], chunk, tap + k, place_ref)
                    for k in range(3)
                ],
                axis=1,
            )
            total_ref[pl.ds(source * columns, extent * columns), :] += lax.dot_general(
                grads[branch][pl.ds(target * columns, extent * columns), :],
                matrix,
                turned,
                preferred_element_type=jnp.float32,
            )
    out_ref[...] = total_ref[...].astype(jnp.bfloat16)


def coarse_input(point_dz, pool_dz, spread, grads, parts, shape, width, tie=None):
    height, columns, channels = shape
    plan = {
        "columns": columns,
        "height": height,
        "rows": GATHER.rows,
    }
    args = [point_dz, pool_dz, spread] + list(grads)
    specs = [full_spec(item) for item in args]
    for pair in parts:
        args += list(pair)
        specs += [part_spec(item) for item in pair]
    kernel = functools.partial(coarse_input_kernel, plan)
    if tie is not None:
        kernel = behind_tie(kernel)
        args.insert(0, tie)
        specs.insert(0, pl.BlockSpec(memory_space=pl.ANY))
    out = jax.ShapeDtypeStruct((height * columns, width), jnp.bfloat16)
    return pl.pallas_call(
        kernel,
        out_shape=out,
        grid_spec=pltpu.PrefetchScalarGridSpec(
            num_scalar_prefetch=1,
            grid=(2 * ROUNDS,),
            in_specs=specs,
            out_specs=lane_spec(out),
            scratch_shapes=[pltpu.VMEM((height * columns, width // (2 * ROUNDS)), jnp.float32)],
        ),
        compiler_params=pltpu.CompilerParams(vmem_limit_bytes=VMEM_BYTES),
        cost_estimate=cost(
            coarse_flops([(b, k) for b in range(3) for k in range(3)], shape, width)
            + 2 * height * columns * channels * width,
            args + [out],
        ),
        name="coarse_input",
    )(kernel_place(), *args)


STRIP = 8


def norm_vectors(mean, variance, gain, bias, *more):
    rows = [mean, lax.rsqrt(variance + epsilon), gain, bias] + list(more)
    rows += [jnp.zeros_like(mean)] * (8 - len(rows))
    return jnp.stack(rows)


def sigmoid(values):
    return 0.5 * jnp.tanh(0.5 * values) + 0.5


def vector(ref, index):
    return ref[index : index + 1, :]


def shaped_of(values, vector_ref):
    centered = (values - vector(vector_ref, 0)) * vector(vector_ref, 1)
    return (centered, centered * vector(vector_ref, 2) + vector(vector_ref, 3))


def slope_of(shaped, gate):
    return gate * (1.0 + shaped * (1.0 - gate))


def merge_vectors(rows_ref, params_ref, vector_ref, sums_ref=None):
    width = vector_ref.shape[1]
    means = rows_ref[:, :width]
    squares = rows_ref[:, width : 2 * width]
    counts = rows_ref[:, 2 * width : 2 * width + 1]
    total = jnp.sum(counts, axis=0, keepdims=True)
    mean = jnp.sum(counts * means, axis=0, keepdims=True) / total
    gap = means - mean
    variance = jnp.sum(squares + counts * gap * gap, axis=0, keepdims=True) / total
    vector_ref[0:1, :] = mean
    vector_ref[1:2, :] = lax.rsqrt(variance + epsilon)
    vector_ref[2:4, :] = params_ref[...]
    if sums_ref is not None:
        for index in range(2):
            part = sums_ref[:, index * width : (index + 1) * width]
            vector_ref[6 + index : 7 + index, :] = jnp.sum(part, axis=0, keepdims=True)
            vector_ref[4 + index : 5 + index, :] = vector_ref[6 + index : 7 + index, :] / total


def send_rows(rows_ref, pieces):
    joined = jnp.concatenate(pieces, axis=1)
    rows_ref[...] = jnp.broadcast_to(joined, rows_ref.shape)


def send_moments(rows_ref, stats_ref, masks_ref, steps):
    count = jnp.sum(masks_ref[:, 0:1]) * steps
    send_rows(
        rows_ref,
        [stats_ref[0:1, :], stats_ref[1:2, :], jnp.full((1, 128), 1.0, jnp.float32) * count],
    )


def lag_specs(steps):
    def ahead(array, block):
        return pl.BlockSpec(block, lambda step: (jnp.minimum(step, steps - 1), 0))

    def behind(array, block):
        return pl.BlockSpec(block, lambda step: (jnp.maximum(step - 1, 0), 0))

    return (ahead, behind)


def whole(array):
    return pl.BlockSpec(array.shape, lambda step: (0,) * len(array.shape))


def window(ref, start, step, columns):
    return ref[pl.ds(pl.multiple_of((start + step) * columns, columns), STRIP * columns), :]


def run_moments(values, mask, stats_ref, step):
    count = jnp.sum(mask)
    mean = jnp.sum(values * mask, axis=0, keepdims=True) / count
    centered = (values - mean) * mask
    squares = jnp.sum(centered * centered, axis=0, keepdims=True)
    done = (step - 1).astype(jnp.float32)
    old_mean = jnp.where(step > 1, stats_ref[0:1, :], mean)
    old_squares = jnp.where(step > 1, stats_ref[1:2, :], 0.0)
    gap = mean - old_mean
    stats_ref[0:1, :] = old_mean + gap / (done + 1.0)
    stats_ref[1:2, :] = old_squares + squares + gap * gap * (count * done / (done + 1.0))


def spread_columns(products, masks_ref):
    size = products.shape[0]
    width = products.shape[1] // 3
    result = products[:, width : 2 * width]
    result = result + masks_ref[:, 1:2] * pltpu.roll(products[:, :width], 1, 0)
    return result + masks_ref[:, 2:3] * pltpu.roll(products[:, 2 * width :], size - 1, 0)


def clear_edges(ref, columns):
    ref[:columns, :] = jnp.zeros((columns, ref.shape[1]), ref.dtype)
    ref[ref.shape[0] - columns :, :] = jnp.zeros((columns, ref.shape[1]), ref.dtype)


def row_taps(w_ref, row, start, stop):
    return jnp.concatenate([w_ref[3 * row + k, start:stop, :] for k in range(3)], axis=1)


def low_lanes(width):
    return lax.broadcasted_iota(jnp.int32, (1, width), 1)


def decode_forward_kernel(
    steps, act_ref, table_ref, low_ref, wide_ref, vector_ref, masks_ref, w_ref, z_ref, rows_ref,
    up_ref, joined_ref, reduced_ref, stats_ref
):
    step = pl.program_id(0)
    columns = table_ref.shape[0]
    channels = act_ref.shape[2]
    rows = act_ref.shape[0]

    @pl.when(step == 0)
    def _():
        clear_edges(joined_ref, columns)
        clear_edges(reduced_ref, columns)

    @pl.when(step < steps)
    def _():
        for offset in range(STRIP):
            base = step * (STRIP // 4) + offset // 4 + (offset % 4 - 2) // 2
            fraction = ((2 * (offset % 4) - 3) % 8) / 8.0
            lower = act_ref[jnp.maximum(base, 0)]
            upper = act_ref[jnp.minimum(base + 1, rows - 1)]
            mixed = (1.0 - fraction) * lower + fraction * upper
            coarse = mixed.astype(jnp.bfloat16)
            fine = (mixed - coarse.astype(jnp.float32)).astype(jnp.bfloat16)
            value = jnp.dot(
                table_ref[...],
                jnp.concatenate([coarse, fine], axis=0),
                preferred_element_type=jnp.float32,
            ).astype(jnp.bfloat16)
            up_ref[offset * columns : (offset + 1) * columns, :] = value
            start = pl.multiple_of((step * STRIP + offset + 1) * columns, columns)
            joined_ref[pl.ds(start, columns), :] = value
        reduced = jnp.dot(low_ref[...], wide_ref[...], preferred_element_type=jnp.float32)
        _, shaped = shaped_of(reduced, vector_ref)
        value = masks_ref[:, 0:1] * (shaped * sigmoid(shaped))
        start = pl.multiple_of((step * STRIP + 1) * columns, columns)
        reduced_ref[pl.ds(start, STRIP * columns), :] = value.astype(jnp.bfloat16)

    @pl.when(step > 0)
    def _():
        start = (step - 1) * STRIP
        lane = low_lanes(reduced_ref.shape[1])
        lows = [window(reduced_ref, start, k, columns) for k in range(3)]
        low = jnp.where(lane < 64, lows[0], jnp.where(lane < 128, lows[1], lows[2]))
        values = jnp.concatenate(
            [window(joined_ref, start, k, columns) for k in range(3)] + [low], axis=1
        )
        extra = w_ref.shape[1] - channels
        parts = [row_taps(w_ref, k, 0, channels) for k in range(3)]
        for k in range(3):
            parts.append(row_taps(w_ref, k, channels, channels + extra))
            parts.append(jnp.zeros((64 - extra, 3 * channels), jnp.bfloat16))
        parts.append(jnp.zeros((64, 3 * channels), jnp.bfloat16))
        products = jnp.dot(
            values, jnp.concatenate(parts, axis=0), preferred_element_type=jnp.float32
        )
        result = spread_columns(products, masks_ref)
        z_ref[...] = result
        run_moments(result, masks_ref[:, 0:1], stats_ref, step)

    @pl.when(step == steps)
    def _():
        send_moments(rows_ref, stats_ref, masks_ref, steps)


def decode_forward(act, table, low, wide, vectors, masks, weights, devices):
    positions = low.shape[0]
    columns = table.shape[0]
    block = STRIP * columns
    steps = positions // block
    channels = act.shape[2]
    ahead, behind = lag_specs(steps)
    flat = jax.ShapeDtypeStruct((positions, channels), jnp.float32)
    stats = jax.ShapeDtypeStruct((devices, 2 * channels + 128), jnp.float32)
    up = jax.ShapeDtypeStruct((positions, channels), jnp.bfloat16)
    return pl.pallas_call(
        functools.partial(decode_forward_kernel, steps),
        out_shape=[flat, stats, up],
        grid=(steps + 1,),
        in_specs=[
            whole(act),
            whole(table),
            ahead(low, (block, low.shape[1])),
            whole(wide),
            whole(vectors),
            whole(masks),
            whole(weights),
        ],
        out_specs=[
            behind(flat, (block, channels)),
            whole(stats),
            ahead(up, (block, channels)),
        ],
        scratch_shapes=[
            pltpu.VMEM((positions + 2 * columns, channels), jnp.bfloat16),
            pltpu.VMEM((positions + 2 * columns, wide.shape[1]), jnp.bfloat16),
            pltpu.VMEM((8, channels), jnp.float32),
        ],
        compiler_params=pltpu.CompilerParams(vmem_limit_bytes=VMEM_BYTES),
        cost_estimate=cost(2 * positions * 3 * channels * 4 * channels, [low, flat, up]),
        name="decode_forward",
    )(act, table, low, wide, vectors, masks, weights)


def refine_forward_kernel(
    steps, columns, z_in_ref, rows_in_ref, params_ref, masks_ref, w_ref, z_ref, rows_ref, act_ref,
    vector_ref, stats_ref
):
    step = pl.program_id(0)
    channels = w_ref.shape[1]

    @pl.when(step == 0)
    def _():
        clear_edges(act_ref, columns)
        merge_vectors(rows_in_ref, params_ref, vector_ref)

    @pl.when(step < steps)
    def _():
        _, shaped = shaped_of(z_in_ref[...], vector_ref)
        value = masks_ref[:, 0:1] * (shaped * sigmoid(shaped))
        start = pl.multiple_of((step * STRIP + 1) * columns, columns)
        act_ref[pl.ds(start, STRIP * columns), :] = value.astype(jnp.bfloat16)

    @pl.when(step > 0)
    def _():
        start = (step - 1) * STRIP
        values = jnp.concatenate([window(act_ref, start, k, columns) for k in range(3)], axis=1)
        matrix = jnp.concatenate([row_taps(w_ref, k, 0, channels) for k in range(3)], axis=0)
        products = jnp.dot(values, matrix, preferred_element_type=jnp.float32)
        result = spread_columns(products, masks_ref)
        z_ref[...] = result
        run_moments(result, masks_ref[:, 0:1], stats_ref, step)

    @pl.when(step == steps)
    def _():
        send_moments(rows_ref, stats_ref, masks_ref, steps)


def refine_forward(z_in, rows, params, masks, weights):
    positions, channels = z_in.shape
    block = masks.shape[0]
    columns = block // STRIP
    steps = positions // block
    ahead, behind = lag_specs(steps)
    flat = jax.ShapeDtypeStruct((positions, channels), jnp.float32)
    stats = jax.ShapeDtypeStruct(rows.shape, jnp.float32)
    return pl.pallas_call(
        functools.partial(refine_forward_kernel, steps, columns),
        out_shape=[flat, stats],
        grid=(steps + 1,),
        in_specs=[
            ahead(z_in, (block, channels)),
            whole(rows),
            whole(params),
            whole(masks),
            whole(weights),
        ],
        out_specs=[behind(flat, (block, channels)), whole(stats)],
        scratch_shapes=[
            pltpu.VMEM((positions + 2 * columns, channels), jnp.bfloat16),
            pltpu.VMEM((8, channels), jnp.float32),
            pltpu.VMEM((8, channels), jnp.float32),
        ],
        compiler_params=pltpu.CompilerParams(vmem_limit_bytes=VMEM_BYTES),
        cost_estimate=cost(2 * positions * 9 * channels * channels, [z_in, flat]),
        name="refine_forward",
    )(z_in, rows, params, masks, weights)


def class_kernel(
    steps, z_ref, grad_ref, rows_ref, params_ref, masks_ref, w_ref, b_ref, logits_ref, out_ref,
    vector_ref, sums_ref, weight_ref, bias_ref
):
    step = pl.program_id(0)

    @pl.when(step == 0)
    def _():
        merge_vectors(rows_ref, params_ref, vector_ref)
        sums_ref[...] = jnp.zeros_like(sums_ref)
        weight_ref[...] = jnp.zeros_like(weight_ref)
        bias_ref[...] = jnp.zeros_like(bias_ref)

    mask = masks_ref[:, 0:1]
    centered, shaped = shaped_of(z_ref[...], vector_ref)
    gate = sigmoid(shaped)
    act = (mask * (shaped * gate)).astype(jnp.bfloat16)
    logits = jnp.dot(act, w_ref[...], preferred_element_type=jnp.float32) + b_ref[...]
    logits_ref[...] = (mask * logits).astype(jnp.bfloat16)
    grad = (mask * grad_ref[...].astype(jnp.float32)).astype(jnp.bfloat16)
    upstream = lax.dot_general(
        grad, w_ref[...], (((1,), (1,)), ((), ())), preferred_element_type=jnp.float32
    )
    local = mask * upstream * slope_of(shaped, gate)
    sums_ref[0:1, :] += jnp.sum(local * centered, axis=0, keepdims=True)
    sums_ref[1:2, :] += jnp.sum(local, axis=0, keepdims=True)
    weight_ref[...] += lax.dot_general(
        grad, act, (((0,), (0,)), ((), ())), preferred_element_type=jnp.float32
    )
    bias_ref[...] += jnp.sum(grad.astype(jnp.float32), axis=0, keepdims=True)

    @pl.when(step == steps - 1)
    def _():
        width = vector_ref.shape[1]
        classes = bias_ref.shape[1]
        shape = (classes, width)
        place = lax.broadcasted_iota(jnp.int32, shape, 0) == lax.broadcasted_iota(jnp.int32, shape, 1)
        wide_bias = jnp.dot(
            bias_ref[...],
            jnp.where(place, 1.0, 0.0),
            preferred_element_type=jnp.float32,
            precision=highest,
        )
        out_ref[...] = jnp.zeros_like(out_ref)
        send_rows(out_ref.at[:, : 2 * width], [sums_ref[0:1, :], sums_ref[1:2, :]])
        out_ref[:classes, 2 * width :] = weight_ref[...]
        out_ref[classes : classes + 1, 2 * width :] = wide_bias


def classify(z, grad, rows, params, masks, weights, bias):
    positions, channels = z.shape
    block = masks.shape[0]
    classes = grad.shape[1]
    steps = positions // block
    outs = [
        jax.ShapeDtypeStruct((positions, classes), jnp.bfloat16),
        jax.ShapeDtypeStruct((rows.shape[0], 3 * channels), jnp.float32),
    ]

    def strip(width):
        return pl.BlockSpec((block, width), lambda step: (step, 0))

    return pl.pallas_call(
        functools.partial(class_kernel, steps),
        out_shape=outs,
        grid=(steps,),
        in_specs=[
            strip(channels),
            strip(classes),
            whole(rows),
            whole(params),
            whole(masks),
            whole(weights),
            whole(bias),
        ],
        out_specs=[strip(classes), whole(outs[1])],
        scratch_shapes=[
            pltpu.VMEM((8, channels), jnp.float32),
            pltpu.VMEM((8, channels), jnp.float32),
            pltpu.VMEM((classes, channels), jnp.float32),
            pltpu.VMEM((1, classes), jnp.float32),
        ],
        compiler_params=pltpu.CompilerParams(vmem_limit_bytes=VMEM_BYTES),
        cost_estimate=cost(6 * positions * channels * 128, [z, grad, grad]),
        name="classify",
    )(z, grad, rows, params, masks, weights, bias)


def finish_grad(local, centered, mask, vector_ref):
    inner = local - vector(vector_ref, 5) - centered * vector(vector_ref, 4)
    return mask * vector(vector_ref, 2) * vector(vector_ref, 1) * inner


def store_sides(grad, masks_ref, side_ref, start):
    size, width = grad.shape
    grad = grad.astype(jnp.bfloat16).astype(jnp.float32)
    rows = pl.ds(start, size)
    side_ref[rows, :width] = pltpu.roll(masks_ref[:, 1:2] * grad, size - 1, 0).astype(jnp.bfloat16)
    side_ref[rows, width : 2 * width] = grad.astype(jnp.bfloat16)
    side_ref[rows, 2 * width :] = pltpu.roll(masks_ref[:, 2:3] * grad, 1, 0).astype(jnp.bfloat16)


def refine_backward_kernel(
    steps, columns, z_ref, grad_ref, rows_ref, sums_in_ref, params_ref, cls_ref, z_in_ref,
    rows_in_ref, params_in_ref, masks_ref, w_ref, local_ref, out_ref, totals_ref, weight_ref,
    side_ref, vector_ref, vector_in_ref, sums_ref
):
    step = pl.program_id(0)
    channels = w_ref.shape[1]
    mask = masks_ref[:, 0:1]

    @pl.when(step == 0)
    def _():
        clear_edges(side_ref, columns)
        merge_vectors(rows_ref, params_ref, vector_ref, sums_in_ref)
        merge_vectors(rows_in_ref, params_in_ref, vector_in_ref)
        totals_ref[...] = vector_ref[...]
        sums_ref[...] = jnp.zeros_like(sums_ref)
        weight_ref[...] = jnp.zeros_like(weight_ref)

    @pl.when(step < steps)
    def _():
        centered, shaped = shaped_of(z_ref[...], vector_ref)
        grad = (mask * grad_ref[...].astype(jnp.float32)).astype(jnp.bfloat16)
        upstream = lax.dot_general(
            grad, cls_ref[...], (((1,), (1,)), ((), ())), preferred_element_type=jnp.float32
        )
        local = mask * upstream * slope_of(shaped, sigmoid(shaped))
        start = pl.multiple_of((step * STRIP + 1) * columns, columns)
        store_sides(finish_grad(local, centered, mask, vector_ref), masks_ref, side_ref, start)

    @pl.when(step > 0)
    def _():
        start = (step - 1) * STRIP
        centered, shaped = shaped_of(z_in_ref[...], vector_in_ref)
        gate = sigmoid(shaped)
        act = (mask * (shaped * gate)).astype(jnp.bfloat16)
        sides = [window(side_ref, start, 2 - k, columns) for k in range(3)]
        upstream = lax.dot_general(
            jnp.concatenate(sides, axis=1),
            jnp.concatenate([w_ref[tap] for tap in range(9)], axis=1),
            (((1,), (1,)), ((), ())),
            preferred_element_type=jnp.float32,
        )
        local = mask * upstream * slope_of(shaped, gate)
        local_ref[...] = local
        sums_ref[0:1, :] += jnp.sum(local * centered, axis=0, keepdims=True)
        sums_ref[1:2, :] += jnp.sum(local, axis=0, keepdims=True)
        turned = act.T
        for k in range(3):
            weight_ref[k] += jnp.dot(turned, sides[k], preferred_element_type=jnp.float32)

    @pl.when(step == steps)
    def _():
        share = jnp.sum(sums_in_ref[:, 2 * channels :], axis=0, keepdims=True)
        send_rows(out_ref, [sums_ref[0:1, :], sums_ref[1:2, :], share])


def refine_backward(
    z, grad, rows, sums, params, classes, z_in, rows_in, params_in, masks, weights
):
    positions, channels = z.shape
    block = masks.shape[0]
    columns = block // STRIP
    steps = positions // block
    ahead, behind = lag_specs(steps)
    outs = [
        jax.ShapeDtypeStruct((positions, channels), jnp.float32),
        jax.ShapeDtypeStruct(sums.shape, jnp.float32),
        jax.ShapeDtypeStruct((8, channels), jnp.float32),
        jax.ShapeDtypeStruct((3, channels, 3 * channels), jnp.float32),
    ]
    return pl.pallas_call(
        functools.partial(refine_backward_kernel, steps, columns),
        out_shape=outs,
        grid=(steps + 1,),
        in_specs=[
            ahead(z, (block, channels)),
            ahead(grad, (block, grad.shape[1])),
            whole(rows),
            whole(sums),
            whole(params),
            whole(classes),
            behind(z_in, (block, channels)),
            whole(rows_in),
            whole(params_in),
            whole(masks),
            whole(weights),
        ],
        out_specs=[behind(z, (block, channels))] + [whole(item) for item in outs[1:]],
        scratch_shapes=[
            pltpu.VMEM((positions + 2 * columns, 3 * channels), jnp.bfloat16),
            pltpu.VMEM((8, channels), jnp.float32),
            pltpu.VMEM((8, channels), jnp.float32),
            pltpu.VMEM((8, channels), jnp.float32),
        ],
        compiler_params=pltpu.CompilerParams(vmem_limit_bytes=VMEM_BYTES),
        cost_estimate=cost(4 * positions * 9 * channels * channels, [z, z_in, grad, outs[0], weights]),
        name="refine_backward",
    )(z, grad, rows, sums, params, classes, z_in, rows_in, params_in, masks, weights)


def decode_backward_kernel(
    steps, columns, local_ref, z_ref, rows_ref, sums_in_ref, params_ref, up_ref, low_ref, wide_ref,
    low_vector_ref, table_ref, masks_ref, w_ref, coarse_ref, low_local_ref, sums_ref, totals_ref,
    weight_ref, low_weight_ref, side_ref, total_ref, vector_ref
):
    step = pl.program_id(0)
    channels = w_ref.shape[2]
    extra = w_ref.shape[1] - channels
    mask = masks_ref[:, 0:1]

    @pl.when(step == 0)
    def _():
        clear_edges(side_ref, columns)
        merge_vectors(rows_ref, params_ref, vector_ref, sums_in_ref)
        totals_ref[...] = vector_ref[...]
        sums_ref[...] = jnp.zeros_like(sums_ref)
        weight_ref[...] = jnp.zeros_like(weight_ref)
        low_weight_ref[...] = jnp.zeros_like(low_weight_ref)
        total_ref[...] = jnp.zeros_like(total_ref)

    @pl.when(step < steps)
    def _():
        centered, _ = shaped_of(z_ref[...], vector_ref)
        start = pl.multiple_of((step * STRIP + 1) * columns, columns)
        grad = finish_grad(local_ref[...], centered, mask, vector_ref)
        store_sides(grad, masks_ref, side_ref, start)

    @pl.when(step > 0)
    def _():
        start = (step - 1) * STRIP
        sides = [window(side_ref, start, 2 - k, columns) for k in range(3)]
        pieces = []
        for tap in range(9):
            pieces.append(
                jnp.concatenate(
                    [w_ref[tap], jnp.zeros((64 - extra, channels), jnp.bfloat16)], axis=0
                )
            )
        upstream = lax.dot_general(
            jnp.concatenate(sides, axis=1),
            jnp.concatenate(pieces, axis=1),
            (((1,), (1,)), ((), ())),
            preferred_element_type=jnp.float32,
        )
        for offset in range(STRIP):
            base = (step - 1) * (STRIP // 4) + offset // 4 + (offset % 4 - 2) // 2
            fraction = ((2 * (offset % 4) - 3) % 8) / 8.0
            value = upstream[offset * columns : (offset + 1) * columns, :channels]
            value = value.astype(jnp.bfloat16).astype(jnp.float32)
            total_ref[base + 1] += (1.0 - fraction) * value
            total_ref[base + 2] += fraction * value
        reduced = jnp.dot(low_ref[...], wide_ref[...], preferred_element_type=jnp.float32)
        centered, shaped = shaped_of(reduced, low_vector_ref)
        gate = sigmoid(shaped)
        low_act = (mask * (shaped * gate)).astype(jnp.bfloat16)
        low_up = upstream[:, channels:]
        local = mask * low_up * slope_of(shaped, gate)[:, :64]
        low_local_ref[...] = local
        sums_ref[0:1, :64] += jnp.sum(local * centered[:, :64], axis=0, keepdims=True)
        sums_ref[1:2, :64] += jnp.sum(local, axis=0, keepdims=True)
        turned = up_ref[...].T
        low_turned = low_act[:, :128].T[:64]
        for k in range(3):
            weight_ref[k] += jnp.dot(turned, sides[k], preferred_element_type=jnp.float32)
            low_weight_ref[k] += jnp.dot(low_turned, sides[k], preferred_element_type=jnp.float32)

    @pl.when(step == steps)
    def _():
        rows = coarse_ref.shape[0]
        total_ref[1] += total_ref[0]
        total_ref[rows] += total_ref[rows + 1]
        for row in range(rows):
            value = total_ref[row + 1]
            upper = value.astype(jnp.bfloat16)
            lower = (value - upper.astype(jnp.float32)).astype(jnp.bfloat16)
            coarse_ref[row] = jnp.dot(
                table_ref[...],
                jnp.concatenate([upper, lower], axis=0),
                preferred_element_type=jnp.float32,
            )


def decode_backward(
    local, z, rows, sums, params, up, low, wide, low_vectors, table, masks, weights, shape
):
    positions, channels = z.shape
    block = masks.shape[0]
    columns = block // STRIP
    steps = positions // block
    height, coarse_columns, _ = shape
    ahead, behind = lag_specs(steps)
    outs = [
        jax.ShapeDtypeStruct((height, coarse_columns, channels), jnp.float32),
        jax.ShapeDtypeStruct((positions, 64), jnp.float32),
        jax.ShapeDtypeStruct((8, channels), jnp.float32),
        jax.ShapeDtypeStruct((8, channels), jnp.float32),
        jax.ShapeDtypeStruct((3, channels, 3 * channels), jnp.float32),
        jax.ShapeDtypeStruct((3, 64, 3 * channels), jnp.float32),
    ]
    return pl.pallas_call(
        functools.partial(decode_backward_kernel, steps, columns),
        out_shape=outs,
        grid=(steps + 1,),
        in_specs=[
            ahead(local, (block, channels)),
            ahead(z, (block, channels)),
            whole(rows),
            whole(sums),
            whole(params),
            behind(up, (block, channels)),
            behind(low, (block, low.shape[1])),
            whole(wide),
            whole(low_vectors),
            whole(table),
            whole(masks),
            whole(weights),
        ],
        out_specs=[whole(outs[0]), behind(outs[1], (block, 64))]
        + [whole(item) for item in outs[2:]],
        scratch_shapes=[
            pltpu.VMEM((positions + 2 * columns, 3 * channels), jnp.bfloat16),
            pltpu.VMEM((height + 2, columns, channels), jnp.float32),
            pltpu.VMEM((8, channels), jnp.float32),
        ],
        compiler_params=pltpu.CompilerParams(vmem_limit_bytes=VMEM_BYTES),
        cost_estimate=cost(4 * positions * 9 * channels * (channels + 64), [local, z, up, low, outs[1], weights]),
        name="decode_backward",
    )(local, z, rows, sums, params, up, low, wide, low_vectors, table, masks, weights)


def branch_back(
    upstream, z, vectors, joined, weights, branch_z, pool_z, branch_vectors, mask, pool_mask, member,
    devices
):
    positions, channels = z.shape
    width = joined.shape[1]
    count = len(branch_z)
    outs = [
        jax.ShapeDtypeStruct((width, channels), jnp.float32),
        jax.ShapeDtypeStruct((positions, count * channels), jnp.float32),
        jax.ShapeDtypeStruct(pool_z.shape, jnp.float32),
        jax.ShapeDtypeStruct((devices, 2 * width), jnp.float32),
    ]
    args = [upstream, z, vectors, joined, weights, pool_z, branch_vectors, mask, pool_mask, member]
    args += list(branch_z)

    def body(*refs):
        (up_ref, z_ref, vector_ref, joined_ref, w_ref, pool_ref, branch_ref, mask_ref) = refs[:8]
        pool_mask_ref, member_ref = refs[8:10]
        z_refs = refs[10 : 10 + count]
        weight_ref, local_ref, pool_local_ref, rows_ref = refs[10 + count :]
        valid = mask_ref[...]
        centered, shaped = shaped_of(z_ref[...], vector_ref)
        local = valid * up_ref[...] * slope_of(shaped, sigmoid(shaped))
        grad = finish_grad(local, centered, valid, vector_ref).astype(jnp.bfloat16)
        weight_ref[...] = lax.dot_general(
            joined_ref[...], grad, (((0,), (0,)), ((), ())), preferred_element_type=jnp.float32
        )
        spread = lax.dot_general(
            grad, w_ref[...], (((1,), (1,)), ((), ())), preferred_element_type=jnp.float32
        )
        gains = []
        biases = []
        for index in range(count + 1):
            lanes = slice(index * channels, (index + 1) * channels)
            values = spread[:, lanes]
            if index < count:
                source, allowed = z_refs[index], valid
            else:
                source, allowed = pool_ref, pool_mask_ref[...]
                upper = values.astype(jnp.bfloat16)
                lower = (values - upper.astype(jnp.float32)).astype(jnp.bfloat16)
                values = jnp.dot(member_ref[...], upper, preferred_element_type=jnp.float32)
                values += jnp.dot(member_ref[...], lower, preferred_element_type=jnp.float32)
            centered, shaped = shaped_of(source[...], branch_ref.at[:, lanes])
            term = allowed * values * slope_of(shaped, sigmoid(shaped))
            if index < count:
                local_ref[:, lanes] = term
            else:
                pool_local_ref[...] = term
            gains.append(jnp.sum(term * centered, axis=0, keepdims=True))
            biases.append(jnp.sum(term, axis=0, keepdims=True))
        send_rows(rows_ref, gains + biases)

    return one_step(body, outs, args, vmem=60 * 1024 * 1024)


def branch_grads(rows, local, pool_local, branch_z, pool_z, branch_vectors, counts, mask, pool_mask):
    positions, channels = branch_z[0].shape
    count = len(branch_z)
    width = (count + 1) * channels
    outs = [jax.ShapeDtypeStruct((positions, channels), jnp.bfloat16)] * count
    outs += [jax.ShapeDtypeStruct(pool_z.shape, jnp.bfloat16)]
    outs += [jax.ShapeDtypeStruct((8, width), jnp.float32)]
    args = [rows, local, pool_local, pool_z, branch_vectors, counts, mask, pool_mask]
    args += list(branch_z)

    def body(*refs):
        rows_ref, local_ref, pool_local_ref, pool_ref, branch_ref, counts_ref = refs[:6]
        mask_ref, pool_mask_ref = refs[6:8]
        z_refs = refs[8 : 8 + count]
        grad_refs, totals_ref = refs[8 + count : -1], refs[-1]
        totals_ref[...] = jnp.zeros_like(totals_ref)
        totals_ref[0:1, :] = jnp.sum(rows_ref[:, :width], axis=0, keepdims=True)
        totals_ref[1:2, :] = jnp.sum(rows_ref[:, width:], axis=0, keepdims=True)
        for index in range(count + 1):
            lanes = slice(index * channels, (index + 1) * channels)
            vectors = branch_ref.at[:, lanes]
            source = z_refs[index] if index < count else pool_ref
            allowed = mask_ref[...] if index < count else pool_mask_ref[...]
            term = local_ref[:, lanes] if index < count else pool_local_ref[...]
            centered, _ = shaped_of(source[...], vectors)
            share = 1.0 / counts_ref[:, lanes]
            inner = term - totals_ref[1:2, lanes] * share
            inner = inner - centered * (totals_ref[0:1, lanes] * share)
            grad = allowed * vector(vectors, 2) * vector(vectors, 1) * inner
            grad_refs[index][...] = grad.astype(jnp.bfloat16)

    return one_step(body, outs, args, vmem=60 * 1024 * 1024)


def low_backward_kernel(
    vector_ref, local_ref, low_ref, wide_ref, masks_ref, out_ref, weight_ref
):
    @pl.when(pl.program_id(0) == 0)
    def _():
        weight_ref[...] = jnp.zeros_like(weight_ref)

    low = low_ref[...]
    weights = wide_ref[:, :128]
    reduced = jnp.dot(low, weights, preferred_element_type=jnp.float32)
    mean, scale, gain = (vector_ref[k : k + 1, :64] for k in range(3))
    centered = (reduced[:, :64] - mean) * scale
    inner = local_ref[...] - vector_ref[5:6, :64] - centered * vector_ref[4:5, :64]
    grad = (masks_ref[:, 0:1] * gain * scale * inner).astype(jnp.bfloat16)
    out_ref[...] = lax.dot_general(
        grad, weights[:, :64], (((1,), (1,)), ((), ())), preferred_element_type=jnp.float32
    ).astype(jnp.bfloat16)
    weight_ref[...] += lax.dot_general(
        grad, low, (((0,), (0,)), ((), ())), preferred_element_type=jnp.float32
    )


def low_backward(local, low, wide, vectors, masks, tie):
    positions, width = low.shape
    block = masks.shape[0]
    outs = [
        jax.ShapeDtypeStruct((positions, width), jnp.bfloat16),
        jax.ShapeDtypeStruct((64, width), jnp.float32),
    ]
    return pl.pallas_call(
        behind_tie(low_backward_kernel),
        out_shape=outs,
        grid=(positions // block,),
        in_specs=[
            whole(vectors),
            pl.BlockSpec(memory_space=pl.ANY),
            pl.BlockSpec((block, 64), lambda step: (step, 0)),
            pl.BlockSpec((block, width), lambda step: (step, 0)),
            whole(wide),
            whole(masks),
        ],
        out_specs=[pl.BlockSpec((block, width), lambda step: (step, 0)), whole(outs[1])],
        compiler_params=pltpu.CompilerParams(vmem_limit_bytes=VMEM_BYTES),
        cost_estimate=whole_cost(6 * positions * width * 128, [local, low, low]),
        name="low_backward",
    )(vectors, tie, local, low, wide, masks)


def side_values(values, image_ids, dilation):
    result = []
    for step in (-dilation, dilation):
        mask = tap_mask(image_ids, values.shape[1], 0, step).astype(values.dtype)
        result.append(mask * shifted(values, 0, step))
    return [result[0], values, result[1]]


def side_grads(values, image_ids, dilation):
    result = []
    for step in (-dilation, 0, dilation):
        masked = tap_mask(image_ids, values.shape[1], 0, step).astype(values.dtype) * values
        result.append(shifted(masked, 0, -step))
    return jnp.concatenate(result, axis=-1)


def settle_core(values):
    core = place()[3]
    taps, rows, cols = values.shape
    parts = values.reshape(taps, rows, 2, cols // 2)
    kept = lax.dynamic_index_in_dim(parts, core, 2, keepdims=False)
    given = lax.dynamic_index_in_dim(parts, 1 - core, 2, keepdims=False).astype(jnp.bfloat16)
    got = exchange(given, "narrow", 1).astype(jnp.float32)
    lower = jnp.where(core == 0, kept, got)
    upper = jnp.where(core == 0, got, kept)
    return jnp.concatenate([lower, upper], axis=1)


def band_ids(widths, columns):
    ends_all = jnp.cumsum(widths, axis=1)
    position = jnp.arange(columns, dtype=jnp.int32)
    band_index = jnp.sum(
        (position[None, :, None] >= ends_all[:, None, :]).astype(jnp.int32), axis=2
    )
    return jnp.where(band_index < widths.shape[1] - 1, band_index, -1)


def shifted(values, row_shift, col_shift):
    height = values.shape[1]
    columns = values.shape[2]
    padded = jnp.pad(
        values, ((0, 0), (abs(row_shift), abs(row_shift)), (abs(col_shift), abs(col_shift)), (0, 0))
    )
    row_start = abs(row_shift) + row_shift
    col_start = abs(col_shift) + col_shift
    return padded[:, row_start : row_start + height, col_start : col_start + columns, :]


def tap_mask(image_ids, height, row_shift, col_shift):
    columns = image_ids.shape[1]
    padded = jnp.pad(image_ids, ((0, 0), (abs(col_shift), abs(col_shift))), constant_values=-2)
    col_start = abs(col_shift) + col_shift
    other_ids = padded[:, col_start : col_start + columns]
    same_image = (other_ids == image_ids).astype(jnp.float32)
    row_place = jnp.arange(height) + row_shift
    inside = ((row_place >= 0) & (row_place < height)).astype(jnp.float32)
    return (inside[None, :, None] * same_image[:, None, :])[..., None]


def tap_offsets(dilation):
    return [
        ((tap_index // 3 - 1) * dilation, (tap_index % 3 - 1) * dilation) for tap_index in range(9)
    ]


def linear_weights(out_count, in_count):
    position = jnp.arange(out_count, dtype=jnp.int32)
    scaled = 2 * position - 3
    left_index = jnp.floor_divide(scaled, 8)
    fraction = (scaled - 8 * left_index).astype(jnp.float32) / 8.0
    lower_index = jnp.clip(left_index, 0, in_count - 1)
    upper_index = jnp.clip(left_index + 1, 0, in_count - 1)
    return (position, lower_index, upper_index, fraction)


def column_table(image_ids):
    columns = image_ids.shape[1]
    position, lower_index, upper_index, fraction = linear_weights(4 * columns, columns)
    source = jnp.arange(columns, dtype=jnp.int32)[None, :]

    def picker(index_row):
        return (source == index_row[:, None]).astype(jnp.int32)

    def lookup(index_row):
        return jnp.sum(image_ids[:, None, :] * picker(index_row)[None], axis=2)

    own_index = position // 4
    own_id = lookup(own_index)
    weight_lower = (1.0 - fraction)[None, :] * (lookup(lower_index) == own_id).astype(jnp.float32)
    weight_upper = fraction[None, :] * (lookup(upper_index) == own_id).astype(jnp.float32)
    weight_own = 1.0 - weight_lower - weight_upper
    table = weight_lower[:, :, None] * picker(lower_index)[None].astype(jnp.float32)
    table = table + weight_upper[:, :, None] * picker(upper_index)[None].astype(jnp.float32)
    table = table + weight_own[:, :, None] * picker(own_index)[None].astype(jnp.float32)
    return table


def normalize(values, valid_map, mean_row, variance, gain_row, bias_row):
    norm_scale = lax.rsqrt(variance + epsilon)
    centered = (values - mean_row) * norm_scale
    shaped = centered * gain_row + bias_row
    return (valid_map * jax.nn.silu(shaped), centered, shaped, norm_scale)


def norm_grad_terms(upstream, valid_map, centered, shaped):
    sigmoid_value = jax.nn.sigmoid(shaped)
    local_term = valid_map * upstream * sigmoid_value * (1.0 + shaped * (1.0 - sigmoid_value))
    axes = tuple(range(local_term.ndim - 1))
    return (local_term, jnp.sum(local_term * centered, axis=axes), jnp.sum(local_term, axis=axes))


def moments(values, valid_map, local_count, count_all):
    mean, squares = local_moments(values, valid_map, local_count)
    return merged(jnp.stack([mean, squares]), local_count, count_all)


def merged(stats, local_count, count_all):
    width = stats.shape[1]
    own = jnp.concatenate([stats[0], stats[1], jnp.full((1,), 1.0) * local_count])
    rows = from_all(own)
    counts, means, squares = merge_rows(
        rows[:, 2 * width :], rows[:, :width], rows[:, width : 2 * width]
    )
    return (means, squares / count_all)


def pack_pairs(pairs):
    return jnp.concatenate(
        [pair_item[0] for pair_item in pairs] + [pair_item[1] for pair_item in pairs]
    )


def unpack_pairs(flat, pairs):
    lengths = [pair_item[0].shape[0] for pair_item in pairs]
    half_point = sum(lengths)
    result_pairs = []
    offset = 0
    for length_now in lengths:
        result_pairs.append(
            (
                flat[offset : offset + length_now],
                flat[half_point + offset : half_point + offset + length_now],
            )
        )
        offset = offset + length_now
    return result_pairs


def gradient_sums(pairs):
    return unpack_pairs(jnp.sum(from_all(pack_pairs(pairs)), axis=0), pairs)


def small_block(items):
    proj, reduce, decode, refine = items
    taps, rows, cols = refine.shape
    count = proj.shape[0] // rows
    proj = proj.reshape(2, count, rows // 2, cols).swapaxes(0, 1).reshape(count, rows, cols)
    reduce = jnp.pad(reduce, ((0, 0), (0, cols - reduce.shape[1])))[None]
    shared = share_core(jnp.concatenate([refine, proj, reduce]))
    lanes = shared.shape[2]
    decode = decode.swapaxes(1, 2)
    decode = jnp.pad(decode, ((0, 0), (0, 0), (0, lanes - decode.shape[2])))
    return jnp.concatenate([shared, decode.reshape(-1, shared.shape[1], lanes)])


def settle_small(owned, shapes):
    shape_p, shape_r, shape_d, shape_f = shapes
    taps, rows, cols = shape_f
    count = shape_p[0] // rows
    first = taps + count + 1
    settled = settle_core(owned[:first])
    proj = settled[taps : taps + count].reshape(count, 2, rows // 2, cols)
    proj = proj.swapaxes(0, 1).reshape(shape_p)
    reduce = settled[taps + count, :, : shape_r[1]]
    decode = owned[first:].reshape(taps, shape_d[2], -1)[:, :, : shape_d[1]].swapaxes(1, 2)
    return (proj, reduce, decode, settled[:taps])


def reduce_lanes(width, row, core, half):
    start = (2 * row + core) * width
    return start, core * half


def unpack_kernel(shapes, place_ref, own_ref, other_ref, proj_ref, wide_ref, decode_ref, refine_ref):
    deep, side, row, core = (place_ref[index] for index in range(4))
    shape_p, shape_r, shape_d, shape_f = shapes
    taps = shape_f[0]
    rows = shape_f[1] // 2
    count = shape_p[0] // (2 * rows)
    lanes = own_ref.shape[-1]

    def load(ref, z, x, y, start, size):
        slot = lax.bitwise_xor(deep, z)
        return ref[slot, lax.rem(y + row, 2), lax.rem(x + side, 2), start : start + size]

    def both(z, x, y, start, size):
        mine = load(own_ref, z, x, y, start, size)
        others = load(other_ref, z, x, y, start, size)
        return (jnp.where(core == 0, mine, others), jnp.where(core == 0, others, mine))

    lane = lax.broadcasted_iota(jnp.int32, (1, lanes), 1)
    for z in range(ROUNDS):
        for x in range(2):
            wide = 2 * z + x
            halves = [both(z, x, y, 0, taps + count + 1) for y in range(2)]
            for h in range(2):
                joined = jnp.concatenate([halves[0][h], halves[1][h]], axis=-1)
                base = (2 * wide + h) * rows
                refine_ref[:, base : base + rows, :] = joined[:taps]
                base = (2 * wide + h) * rows * count
                proj_ref[base : base + rows * count, :] = joined[taps : taps + count].reshape(
                    rows * count, 2 * lanes
                )
                total = jnp.zeros((rows, lanes), jnp.float32)
                for y in range(2):
                    value = halves[y][h][taps + count].astype(jnp.float32)
                    for c in range(2):
                        start, held = reduce_lanes(shape_r[1], y, c, lanes // 2)
                        moved = pltpu.roll(value, (start - held) % lanes, 1)
                        inside = (lane >= start) & (lane < start + shape_r[1])
                        total = total + jnp.where(inside, moved, 0.0)
                base = (2 * wide + h) * rows
                left = total + pltpu.roll(total, 64, 1)
                wide_ref[base : base + rows, :] = jnp.concatenate([left, total], axis=1).astype(
                    jnp.bfloat16
                )
    height, width = shape_d[1], shape_d[2]
    blocks = width // rows
    for tap in range(taps):
        start = taps + count + 1 + tap * blocks
        pieces = []
        for y in range(2):
            columns = ([], [])
            for z in range(ROUNDS):
                for x in range(2):
                    for c, value in enumerate(both(z, x, y, start, blocks)):
                        columns[c].append(value.reshape(width, lanes))
            for c in range(2):
                joined = jnp.concatenate(columns[c], axis=0).astype(jnp.float32)
                pieces.append(joined.T[:height])
        decode_ref[tap] = jnp.concatenate(pieces, axis=0).astype(jnp.bfloat16)


def unpack_block(own, other, shapes):
    wide = 2 * ROUNDS
    shape_p, shape_r, shape_d, shape_f = shapes
    outs = [
        jax.ShapeDtypeStruct((wide * shape_p[0], 4 * shape_p[1]), jnp.bfloat16),
        jax.ShapeDtypeStruct((wide * shape_r[0], 256), jnp.bfloat16),
        jax.ShapeDtypeStruct((shape_d[0], 4 * shape_d[1], wide * shape_d[2]), jnp.bfloat16),
        jax.ShapeDtypeStruct((shape_f[0], wide * shape_f[1], 4 * shape_f[2]), jnp.bfloat16),
    ]
    return pl.pallas_call(
        functools.partial(unpack_kernel, shapes),
        out_shape=outs,
        in_specs=[pl.BlockSpec(memory_space=pltpu.SMEM)]
        + [pl.BlockSpec(memory_space=pltpu.VMEM)] * 2,
        out_specs=[pl.BlockSpec(memory_space=pltpu.VMEM)] * 4,
        compiler_params=pltpu.CompilerParams(vmem_limit_bytes=VMEM_BYTES),
        cost_estimate=whole_cost(0, [own, other] + outs + outs),
        name="unpack_weights",
    )(kernel_place(), own, other)


def pack_kernel(
    shapes, place_ref, proj_ref, reduce_ref, decode_ref, low_ref, refine_ref, keep_ref, give_ref
):
    deep, side, row, core = (place_ref[index] for index in range(4))
    shape_p, shape_r, shape_d, shape_f = shapes
    taps = shape_f[0]
    rows = shape_f[1] // 2
    count = shape_p[0] // (2 * rows)
    lanes = keep_ref.shape[-1]
    channels = 2 * lanes

    def store(z, x, y, start, size, values):
        values = [value.astype(jnp.bfloat16) for value in values]
        index = (
            lax.rem(x + side, 2),
            lax.rem(y + row, 2),
            lax.bitwise_xor(deep, z),
            pl.ds(start, size),
        )
        keep_ref[index] = jnp.where(core == 0, values[0], values[1])
        give_ref[index] = jnp.where(core == 0, values[1], values[0])

    lane = lax.broadcasted_iota(jnp.int32, (1, lanes), 1)
    reduce = jnp.concatenate(
        [reduce_ref[...], jnp.zeros((lanes - reduce_ref.shape[0], reduce_ref.shape[1]), jnp.float32)]
    ).T
    moved = []
    for y in range(2):
        total = jnp.zeros_like(reduce)
        for c in range(2):
            start, held = reduce_lanes(shape_r[1], y, c, lanes // 2)
            inside = (lane >= held) & (lane < held + shape_r[1])
            total = total + jnp.where(inside, pltpu.roll(reduce, (held - start) % lanes, 1), 0.0)
        moved.append(total)
    for z in range(ROUNDS):
        for x in range(2):
            wide = 2 * z + x
            for y in range(2):
                columns = slice(y * lanes, (y + 1) * lanes)
                for tap in range(taps):
                    line, k = tap // 3, tap % 3
                    left = k * channels + y * lanes
                    values = []
                    for h in range(2):
                        base = (2 * wide + h) * rows
                        values.append(
                            refine_ref[line, base : base + rows, left : left + lanes][None]
                        )
                    store(z, x, y, tap, 1, values)
                values = []
                for h in range(2):
                    base = (2 * wide + h) * rows * count
                    values.append(
                        proj_ref[base : base + rows * count, columns].reshape(count, rows, lanes)
                    )
                store(z, x, y, taps, count, values)
                values = [
                    moved[y][(2 * wide + h) * rows : (2 * wide + h + 1) * rows][None]
                    for h in range(2)
                ]
                store(z, x, y, taps + count, 1, values)
    height, width = shape_d[1], shape_d[2]
    blocks = width // rows
    for tap in range(taps):
        line, k = tap // 3, tap % 3
        columns = slice(k * channels, (k + 1) * channels)
        whole_tap = jnp.concatenate(
            [
                decode_ref[line, :, columns],
                low_ref[line, :, columns],
                jnp.zeros((lanes, channels), jnp.float32),
            ],
            axis=0,
        )
        turned = [whole_tap[n * height : n * height + lanes].T for n in range(4)]
        for z in range(ROUNDS):
            for x in range(2):
                base = (2 * z + x) * width
                for y in range(2):
                    values = [
                        turned[2 * y + c][base : base + width].reshape(blocks, rows, lanes)
                        for c in range(2)
                    ]
                    store(z, x, y, taps + count + 1 + tap * blocks, blocks, values)


def pack_block(proj, reduce, decode, low, refine, shapes, tie):
    shape_p, shape_r, shape_d, shape_f = shapes
    rows = shape_f[1] // 2
    total = shape_f[0] + shape_p[0] // (2 * rows) + 1 + shape_d[0] * shape_d[2] // rows
    out = jax.ShapeDtypeStruct((2, 2, ROUNDS, total, rows, 2 * shape_f[2]), jnp.bfloat16)
    return pl.pallas_call(
        behind_tie(functools.partial(pack_kernel, shapes)),
        out_shape=[out, out],
        in_specs=[pl.BlockSpec(memory_space=pltpu.SMEM), pl.BlockSpec(memory_space=pl.ANY)]
        + [pl.BlockSpec(memory_space=pltpu.VMEM)] * 5,
        out_specs=[pl.BlockSpec(memory_space=pltpu.VMEM)] * 2,
        compiler_params=pltpu.CompilerParams(vmem_limit_bytes=VMEM_BYTES),
        cost_estimate=whole_cost(0, [proj, decode, low, refine, out, out, out]),
        name="pack_gradients",
    )(kernel_place(), tie, proj, reduce, decode, low, refine)


def low_moments_kernel(low_ref, wide_ref, masks_ref, stats_ref):
    reduced = jnp.dot(low_ref[...], wide_ref[...], preferred_element_type=jnp.float32)
    run_moments(reduced, masks_ref[:, 0:1], stats_ref, pl.program_id(0) + 1)


def low_moments(low, wide, masks):
    block = masks.shape[0]
    out = jax.ShapeDtypeStruct((8, wide.shape[1]), jnp.float32)
    return pl.pallas_call(
        low_moments_kernel,
        out_shape=out,
        grid=(low.shape[0] // block,),
        in_specs=[
            pl.BlockSpec((block, low.shape[1]), lambda step: (step, 0)),
            whole(wide),
            whole(masks),
        ],
        out_specs=whole(out),
        compiler_params=pltpu.CompilerParams(vmem_limit_bytes=VMEM_BYTES),
        cost_estimate=whole_cost(2 * low.shape[0] * low.shape[1] * 256, [low]),
        name="low_moments",
    )(low, wide, masks)


def by_tap(values):
    width = values.shape[2] // 3
    split = values.reshape(3, values.shape[1], 3, width)
    return split.transpose(0, 2, 1, 3).reshape(9, values.shape[1], width)


def widen(values):
    padded = jnp.pad(values, ((0, 0), (0, 64 - values.shape[1])))
    return jnp.concatenate([padded, padded, padded, jnp.zeros_like(padded)], axis=1)


def pack_small(items):
    total = sum(item.size for item in items)
    padded = -(-total // 2048) * 2048
    flats = [item.reshape(-1) for item in items]
    return jnp.concatenate(flats + [jnp.zeros((padded - total,), jnp.bfloat16)]).reshape(-1, 128)


def unpack_small(everything, items):
    wide, narrow = everything.shape[:2]
    everything = everything.reshape(wide, narrow, -1)
    pieces = []
    start = 0
    for item in items:
        pieces.append(
            everything[:, :, start : start + item.size].reshape((wide, narrow) + item.shape)
        )
        start += item.size
    proj, reduce, decode, refine = pieces
    proj = proj.transpose(0, 2, 1, 3).reshape(wide * proj.shape[2], -1)
    reduce = reduce.transpose(0, 2, 1, 3).reshape(wide * reduce.shape[2], -1)
    decode = decode.transpose(2, 1, 3, 0, 4).reshape(decode.shape[2], narrow * decode.shape[3], -1)
    refine = refine.transpose(2, 0, 3, 1, 4).reshape(refine.shape[2], wide * refine.shape[3], -1)
    return (proj, widen(reduce), decode, refine)


def pack_grads(reduce, proj, decode, low, refine, shapes):
    wide = lax.axis_size("wide")
    narrow = lax.axis_size("narrow")
    extra = narrow * shapes[1][1]
    reduce = reduce[:extra].T
    decode = jnp.concatenate([by_tap(decode), by_tap(low)[:, :extra]], axis=1)
    refine = by_tap(refine)
    shape_p, shape_r, shape_d, shape_f = shapes
    proj = proj.reshape(wide, shape_p[0], narrow, shape_p[1]).transpose(0, 2, 1, 3)
    reduce = reduce.reshape(wide, shape_r[0], narrow, shape_r[1]).transpose(0, 2, 1, 3)
    decode = decode.reshape(shape_d[0], narrow, shape_d[1], wide, shape_d[2]).transpose(3, 1, 0, 2, 4)
    refine = refine.reshape(shape_f[0], wide, shape_f[1], narrow, shape_f[2]).transpose(1, 3, 0, 2, 4)
    flats = [
        item.astype(jnp.bfloat16).reshape(wide, narrow, -1)
        for item in (proj, reduce, decode, refine)
    ]
    total = sum(item.shape[2] for item in flats)
    padded = -(-total // 2048) * 2048
    flats.append(jnp.zeros((wide, narrow, padded - total), jnp.bfloat16))
    return jnp.concatenate(flats, axis=2).reshape(wide, narrow, -1, 128)


def unpack_grads(owned, shapes):
    owned = owned.reshape(-1)
    pieces = []
    start = 0
    for shape in shapes:
        size = 1
        for extent in shape:
            size *= extent
        pieces.append(owned[start : start + size].reshape(shape))
        start += size
    return pieces


def per_device(
    features,
    low_level,
    widths,
    w_point,
    w_atrous,
    w_proj,
    w_low,
    w_dec1,
    w_dec2,
    w_cls,
    b_cls,
    gains,
    biases,
    low_gain,
    low_bias,
    logit_grad,
):
    canvases = features.shape[0]
    height = features.shape[1]
    columns = features.shape[2]
    fine_columns = low_level.shape[2]
    images = widths.shape[1] - 1
    channels = gains.shape[1]
    images_total = float(canvases * lax.axis_size("wide") * lax.axis_size("narrow") * images)
    small = [w_proj, w_low, w_dec1, w_dec2]
    ids_coarse = band_ids(widths, columns)
    ids_fine = band_ids(4 * widths, fine_columns)
    valid_coarse = (ids_coarse >= 0).astype(jnp.float32)[:, None, :, None]
    valid_fine = (ids_fine >= 0).astype(jnp.float32)[:, None, :, None]
    all_ones = jnp.ones((1, 1, 1), jnp.float32)
    local_count = (height * jnp.sum(widths[:, :images])).astype(jnp.float32)
    member = (ids_coarse[:, :, None] == jnp.arange(images, dtype=jnp.int32)[None, None, :]).astype(
        jnp.float32
    )
    member_low = member.astype(jnp.bfloat16)
    image_sizes = (height * widths[:, :images]).astype(jnp.float32)
    positions = low_level.shape[1] * fine_columns
    low_flat = low_level.reshape(positions, -1)
    extra = low_gain.shape[0]
    side_masks = [tap_mask(ids_fine, STRIP, 0, step) for step in (-1, 1)]
    masks = jnp.concatenate([valid_fine * jnp.ones((1, STRIP, 1, 1))] + side_masks, axis=-1)
    masks = masks.reshape(STRIP * fine_columns, 3)
    coarse_shape = (height, columns, channels)
    mask_column = jnp.broadcast_to(valid_coarse, (1, height, columns, 1)).reshape(-1, 1)
    member_wide = jnp.pad(member[0], ((0, 0), (0, 8 - images)))
    member_rows = jnp.tile(member_wide, (height, 1))
    sizes_inverse = jnp.pad(1.0 / image_sizes[0], (0, 8 - images)).reshape(8, 1)
    pool_inputs = (member_rows.T.astype(jnp.bfloat16), sizes_inverse)

    cols_table = column_table(ids_coarse)[0].astype(jnp.bfloat16)
    up_table = jnp.concatenate([cols_table, cols_table], axis=1)
    down_table = jnp.concatenate([cols_table.T, cols_table.T], axis=1)
    decode_params = jnp.stack([gains[6], biases[6]])
    refine_params = jnp.stack([gains[7], biases[7]])
    pool_mask = (jnp.arange(8) < images).astype(jnp.float32).reshape(8, 1)
    grad_flat = logit_grad.reshape(-1, logit_grad.shape[-1])
    spread_rows = member_rows * sizes_inverse.reshape(1, 8)
    tall_masks = jnp.concatenate([masks, masks])
    prepared = [
        masks,
        tall_masks,
        mask_column,
        sizes_inverse,
        pool_inputs[0],
        up_table,
        down_table,
        decode_params,
        refine_params,
        pool_mask,
        grad_flat,
        w_cls,
        spread_rows,
    ]

    def all_sides():
        sides = [
            [
                item.reshape(height * columns, -1)
                for item in side_values(features, ids_coarse, dilation)
            ]
            for dilation in dilations
        ]
        return (sides, grad_flat)

    def low_part(proj, wide, decode, refine):
        return low_moments(low_flat, wide, tall_masks)

    def forward(part, ready, pair, before, tie=None):
        sums, stats, pooling = ({}, {}, ()) if before is None else before
        more, more_stats, more_pooling = coarse_forward(
            part,
            mask_column,
            ready[0],
            pair,
            coarse_shape,
            sums,
            pool_inputs if GATHER.has_point(part) else None,
            tie,
        )
        return ({**sums, **more}, {**stats, **more_stats}, tuple(pooling) + tuple(more_pooling))

    parts, unpacked, ready, low_stats, coarse = gather_taps(
        GATHER.order(w_point, w_atrous),
        small,
        [all_sides, low_part],
        [functools.partial(forward, part) for part in range(len(GATHER.parts))],
        prepared,
    )
    proj_full, low_wide, decode_full, refine_full = unpacked
    sides, grad_flat = ready
    sums, stats, pool_results = coarse
    point_z, point_stats, pool_z, pooled = pool_results
    pool_wide = pool_z
    pool_z = pool_z[None, :images]
    coarse_stats = [point_stats, stats[0], stats[1], stats[2]]
    coarse_z = [
        item.reshape(1, height, columns, channels) for item in (point_z, sums[0], sums[1], sums[2])
    ]
    blocks = [(item_z, valid_coarse) for item_z in coarse_z] + [(pool_z, all_ones)]
    local_images = float(canvases * images)
    states = [(item[0], item[1]) for item in coarse_stats] + [
        local_moments(pool_z, all_ones, local_images),
    ]
    own = [state[item] for item in range(2) for state in states]
    rows = from_all(jnp.concatenate(own + [jnp.full((1,), 1.0) * local_count]))
    width = 5 * channels
    pixels = rows[:, 2 * width :]
    count_rows = jnp.concatenate(
        [
            jnp.broadcast_to(pixels, (rows.shape[0], 4 * channels)),
            jnp.full((rows.shape[0], channels), local_images),
        ],
        axis=1,
    )
    counts_flat, means_flat, squares_flat = merge_rows(
        count_rows, rows[:, :width], rows[:, width : 2 * width]
    )
    vars_flat = squares_flat / counts_flat
    section_means = []
    section_vars = []
    offset = 0
    for width in [channels] * 5:
        section_means.append(means_flat[offset : offset + width])
        section_vars.append(vars_flat[offset : offset + width])
        offset += width
    pixel_count = counts_flat[0]
    fine_count = 16.0 * pixel_count
    gain_rows = [gains[0], gains[1], gains[2], gains[3], gains[4], low_gain]
    bias_rows = [biases[0], biases[1], biases[2], biases[3], biases[4], low_bias]
    kept = []
    activations = []
    for index in range(5):
        block_values, block_valid = blocks[index]
        result = normalize(
            block_values,
            block_valid,
            section_means[index],
            section_vars[index],
            gain_rows[index],
            bias_rows[index],
        )
        kept.append(result[1:])
        activations.append(result[0].astype(jnp.bfloat16))
    spread = jnp.einsum(
        "nwk,nkd->nwd", member_low, activations[4], preferred_element_type=jnp.float32
    ).astype(jnp.bfloat16)
    spread = jnp.broadcast_to(spread[:, None], (canvases, height, columns, channels))
    joined_coarse = jnp.concatenate(activations[:4] + [spread], axis=-1)
    proj_z = jnp.einsum(
        "nhwc,cd->nhwd", joined_coarse, proj_full, preferred_element_type=jnp.float32
    )
    proj_moments = local_moments(proj_z, valid_coarse, local_count)
    joint_mean, joint_var = merged(
        jnp.stack(
            [
                jnp.concatenate([proj_moments[0], low_stats[0, :extra]]),
                jnp.concatenate([proj_moments[1], low_stats[1, :extra] / 16.0]),
            ]
        ),
        local_count,
        pixel_count,
    )
    proj_mean, low_mean = joint_mean[:channels], joint_mean[channels:]
    proj_var, low_var = joint_var[:channels], joint_var[channels:]
    proj_act, proj_centered, proj_shaped, proj_scale = normalize(
        proj_z, valid_coarse, proj_mean, proj_var, gains[5], biases[5]
    )
    proj_act = proj_act.astype(jnp.bfloat16).astype(jnp.float32)
    low_vectors = widen(norm_vectors(low_mean, low_var, low_gain, low_bias))
    devices = device_count()
    decode_z, rows, upsampled = decode_forward(
        proj_act[0],
        up_table,
        low_flat,
        low_wide,
        low_vectors,
        masks,
        decode_full,
        devices,
    )
    decode_rows = hand_out(rows)
    refine_z, rows = refine_forward(decode_z, decode_rows, decode_params, masks, refine_full)
    refine_rows = hand_out(rows)
    logits, rows = classify(
        refine_z, grad_flat, refine_rows, refine_params, tall_masks, w_cls, b_cls.reshape(1, -1)
    )
    logits = logits.reshape(logit_grad.shape)
    refine_sums = hand_out(rows)
    decode_local, rows, refine_totals, refine_kernel_grad = refine_backward(
        refine_z,
        grad_flat,
        refine_rows,
        refine_sums,
        refine_params,
        w_cls,
        decode_z,
        decode_rows,
        decode_params,
        masks,
        refine_full,
    )
    decode_sums = hand_out(rows)
    classes = w_cls.shape[1]
    cls_weight_grad = decode_sums[:classes, 2 * channels :].T
    cls_bias_grad = decode_sums[classes, 2 * channels : 2 * channels + classes]
    refine_gain, refine_bias = refine_totals[6], refine_totals[7]
    (
        proj_up,
        reduce_local,
        reduce_sums,
        decode_totals,
        decode_kernel_grad,
        low_kernel_grad,
    ) = decode_backward(
        decode_local,
        decode_z,
        decode_rows,
        decode_sums,
        decode_params,
        upsampled,
        low_flat,
        low_wide,
        low_vectors,
        down_table,
        masks,
        decode_full,
        coarse_shape,
    )
    decode_gain, decode_bias = decode_totals[6], decode_totals[7]
    proj_up = proj_up[None]
    reduce_gain, reduce_bias = reduce_sums[0, :extra], reduce_sums[1, :extra]

    proj_local, proj_gain, proj_bias = norm_grad_terms(
        proj_up, valid_coarse, proj_centered, proj_shaped
    )
    summed_pairs = gradient_sums([(proj_gain, proj_bias), (reduce_gain, reduce_bias)])
    proj_gain, proj_bias = summed_pairs[0]
    reduce_gain, reduce_bias = summed_pairs[1]
    flat_z = [item.reshape(height * columns, channels) for item in coarse_z]
    branch_vectors = jnp.concatenate(
        [
            norm_vectors(section_means[index], section_vars[index], gains[index], biases[index])
            for index in range(5)
        ],
        axis=1,
    )
    branch_counts = jnp.concatenate(
        [
            jnp.full((1, 4 * channels), 1.0) * pixel_count,
            jnp.full((1, channels), images_total, jnp.float32),
        ],
        axis=1,
    )
    proj_kernel_grad, branch_local, pool_local, rows = branch_back(
        proj_up.reshape(height * columns, channels),
        proj_z.reshape(height * columns, channels),
        norm_vectors(
            proj_mean,
            proj_var,
            gains[5],
            biases[5],
            proj_gain / pixel_count,
            proj_bias / pixel_count,
        ),
        joined_coarse.reshape(height * columns, -1),
        proj_full,
        flat_z,
        pool_wide,
        branch_vectors,
        mask_column,
        pool_mask,
        pool_inputs[0],
        devices,
    )
    rows = hand_out(rows)
    branch_dz = branch_grads(
        rows,
        branch_local,
        pool_local,
        flat_z,
        pool_wide,
        branch_vectors,
        branch_counts,
        mask_column,
        pool_mask,
    )
    flat_dz, pool_dz, branch_totals = list(branch_dz[:4]), branch_dz[4], branch_dz[5]
    last_pairs = [
        (
            branch_totals[0, index * channels : (index + 1) * channels],
            branch_totals[1, index * channels : (index + 1) * channels],
        )
        for index in range(5)
    ]
    low_vectors = widen(
        norm_vectors(
            low_mean,
            low_var,
            low_gain,
            low_bias,
            reduce_gain / fine_count,
            reduce_bias / fine_count,
        )
    )

    def low_late(tie):
        return low_backward(reduce_local, low_flat, low_wide, low_vectors, tall_masks, tie)

    def input_late(tie):
        side_dz = [
            side_grads(
                flat_dz[branch + 1].reshape(1, height, columns, channels),
                ids_coarse,
                dilations[branch],
            ).reshape(height * columns, -1)
            for branch in range(3)
        ]
        return coarse_input(
            flat_dz[0],
            pool_dz,
            spread_rows,
            side_dz,
            parts,
            coarse_shape,
            features.shape[3],
            tie,
        )

    def weight_part(part, grads, tie=None):
        return coarse_weight(
            part,
            sides,
            grads[1:4],
            coarse_shape,
            (grads[0], pooled, grads[4]) if SCATTER.has_point(part) else None,
            tie,
        )

    owned, small_owned, low_level_grad, features_grad = scatter_taps(
        flat_dz + [pool_dz],
        [item.shape for item in small],
        [functools.partial(weight_part, part) for part in range(len(SCATTER.parts))],
        (proj_kernel_grad, decode_kernel_grad, low_kernel_grad, refine_kernel_grad),
        [low_late, input_late],
    )
    low_level_grad = low_level_grad.reshape(low_level.shape)
    features_grad = features_grad.reshape(features.shape)
    proj_owned, reduce_owned, decode_owned, refine_owned = small_owned
    point_owned, atrous_owned = SCATTER.restore(owned, w_atrous.shape)
    gains_grad = jnp.stack(
        [
            last_pairs[0][0],
            last_pairs[1][0],
            last_pairs[2][0],
            last_pairs[3][0],
            last_pairs[4][0],
            proj_gain,
            decode_gain,
            refine_gain,
        ]
    )
    biases_grad = jnp.stack(
        [
            last_pairs[0][1],
            last_pairs[1][1],
            last_pairs[2][1],
            last_pairs[3][1],
            last_pairs[4][1],
            proj_bias,
            decode_bias,
            refine_bias,
        ]
    )
    return (
        logits,
        features_grad,
        low_level_grad,
        point_owned,
        atrous_owned,
        proj_owned,
        reduce_owned,
        decode_owned,
        refine_owned,
        cls_weight_grad,
        cls_bias_grad,
        gains_grad,
        biases_grad,
        reduce_gain,
        reduce_bias,
    )


def solution(mesh):
    in_specs = (
        P(("wide", "narrow"), None, None, None),
        P(("wide", "narrow"), None, None, None),
        P(("wide", "narrow"), None),
        P(None, "wide", "narrow"),
        P(None, None, "wide", "narrow"),
        P("wide", "narrow"),
        P("wide", "narrow"),
        P(None, "narrow", "wide"),
        P(None, "wide", "narrow"),
        P(),
        P(),
        P(),
        P(),
        P(),
        P(),
        P(("wide", "narrow"), None, None, None),
    )
    out_specs = (
        P(("wide", "narrow"), None, None, None),
        P(("wide", "narrow"), None, None, None),
        P(("wide", "narrow"), None, None, None),
        P(None, "wide", "narrow"),
        P(None, None, "wide", "narrow"),
        P("wide", "narrow"),
        P("wide", "narrow"),
        P(None, "narrow", "wide"),
        P(None, "wide", "narrow"),
        P(),
        P(),
        P(),
        P(),
        P(),
        P(),
    )
    return jax.shard_map(
        per_device, mesh=mesh, in_specs=in_specs, out_specs=out_specs, check_vma=False
    )
```
